32 devices in a mesh: seq: 8 (over z, y), head: 4 (over x, core).
Axes of the slice: x: 2, y: 2, z: 4, core: 2. Of those that a mesh axis runs over, the one named last changes fastest.
Arguments:
- tokens: bfloat16 [16384, 512], P(('seq', 'head')), may hold values from -6 to 6
- lengths: int32 [3], replicated, may hold values from 512 to 14336, as said below
- feature_seed: int32 [1], replicated, may hold values from 0 to 1048575
- norm_gain: bfloat16 [512], P('seq'), may hold values from 0.5 to 1.5
- norm_shift: bfloat16 [512], P('seq'), may hold values from -1.5 to 1.5
- query_weight: bfloat16 [512, 512], P('seq', 'head'), may hold values from -0.25 to 0.25
- key_weight: bfloat16 [512, 512], P('seq', 'head'), may hold values from -0.25 to 0.25
- value_weight: bfloat16 [512, 512], P('seq', 'head'), may hold values from -0.25 to 0.25
- gate_weight: bfloat16 [512, 8], P('seq', 'head'), may hold values from -0.25 to 0.25
- gate_bias: float32 [8], P('head'), may hold values from 3.5 to 14
- out_weight: bfloat16 [512, 512], P('head', 'seq'), may hold values from -0.75 to 0.75
- ffn_gain: bfloat16 [512], P('seq'), may hold values from 0.5 to 1.5
- ffn_shift: bfloat16 [512], P('seq'), may hold values from -1.5 to 1.5
- up_weight: bfloat16 [512, 2048], P('seq', 'head'), may hold values from -0.25 to 0.25
- down_weight: bfloat16 [2048, 512], P('head', 'seq'), may hold values from -0.125 to 0.125
- cotangent: bfloat16 [16384, 512], P(('seq', 'head')), may hold values from -6 to 6
Outputs:
- result: bfloat16 [16384, 512], P(('seq', 'head'))
- grad_tokens: float32 [16384, 512], P(('seq', 'head'))
- grad_norm_gain: float32 [512], P('seq')
- grad_norm_shift: float32 [512], P('seq')
- grad_query_weight: float32 [512, 512], P('seq', 'head')
- grad_key_weight: float32 [512, 512], P('seq', 'head')
- grad_value_weight: float32 [512, 512], P('seq', 'head')
- grad_gate_weight: float32 [512, 8], P('seq', 'head')
- grad_gate_bias: float32 [8], P('head')
- grad_out_weight: float32 [512, 512], P('head', 'seq')
- grad_ffn_gain: float32 [512], P('seq')
- grad_ffn_shift: float32 [512], P('seq')
- grad_up_weight: float32 [512, 2048], P('seq', 'head')
- grad_down_weight: float32 [2048, 512], P('head', 'seq')
The draws below stay inside these ranges and needn't reach their ends.
Inputs may be any that keep to these rules, and one draw needn't show every extreme that they name: `lengths`: the documents lie end to end from the first token; the tokens from filled on are padding, at least two. Two entries are sentences of 512 to 1023 tokens; the other, second or third in the list, is one document of exactly 14336 tokens, which begins among the first 2048 tokens and ends among the last 2048.
All inputs are finite; a program needn't handle non-finite values.
Results may differ from the reference program's by a relative error of at most 0.02.
The reference program's roundings to bfloat16 on the way count: a program that leaves them out, or rounds other values in their place, can miss the bound.
Values may be sent and summed in bfloat16 or wider, within the bound.
A program may use at most 128 MiB of HBM per device.

```python
import math
import jax
import jax.numpy as jnp
from jax import lax

D = 512
HEADS = 8
HEAD_DIM = 64
FEATS = 128
FF = 2048
TOK_DEV = 2048
DOCS = 3
TOKENS = 16384


def draw_lengths(key, part):
    key = jax.random.fold_in(key, 7)
    key_short, key_pick = jax.random.split(key, 2)
    shorts = jax.random.randint(key_short, (DOCS,), TOK_DEV // 4, TOK_DEV // 2)
    chosen = jax.random.randint(key_pick, (), 1, DOCS)
    places = jnp.arange(DOCS)
    longest = TOKENS - TOK_DEV
    return jnp.where(places == chosen, longest, shorts).astype(jnp.int32)


def level_of(rng, shape, cuts, low, largest):
    level = 1.0
    for dim, blocks in cuts:
        steps = jax.random.uniform(jax.random.fold_in(jax.random.fold_in(rng, 6), dim), (blocks,), jnp.float32, low / len(cuts), largest / len(cuts))
        level = level * jnp.repeat(jnp.exp(steps), shape[dim] // blocks).reshape((-1,) + (1,) * (len(shape) - 1 - dim))
    return level


def centred(rng, extent, scale, limit, cuts=(), kind=jnp.bfloat16):
    loudness = level_of(rng, extent, cuts, -0.22, 0.18) if cuts else 1.0
    values = jax.random.normal(rng, extent, jnp.float32) * scale * loudness
    return jnp.minimum(jnp.maximum(values, -limit), limit).astype(kind)


def setup_inputs(seed: int = 0) -> dict:
    key_of = jax.random.split(jax.random.key(seed), 17)
    tokens = centred(key_of[0], (TOKENS, D), 1.0, 6.0, ((0, 32),))
    lengths = draw_lengths(jax.random.fold_in(key_of[16], 71), 0)
    feature_seed = jax.random.randint(key_of[2], (1,), 0, 1048576).astype(jnp.int32)
    norm_gain = jnp.clip(1.0 + 0.1 * jax.random.normal(key_of[3], (D,), jnp.float32), 0.5, 1.5).astype(jnp.bfloat16)
    norm_shift = centred(key_of[4], (D,), 0.3, 1.5, ((0, 8),))
    query_weight = centred(key_of[5], (D, D), D ** -0.5, 0.25, ((0, 8), (1, 4)))
    key_weight = centred(key_of[6], (D, D), D ** -0.5, 0.25, ((0, 8), (1, 4)))
    value_weight = centred(key_of[7], (D, D), D ** -0.5, 0.25, ((0, 8), (1, 4)))
    gate_weight = centred(key_of[8], (D, HEADS), D ** -0.5, 0.25, ((0, 8), (1, 4)))
    gate_bias = jnp.clip(3.5 + 10.5 * jax.random.uniform(key_of[9], (HEADS,), jnp.float32) ** level_of(key_of[9], (HEADS,), ((0, 4),), -0.2, 0.2), 3.5, 14.0)
    out_weight = centred(key_of[10], (D, D), (D // 8) ** -0.5, 0.75, ((0, 4), (1, 8)))
    ffn_gain = jnp.clip(1.0 + 0.1 * jax.random.normal(key_of[11], (D,), jnp.float32), 0.5, 1.5).astype(jnp.bfloat16)
    ffn_shift = centred(key_of[12], (D,), 0.3, 1.5, ((0, 8),))
    up_weight = centred(key_of[13], (D, FF), D ** -0.5, 0.25, ((0, 8), (1, 4)))
    down_weight = centred(key_of[14], (FF, D), FF ** -0.5, 0.125, ((0, 4), (1, 8)))
    cotangent = centred(key_of[15], (TOKENS, D), 1.0, 6.0, ((0, 32),))
    return {"tokens": tokens, "lengths": lengths, "feature_seed": feature_seed, "norm_gain": norm_gain, "norm_shift": norm_shift, "query_weight": query_weight, "key_weight": key_weight, "value_weight": value_weight, "gate_weight": gate_weight, "gate_bias": gate_bias, "out_weight": out_weight, "ffn_gain": ffn_gain, "ffn_shift": ffn_shift, "up_weight": up_weight, "down_weight": down_weight, "cotangent": cotangent}


@jax.custom_vjp
def low(v):
    return lax.optimization_barrier(v.astype(jnp.bfloat16)).astype(jnp.float32)

@jax.custom_vjp
def low_back(v):
    return v

def low_keep(v):
    return (low(v), None)

def low_pass(kept, grad):
    return (grad,)

def back_keep(v):
    return (v, None)

def back_low(kept, grad):
    return (low(grad),)
low.defvjp(low_keep, low_pass)
low_back.defvjp(back_keep, back_low)
eps = 1e-05
den_floor = 0.25
gate_pen = 0.5
highest = lax.Precision.HIGHEST

def gauss_table(feature_seed, entries):
    positions = jnp.arange(entries, dtype=jnp.int32)
    hashed = positions * jnp.int32(-1640531535) + feature_seed[0].astype(jnp.int32) * jnp.int32(-2048144789)
    hashed = hashed ^ lax.shift_right_logical(hashed, jnp.int32(15))
    hashed = hashed * jnp.int32(739982445)
    hashed = hashed ^ lax.shift_right_logical(hashed, jnp.int32(13))
    hashed = hashed * jnp.int32(695872825)
    hashed = hashed ^ lax.shift_right_logical(hashed, jnp.int32(16))
    summed = jnp.zeros((entries,), jnp.int32)
    for shift_step in range(4):
        summed = summed + (lax.shift_right_logical(hashed, jnp.int32(8 * shift_step)) & jnp.int32(255))
    return (summed.astype(jnp.float32) - 510.0) / math.sqrt(21845.0)

def layer_norm(values, gain, shift):
    center = lax.optimization_barrier(jnp.mean(values, axis=-1, keepdims=True))
    spread = lax.optimization_barrier(jnp.mean(values * values, axis=-1, keepdims=True)) - center * center
    return (values - center) * lax.rsqrt(spread + eps) * gain + shift

def features(vectors, table):
    scaled = vectors * lax.rsqrt(lax.optimization_barrier(jnp.sum(vectors * vectors, axis=-1, keepdims=True)) + 1e-06)
    angles = jnp.einsum('nhe,hef->nhf', scaled, table, precision=highest)
    return jnp.concatenate([jnp.sin(angles), jnp.cos(angles)], axis=-1) / math.sqrt(table.shape[-1])

def token_marks(lengths, offset, amount):
    positions = offset + jnp.arange(amount, dtype=jnp.int32)
    starts = (jnp.cumsum(lengths) - lengths).astype(jnp.int32)
    filled = jnp.sum(lengths).astype(jnp.int32)
    segment = lax.optimization_barrier(jnp.sum((positions[:, None] >= starts[None, :]).astype(jnp.int32), axis=1)) + (positions >= filled).astype(jnp.int32)
    resets = jnp.any(positions[:, None] == starts[None, :], axis=1).astype(jnp.int32)
    live_mask = (positions < filled).astype(jnp.float32)
    return (segment, resets, live_mask)

def block_step(state_pair, inputs):
    memory, normal = state_pair
    query_feat, key_feat, values, log_decay, segment, resets, live_mask = inputs
    block_len = log_decay.shape[0]
    log_run = jnp.cumsum(log_decay, axis=0)
    carry_flag = (jnp.cumsum(resets) == 0).astype(jnp.float32)
    log_gap = jnp.minimum(log_run[:, None, :] - log_run[None, :, :], 0.0)
    places = jnp.arange(block_len)
    linked = ((segment[:, None] == segment[None, :]) & (places[None, :] <= places[:, None])).astype(jnp.float32)
    weights = jnp.einsum('ihm,shm->ish', query_feat, key_feat, precision=highest) * jnp.exp(log_gap) * (linked * live_mask[None, :])[:, :, None]
    carried = jnp.exp(log_run) * carry_flag[:, None]
    numerator = jnp.einsum('ish,she->ihe', low(weights), values, precision=highest)
    numerator = numerator + carried[:, :, None] * jnp.einsum('ihm,hme->ihe', query_feat, memory, precision=highest)
    norm_sum = lax.optimization_barrier(jnp.sum(weights, axis=1)) + carried * jnp.einsum('ihm,hm->ih', query_feat, normal, precision=highest)
    to_end = jnp.exp(log_run[-1][None, :] - log_run) * ((segment == segment[-1]).astype(jnp.float32) * live_mask)[:, None]
    memory = carried[-1][:, None, None] * memory + jnp.einsum('shm,she->hme', low(key_feat * to_end[:, :, None]), values, precision=highest)
    normal = carried[-1][:, None] * normal + jnp.einsum('shm,sh->hm', key_feat, to_end, precision=highest)
    return ((memory, normal), (numerator, norm_sum))

def layer_forward(tokens, norm_gain, norm_shift, query_weight, key_weight, value_weight, gate_weight, gate_bias, out_weight, ffn_gain, ffn_shift, up_weight, down_weight, table, segment, resets, live_mask, pen_scale):
    rows_all = tokens.shape[0]
    block_len = min(512, TOK_DEV)
    blocks = rows_all // block_len
    normed = low(layer_norm(tokens, norm_gain, norm_shift))
    queries = low(low_back(jnp.dot(normed, query_weight, precision=highest)))
    keys_all = low(low_back(jnp.dot(normed, key_weight, precision=highest)))
    values = low(low_back(jnp.dot(normed, value_weight, precision=highest)))
    logits = jnp.dot(normed, gate_weight, precision=highest) + gate_bias
    log_decay = -jax.nn.softplus(-logits) * (live_mask * (1 - resets))[:, None]
    query_feat = low(features(queries.reshape(rows_all, HEADS, HEAD_DIM), table))
    key_feat = low(features(keys_all.reshape(rows_all, HEADS, HEAD_DIM), table))

    def blocked(array):
        return array.reshape((blocks, block_len) + array.shape[1:])
    start = (jnp.zeros((HEADS, 2 * FEATS, HEAD_DIM), jnp.float32), jnp.zeros((HEADS, 2 * FEATS), jnp.float32))
    xs = (blocked(query_feat), blocked(key_feat), blocked(values.reshape(rows_all, HEADS, HEAD_DIM)), blocked(log_decay), blocked(segment), blocked(resets), blocked(live_mask))
    final_pair, (numerator, norm_sum) = lax.scan(jax.checkpoint(block_step), start, xs)
    numerator = numerator.reshape(rows_all, HEADS, HEAD_DIM)
    norm_sum = norm_sum.reshape(rows_all, HEADS)
    attended = live_mask[:, None, None] * numerator / jnp.sqrt(norm_sum * norm_sum + den_floor ** 2)[:, :, None]
    attended = low(low_back(attended.reshape(rows_all, HEADS * HEAD_DIM)))
    branch = low_back(jnp.dot(attended, out_weight, precision=highest))
    middle = tokens + branch
    normed_two = low(layer_norm(middle, ffn_gain, ffn_shift))
    hidden = low_back(jnp.dot(normed_two, up_weight, precision=highest))
    active = low(jax.nn.gelu(hidden, approximate=False))
    result = middle + jnp.dot(active, down_weight, precision=highest)
    penalty = pen_scale * jnp.sum(jax.nn.sigmoid(logits) * live_mask[:, None]) / HEADS
    return (result, penalty)

def reference(tokens, lengths, feature_seed, norm_gain, norm_shift, query_weight, key_weight, value_weight, gate_weight, gate_bias, out_weight, ffn_gain, ffn_shift, up_weight, down_weight, cotangent):
    table = gauss_table(feature_seed, HEADS * HEAD_DIM * FEATS).reshape(HEADS, HEAD_DIM, FEATS)
    segment, resets, live_mask = token_marks(lengths, 0, TOKENS)
    pen_scale = gate_pen * TOKENS / jnp.sum(lengths).astype(jnp.float32)
    params = tuple((member.astype(jnp.float32) for member in (tokens, norm_gain, norm_shift, query_weight, key_weight, value_weight, gate_weight, gate_bias, out_weight, ffn_gain, ffn_shift, up_weight, down_weight)))

    def forward(*weights):
        return layer_forward(*weights, table, segment, resets, live_mask, pen_scale)
    (result, penalty), pullback = jax.vjp(forward, *params)
    grads = pullback((cotangent.astype(jnp.float32), jnp.ones_like(penalty)))
    return (result.astype(jnp.bfloat16), grads[0], grads[1], grads[2], grads[3], grads[4], grads[5], grads[6], grads[7], grads[8], grads[9], grads[10], grads[11], grads[12])
```

```python
import functools
import math

import jax
import jax.numpy as jnp
from jax import lax
from jax.experimental import pallas as pl
from jax.experimental.pallas import tpu as pltpu
from jax.sharding import PartitionSpec as P

BF, F32, I32 = jnp.bfloat16, jnp.float32, jnp.int32
MESH = pl.DeviceIdType.MESH
HEADS, HEAD_DIM, FEATS = 8, 64, 128
PAIRS = HEADS // 2
LANES = 128
EPS, FLOOR2, GATE_PEN = 1e-5, 0.0625, 0.5
TABLE_SCALE = 1.0 / math.sqrt(21845.0)
FEAT_SCALE = 1.0 / math.sqrt(FEATS)
INV_TWO_PI, TWO_PI = 1.0 / (2.0 * math.pi), 2.0 * math.pi
SIN = (0.9999996027571254, -0.16666553170295112, 0.008332405799301931, -0.00019808693226998236,
       2.6997700314773084e-06, -2.036409109746239e-08)
COS = (0.9999992193982472, -0.4999942543676011, 0.04165980908449851, -0.0013858873219640337,
       2.420384320646774e-05, -2.1976364824224383e-07)
ERFC = (0.254829592, -0.284496736, 1.421413741, -1.453152027, 1.061405429)
ATT = 4 * LANES
VMEM_BYTES = 56 * 1024 * 1024


def nn(a, b):
    return lax.dot_general(a, b, (((1,), (0,)), ((), ())), preferred_element_type=F32)


def nt(a, b):
    return lax.dot_general(a, b, (((1,), (1,)), ((), ())), preferred_element_type=F32)


def tn(a, b):
    return lax.dot_general(a, b, (((0,), (0,)), ((), ())), preferred_element_type=F32)


def halves(x, axis=1):
    hi = x.astype(BF)
    return jnp.concatenate([hi, (x - hi.astype(F32)).astype(BF)], axis=axis)


def iota(shape, dim):
    return lax.broadcasted_iota(I32, shape, dim)


def rows_loop(total, step, body):
    step = min(step, total)

    def one(i, carry):
        body(pl.ds(pl.multiple_of(i * step, step), step), i * step, step)
        return carry

    lax.fori_loop(0, total // step, one, 0)


def pair_loop(body):
    def one(p, carry):
        body(p)
        return carry

    lax.fori_loop(0, PAIRS, one, 0)


def head_ones(rows, cols, row_span, col_span):
    same = (iota((rows, cols), 0) // row_span) % 2 == iota((rows, cols), 1) // col_span
    return jnp.where(same, 1.0, 0.0).astype(BF)


def marks(pos, base, lengths_ref):
    start = jnp.int32(0)
    segment = jnp.zeros(pos.shape, I32)
    reset = jnp.zeros(pos.shape, F32)
    carry = jnp.ones(pos.shape, F32)
    for d in range(lengths_ref.shape[0]):
        segment = segment + jnp.where(pos >= start, 1, 0)
        reset = jnp.where(pos == start, 1.0, reset)
        carry = jnp.where((pos >= start) & (pos - start <= pos - base), 0.0, carry)
        start = start + lengths_ref[d]
    live = jnp.where(pos < start, 1.0, 0.0)
    segment = segment + jnp.where(pos >= start, 1, 0)
    return segment, reset, live, carry, start


def horner(coefs, t):
    acc = jnp.full_like(t, coefs[-1])
    for c in coefs[-2::-1]:
        acc = acc * t + c
    return acc


def sincos(angle):
    r = angle - jnp.round(angle * INV_TWO_PI) * TWO_PI
    t = r * r
    return r * horner([c * FEAT_SCALE for c in SIN], t), horner([c * FEAT_SCALE for c in COS], t)


def gelu_parts(x):
    t = 1.0 / (1.0 + (0.3275911 / math.sqrt(2.0)) * jnp.abs(x))
    e = jnp.exp(-0.5 * x * x)
    q = 0.5 * t * horner(ERFC, t) * e
    cdf = jnp.where(x < 0.0, q, 1.0 - q)
    return x * cdf, cdf + x * e * (1.0 / math.sqrt(2.0 * math.pi))


def norm_stats(x):
    center = jnp.mean(x, axis=-1, keepdims=True)
    spread = jnp.mean(x * x, axis=-1, keepdims=True) - center * center
    inv = lax.rsqrt(spread + EPS)
    return (x - center) * inv, inv


def norm_back(grad, xhat, inv, gain):
    p = grad * gain
    return inv * (p - jnp.mean(p, axis=-1, keepdims=True) - xhat * jnp.mean(p * xhat, axis=-1, keepdims=True))


def by_eight(x):
    return jnp.sum(x.reshape(x.shape[0] // 8, 8, x.shape[1]), axis=0)


def panel(ref, p, cols):
    x = ref[p, :, :, :, cols]
    return x.reshape(x.shape[0] * x.shape[1] * x.shape[2], x.shape[3])


def low_lanes(rows):
    return iota((rows, LANES), 1) < HEAD_DIM


def widen(pair, a):
    return pair[:, a * HEAD_DIM : a * HEAD_DIM + 1]


def head_values(v, a, low):
    one = jnp.ones_like(v)
    return jnp.where(low, v, one) if a == 0 else jnp.where(low, one, v)


def state_of(mem, nrm, p, a):
    own = mem[p, a * HEAD_DIM : (a + 1) * HEAD_DIM, :]
    rest = jnp.broadcast_to(nrm[pl.ds(2 * p + a, 1), :], own.shape).astype(BF)
    return jnp.concatenate([own, rest] if a == 0 else [rest, own], axis=0)


def front(T, base, r):
    D = r.tok.shape[1]
    pick = jnp.where(iota((16, LANES), 0) == iota((16, LANES), 1), 1.0, 0.0).astype(BF)
    for p in range(PAIRS):
        rows = nt(pick, panel(r.ga, p, slice(3 * LANES, 4 * LANES)))
        r.gate[2 * p : 2 * p + 2, :] = rows[0:2]
        r.gate[8 + 2 * p : 10 + 2 * p, :] = rows[0:2]
        r.bias[2 * p : 2 * p + 1, :] = rows[6:7] + rows[7:8] + rows[8:9]
        r.bias[2 * p + 1 : 2 * p + 2, :] = rows[9:10] + rows[10:11] + rows[11:12]
        if p == 0:
            r.vec[...] = rows[0:8]

    def norm_rows(rows, at, n):
        xhat, _ = norm_stats(r.tok[rows, :].astype(F32))
        r.normed[rows, :] = (xhat * r.vec[2:3, :] + r.vec[3:4, :]).astype(BF)

    rows_loop(T, 64, norm_rows)

    logits = nt(r.gate[...].astype(BF), r.normed[...])[0:8] + r.bias[:, 0:1]
    r.logits[...] = logits
    pos = base + iota((8, T), 1)
    seg_row, reset_row, live_row, carry_row, _ = marks(pos, base, r.lengths)
    decay = -(jnp.log1p(jnp.exp(-jnp.abs(logits))) + jnp.maximum(-logits, 0.0)) * live_row * (1.0 - reset_row)
    run = decay
    lane = iota((8, T), 1)
    shift = 1
    while shift < T:
        run = run + jnp.where(lane >= shift, pltpu.roll(run, shift, 1), 0.0)
        shift *= 2
    r.run[...] = run
    r.total[...] = jnp.broadcast_to(jnp.exp(run[:, T - 1 : T]) * carry_row[:, T - 1 : T], (8, LANES))
    hi = run.astype(BF).astype(F32)
    mid = (run - hi).astype(BF).astype(F32)
    low3 = run - hi - mid
    run3 = jnp.concatenate([hi, mid, low3, jnp.zeros_like(hi)], axis=0).astype(BF)

    def mask_rows(rows, at, n):
        row_pos = base + at + iota((n, 1), 0)
        seg_col = marks(row_pos, base, r.lengths)[0]
        seg1, live1, pos1 = seg_row[0:1], live_row[0:1], pos[0:1]
        allowed = (seg_col == seg1) & (pos1 <= row_pos) & (live1 > 0.0)
        r.mask[rows, :] = jnp.where(allowed, 0.0, -1e30)

    rows_loop(T, 64, mask_rows)

    hash_seed = r.seed[0] * jnp.int32(-2048144789)
    ones2 = head_ones(2 * LANES, 2 * LANES, HEAD_DIM, LANES)
    low = low_lanes(T)
    last_seg = marks(base + T - 1 + iota((8, LANES), 1) * 0, base, r.lengths)[0][0:1, 0:1]
    col_pos = base + iota((T, LANES), 0)
    seg_col, _, live_col, _, _ = marks(col_pos, base, r.lengths)
    end_live = jnp.where(seg_col == last_seg, live_col, 0.0)

    def features(p, u, out):
        r.s1[...] = nn(jnp.concatenate([u, u], axis=1), r.tab[p])
        uf = u.astype(F32)
        r.s2[...] = nn(halves(uf * uf), ones2)

        def body(rows, at, n):
            s, c = sincos(r.s1[rows, :] * (lax.rsqrt(r.s2[rows, :] + 1e-6) * TABLE_SCALE))
            for a in range(2):
                out[2 * p + a, rows, 0:FEATS] = s[:, a * FEATS : (a + 1) * FEATS].astype(BF)
                out[2 * p + a, rows, FEATS : 2 * FEATS] = c[:, a * FEATS : (a + 1) * FEATS].astype(BF)

        rows_loop(T, 64, body)

    def first(p):
        place = (p * LANES + iota((LANES, LANES), 0)) * FEATS + iota((LANES, LANES), 1)
        y = place * jnp.int32(-1640531535) + hash_seed
        y = y ^ lax.shift_right_logical(y, jnp.int32(15))
        y = y * jnp.int32(739982445)
        y = y ^ lax.shift_right_logical(y, jnp.int32(13))
        y = y * jnp.int32(695872825)
        y = y ^ lax.shift_right_logical(y, jnp.int32(16))
        s = jnp.full(y.shape, -510, I32)
        for k in range(4):
            s = s + (lax.shift_right_logical(y, jnp.int32(8 * k)) & jnp.int32(255))
        top = iota((LANES, LANES), 0) < HEAD_DIM
        odd = s & 1

        def diagonal(x):
            x = x.astype(F32)
            return jnp.concatenate([jnp.where(top, x, 0.0), jnp.where(top, 0.0, x)], axis=1).astype(BF)

        r.tab[p, 0:LANES, :] = diagonal(s - odd)
        r.tab[p, LANES:, :] = diagonal(odd)
        r.tabn[p] = diagonal(s)
        qkv = nn(r.normed[...], panel(r.ga, p, slice(0, 3 * LANES))).astype(BF)
        r.q[p] = qkv[:, 0:LANES]
        r.k[p] = qkv[:, LANES : 2 * LANES]
        r.v[p] = qkv[:, 2 * LANES :]
        chosen = iota((32, LANES), 0) % 8 == 2 * p + iota((32, LANES), 1) // HEAD_DIM
        r.rb[p] = tn(run3, jnp.where(chosen, 1.0, 0.0).astype(BF))

        features(p, r.k[p], r.kf)
        decay_end = jnp.exp(r.rb[p, T - 1 : T, :] - r.rb[p]) * end_live
        v = r.v[p].astype(F32)
        for a in range(2):
            scaled = (head_values(v, a, low) * widen(decay_end, a)).astype(BF)
            state = tn(scaled, r.kf[2 * p + a])
            r.mem[p, a * HEAD_DIM : (a + 1) * HEAD_DIM, :] = state[a * HEAD_DIM : (a + 1) * HEAD_DIM].astype(BF)
            at = HEAD_DIM if a == 0 else 0
            r.nrm32[pl.ds(2 * p + a, 1), :] = state[at : at + 1]

    r.nrm32[...] = jnp.zeros_like(r.nrm32)
    pair_loop(first)
    r.nrm[...] = r.nrm32[...].astype(BF)

    def second(p):
        features(p, r.q[p], r.qf)
        v = r.v[p]
        for a in range(2):
            h = 2 * p + a
            r.s[...] = nt(r.qf[h], r.kf[h])
            run_row = r.run[pl.ds(h, 1), :]

            def body(rows, at, n):
                gap = jnp.minimum(widen(r.rb[p, rows, :], a) - run_row, r.mask[rows, :])
                r.w[h, rows, :] = (r.s[rows, :] * jnp.exp(gap)).astype(BF)

            rows_loop(T, 64, body)
            r.own[h] = nn(r.w[h], head_values(v, a, low))

    pair_loop(second)


def middle(T, base, r):
    D = r.tok.shape[1]
    low = low_lanes(T)
    col_pos = base + iota((T, LANES), 0)
    _, _, live_col, carry_col, _ = marks(col_pos, base, r.lengths)
    r.nin32[...] = r.nin[...].astype(F32)

    def join(p):
        factor = jnp.exp(r.rb[p]) * carry_col
        total = []
        for a in range(2):
            h = 2 * p + a
            carried = nt(r.qf[h], state_of(r.min, r.nin32, p, a))
            joined = r.own[h] + widen(factor, a) * carried
            r.joined[h] = joined
            total.append(joined)
        num = jnp.where(low, total[0], total[1])
        z = pltpu.roll(jnp.where(low, total[1], total[0]), HEAD_DIM, 1)
        r.num[p] = num
        r.z[p] = z
        r.att[p] = (live_col * num * lax.rsqrt(z * z + FLOOR2)).astype(BF)

    pair_loop(join)
    o = slice(0, LANES)
    branch = None
    for p in range(0, PAIRS, 2):
        part = nt(
            jnp.concatenate([r.att[p], r.att[p + 1]], axis=1),
            jnp.concatenate([panel(r.gf, p, o), panel(r.gf, p + 1, o)], axis=1),
        )
        branch = part if branch is None else branch + part
    r.mid[...] = branch

    def norm_rows(rows, at, n):
        mid = r.mid[rows, :] + r.tok[rows, :].astype(F32)
        r.mid[rows, :] = mid
        xhat, inv = norm_stats(mid)
        r.xhat[rows, :] = xhat
        r.inv[rows, :] = jnp.broadcast_to(inv, (n, LANES))
        r.two[rows, :] = (xhat * r.vec[4:5, :] + r.vec[5:6, :]).astype(BF)

    rows_loop(T, 64, norm_rows)
    r.acc1[...] = jnp.zeros_like(r.acc1)
    r.acc2[...] = jnp.zeros_like(r.acc2)
    ff = (r.gf.shape[-1] - LANES) // 2
    u, d = slice(LANES, LANES + ff), slice(LANES + ff, LANES + 2 * ff)

    def feed(p):
        up, down = panel(r.gf, p, u), panel(r.gf, p, d)
        r.h1[...] = nn(r.two[...], up)
        r.h2[...] = nn(r.cot[...], down)

        def body(rows, at, n):
            value, slope = gelu_parts(r.h1[rows, :])
            r.act[rows, :] = value.astype(BF)
            r.gh[rows, :] = (r.h2[rows, :] * slope).astype(BF)

        rows_loop(T, 64, body)
        r.acc1[...] += nt(r.act[...], down)
        r.acc2[...] += nt(r.gh[...], up)
        put_panel(r.ggf, p, u, tn(r.two[...], r.gh[...]))
        put_panel(r.ggf, p, d, tn(r.cot[...], r.act[...]))

    pair_loop(feed)
    r.sums[...] = jnp.zeros_like(r.sums)

    def finish(rows, at, n):
        r.result[rows, :] = (r.mid[rows, :] + r.acc1[rows, :]).astype(BF)
        xhat, gn = r.xhat[rows, :], r.acc2[rows, :]
        r.sums[0:8, :] += by_eight(gn * xhat)
        r.sums[8:16, :] += by_eight(gn)
        back = norm_back(gn, xhat, r.inv[rows, 0:1], r.vec[4:5, :])
        grad = r.cot[rows, :].astype(F32) + back
        r.gmid[rows, :] = grad
        r.gb[rows, :] = grad.astype(BF)

    rows_loop(T, 64, finish)
    r.fsum[0:1, :] = jnp.sum(r.sums[0:8, :], axis=0, keepdims=True)
    r.fsum[1:2, :] = jnp.sum(r.sums[8:16, :], axis=0, keepdims=True)
    ones1 = head_ones(2 * LANES, LANES, HEAD_DIM, HEAD_DIM)
    row_ones = jnp.ones((16, 2 * LANES), BF)
    first_half = iota((T, LANES), 1) % HEAD_DIM < HEAD_DIM // 2
    r.bn32[...] = jnp.zeros_like(r.bn32)

    def back(p):
        put_panel(r.ggf, p, o, tn(r.gb[...], r.att[p]))
        g = nn(r.gb[...], panel(r.gf, p, o)).astype(BF).astype(F32) * live_col
        num, z = r.num[p], r.z[p]
        rden = lax.rsqrt(z * z + FLOOR2)
        dn = (g * rden).astype(BF).astype(F32)
        dz = nn(halves(dn * num), ones1) * (z * rden * rden)
        dz = pltpu.roll(dz * (-2.0 / HEAD_DIM), HEAD_DIM, 1)
        rough = dz.astype(BF).astype(F32)
        dz = jnp.where(first_half, rough, dz - rough)
        factor = jnp.exp(r.rb[p]) * carry_col
        for a in range(2):
            h = 2 * p + a
            joint = (jnp.where(low, dn, dz) if a == 0 else jnp.where(low, dz, dn)).astype(BF)
            r.dn[h] = joint
            r.dr[pl.ds(h, 1), :] = nt(row_ones, halves(joint.astype(F32) * r.joined[h]))[0:1]
            adj = tn(joint, (r.qf[h].astype(F32) * widen(factor, a)).astype(BF))
            r.adj[p, a * HEAD_DIM : (a + 1) * HEAD_DIM, :] = adj[a * HEAD_DIM : (a + 1) * HEAD_DIM].astype(BF)
            at, half = (1 - a) * HEAD_DIM, HEAD_DIM // 2
            r.bn32[pl.ds(h, 1), :] = 0.5 * (adj[at : at + 1] + adj[at + half : at + half + 1])

    pair_loop(back)
    r.bn[...] = r.bn32[...].astype(BF)


def put_panel(ref, p, cols, x):
    shape = ref.shape[1:4] + (x.shape[1],)
    ref[p, :, :, :, cols] = x.astype(BF).reshape(shape)


def back(T, base, r, tokens_all):
    D = r.tok.shape[1]
    low = low_lanes(T)
    col_pos = base + iota((T, LANES), 0)
    seg_col, _, live_col, carry_col, _ = marks(col_pos, base, r.lengths)
    last_seg = marks(base + T - 1 + iota((8, LANES), 1) * 0, base, r.lengths)[0][0:1, 0:1]
    end_live = jnp.where(seg_col == last_seg, live_col, 0.0)
    r.nin32[...] = r.nin[...].astype(F32)
    r.bend32[...] = r.bend[...].astype(F32)
    ones1 = head_ones(2 * LANES, LANES, HEAD_DIM, HEAD_DIM)
    row_ones = jnp.ones((16, 2 * LANES), BF)
    r.acc1[...] = jnp.zeros_like(r.acc1)

    def feature_back(p, u, da):
        ds = nt(da, r.tabn[p]) * TABLE_SCALE
        uf = u.astype(F32)
        inv = lax.rsqrt(nn(halves(uf * uf), ones1) + 1e-6)
        uh = uf * inv
        return (inv * (ds - uh * nn(halves(uh * ds), ones1))).astype(BF)

    def pair(p):
        v, vf = r.v[p], None
        factor = jnp.exp(r.rb[p]) * carry_col
        decay_end = jnp.exp(r.rb[p, T - 1 : T, :] - r.rb[p]) * end_live
        grad_v = []
        for a in range(2):
            h = 2 * p + a
            r.s[...] = nt(r.dn[h], head_values(v, a, low))
            run_row = r.run[pl.ds(h, 1), :]

            def body(rows, at, n):
                gap = jnp.minimum(widen(r.rb[p, rows, :], a) - run_row, r.mask[rows, :])
                r.ds[rows, :] = (r.s[rows, :] * jnp.exp(gap)).astype(BF)

            rows_loop(T, 64, body)
            end = state_of(r.aend, r.bend32, p, a)
            kf, qf = r.kf[h], r.qf[h]
            hv = head_values(v, a, low)
            r.s1[...] = nn(r.ds[...], kf) + widen(factor, a) * nn(r.dn[h], state_of(r.min, r.nin32, p, a))
            r.s2[...] = tn(r.ds[...], qf) + widen(decay_end, a) * nn(hv, end)
            late = widen(decay_end, a) * nt(kf, end)
            grad_hv = tn(r.w[h], r.dn[h]) + late
            grad_v.append(grad_hv)
            lanes = slice(a * FEATS, (a + 1) * FEATS)

            def angles(rows, at, n):
                for source, feat, to in ((r.s1, r.qf, r.daq), (r.s2, r.kf, r.dak)):
                    x = source[rows, :]
                    f = feat[h, rows, :].astype(F32)
                    to[rows, lanes] = (x[:, :FEATS] * f[:, FEATS:] - x[:, FEATS:] * f[:, :FEATS]).astype(BF)

            rows_loop(T, 64, angles)
            hvf = hv.astype(F32)
            k_side = nt(row_ones, halves(hvf * grad_hv))
            r.drun[pl.ds(h, 1), :] = r.dr[pl.ds(h, 1), :] - k_side[0:1]
            own = slice(a * HEAD_DIM, (a + 1) * HEAD_DIM)
            owed = jnp.sum(r.aend[p, own, :].astype(F32) * r.min[p, own, :].astype(F32), axis=0, keepdims=True)
            owed = owed + HEAD_DIM * r.bend32[pl.ds(h, 1), :] * r.nin32[pl.ds(h, 1), :]
            owed = r.total[pl.ds(h, 1), 0:1] * jnp.sum(owed, axis=1, keepdims=True)
            owed = owed + jnp.sum(jnp.sum(hvf * late, axis=0, keepdims=True), axis=1, keepdims=True)
            r.owed[pl.ds(h, 1), :] = jnp.broadcast_to(owed, (1, LANES))
        grads = jnp.concatenate(
            [
                feature_back(p, r.q[p], r.daq[...]),
                feature_back(p, r.k[p], r.dak[...]),
                jnp.where(low, grad_v[0], grad_v[1]).astype(BF),
            ],
            axis=1,
        )
        r.acc1[...] += nt(grads, panel(r.ga, p, slice(0, 3 * LANES)))
        put_panel(r.gga, p, slice(0, 3 * LANES), tn(r.normed[...], grads))

    pair_loop(pair)
    pos = base + iota((8, T), 1)
    _, reset_row, live_row, _, filled = marks(pos, base, r.lengths)
    lane = iota((8, T), 1)
    run = r.drun[...]
    shift = 1
    while shift < T:
        run = run + jnp.where(lane < T - shift, pltpu.roll(run, T - shift, 1), 0.0)
        shift *= 2
    grad_decay = run + r.owed[:, 0:1]
    logits = r.logits[...]
    e = jnp.exp(-jnp.abs(logits))
    small, large = e / (1.0 + e), 1.0 / (1.0 + e)
    gate = jnp.where(logits >= 0.0, large, small)
    rest = jnp.where(logits >= 0.0, small, large)
    penalty = GATE_PEN * tokens_all / HEADS / jnp.broadcast_to(filled, (8, T)).astype(F32)
    grad_logits = grad_decay * live_row * (1.0 - reset_row) * rest + penalty * live_row * gate * rest
    both = halves(grad_logits, 0)
    r.acc1[...] += tn(both, r.gate[...].astype(BF))
    gate_rows = nn(both, r.normed[...])
    gate_rows = gate_rows[0:8] + gate_rows[8:16]
    bias = jnp.broadcast_to(jnp.sum(grad_logits, axis=1, keepdims=True), (8, D))
    r.sums[...] = jnp.zeros_like(r.sums)

    def finish(rows, at, n):
        xhat, inv = norm_stats(r.tok[rows, :].astype(F32))
        gn = r.acc1[rows, :]
        r.sums[0:8, :] += by_eight(gn * xhat)
        r.sums[8:16, :] += by_eight(gn)
        r.gtok[rows, :] = r.gmid[rows, :] + norm_back(gn, xhat, inv, r.vec[2:3, :])

    rows_loop(T, 64, finish)
    norm_gain = jnp.sum(r.sums[0:8, :], axis=0, keepdims=True)
    norm_shift = jnp.sum(r.sums[8:16, :], axis=0, keepdims=True)
    spread = jnp.where(iota((16, LANES), 0) == iota((16, LANES), 1), 1.0, 0.0).astype(BF)
    for p in range(PAIRS):
        pair_bias = bias[2 * p : 2 * p + 2]
        rough = pair_bias.astype(BF).astype(F32)
        rows = jnp.concatenate(
            [gate_rows[2 * p : 2 * p + 2], norm_gain, norm_shift, r.fsum[0:2, :], rough, pair_bias - rough, jnp.zeros((6, D), F32)],
            axis=0,
        )
        put_panel(r.gga, p, slice(3 * LANES, 4 * LANES), tn(rows.astype(BF), spread))


class Refs:
    def __init__(self, **refs):
        self.__dict__.update(refs)


def buffers(T, D, att, rest, ff, seq):
    z = (PAIRS, seq // 2, 2, D // seq)
    pair = (PAIRS, T, LANES)
    return {
        "ga": (z + (att,), BF), "gf": (z + (rest,), BF), "gga": (z + (att,), BF), "ggf": (z + (rest,), BF),
        "gate": ((16, D), F32), "bias": ((8, D), F32), "vec": ((8, D), F32), "normed": ((T, D), BF),
        "logits": ((8, T), F32), "run": ((8, T), F32), "total": ((8, LANES), F32), "mask": ((T, T), F32),
        "s1": ((T, 2 * FEATS), F32), "s2": ((T, 2 * FEATS), F32), "s": ((T, T), F32),
        "tab": ((PAIRS, 2 * LANES, 2 * FEATS), BF), "tabn": ((PAIRS, LANES, 2 * FEATS), BF),
        "q": (pair, BF), "k": (pair, BF), "v": (pair, BF), "rb": (pair, F32),
        "qf": ((HEADS, T, 2 * FEATS), BF), "kf": ((HEADS, T, 2 * FEATS), BF),
        "mem": ((PAIRS, LANES, 2 * FEATS), BF), "nrm": ((16, 2 * FEATS), BF), "nrm32": ((16, 2 * FEATS), F32),
        "min": ((PAIRS, LANES, 2 * FEATS), BF), "nin": ((16, 2 * FEATS), BF), "nin32": ((16, 2 * FEATS), F32),
        "adj": ((PAIRS, LANES, 2 * FEATS), BF), "bn": ((16, 2 * FEATS), BF), "bn32": ((16, 2 * FEATS), F32),
        "aend": ((PAIRS, LANES, 2 * FEATS), BF), "bend": ((16, 2 * FEATS), BF), "bend32": ((16, 2 * FEATS), F32),
        "w": ((HEADS, T, T), BF), "own": ((HEADS, T, LANES), F32), "joined": ((HEADS, T, LANES), F32), "num": (pair, F32), "z": (pair, F32),
        "att": (pair, BF), "mid": ((T, D), F32), "xhat": ((T, D), F32), "inv": ((T, LANES), F32), "two": ((T, D), BF),
        "acc1": ((T, D), F32), "acc2": ((T, D), F32), "h1": ((T, ff), F32), "h2": ((T, ff), F32),
        "act": ((T, ff), BF), "gh": ((T, ff), BF), "sums": ((16, D), F32), "fsum": ((8, D), F32),
        "result": ((T, D), BF), "gmid": ((T, D), F32), "gb": ((T, D), BF), "dr": ((8, T), F32), "dn": ((HEADS, T, LANES), BF),
        "ds": ((T, T), BF), "daq": ((T, 2 * FEATS), BF), "dak": ((T, 2 * FEATS), BF),
        "drun": ((8, T), F32), "owed": ((8, LANES), F32), "gtok": ((T, D), F32),
    }


FRONT = (
    ("ga",),
    ("gate", "vec", "normed", "logits", "run", "total", "mask", "tabn", "q", "k", "v", "rb", "qf", "kf", "mem", "nrm", "w", "own"),
    ("bias", "s1", "s2", "s", "tab", "nrm32"),
)
MIDDLE = (
    ("gf", "vec", "rb", "qf", "own", "min", "nin"),
    ("ggf", "result", "gmid", "fsum", "dr", "dn", "adj", "bn"),
    ("nin32", "joined", "num", "z", "att", "mid", "xhat", "inv", "two", "acc1", "acc2", "h1", "h2", "act", "gh", "sums", "gb", "bn32"),
)
BACK = (
    ("ga", "gate", "vec", "normed", "logits", "run", "total", "mask", "tabn", "q", "k", "v", "rb", "qf", "kf",
     "w", "min", "nin", "aend", "bend", "gmid", "fsum", "dr", "dn"),
    ("gga", "gtok"),
    ("nin32", "bend32", "s", "s1", "s2", "ds", "daq", "dak", "drun", "owed", "acc1", "sums"),
)


def here(T):
    return (lax.axis_index("seq") * lax.axis_size("head") + lax.axis_index("head")) * T


def stage(which, names, specs, outer, args, state):
    reads, writes, scratch = names
    shape = lambda n: jax.ShapeDtypeStruct(*specs[n])
    vmem, smem = pl.BlockSpec(memory_space=pltpu.VMEM), pl.BlockSpec(memory_space=pltpu.SMEM)

    def kernel(*refs):
        base_ref, lengths, seed, tok, cot = refs[:5]
        rest = dict(zip(reads + writes + scratch, refs[5:]))
        which(base_ref[0], Refs(lengths=lengths, seed=seed, tok=tok, cot=cot, **rest))

    out = pl.pallas_call(
        kernel,
        out_shape=[shape(n) for n in writes],
        in_specs=[smem] * 3 + [vmem] * (2 + len(reads)),
        out_specs=[vmem] * len(writes),
        scratch_shapes=[pltpu.VMEM(*specs[n]) for n in scratch],
        compiler_params=pltpu.CompilerParams(vmem_limit_bytes=VMEM_BYTES),
        name=outer,
    )(*args, *[state[n] for n in reads])
    state.update(zip(writes, out))


def scan_states(mem, nrm, total, reverse):
    seq, head = lax.axis_size("seq"), lax.axis_size("head")
    count = seq * head
    me = lax.axis_index("seq") * head + lax.axis_index("head")
    factor = total[:, 0]
    by_head = lambda x: jnp.repeat(x.reshape(PAIRS, 2), HEAD_DIM, axis=1)[:, :, None]
    state = (factor, mem.astype(F32), nrm[:HEADS].astype(F32))
    step = 1
    order = lambda pairs: [(b, a) for a, b in pairs] if reverse else pairs
    axes = ("seq", "head")
    while step < count:
        moved = jax.tree.map(lambda x: lax.ppermute(x, axes, order([(i, i + step) for i in range(count - step)])), state)
        has = (me < count - step) if reverse else (me >= step)
        f, m, n = state
        state = (
            jnp.where(has, f * moved[0], f),
            m + jnp.where(has, by_head(f) * moved[1], 0.0),
            n + jnp.where(has, f[:, None] * moved[2], 0.0),
        )
        step *= 2
    moved = [lax.ppermute(x, axes, order([(i, i + 1) for i in range(count - 1)])) for x in state[1:]]
    return moved[0].astype(BF), jnp.concatenate([moved[1], jnp.zeros_like(moved[1])], 0).astype(BF)


def bias_columns(gate_bias):
    hi = lax.reduce_precision(gate_bias, 8, 7)
    mid = lax.reduce_precision(gate_bias - hi, 8, 7)
    return jnp.stack([hi, mid, gate_bias - hi - mid], axis=1).astype(BF)


def gather_blocks(att, rest, seq):
    def gather(block):
        full = lax.all_gather(lax.all_gather(block, "seq", axis=0, tiled=True), "head", axis=0)
        return full.reshape(PAIRS, seq // 2, 2, full.shape[1] // seq, full.shape[2])

    return gather(att), gather(rest)


def gather_any(q, k, v, gate, vectors, bias, out, up, down, seq):
    D = q.shape[0] * seq

    def whole(w, rows, cols):
        w = lax.all_gather(w, rows, axis=0, tiled=True)
        return lax.all_gather(w, cols, axis=1, tiled=True)

    def panels(w):
        return w.reshape(D, PAIRS, w.shape[1] // PAIRS).transpose(1, 0, 2)

    grid = [panels(whole(w, "seq", "head")) for w in (q, k, v)]
    gates = panels(whole(gate, "seq", "head"))
    lines = [jnp.broadcast_to(lax.all_gather(w, "seq", tiled=True)[None, :, None], (PAIRS, D, 1)) for w in vectors]
    bias = bias_columns(lax.all_gather(bias, "head", tiled=True)).reshape(PAIRS, 1, 6)
    pad = jnp.zeros((PAIRS, D, LANES - 12), BF)
    ga = jnp.concatenate(grid + [gates] + lines + [jnp.broadcast_to(bias, (PAIRS, D, 6)), pad], axis=2)
    gf = [panels(whole(out, "head", "seq").T), panels(whole(up, "seq", "head")), panels(whole(down, "head", "seq").T)]
    gf = jnp.concatenate(gf, axis=2)
    shape = (PAIRS, seq // 2, 2, D // seq)
    return ga.reshape(shape + ga.shape[2:]), gf.reshape(shape + gf.shape[2:])


def scatter_blocks(gga, ggf):
    def scattered(x):
        x = x.reshape(PAIRS, -1, x.shape[-1]).astype(F32)
        x = lax.psum_scatter(x, "head", scatter_dimension=0, tiled=True)[0]
        return lax.psum_scatter(x, "seq", scatter_dimension=0, tiled=True)

    return scattered(gga), scattered(ggf)


def unpack(grad_a, grad_f, ff):
    block = lambda i: grad_a[:, i * LANES : (i + 1) * LANES]
    small = block(3)
    return (
        small[:, 2], small[:, 3], block(0), block(1), block(2), small[:, 0:2], small[0, 6:8] + small[0, 8:10],
        grad_f[:, :LANES].T, small[:, 4], small[:, 5], grad_f[:, LANES : LANES + ff], grad_f[:, LANES + ff :].T,
    )


def scatter_any(gga, ggf, ff):
    gga, ggf = (x.reshape(PAIRS, -1, x.shape[-1]).astype(F32) for x in (gga, ggf))

    def grid(x):
        x = x.transpose(1, 0, 2).reshape(x.shape[1], -1)
        x = lax.psum_scatter(x, "seq", scatter_dimension=0, tiled=True)
        return lax.psum_scatter(x, "head", scatter_dimension=1, tiled=True)

    block = lambda i: gga[:, :, i * LANES : (i + 1) * LANES]
    small = block(3)
    lines = lax.psum_scatter(lax.psum(small[0, :, 2:6], "head"), "seq", scatter_dimension=0, tiled=True)
    bias = (small[:, 0, 6:8] + small[:, 0, 8:10]).reshape(HEADS)
    bias = lax.psum_scatter(lax.psum(bias, "seq"), "head", scatter_dimension=0, tiled=True)
    return (
        lines[:, 0], lines[:, 1], grid(block(0)), grid(block(1)), grid(block(2)), grid(small[:, :, 0:2]), bias,
        grid(ggf[:, :, :LANES]).T, lines[:, 2], lines[:, 3], grid(ggf[:, :, LANES : LANES + ff]),
        grid(ggf[:, :, LANES + ff :]).T,
    )


def shards(
    tokens, lengths, feature_seed, norm_gain, norm_shift, query_weight, key_weight, value_weight, gate_weight, gate_bias,
    out_weight, ffn_gain, ffn_shift, up_weight, down_weight, cotangent,
):
    seq, head = lax.axis_size("seq"), lax.axis_size("head")
    T, D = tokens.shape
    rows = D // seq
    ff = up_weight.shape[1] * head // PAIRS
    base = here(T).astype(I32).reshape(1)
    by_pair = head == PAIRS
    vectors = (norm_gain, norm_shift, ffn_gain, ffn_shift)
    if by_pair:
        bias = jnp.broadcast_to(bias_columns(gate_bias).reshape(1, 6), (rows, 6))
        small = [gate_weight] + [w[:, None] for w in vectors] + [bias, jnp.zeros((rows, LANES - 12), BF)]
        att = jnp.concatenate([query_weight, key_weight, value_weight] + small, axis=1)
        ga, gf = gather_blocks(att, jnp.concatenate([out_weight.T, up_weight, down_weight.T], axis=1), seq)
    else:
        ga, gf = gather_any(query_weight, key_weight, value_weight, gate_weight, vectors, gate_bias, out_weight,
                            up_weight, down_weight, seq)
    specs = buffers(T, D, ATT, LANES + 2 * ff, ff, seq)
    args = (base, lengths, feature_seed, tokens, cotangent)
    state = {"ga": ga, "gf": gf}
    stage(lambda base, r: front(T, base, r), FRONT, specs, "front", args, state)
    state["min"], state["nin"] = scan_states(state["mem"], state["nrm"], state["total"], False)
    stage(lambda base, r: middle(T, base, r), MIDDLE, specs, "middle", args, state)
    state["aend"], state["bend"] = scan_states(state["adj"], state["bn"], state["total"], True)
    stage(lambda base, r: back(T, base, r, T * seq * head), BACK, specs, "back", args, state)
    if by_pair:
        weights = unpack(*scatter_blocks(state["gga"], state["ggf"]), ff)
    else:
        weights = scatter_any(state["gga"], state["ggf"], ff)
    return (state["result"], state["gtok"]) + weights


def solution(mesh):
    both, rows, grid = P(("seq", "head"), None), P("seq"), P("seq", "head")
    return jax.shard_map(
        shards,
        mesh=mesh,
        in_specs=(both, P(), P(), rows, rows, grid, grid, grid, grid, P("head"), P("head", "seq"), rows, rows, grid,
                  P("head", "seq"), both),
        out_specs=(both, both, rows, rows, grid, grid, grid, grid, P("head"), P("head", "seq"), rows, rows, grid,
                   P("head", "seq")),
        check_vma=False,
    )
```

```python
import functools
import math

import jax
import jax.numpy as jnp
from jax import lax
from jax.experimental import pallas as pl
from jax.experimental.pallas import tpu as pltpu
from jax.sharding import PartitionSpec as P

BF, F32, I32 = jnp.bfloat16, jnp.float32, jnp.int32
MESH = pl.DeviceIdType.MESH
HEADS, HEAD_DIM, FEATS = 8, 64, 128
PAIRS = HEADS // 2
LANES = 128
EPS, FLOOR2, GATE_PEN = 1e-5, 0.0625, 0.5
TABLE_SCALE = 1.0 / math.sqrt(21845.0)
FEAT_SCALE = 1.0 / math.sqrt(FEATS)
INV_TWO_PI, TWO_PI = 1.0 / (2.0 * math.pi), 2.0 * math.pi
SIN = (0.9999996027571254, -0.16666553170295112, 0.008332405799301931, -0.00019808693226998236,
       2.6997700314773084e-06, -2.036409109746239e-08)
COS = (0.9999992193982472, -0.4999942543676011, 0.04165980908449851, -0.0013858873219640337,
       2.420384320646774e-05, -2.1976364824224383e-07)
ERFC = (0.254829592, -0.284496736, 1.421413741, -1.453152027, 1.061405429)
ATT = 4 * LANES
KV, SMALL, QUERY = slice(0, 2 * LANES), slice(2 * LANES, 3 * LANES), slice(3 * LANES, 4 * LANES)
NORMAL, DECAY, STATE_ROWS = HEAD_DIM, HEAD_DIM + 1, HEAD_DIM + 8
STATES = (HEADS, STATE_ROWS, 2 * FEATS)
VMEM_BYTES = 56 * 1024 * 1024
LAYER_BYTES = 63 * 1024 * 1024


def nn(a, b):
    return lax.dot_general(a, b, (((1,), (0,)), ((), ())), preferred_element_type=F32)


def nt(a, b):
    return lax.dot_general(a, b, (((1,), (1,)), ((), ())), preferred_element_type=F32)


def tn(a, b):
    return lax.dot_general(a, b, (((0,), (0,)), ((), ())), preferred_element_type=F32)


def halves(x, axis=1):
    hi = x.astype(BF)
    return jnp.concatenate([hi, (x - hi.astype(F32)).astype(BF)], axis=axis)


def iota(shape, dim):
    return lax.broadcasted_iota(I32, shape, dim)


def rows_loop(total, step, body):
    step = min(step, total)

    def one(i, carry):
        body(pl.ds(pl.multiple_of(i * step, step), step), i * step, step)
        return carry

    lax.fori_loop(0, total // step, one, 0)


def pair_loop(body):
    def one(p, carry):
        body(p)
        return carry

    lax.fori_loop(0, PAIRS, one, 0)


def head_ones(rows, cols, row_span, col_span):
    same = (iota((rows, cols), 0) // row_span) % 2 == iota((rows, cols), 1) // col_span
    return jnp.where(same, 1.0, 0.0).astype(BF)


def marks(pos, base, lengths_ref):
    start = jnp.int32(0)
    segment = jnp.zeros(pos.shape, I32)
    reset = jnp.zeros(pos.shape, F32)
    carry = jnp.ones(pos.shape, F32)
    for d in range(lengths_ref.shape[0]):
        segment = segment + jnp.where(pos >= start, 1, 0)
        reset = jnp.where(pos == start, 1.0, reset)
        carry = jnp.where((pos >= start) & (pos - start <= pos - base), 0.0, carry)
        start = start + lengths_ref[d]
    live = jnp.where(pos < start, 1.0, 0.0)
    segment = segment + jnp.where(pos >= start, 1, 0)
    return segment, reset, live, carry, start


def horner(coefs, t):
    acc = jnp.full_like(t, coefs[-1])
    for c in coefs[-2::-1]:
        acc = acc * t + c
    return acc


def sincos(angle):
    r = angle - jnp.round(angle * INV_TWO_PI) * TWO_PI
    t = r * r
    return r * horner([c * FEAT_SCALE for c in SIN], t), horner([c * FEAT_SCALE for c in COS], t)


def gelu_parts(x):
    t = 1.0 / (1.0 + (0.3275911 / math.sqrt(2.0)) * jnp.abs(x))
    e = jnp.exp(-0.5 * x * x)
    q = 0.5 * t * horner(ERFC, t) * e
    cdf = jnp.where(x < 0.0, q, 1.0 - q)
    return x * cdf, cdf + x * e * (1.0 / math.sqrt(2.0 * math.pi))


def norm_stats(x):
    center = jnp.mean(x, axis=-1, keepdims=True)
    spread = jnp.mean(x * x, axis=-1, keepdims=True) - center * center
    inv = lax.rsqrt(spread + EPS)
    return (x - center) * inv, inv


def norm_back(grad, xhat, inv, gain):
    p = grad * gain
    return inv * (p - jnp.mean(p, axis=-1, keepdims=True) - xhat * jnp.mean(p * xhat, axis=-1, keepdims=True))


def by_eight(x):
    return jnp.sum(x.reshape(x.shape[0] // 8, 8, x.shape[1]), axis=0)


def panel(ref, p, cols):
    x = ref[p, :, :, :, cols]
    return x.reshape(x.shape[0] * x.shape[1] * x.shape[2], x.shape[3])


def low_lanes(rows):
    return iota((rows, LANES), 1) < HEAD_DIM


def widen(pair, a):
    return pair[:, a * HEAD_DIM : a * HEAD_DIM + 1]


def head_values(v, a, low):
    one = jnp.ones_like(v)
    return jnp.where(low, v, one) if a == 0 else jnp.where(low, one, v)


def state_of(states, p, a):
    own = states[2 * p + a, 0:HEAD_DIM, :]
    rest = jnp.broadcast_to(states[2 * p + a, NORMAL : NORMAL + 1, :], own.shape)
    return jnp.concatenate([own, rest] if a == 0 else [rest, own], axis=0)


def put_state(states, h, own, normal, decay):
    states[h, 0:HEAD_DIM, :] = own
    rest = jnp.zeros((STATE_ROWS - DECAY - 1, 2 * FEATS), F32)
    states[h, NORMAL:, :] = jnp.concatenate([normal, twice(decay), rest], axis=0)


def twice(x):
    return jnp.concatenate([x, x], axis=1)


def run_pairs(body, hook):
    def one(p):
        body(p)
        for at, act in (hook or {}).items():
            pl.when(p == at)(act)

    pair_loop(one)


def tables(T, base, r):
    pos = base + iota((8, T), 1)
    seg_row, _, live_row, _, _ = marks(pos, base, r.lengths)
    seg1, live1, pos1 = seg_row[0:1], live_row[0:1], pos[0:1]

    def mask_rows(rows, at, n):
        row_pos = base + at + iota((n, 1), 0)
        seg_col = marks(row_pos, base, r.lengths)[0]
        allowed = (seg_col == seg1) & (pos1 <= row_pos) & (live1 > 0.0)
        r.mask[rows, :] = jnp.where(allowed, 0.0, -1e30)

    rows_loop(T, 64, mask_rows)
    hash_seed = r.seed[0] * jnp.int32(-2048144789)

    def table(p):
        place = (p * LANES + iota((LANES, LANES), 0)) * FEATS + iota((LANES, LANES), 1)
        y = place * jnp.int32(-1640531535) + hash_seed
        y = y ^ lax.shift_right_logical(y, jnp.int32(15))
        y = y * jnp.int32(739982445)
        y = y ^ lax.shift_right_logical(y, jnp.int32(13))
        y = y * jnp.int32(695872825)
        y = y ^ lax.shift_right_logical(y, jnp.int32(16))
        s = jnp.full(y.shape, -510, I32)
        for k in range(4):
            s = s + (lax.shift_right_logical(y, jnp.int32(8 * k)) & jnp.int32(255))
        top = iota((LANES, LANES), 0) < HEAD_DIM
        odd = s & 1

        def diagonal(x):
            x = x.astype(F32)
            return jnp.concatenate([jnp.where(top, x, 0.0), jnp.where(top, 0.0, x)], axis=1).astype(BF)

        r.tab[p, 0:LANES, :] = diagonal(s - odd)
        r.tab[p, LANES:, :] = diagonal(odd)
        r.tabn[p] = diagonal(s)

    pair_loop(table)


def first_norm(T, base, r):
    pick = jnp.where(iota((16, LANES), 0) == iota((16, LANES), 1), 1.0, 0.0).astype(BF)
    for p in range(PAIRS):
        rows = nt(pick, panel(r.ga, p, SMALL))
        r.gate[2 * p : 2 * p + 2, :] = rows[0:2]
        r.gate[8 + 2 * p : 10 + 2 * p, :] = rows[0:2]
        r.bias[2 * p : 2 * p + 1, :] = rows[6:7] + rows[7:8] + rows[8:9]
        r.bias[2 * p + 1 : 2 * p + 2, :] = rows[9:10] + rows[10:11] + rows[11:12]
        if p == 0:
            r.vec[...] = rows[0:8]

    def norm_rows(rows, at, n):
        xhat, _ = norm_stats(r.tok[rows, :].astype(F32))
        r.normed[rows, :] = (xhat * r.vec[2:3, :] + r.vec[3:4, :]).astype(BF)

    rows_loop(T, 64, norm_rows)
    logits = nt(r.gate[...].astype(BF), r.normed[...])[0:8] + r.bias[:, 0:1]
    r.logits[...] = logits
    pos = base + iota((8, T), 1)
    _, reset_row, live_row, carry_row, _ = marks(pos, base, r.lengths)
    decay = -(jnp.log1p(jnp.exp(-jnp.abs(logits))) + jnp.maximum(-logits, 0.0)) * live_row * (1.0 - reset_row)
    run = decay
    lane = iota((8, T), 1)
    shift = 1
    while shift < T:
        run = run + jnp.where(lane >= shift, pltpu.roll(run, shift, 1), 0.0)
        shift *= 2
    r.run[...] = run
    r.total[...] = jnp.broadcast_to(jnp.exp(run[:, T - 1 : T]) * carry_row[:, T - 1 : T], (8, LANES))
    hi = run.astype(BF).astype(F32)
    mid = (run - hi).astype(BF).astype(F32)
    run3 = jnp.concatenate([hi, mid, run - hi - mid, jnp.zeros_like(hi)], axis=0).astype(BF)

    def spread(p):
        chosen = iota((32, LANES), 0) % 8 == 2 * p + iota((32, LANES), 1) // HEAD_DIM
        r.rb[p] = tn(run3, jnp.where(chosen, 1.0, 0.0).astype(BF))

    pair_loop(spread)


def features(T, r, p, u, out):
    ones2 = head_ones(2 * LANES, 2 * LANES, HEAD_DIM, LANES)
    r.s1[...] = nn(jnp.concatenate([u, u], axis=1), r.tab[p])
    uf = u.astype(F32)
    r.s2[...] = nn(halves(uf * uf), ones2)

    def body(rows, at, n):
        s, c = sincos(r.s1[rows, :] * (lax.rsqrt(r.s2[rows, :] + 1e-6) * TABLE_SCALE))
        for a in range(2):
            out[2 * p + a, rows, 0:FEATS] = s[:, a * FEATS : (a + 1) * FEATS].astype(BF)
            out[2 * p + a, rows, FEATS : 2 * FEATS] = c[:, a * FEATS : (a + 1) * FEATS].astype(BF)

    rows_loop(T, 64, body)


def end_factor(T, base, r):
    last_seg = marks(base + T - 1 + iota((8, LANES), 1) * 0, base, r.lengths)[0][0:1, 0:1]
    seg_col, _, live_col, _, _ = marks(base + iota((T, LANES), 0), base, r.lengths)
    return jnp.where(seg_col == last_seg, live_col, 0.0)


def keys(T, base, r, hook=None):
    low = low_lanes(T)
    end_live = end_factor(T, base, r)

    def pair(p):
        kv = nn(r.normed[...], panel(r.ga, p, KV)).astype(BF)
        r.k[p] = kv[:, 0:LANES]
        r.v[p] = kv[:, LANES:]
        features(T, r, p, r.k[p], r.kf)
        decay_end = jnp.exp(r.rb[p, T - 1 : T, :] - r.rb[p]) * end_live
        four = [decay_end[:, 0:1], decay_end[:, 0:1], decay_end[:, HEAD_DIM : HEAD_DIM + 1], decay_end[:, HEAD_DIM : HEAD_DIM + 1]]
        lane = iota((T, LANES), 1)
        first = jnp.where(lane < 2, four[0], four[2])
        rough = first.astype(BF).astype(F32)
        first = jnp.where(lane % 2 == 0, rough, first - rough)
        ends = tn(first.astype(BF), jnp.concatenate([r.kf[2 * p], r.kf[2 * p + 1]], axis=1))
        for a in range(2):
            h = 2 * p + a
            scaled = (r.kf[h].astype(F32) * widen(decay_end, a)).astype(BF)
            state = tn(r.v[p], scaled)[a * HEAD_DIM : (a + 1) * HEAD_DIM]
            normal = ends[2 * a : 2 * a + 1, a * 2 * FEATS : (a + 1) * 2 * FEATS]
            normal = normal + ends[2 * a + 1 : 2 * a + 2, a * 2 * FEATS : (a + 1) * 2 * FEATS]
            put_state(r.out, h, state, normal, r.total[pl.ds(h, 1), :])

    run_pairs(pair, hook)


def queries(T, base, r, hook=None):
    low = low_lanes(T)

    def pair(p):
        r.q[p] = nn(r.normed[...], panel(r.ga, p, QUERY)).astype(BF)
        features(T, r, p, r.q[p], r.qf)
        v = r.v[p]
        for a in range(2):
            h = 2 * p + a
            r.s[...] = nt(r.qf[h], r.kf[h])
            run_row = r.run[pl.ds(h, 1), :]

            def body(rows, at, n):
                gap = jnp.minimum(widen(r.rb[p, rows, :], a) - run_row, r.mask[rows, :])
                w = r.s[rows, :] * jnp.exp(gap)
                rounded = w.astype(BF)
                r.w[h, rows, :] = rounded
                rest = jnp.sum(w - rounded.astype(F32), axis=1, keepdims=True)
                r.zfix[p, rows, a * HEAD_DIM : (a + 1) * HEAD_DIM] = jnp.broadcast_to(rest, (n, HEAD_DIM)).astype(BF)

            rows_loop(T, 64, body)
            r.own[h] = nn(r.w[h], head_values(v, a, low))

    run_pairs(pair, hook)


def carry_factor(T, base, r):
    _, _, live_col, carry_col, _ = marks(base + iota((T, LANES), 0), base, r.lengths)
    return live_col, carry_col


def attend(T, base, r):
    low = low_lanes(T)
    live_col, carry_col = carry_factor(T, base, r)

    def join(p):
        factor = jnp.exp(r.rb[p]) * carry_col
        total = []
        for a in range(2):
            h = 2 * p + a
            carried = nt(twice(r.qf[h]), halves(state_of(r.inn, p, a)))
            joined = r.own[h] + widen(factor, a) * carried
            r.joined[h] = joined
            total.append(joined)
        num = jnp.where(low, total[0], total[1])
        z = pltpu.roll(jnp.where(low, total[1], total[0]), HEAD_DIM, 1) + r.zfix[p].astype(F32)
        r.att[p] = (live_col * num * lax.rsqrt(z * z + FLOOR2)).astype(BF)

    pair_loop(join)
    o = slice(0, LANES)
    branch = None
    for p in range(0, PAIRS, 2):
        part = nt(
            jnp.concatenate([r.att[p], r.att[p + 1]], axis=1),
            jnp.concatenate([panel(r.gf, p, o), panel(r.gf, p + 1, o)], axis=1),
        )
        branch = part if branch is None else branch + part
    r.mid[...] = branch

    def norm_rows(rows, at, n):
        mid = r.mid[rows, :] + r.tok[rows, :].astype(F32)
        r.mid[rows, :] = mid
        xhat, inv = norm_stats(mid)
        r.xhat[rows, :] = xhat
        r.inv[rows, :] = jnp.broadcast_to(inv, (n, LANES))
        r.two[rows, :] = (xhat * r.vec[4:5, :] + r.vec[5:6, :]).astype(BF)

    rows_loop(T, 64, norm_rows)


def feed_columns(r):
    ff = (r.gf.shape[-1] - LANES) // 2
    return slice(LANES, LANES + ff), slice(LANES + ff, LANES + 2 * ff)


def feed(T, base, r):
    low = low_lanes(T)
    live_col, carry_col = carry_factor(T, base, r)
    r.acc1[...] = jnp.zeros_like(r.acc1)
    r.acc2[...] = jnp.zeros_like(r.acc2)
    u, d = feed_columns(r)
    o = slice(0, LANES)

    def part(p):
        up, down = panel(r.gf, p, u), panel(r.gf, p, d)
        r.h1[...] = nn(r.two[...], up)
        r.h2[...] = nn(r.cot[...], down)

        def body(rows, at, n):
            value, slope = gelu_parts(r.h1[rows, :])
            r.act[p, rows, :] = value.astype(BF)
            r.gh[p, rows, :] = (r.h2[rows, :] * slope).astype(BF)

        rows_loop(T, 64, body)
        r.acc1[...] += nt(r.act[p], down)
        r.acc2[...] += nt(r.gh[p], up)

    pair_loop(part)
    r.sums[...] = jnp.zeros_like(r.sums)

    def finish(rows, at, n):
        r.result[rows, :] = (r.mid[rows, :] + r.acc1[rows, :]).astype(BF)
        xhat, gn = r.xhat[rows, :], r.acc2[rows, :]
        r.sums[0:8, :] += by_eight(gn * xhat)
        r.sums[8:16, :] += by_eight(gn)
        back = norm_back(gn, xhat, r.inv[rows, 0:1], r.vec[4:5, :])
        grad = r.cot[rows, :].astype(F32) + back
        r.gmid[rows, :] = grad
        r.gb[rows, :] = grad.astype(BF)

    rows_loop(T, 64, finish)
    r.fsum[0:1, :] = jnp.sum(r.sums[0:8, :], axis=0, keepdims=True)
    r.fsum[1:2, :] = jnp.sum(r.sums[8:16, :], axis=0, keepdims=True)
    ones1 = head_ones(2 * LANES, LANES, HEAD_DIM, HEAD_DIM)
    row_ones = jnp.ones((16, 2 * LANES), BF)
    first_half = iota((T, LANES), 1) % HEAD_DIM < HEAD_DIM // 2

    def back(p):
        g = nn(r.gb[...], panel(r.gf, p, o)).astype(BF).astype(F32) * live_col
        total = [r.joined[2 * p], r.joined[2 * p + 1]]
        num = jnp.where(low, total[0], total[1])
        z = pltpu.roll(jnp.where(low, total[1], total[0]), HEAD_DIM, 1) + r.zfix[p].astype(F32)
        rden = lax.rsqrt(z * z + FLOOR2)
        dn = (g * rden).astype(BF).astype(F32)
        dz = nn(halves(dn * num), ones1) * (z * rden * rden)
        dz = pltpu.roll(dz * (-2.0 / HEAD_DIM), HEAD_DIM, 1)
        rough = dz.astype(BF).astype(F32)
        dz = jnp.where(first_half, rough, dz - rough)
        factor = jnp.exp(r.rb[p]) * carry_col
        for a in range(2):
            h = 2 * p + a
            joint = (jnp.where(low, dn, dz) if a == 0 else jnp.where(low, dz, dn)).astype(BF)
            r.dn[h] = joint
            r.dr[pl.ds(h, 1), :] = nt(row_ones, halves(joint.astype(F32) * total[a]))[0:1]
            adj = tn(joint, (r.qf[h].astype(F32) * widen(factor, a)).astype(BF))
            at, half = (1 - a) * HEAD_DIM, HEAD_DIM // 2
            normal = 0.5 * (adj[at : at + 1] + adj[at + half : at + half + 1])
            put_state(r.adj, h, adj[a * HEAD_DIM : (a + 1) * HEAD_DIM], normal, r.total[pl.ds(h, 1), :])

    pair_loop(back)


def feed_grads(T, base, r, hook=None):
    u, d = feed_columns(r)

    def part(p):
        put_panel(r.ggf, p, u, tn(r.two[...], r.gh[p]))
        put_panel(r.ggf, p, d, tn(r.cot[...], r.act[p]))
        put_panel(r.ggf, p, slice(0, LANES), tn(r.gb[...], r.att[p]))

    run_pairs(part, hook)


def put_panel(ref, p, cols, x):
    shape = ref.shape[1:4] + (x.shape[1],)
    ref[p, :, :, :, cols] = x.astype(BF).reshape(shape)


def back(T, base, r, tokens_all, near_hook=None, between=lambda: None, far_hook=None):
    D = r.tok.shape[1]
    low = low_lanes(T)
    _, carry_col = carry_factor(T, base, r)
    end_live = end_factor(T, base, r)
    ones1 = head_ones(2 * LANES, LANES, HEAD_DIM, HEAD_DIM)
    row_ones = jnp.ones((16, 2 * LANES), BF)
    r.acc1[...] = jnp.zeros_like(r.acc1)

    def feature_back(p, u, da):
        ds = nt(da, r.tabn[p]) * TABLE_SCALE
        uf = u.astype(F32)
        inv = lax.rsqrt(nn(halves(uf * uf), ones1) + 1e-6)
        uh = uf * inv
        return (inv * (ds - uh * nn(halves(uh * ds), ones1))).astype(BF)

    def angles(rows, source, feat, h):
        x, f = source[rows, :], feat[h, rows, :].astype(F32)
        return x[:, :FEATS] * f[:, FEATS:] - x[:, FEATS:] * f[:, :FEATS]

    def near(p):
        v = r.v[p]
        factor = jnp.exp(r.rb[p]) * carry_col
        for a in range(2):
            h = 2 * p + a
            r.s[...] = nt(r.dn[h], head_values(v, a, low))
            run_row = r.run[pl.ds(h, 1), :]

            def body(rows, at, n):
                gap = jnp.minimum(widen(r.rb[p, rows, :], a) - run_row, r.mask[rows, :])
                r.ds[rows, :] = (r.s[rows, :] * jnp.exp(gap)).astype(BF)

            rows_loop(T, 64, body)
            before = halves(state_of(r.inn, p, a), 0)
            r.s1[...] = nn(r.ds[...], r.kf[h]) + widen(factor, a) * nn(twice(r.dn[h]), before)
            r.s2[...] = tn(r.ds[...], r.qf[h])
            r.ghv[h] = tn(r.w[h], r.dn[h])

            def turn(rows, at, n):
                r.da[p, rows, a * FEATS : (a + 1) * FEATS] = angles(rows, r.s1, r.qf, h).astype(BF)
                r.da[p, rows, (2 + a) * FEATS : (3 + a) * FEATS] = angles(rows, r.s2, r.kf, h).astype(BF)

            rows_loop(T, 64, turn)

    def far(p):
        v = r.v[p]
        decay_end = jnp.exp(r.rb[p, T - 1 : T, :] - r.rb[p]) * end_live
        grad_v = []
        for a in range(2):
            h = 2 * p + a
            end, hv = state_of(r.aend, p, a), head_values(v, a, low)
            late = widen(decay_end, a) * nt(twice(r.kf[h]), halves(end))
            r.s2[...] = widen(decay_end, a) * nn(twice(hv), halves(end, 0))
            grad_hv = r.ghv[h] + late
            grad_v.append(grad_hv)

            def turn(rows, at, n):
                lanes = slice((2 + a) * FEATS, (3 + a) * FEATS)
                r.da[p, rows, lanes] = (r.da[p, rows, lanes].astype(F32) + angles(rows, r.s2, r.kf, h)).astype(BF)

            rows_loop(T, 64, turn)
            hvf = hv.astype(F32)
            k_side = nt(row_ones, halves(hvf * grad_hv))
            r.drun[pl.ds(h, 1), :] = r.dr[pl.ds(h, 1), :] - k_side[0:1]
            owed = jnp.sum(end * state_of(r.inn, p, a), axis=0, keepdims=True)
            owed = r.total[pl.ds(h, 1), 0:1] * jnp.sum(owed, axis=1, keepdims=True)
            owed = owed + jnp.sum(jnp.sum(hvf * late, axis=0, keepdims=True), axis=1, keepdims=True)
            r.owed[pl.ds(h, 1), :] = jnp.broadcast_to(owed, (1, LANES))
        grads = jnp.concatenate(
            [
                feature_back(p, r.k[p], r.da[p, :, 2 * FEATS :]),
                jnp.where(low, grad_v[0], grad_v[1]).astype(BF),
                feature_back(p, r.q[p], r.da[p, :, : 2 * FEATS]),
            ],
            axis=1,
        )
        weights = jnp.concatenate([panel(r.ga, p, KV), panel(r.ga, p, QUERY)], axis=1)
        r.acc1[...] += nt(grads, weights)
        put_panel(r.gga, p, slice(0, 3 * LANES), tn(r.normed[...], grads))

    run_pairs(near, near_hook)
    between()
    run_pairs(far, far_hook)
    pos = base + iota((8, T), 1)
    _, reset_row, live_row, _, filled = marks(pos, base, r.lengths)
    lane = iota((8, T), 1)
    run = r.drun[...]
    shift = 1
    while shift < T:
        run = run + jnp.where(lane < T - shift, pltpu.roll(run, T - shift, 1), 0.0)
        shift *= 2
    grad_decay = run + r.owed[:, 0:1]
    logits = r.logits[...]
    e = jnp.exp(-jnp.abs(logits))
    small, large = e / (1.0 + e), 1.0 / (1.0 + e)
    gate = jnp.where(logits >= 0.0, large, small)
    rest = jnp.where(logits >= 0.0, small, large)
    penalty = GATE_PEN * tokens_all / HEADS / jnp.broadcast_to(filled, (8, T)).astype(F32)
    grad_logits = grad_decay * live_row * (1.0 - reset_row) * rest + penalty * live_row * gate * rest
    both = halves(grad_logits, 0)
    r.acc1[...] += tn(both, r.gate[...].astype(BF))
    gate_rows = nn(both, r.normed[...])
    gate_rows = gate_rows[0:8] + gate_rows[8:16]
    bias = jnp.broadcast_to(jnp.sum(grad_logits, axis=1, keepdims=True), (8, D))
    r.sums[...] = jnp.zeros_like(r.sums)

    def finish(rows, at, n):
        xhat, inv = norm_stats(r.tok[rows, :].astype(F32))
        gn = r.acc1[rows, :]
        r.sums[0:8, :] += by_eight(gn * xhat)
        r.sums[8:16, :] += by_eight(gn)
        r.gtok[rows, :] = r.gmid[rows, :] + norm_back(gn, xhat, inv, r.vec[2:3, :])

    rows_loop(T, 64, finish)
    norm_gain = jnp.sum(r.sums[0:8, :], axis=0, keepdims=True)
    norm_shift = jnp.sum(r.sums[8:16, :], axis=0, keepdims=True)
    lines = [norm_gain, norm_shift, r.fsum[0:2, :]]
    for p in range(PAIRS):
        rows = jnp.concatenate([gate_rows[2 * p : 2 * p + 2]] + lines + [bias[2 * p : 2 * p + 2]], axis=0)
        for g in range(D // LANES):
            r.lines[p, g] = rows[:, g * LANES : (g + 1) * LANES]


class Refs:
    def __init__(self, **refs):
        self.__dict__.update(refs)


def buffers(T, D, att, rest, ff, seq):
    z = (PAIRS, seq // 2, 2, D // seq)
    pair = (PAIRS, T, LANES)
    return {
        "ga": (z + (att,), BF), "gf": (z + (rest,), BF), "gga": (z + (att - LANES,), BF), "ggf": (z + (rest,), BF),
        "gate": ((16, D), F32), "bias": ((8, D), F32), "vec": ((8, D), F32), "normed": ((T, D), BF),
        "logits": ((8, T), F32), "run": ((8, T), F32), "total": ((8, LANES), F32), "mask": ((T, T), F32),
        "s1": ((T, 2 * FEATS), F32), "s2": ((T, 2 * FEATS), F32), "s": ((T, T), F32),
        "tab": ((PAIRS, 2 * LANES, 2 * FEATS), BF), "tabn": ((PAIRS, LANES, 2 * FEATS), BF),
        "q": (pair, BF), "k": (pair, BF), "v": (pair, BF), "rb": (pair, F32),
        "qf": ((HEADS, T, 2 * FEATS), BF), "kf": ((HEADS, T, 2 * FEATS), BF),
        "out": (STATES, F32), "inn": (STATES, F32), "adj": (STATES, F32), "aend": (STATES, F32),
        "w": ((HEADS, T, T), BF), "own": ((HEADS, T, LANES), F32), "joined": ((HEADS, T, LANES), F32),
        "att": (pair, BF), "zfix": (pair, BF), "mid": ((T, D), F32), "xhat": ((T, D), F32), "inv": ((T, LANES), F32), "two": ((T, D), BF),
        "acc1": ((T, D), F32), "acc2": ((T, D), F32), "h1": ((T, ff), F32), "h2": ((T, ff), F32),
        "act": ((PAIRS, T, ff), BF), "gh": ((PAIRS, T, ff), BF), "sums": ((16, D), F32), "fsum": ((8, D), F32),
        "result": ((T, D), BF), "gmid": ((T, D), F32), "gb": ((T, D), BF), "dr": ((8, T), F32),
        "dn": ((HEADS, T, LANES), BF), "ds": ((T, T), BF), "da": ((PAIRS, T, 4 * FEATS), BF), "ghv": ((HEADS, T, LANES), F32),
        "lines": ((PAIRS, D // LANES, 8, LANES), F32),
        "drun": ((8, T), F32), "owed": ((8, LANES), F32), "gtok": ((T, D), F32),
    }


FRONT = (
    ("ga",),
    ("gate", "vec", "normed", "logits", "run", "total", "mask", "tabn", "q", "k", "v", "rb", "qf", "kf", "out", "w", "own", "zfix"),
    ("bias", "s1", "s2", "s", "tab"),
)
MIDDLE = (
    ("gf", "vec", "rb", "qf", "own", "zfix", "inn", "total"),
    ("ggf", "result", "gmid", "fsum", "dr", "dn", "adj"),
    ("joined", "att", "mid", "xhat", "inv", "two", "acc1", "acc2", "h1", "h2", "act", "gh", "sums", "gb"),
)
BACK = (
    ("ga", "gate", "vec", "normed", "logits", "run", "total", "mask", "tabn", "q", "k", "v", "rb", "qf", "kf",
     "w", "inn", "aend", "gmid", "fsum", "dr", "dn"),
    ("gga", "gtok", "lines"),
    ("s", "s1", "s2", "ds", "da", "ghv", "drun", "owed", "acc1", "sums"),
)
SHARED = {"joined": "own", "h1": "s", "gmid": "mid", "ds": "gb", "adj": "out", "da": "act", "ghv": "own"}


def front(T, base, r):
    tables(T, base, r)
    first_norm(T, base, r)
    keys(T, base, r)
    queries(T, base, r)


def middle(T, base, r):
    attend(T, base, r)
    feed(T, base, r)
    feed_grads(T, base, r)


def here(T):
    return (lax.axis_index("seq") * lax.axis_size("head") + lax.axis_index("head")) * T


def stage(which, names, specs, outer, args, state):
    reads, writes, scratch = names
    shape = lambda n: jax.ShapeDtypeStruct(*specs[n])
    vmem, smem = pl.BlockSpec(memory_space=pltpu.VMEM), pl.BlockSpec(memory_space=pltpu.SMEM)

    def kernel(*refs):
        base_ref, lengths, seed, tok, cot = refs[:5]
        rest = dict(zip(reads + writes + scratch, refs[5:]))
        which(base_ref[0], Refs(lengths=lengths, seed=seed, tok=tok, cot=cot, **rest))

    out = pl.pallas_call(
        kernel,
        out_shape=[shape(n) for n in writes],
        in_specs=[smem] * 3 + [vmem] * (2 + len(reads)),
        out_specs=[vmem] * len(writes),
        scratch_shapes=[pltpu.VMEM(*specs[n]) for n in scratch],
        compiler_params=pltpu.CompilerParams(vmem_limit_bytes=VMEM_BYTES),
        name=outer,
    )(*args, *[state[n] for n in reads])
    state.update(zip(writes, out))


def scan_states(out, reverse):
    seq, head = lax.axis_size("seq"), lax.axis_size("head")
    count = seq * head
    me = lax.axis_index("seq") * head + lax.axis_index("head")
    state = (out[:, DECAY : DECAY + 1, 0:1], out[:, :DECAY])
    step = 1
    order = lambda pairs: [(b, a) for a, b in pairs] if reverse else pairs
    axes = ("seq", "head")
    while step < count:
        moved = jax.tree.map(lambda x: lax.ppermute(x, axes, order([(i, i + step) for i in range(count - step)])), state)
        has = (me < count - step) if reverse else (me >= step)
        f, m = state
        state = (jnp.where(has, f * moved[0], f), m + jnp.where(has, f * moved[1], 0.0))
        step *= 2
    moved = lax.ppermute(state[1], axes, order([(i, i + 1) for i in range(count - 1)]))
    return jnp.concatenate([moved, jnp.zeros((HEADS, STATE_ROWS - DECAY, 2 * FEATS), F32)], axis=1)


def remote(src, dst, send, recv, to):
    return pltpu.make_async_remote_copy(
        src_ref=src, dst_ref=dst, send_sem=send, recv_sem=recv, device_id=to, device_id_type=MESH
    )


class Place:
    def __init__(self):
        self.seq, self.head = lax.axis_size("seq"), lax.axis_size("head")
        s, h = lax.axis_index("seq"), lax.axis_index("head")
        self.z, self.y, self.x, self.c = s // 2, s % 2, h // 2, h % 2
        self.depth = self.seq // 2
        self.count = self.seq * self.head
        self.me = s * self.head + h

    def device(self, z=None, y=None, x=None, c=None):
        pick = lambda given, own: own if given is None else given
        z, y, x, c = pick(z, self.z), pick(y, self.y), pick(x, self.x), pick(c, self.c)
        return (z * 2 + y, x * 2 + c)

    def number(self, i):
        return (i // self.head, i % self.head)

    def around(self, k):
        return (self.z + k) % self.depth

class Semaphores:
    def __init__(self, send, recv):
        self.send, self.recv, self.used = send, recv, 0

    def copy(self, src, dst, to):
        i = self.used
        self.used += 1
        return remote(src, dst, self.send.at[i], self.recv.at[i], to)


GATHER_COPIES = 2 * (3 + 1 + 2 + 2)
SCATTER_COPIES = 2 + 2 * (1 + 1 + 3)


def gather_stages(place, g, lanes, sems):
    half = g.shape[3] // 2
    z, y, x, c = place.z, place.y, place.x, place.c
    pair = x * 2 + c
    stages = [[], [], [], []]
    for part in range(2):
        rows = pl.ds(part * half, half)
        same = lambda ref, to: sems.copy(ref, ref, to)
        for k in range(1, place.depth):
            stages[0].append(same(g.at[pair, z, y, rows, lanes], place.device(z=place.around(k))))
        to_y, to_x = place.device(y=1 - y), place.device(x=1 - x)
        if part == 0:
            stages[1].append(same(g.at[pair, :, y, rows, lanes], to_y))
            stages[2].append(same(g.at[pair, :, :, rows, lanes], to_x))
        else:
            stages[1].append(same(g.at[pair, :, y, rows, lanes], to_x))
            for other in range(2):
                stages[2].append(same(g.at[other * 2 + c, :, y, rows, lanes], to_y))
        for other in range(2):
            stages[3].append(same(g.at[other * 2 + c, :, :, rows, lanes], place.device(c=1 - c)))
    return stages


def begin(stage):
    for copy in stage:
        copy.start()


def arrived(stage):
    for copy in stage:
        copy.wait_recv()


def sent(*stages):
    for stage in stages:
        for copy in stage:
            copy.wait_send()


class Gather:
    def __init__(self, place, ga, gf, sems):
        ff = (gf.shape[-1] - LANES) // 2
        lanes = lambda first, count: pl.ds(first, count)
        self.chunks = [
            gather_stages(place, ref, part, sems)
            for ref, part in (
                (ga, lanes(0, 3 * LANES)),
                (ga, lanes(3 * LANES, LANES)),
                (gf, lanes(0, LANES + ff)),
                (gf, lanes(LANES + ff, ff)),
            )
        ]

    def begin(self, chunk):
        begin(self.chunks[chunk][0])

    def step(self, chunk, stage):
        arrived(self.chunks[chunk][stage])
        if stage < 3:
            begin(self.chunks[chunk][stage + 1])

    def finish(self):
        for chunk in self.chunks:
            sent(*chunk)


def add_blocks(to, others, count, where):
    def one(i, carry):
        at = where(i)
        total = to[at].astype(F32)
        for ref, index in others:
            total = total + ref[index(i)].astype(F32)
        to[at] = total.astype(to.dtype)
        return carry

    lax.fori_loop(0, count, one, 0)


class Scatter:
    def __init__(self, place, gg, out, buf, sems):
        self.place, self.gg, self.out = place, gg, out
        self.r1, self.r2a, self.r2b, self.r3a, self.r3b, self.r4a, self.r4b = buf
        z, y, x, c, n = place.z, place.y, place.x, place.c, place.depth
        self.half = half = gg.shape[3] // 2
        first, last = pl.ds(0, half), pl.ds(half, half)
        other, to_y, to_x = place.device(c=1 - c), place.device(y=1 - y), place.device(x=1 - x)
        self.stages = [
            [sems.copy(gg.at[i * 2 + 1 - c], self.r1.at[i], other) for i in range(2)],
            [
                sems.copy(self.r1.at[1 - x, :, :, first], self.r2a, to_x),
                sems.copy(self.r1.at[:, :, 1 - y, last], self.r2b, to_y),
            ],
            [sems.copy(self.r2a.at[:, 1 - y], self.r3a, to_y), sems.copy(self.r2b.at[1 - x], self.r3b, to_x)],
            [
                sems.copy(ref.at[place.around(k)], slots.at[k - 1], place.device(z=place.around(k)))
                for ref, slots in ((self.r3a, self.r4a), (self.r3b, self.r4b))
                for k in range(1, n)
            ],
        ]

    def start(self):
        begin(self.stages[0])

    def step(self, i):
        place, n, half = self.place, self.place.depth, self.half
        y, x, c = place.y, place.x, place.c
        first, last = slice(0, half), slice(half, 2 * half)
        arrived(self.stages[i])
        if i == 0:
            block = lambda j: (j // (2 * n), (j // 2) % n, j % 2)
            add_blocks(self.r1, [(self.gg, lambda j: ((j // (2 * n)) * 2 + c, (j // 2) % n, j % 2))], 4 * n, block)
        elif i == 1:
            add_blocks(self.r2a, [(self.r1, lambda j: (x, j // 2, j % 2, first))], 2 * n, lambda j: (j // 2, j % 2))
            add_blocks(self.r2b, [(self.r1, lambda j: (j // n, j % n, y, last))], 2 * n, lambda j: (j // n, j % n))
        elif i == 2:
            add_blocks(self.r3a, [(self.r2a, lambda j: (j, y))], n, lambda j: (j,))
            add_blocks(self.r3b, [(self.r2b, lambda j: (x, j))], n, lambda j: (j,))
        else:
            for ref, slots, rows in ((self.r3a, self.r4a, first), (self.r3b, self.r4b, last)):
                total = ref[place.z].astype(F32)
                for k in range(n - 1):
                    total = total + slots[k].astype(F32)
                self.out[rows, :] = total
        if i < 3:
            begin(self.stages[i + 1])

    def finish(self):
        sent(*self.stages)


def scatter_buffers(seq, rows, cols):
    n, half = seq // 2, rows // 2
    return [
        pltpu.VMEM(shape + (cols,), BF)
        for shape in ((2, n, 2, rows), (n, 2, half), (2, n, half), (n, half), (n, half), (n - 1, half), (n - 1, half))
    ]


class Scan:
    def __init__(self, place, reverse, out, inn, box, planes, send, recv):
        self.place, self.reverse = place, reverse
        self.out, self.inn, self.box, self.planes = out, inn, box, planes
        self.send, self.recv = send, recv
        self.mine = lax.rem(place.me, HEADS)

    def device(self, j):
        return self.place.number(self.place.me - self.mine + j)

    def peers(self, body):
        def one(k, carry):
            body(lax.rem(self.mine + k, HEADS))
            return carry

        lax.fori_loop(1, HEADS, one, 0)

    def all_at_once(self, ref, count, i):
        most = ref.at[pl.ds(0, count)]
        return remote(most, most, self.send.at[i], self.recv.at[i], self.place.device(c=1 - self.place.c))

    def start(self):
        me = self.mine
        self.peers(lambda j: remote(self.out.at[j], self.box.at[me], self.send.at[0], self.recv.at[0], self.device(j)).start())
        self.box[me] = self.out[me]

    def chain(self, ref, count):
        kept = iota((STATE_ROWS, 2 * FEATS), 0) != DECAY

        def one(i, state):
            d = count - 1 - i if self.reverse else i
            term = ref[d]
            ref[d] = state
            return state * term[DECAY : DECAY + 1, :] + jnp.where(kept, term, 0.0)

        first = jnp.where(iota((STATE_ROWS, 2 * FEATS), 0) == DECAY, 1.0, 0.0)
        return lax.fori_loop(0, count, one, first)

    def plane(self):
        place = self.place
        self.all_at_once(self.box, HEADS - 1, 0).wait_recv()
        self.planes[place.z] = self.chain(self.box, HEADS)
        for copy in self.totals():
            copy.start()

    def totals(self):
        place = self.place
        total = self.planes.at[place.z]
        return [
            remote(total, total, self.send.at[1], self.recv.at[1], place.device(z=place.around(k)))
            for k in range(1, place.depth)
        ]

    def line(self):
        place, me = self.place, self.mine
        self.all_at_once(self.planes, place.depth - 1, 1).wait_recv()
        self.all_at_once(self.planes, place.depth - 1, 1).wait_send()
        self.chain(self.planes, place.depth)
        before = self.planes[place.z]

        def one(j, carry):
            own = self.box[j]
            self.box[j] = own + own[DECAY : DECAY + 1, :] * before
            return carry

        lax.fori_loop(0, HEADS, one, 0)
        self.peers(lambda j: remote(self.box.at[j], self.inn.at[me], self.send.at[2], self.recv.at[2], self.device(j)).start())
        self.inn[me] = self.box[me]

    def receive(self):
        self.all_at_once(self.inn, HEADS - 1, 2).wait_recv()

    def finish(self):
        self.all_at_once(self.out, HEADS - 1, 0).wait_send()
        self.all_at_once(self.box, HEADS - 1, 2).wait_send()


class Lines:
    def __init__(self, place, lines, box, out, send, recv):
        self.place, self.lines, self.box, self.out, self.send, self.recv = place, lines, box, out, send, recv

    def tile(self, j):
        return self.lines.at[lax.rem(j, self.place.head), (j // self.place.head) * self.lines.shape[1] // self.place.seq]

    def start(self):
        me, count = self.place.me, self.place.count

        def one(k, carry):
            j = lax.rem(me + k, count)
            remote(self.tile(j), self.box.at[me], self.send, self.recv, self.place.number(j)).start()
            return carry

        lax.fori_loop(1, count, one, 0)
        self.box[me] = self.tile(me)[...]

    def finish(self):
        most = self.box.at[pl.ds(0, self.place.count - 1)]
        both = remote(most, most, self.send, self.recv, self.place.device(c=1 - self.place.c))
        both.wait_recv()

        def one(i, total):
            return total + self.box[i]

        self.out[...] = lax.fori_loop(0, self.place.count, one, jnp.zeros(self.out.shape, F32))
        both.wait_send()


def greet_all(place):
    barrier = pltpu.get_barrier_semaphore()

    def one(k, carry):
        to = place.number(lax.rem(place.me + k, place.count))
        pl.semaphore_signal(barrier, inc=1, device_id=to, device_id_type=MESH)
        return carry

    lax.fori_loop(1, place.count, one, 0)
    pl.semaphore_wait(barrier, place.count - 1)


def layer_kernel(names, specs, tokens_all, T, lengths, seed, tok, cot, att, rest, result, gtok, grad_a, grad_f, grad_lines, *scratch):
    place = Place()
    base = place.me * T
    arrays = dict(zip(names, scratch))
    arrays.update({name: arrays[other] for name, other in SHARED.items()})
    scratch = scratch[len(names) :]
    r = Refs(lengths=lengths, seed=seed, tok=tok, cot=cot, result=result, gtok=gtok, **arrays)
    scatter_f, scatter_a, scratch = scratch[0:7], scratch[7:14], scratch[14:]
    box, planes, line_box, sems = scratch[0:2], scratch[2:4], scratch[4], scratch[5:]
    pair = place.x * 2 + place.c
    r.ga[pair, place.z, place.y] = att[...]
    r.gf[pair, place.z, place.y] = rest[...]
    gather = Gather(place, r.ga, r.gf, Semaphores(sems[0], sems[1]))
    forth = Scan(place, False, r.out, r.inn, box[0], planes[0], sems[2], sems[3])
    home = Scan(place, True, r.adj, r.aend, box[1], planes[1], sems[4], sems[5])
    later = Semaphores(sems[6], sems[7])
    sum_f = Scatter(place, r.ggf, grad_f, scatter_f, later)
    sum_a = Scatter(place, r.gga, grad_a, scatter_a, later)
    lines = Lines(place, r.lines, line_box, grad_lines, sems[8], sems[9])
    greet_all(place)

    def acts(*each):
        def run():
            for act, *given in each:
                act(*given)

        return run

    gather.begin(0)
    gather.begin(1)
    tables(T, base, r)
    acts((gather.step, 0, 0), (gather.begin, 2), (gather.step, 0, 1), (gather.step, 1, 0), (gather.step, 0, 2),
         (gather.step, 1, 1), (gather.step, 0, 3))()
    first_norm(T, base, r)
    acts((gather.step, 1, 2), (gather.step, 2, 0), (gather.begin, 3))()
    keys(T, base, r, {1: acts((gather.step, 2, 1)), 2: acts((gather.step, 1, 3))})
    forth.start()
    queries(T, base, r, {0: acts((gather.step, 2, 2), (gather.step, 3, 0)), 1: acts((forth.plane,), (gather.step, 3, 1)),
                         2: acts((forth.line,), (gather.step, 2, 3), (gather.step, 3, 2))})
    forth.receive()
    forth.finish()
    attend(T, base, r)
    gather.step(3, 3)
    feed(T, base, r)
    home.start()
    feed_grads(T, base, r, {1: home.plane})
    sum_f.start()
    back(T, base, r, tokens_all, {0: home.line, 2: acts((sum_f.step, 0))}, home.receive,
         {0: acts((sum_f.step, 1)), 2: acts((sum_f.step, 2))})
    lines.start()
    sum_a.start()
    sum_f.step(3)
    for i in range(3):
        sum_a.step(i)
    lines.finish()
    sum_a.step(3)
    gather.finish()
    home.finish()
    sum_f.finish()
    sum_a.finish()


def layer_near(lengths, seed, tokens, cotangent, att, rest, specs, seq, head):
    T, D = tokens.shape
    count = seq * head
    rows, ff = D // seq, specs["act"][0][2]
    held = [n for n in dict.fromkeys(sum((sum(names, ()) for names in (FRONT, MIDDLE, BACK)), ())) if n not in SHARED]
    held = [n for n in held if n not in ("result", "gtok")]
    dma = pltpu.SemaphoreType.DMA
    scratch = [pltpu.VMEM(*specs[n]) for n in held]
    panels = att.shape[1] - LANES
    scratch += scatter_buffers(seq, rows, rest.shape[1]) + scatter_buffers(seq, rows, panels)
    scratch += [pltpu.VMEM(STATES, F32)] * 2 + [pltpu.VMEM((seq // 2,) + STATES[1:], F32)] * 2
    scratch += [pltpu.VMEM((count, 8, LANES), F32)]
    scratch += [dma((4 * GATHER_COPIES,))] * 2 + [dma((3,))] * 4 + [dma((2 * SCATTER_COPIES,))] * 2 + [dma(())] * 2
    vmem, smem = pl.BlockSpec(memory_space=pltpu.VMEM), pl.BlockSpec(memory_space=pltpu.SMEM)
    shape = jax.ShapeDtypeStruct
    return pl.pallas_call(
        functools.partial(layer_kernel, held, specs, T * count, T),
        out_shape=[shape((T, D), BF), shape((T, D), F32), shape((rows, panels), F32), shape((rows, rest.shape[1]), F32),
                   shape((8, LANES), F32)],
        in_specs=[smem] * 2 + [vmem] * 4,
        out_specs=[vmem] * 5,
        scratch_shapes=scratch,
        compiler_params=pltpu.CompilerParams(collective_id=0, has_side_effects=True, vmem_limit_bytes=LAYER_BYTES),
        name="layer",
    )(lengths, seed, tokens, cotangent, att, rest)


def bias_columns(gate_bias):
    hi = lax.reduce_precision(gate_bias, 8, 7)
    mid = lax.reduce_precision(gate_bias - hi, 8, 7)
    return jnp.stack([hi, mid, gate_bias - hi - mid], axis=1).astype(BF)


def gather_any(q, k, v, gate, vectors, bias, out, up, down, seq):
    D = q.shape[0] * seq

    def whole(w, rows, cols):
        w = lax.all_gather(w, rows, axis=0, tiled=True)
        return lax.all_gather(w, cols, axis=1, tiled=True)

    def panels(w):
        return w.reshape(D, PAIRS, w.shape[1] // PAIRS).transpose(1, 0, 2)

    q, k, v = (panels(whole(w, "seq", "head")) for w in (q, k, v))
    gates = panels(whole(gate, "seq", "head"))
    lines = [jnp.broadcast_to(lax.all_gather(w, "seq", tiled=True)[None, :, None], (PAIRS, D, 1)) for w in vectors]
    bias = bias_columns(lax.all_gather(bias, "head", tiled=True)).reshape(PAIRS, 1, 6)
    pad = jnp.zeros((PAIRS, D, LANES - 12), BF)
    ga = jnp.concatenate([k, v, gates] + lines + [jnp.broadcast_to(bias, (PAIRS, D, 6)), pad, q], axis=2)
    gf = [panels(whole(out, "head", "seq").T), panels(whole(up, "seq", "head")), panels(whole(down, "head", "seq").T)]
    gf = jnp.concatenate(gf, axis=2)
    shape = (PAIRS, seq // 2, 2, D // seq)
    return ga.reshape(shape + ga.shape[2:]), gf.reshape(shape + gf.shape[2:])


def unpack(grad_a, grad_f, lines, ff):
    rows = grad_a.shape[0]
    block = lambda i: grad_a[:, i * LANES : (i + 1) * LANES]
    place = lax.axis_index("seq") % (LANES // rows) * rows
    own = lax.dynamic_slice_in_dim(lines, place, rows, 1)
    return (
        own[2], own[3], block(2), block(0), block(1), own[0:2].T, lines[6:8, 0],
        grad_f[:, :LANES].T, own[4], own[5], grad_f[:, LANES : LANES + ff], grad_f[:, LANES + ff :].T,
    )


def scatter_any(gga, ggf, lines, ff):
    gga, ggf = (x.reshape(PAIRS, -1, x.shape[-1]).astype(F32) for x in (gga, ggf))

    def grid(x):
        x = x.transpose(1, 0, 2).reshape(x.shape[1], -1)
        x = lax.psum_scatter(x, "seq", scatter_dimension=0, tiled=True)
        return lax.psum_scatter(x, "head", scatter_dimension=1, tiled=True)

    block = lambda i: gga[:, :, i * LANES : (i + 1) * LANES]
    lines = lines.transpose(0, 2, 1, 3).reshape(PAIRS, 8, -1)
    gates = lines[:, 0:2].transpose(0, 2, 1)
    bias = lines[:, 6:8, 0].reshape(HEADS)
    bias = lax.psum_scatter(lax.psum(bias, "seq"), "head", scatter_dimension=0, tiled=True)
    lines = lax.psum_scatter(lax.psum(lines[0, 2:6].T, "head"), "seq", scatter_dimension=0, tiled=True)
    return (
        lines[:, 0], lines[:, 1], grid(block(2)), grid(block(0)), grid(block(1)), grid(gates), bias,
        grid(ggf[:, :, :LANES]).T, lines[:, 2], lines[:, 3], grid(ggf[:, :, LANES : LANES + ff]),
        grid(ggf[:, :, LANES + ff :]).T,
    )


def shards(
    tokens, lengths, feature_seed, norm_gain, norm_shift, query_weight, key_weight, value_weight, gate_weight, gate_bias,
    out_weight, ffn_gain, ffn_shift, up_weight, down_weight, cotangent,
):
    seq, head = lax.axis_size("seq"), lax.axis_size("head")
    T, D = tokens.shape
    rows = D // seq
    ff = up_weight.shape[1] * head // PAIRS
    vectors = (norm_gain, norm_shift, ffn_gain, ffn_shift)
    specs = buffers(T, D, ATT, LANES + 2 * ff, ff, seq)
    if (seq, head) == (HEADS, PAIRS):
        bias = jnp.broadcast_to(bias_columns(gate_bias).reshape(1, 6), (rows, 6))
        small = [gate_weight] + [w[:, None] for w in vectors] + [bias, jnp.zeros((rows, LANES - 12), BF)]
        att = jnp.concatenate([key_weight, value_weight] + small + [query_weight], axis=1)
        rest = jnp.concatenate([out_weight.T, up_weight, down_weight.T], axis=1)
        result, grad_tokens, grad_a, grad_f, lines = layer_near(
            lengths, feature_seed, tokens, cotangent, att, rest, specs, seq, head)
        return (result, grad_tokens) + unpack(grad_a, grad_f, lines, ff)
    ga, gf = gather_any(query_weight, key_weight, value_weight, gate_weight, vectors, gate_bias, out_weight, up_weight,
                        down_weight, seq)
    args = (here(T).astype(I32).reshape(1), lengths, feature_seed, tokens, cotangent)
    state = {"ga": ga, "gf": gf}
    stage(lambda base, r: front(T, base, r), FRONT, specs, "front", args, state)
    state["inn"] = scan_states(state["out"], False)
    stage(lambda base, r: middle(T, base, r), MIDDLE, specs, "middle", args, state)
    state["aend"] = scan_states(state["adj"], True)
    stage(lambda base, r: back(T, base, r, T * seq * head), BACK, specs, "back", args, state)
    return (state["result"], state["gtok"]) + scatter_any(state["gga"], state["ggf"], state["lines"], ff)


def solution(mesh):
    both, rows, grid = P(("seq", "head"), None), P("seq"), P("seq", "head")
    return jax.shard_map(
        shards,
        mesh=mesh,
        in_specs=(both, P(), P(), rows, rows, grid, grid, grid, grid, P("head"), P("head", "seq"), rows, rows, grid,
                  P("head", "seq"), both),
        out_specs=(both, both, rows, rows, grid, grid, grid, grid, P("head"), P("head", "seq"), rows, rows, grid,
                   P("head", "seq")),
        check_vma=False,
    )
```

```python
import functools
import math

import jax
import jax.numpy as jnp
from jax import lax
from jax.experimental import pallas as pl
from jax.experimental.pallas import tpu as pltpu
from jax.sharding import PartitionSpec as P

BF, F32, I32 = jnp.bfloat16, jnp.float32, jnp.int32
MESH = pl.DeviceIdType.MESH
HEADS, HEAD_DIM, FEATS = 8, 64, 128
PAIRS = HEADS // 2
LANES = 128
EPS, FLOOR2, GATE_PEN = 1e-5, 0.0625, 0.5
TABLE_SCALE = 1.0 / math.sqrt(21845.0)
FEAT_SCALE = 1.0 / math.sqrt(FEATS)
INV_TWO_PI, TWO_PI = 1.0 / (2.0 * math.pi), 2.0 * math.pi
SIN = (0.9999996027571254, -0.16666553170295112, 0.008332405799301931, -0.00019808693226998236,
       2.6997700314773084e-06, -2.036409109746239e-08)
COS = (0.9999992193982472, -0.4999942543676011, 0.04165980908449851, -0.0013858873219640337,
       2.420384320646774e-05, -2.1976364824224383e-07)
ERFC = (0.254829592, -0.284496736, 1.421413741, -1.453152027, 1.061405429)
ATT = 4 * LANES
KV, SMALL, QUERY = slice(0, 2 * LANES), slice(2 * LANES, 3 * LANES), slice(3 * LANES, 4 * LANES)
NORMAL, DECAY, STATE_ROWS = HEAD_DIM, HEAD_DIM + 1, HEAD_DIM + 8
STATES = (HEADS, STATE_ROWS, 2 * FEATS)
VMEM_BYTES = 56 * 1024 * 1024
LAYER_BYTES = 63 * 1024 * 1024


def nn(a, b):
    return lax.dot_general(a, b, (((1,), (0,)), ((), ())), preferred_element_type=F32)


def nt(a, b):
    return lax.dot_general(a, b, (((1,), (1,)), ((), ())), preferred_element_type=F32)


def tn(a, b):
    return lax.dot_general(a, b, (((0,), (0,)), ((), ())), preferred_element_type=F32)


def halves(x, axis=1):
    hi = x.astype(BF)
    return jnp.concatenate([hi, (x - hi.astype(F32)).astype(BF)], axis=axis)


def iota(shape, dim):
    return lax.broadcasted_iota(I32, shape, dim)


def rows_loop(total, step, body):
    body(pl.ds(0, total), 0, total)


def pair_loop(body):
    for p in range(PAIRS):
        body(p)


def head_ones(rows, cols, row_span, col_span):
    same = (iota((rows, cols), 0) // row_span) % 2 == iota((rows, cols), 1) // col_span
    return jnp.where(same, 1.0, 0.0).astype(BF)


def marks(pos, base, lengths_ref):
    start = jnp.int32(0)
    segment = jnp.zeros(pos.shape, I32)
    reset = jnp.zeros(pos.shape, F32)
    carry = jnp.ones(pos.shape, F32)
    for d in range(lengths_ref.shape[0]):
        segment = segment + jnp.where(pos >= start, 1, 0)
        reset = jnp.where(pos == start, 1.0, reset)
        carry = jnp.where((pos >= start) & (pos - start <= pos - base), 0.0, carry)
        start = start + lengths_ref[d]
    live = jnp.where(pos < start, 1.0, 0.0)
    segment = segment + jnp.where(pos >= start, 1, 0)
    return segment, reset, live, carry, start


def horner(coefs, t):
    acc = jnp.full_like(t, coefs[-1])
    for c in coefs[-2::-1]:
        acc = acc * t + c
    return acc


def sincos(angle):
    r = angle - jnp.round(angle * INV_TWO_PI) * TWO_PI
    t = r * r
    return r * horner([c * FEAT_SCALE for c in SIN], t), horner([c * FEAT_SCALE for c in COS], t)


def gelu_parts(x):
    t = 1.0 / (1.0 + (0.3275911 / math.sqrt(2.0)) * jnp.abs(x))
    e = jnp.exp(-0.5 * x * x)
    q = 0.5 * t * horner(ERFC, t) * e
    cdf = jnp.where(x < 0.0, q, 1.0 - q)
    return x * cdf, cdf + x * e * (1.0 / math.sqrt(2.0 * math.pi))


def norm_stats(x):
    center = jnp.mean(x, axis=-1, keepdims=True)
    spread = jnp.mean(x * x, axis=-1, keepdims=True) - center * center
    inv = lax.rsqrt(spread + EPS)
    return (x - center) * inv, inv


def norm_back(grad, xhat, inv, gain):
    p = grad * gain
    return inv * (p - jnp.mean(p, axis=-1, keepdims=True) - xhat * jnp.mean(p * xhat, axis=-1, keepdims=True))


def by_eight(x):
    return jnp.sum(x.reshape(x.shape[0] // 8, 8, x.shape[1]), axis=0)


def panel(ref, p, cols):
    x = ref[p, :, :, :, cols]
    return x.reshape(x.shape[0] * x.shape[1] * x.shape[2], x.shape[3])


def low_lanes(rows):
    return iota((rows, LANES), 1) < HEAD_DIM


def widen(pair, a):
    return pair[:, a * HEAD_DIM : a * HEAD_DIM + 1]


def head_values(v, a, low):
    one = jnp.ones_like(v)
    return jnp.where(low, v, one) if a == 0 else jnp.where(low, one, v)


def state_of(states, p, a):
    own = states[2 * p + a, 0:HEAD_DIM, :]
    rest = jnp.broadcast_to(states[2 * p + a, NORMAL : NORMAL + 1, :], own.shape)
    return jnp.concatenate([own, rest] if a == 0 else [rest, own], axis=0)


def put_state(states, h, own, normal, decay):
    states[h, 0:HEAD_DIM, :] = own
    rest = jnp.zeros((STATE_ROWS - DECAY - 1, 2 * FEATS), F32)
    states[h, NORMAL:, :] = jnp.concatenate([normal, twice(decay), rest], axis=0)


def twice(x):
    return jnp.concatenate([x, x], axis=1)


def run_pairs(body, hook):
    for p in range(PAIRS):
        body(p)
        for act, *given in (hook or {}).get(p, ()):
            act(*given)


def tables(T, base, r):
    pos = base + iota((8, T), 1)
    seg_row, _, live_row, _, _ = marks(pos, base, r.lengths)
    seg1, live1, pos1 = seg_row[0:1], live_row[0:1], pos[0:1]

    def mask_rows(rows, at, n):
        row_pos = base + at + iota((n, 1), 0)
        seg_col = marks(row_pos, base, r.lengths)[0]
        allowed = (seg_col == seg1) & (pos1 <= row_pos) & (live1 > 0.0)
        r.mask[rows, :] = jnp.where(allowed, 0.0, -1e30)

    rows_loop(T, 64, mask_rows)
    hash_seed = r.seed[0] * jnp.int32(-2048144789)

    def table(p):
        place = (p * LANES + iota((LANES, LANES), 0)) * FEATS + iota((LANES, LANES), 1)
        y = place * jnp.int32(-1640531535) + hash_seed
        y = y ^ lax.shift_right_logical(y, jnp.int32(15))
        y = y * jnp.int32(739982445)
        y = y ^ lax.shift_right_logical(y, jnp.int32(13))
        y = y * jnp.int32(695872825)
        y = y ^ lax.shift_right_logical(y, jnp.int32(16))
        s = jnp.full(y.shape, -510, I32)
        for k in range(4):
            s = s + (lax.shift_right_logical(y, jnp.int32(8 * k)) & jnp.int32(255))
        top = iota((LANES, LANES), 0) < HEAD_DIM
        odd = s & 1

        def diagonal(x):
            x = x.astype(F32)
            return jnp.concatenate([jnp.where(top, x, 0.0), jnp.where(top, 0.0, x)], axis=1).astype(BF)

        r.tab[p, 0:LANES, :] = diagonal(s - odd)
        r.tab[p, LANES:, :] = diagonal(odd)
        r.tabn[p] = diagonal(s)

    pair_loop(table)


def first_norm(T, base, r):
    pick = jnp.where(iota((16, LANES), 0) == iota((16, LANES), 1), 1.0, 0.0).astype(BF)
    for p in range(PAIRS):
        rows = nt(pick, panel(r.ga, p, SMALL))
        r.gate[2 * p : 2 * p + 2, :] = rows[0:2]
        r.gate[8 + 2 * p : 10 + 2 * p, :] = rows[0:2]
        r.bias[2 * p : 2 * p + 1, :] = rows[6:7] + rows[7:8] + rows[8:9]
        r.bias[2 * p + 1 : 2 * p + 2, :] = rows[9:10] + rows[10:11] + rows[11:12]
        if p == 0:
            r.vec[...] = rows[0:8]

    def norm_rows(rows, at, n):
        xhat, _ = norm_stats(r.tok[rows, :].astype(F32))
        r.normed[rows, :] = (xhat * r.vec[2:3, :] + r.vec[3:4, :]).astype(BF)

    rows_loop(T, 64, norm_rows)
    logits = nt(r.gate[...].astype(BF), r.normed[...])[0:8] + r.bias[:, 0:1]
    r.logits[...] = logits
    pos = base + iota((8, T), 1)
    _, reset_row, live_row, carry_row, _ = marks(pos, base, r.lengths)
    decay = -(jnp.log1p(jnp.exp(-jnp.abs(logits))) + jnp.maximum(-logits, 0.0)) * live_row * (1.0 - reset_row)
    run = decay
    lane = iota((8, T), 1)
    shift = 1
    while shift < T:
        run = run + jnp.where(lane >= shift, pltpu.roll(run, shift, 1), 0.0)
        shift *= 2
    r.run[...] = run
    r.total[...] = jnp.broadcast_to(jnp.exp(run[:, T - 1 : T]) * carry_row[:, T - 1 : T], (8, LANES))
    hi = run.astype(BF).astype(F32)
    mid = (run - hi).astype(BF).astype(F32)
    run3 = jnp.concatenate([hi, mid, run - hi - mid, jnp.zeros_like(hi)], axis=0).astype(BF)

    def spread(p):
        chosen = iota((32, LANES), 0) % 8 == 2 * p + iota((32, LANES), 1) // HEAD_DIM
        r.rb[p] = tn(run3, jnp.where(chosen, 1.0, 0.0).astype(BF))

    pair_loop(spread)


def features(T, r, p, u, out):
    ones2 = head_ones(2 * LANES, 2 * LANES, HEAD_DIM, LANES)
    r.s1[...] = nn(jnp.concatenate([u, u], axis=1), r.tab[p])
    uf = u.astype(F32)
    r.s2[...] = nn(halves(uf * uf), ones2)

    def body(rows, at, n):
        s, c = sincos(r.s1[rows, :] * (lax.rsqrt(r.s2[rows, :] + 1e-6) * TABLE_SCALE))
        for a in range(2):
            out[2 * p + a, rows, 0:FEATS] = s[:, a * FEATS : (a + 1) * FEATS].astype(BF)
            out[2 * p + a, rows, FEATS : 2 * FEATS] = c[:, a * FEATS : (a + 1) * FEATS].astype(BF)

    rows_loop(T, 64, body)


def end_factor(T, base, r):
    last_seg = marks(base + T - 1 + iota((8, LANES), 1) * 0, base, r.lengths)[0][0:1, 0:1]
    seg_col, _, live_col, _, _ = marks(base + iota((T, LANES), 0), base, r.lengths)
    return jnp.where(seg_col == last_seg, live_col, 0.0)


def keys(T, base, r, hook=None):
    low = low_lanes(T)
    end_live = end_factor(T, base, r)

    def pair(p):
        kv = nn(r.normed[...], panel(r.ga, p, KV)).astype(BF)
        r.k[p] = kv[:, 0:LANES]
        r.v[p] = kv[:, LANES:]
        features(T, r, p, r.k[p], r.kf)
        decay_end = jnp.exp(r.rb[p, T - 1 : T, :] - r.rb[p]) * end_live
        four = [decay_end[:, 0:1], decay_end[:, 0:1], decay_end[:, HEAD_DIM : HEAD_DIM + 1], decay_end[:, HEAD_DIM : HEAD_DIM + 1]]
        lane = iota((T, LANES), 1)
        first = jnp.where(lane < 2, four[0], four[2])
        rough = first.astype(BF).astype(F32)
        first = jnp.where(lane % 2 == 0, rough, first - rough)
        ends = tn(first.astype(BF), jnp.concatenate([r.kf[2 * p], r.kf[2 * p + 1]], axis=1))
        for a in range(2):
            h = 2 * p + a
            scaled = (r.kf[h].astype(F32) * widen(decay_end, a)).astype(BF)
            state = tn(r.v[p], scaled)[a * HEAD_DIM : (a + 1) * HEAD_DIM]
            normal = ends[2 * a : 2 * a + 1, a * 2 * FEATS : (a + 1) * 2 * FEATS]
            normal = normal + ends[2 * a + 1 : 2 * a + 2, a * 2 * FEATS : (a + 1) * 2 * FEATS]
            put_state(r.out, h, state, normal, r.total[pl.ds(h, 1), :])

    run_pairs(pair, hook)


def queries(T, base, r, hook=None):
    low = low_lanes(T)

    def pair(p):
        r.q[p] = nn(r.normed[...], panel(r.ga, p, QUERY)).astype(BF)
        features(T, r, p, r.q[p], r.qf)
        v = r.v[p]
        for a in range(2):
            h = 2 * p + a
            r.s[...] = nt(r.qf[h], r.kf[h])
            run_row = r.run[pl.ds(h, 1), :]

            def body(rows, at, n):
                gap = jnp.minimum(widen(r.rb[p, rows, :], a) - run_row, r.mask[rows, :])
                w = r.s[rows, :] * jnp.exp(gap)
                rounded = w.astype(BF)
                r.w[h, rows, :] = rounded
                rest = jnp.sum(w - rounded.astype(F32), axis=1, keepdims=True)
                r.zfix[p, rows, a * HEAD_DIM : (a + 1) * HEAD_DIM] = jnp.broadcast_to(rest, (n, HEAD_DIM)).astype(BF)

            rows_loop(T, 64, body)
            r.own[h] = nn(r.w[h], head_values(v, a, low))

    run_pairs(pair, hook)


def carry_factor(T, base, r):
    _, _, live_col, carry_col, _ = marks(base + iota((T, LANES), 0), base, r.lengths)
    return live_col, carry_col


def attend(T, base, r):
    low = low_lanes(T)
    live_col, carry_col = carry_factor(T, base, r)

    def join(p):
        factor = jnp.exp(r.rb[p]) * carry_col
        total = []
        for a in range(2):
            h = 2 * p + a
            carried = nt(twice(r.qf[h]), halves(state_of(r.inn, p, a)))
            joined = r.own[h] + widen(factor, a) * carried
            r.joined[h] = joined
            total.append(joined)
        num = jnp.where(low, total[0], total[1])
        z = pltpu.roll(jnp.where(low, total[1], total[0]), HEAD_DIM, 1) + r.zfix[p].astype(F32)
        r.att[p] = (live_col * num * lax.rsqrt(z * z + FLOOR2)).astype(BF)

    pair_loop(join)
    o = out_columns(r)
    branch = None
    for p in range(0, PAIRS, 2):
        part = nt(
            jnp.concatenate([r.att[p], r.att[p + 1]], axis=1),
            jnp.concatenate([panel(r.gf, p, o), panel(r.gf, p + 1, o)], axis=1),
        )
        branch = part if branch is None else branch + part
    r.mid[...] = branch

    def norm_rows(rows, at, n):
        mid = r.mid[rows, :] + r.tok[rows, :].astype(F32)
        r.mid[rows, :] = mid
        xhat, inv = norm_stats(mid)
        r.xhat[rows, :] = xhat
        r.inv[rows, :] = jnp.broadcast_to(inv, (n, LANES))
        r.two[rows, :] = (xhat * r.vec[4:5, :] + r.vec[5:6, :]).astype(BF)

    rows_loop(T, 64, norm_rows)


def feed_columns(r):
    ff = (r.gf.shape[-1] - LANES) // 2
    return slice(0, ff), slice(LANES + ff, LANES + 2 * ff)


def out_columns(r):
    ff = (r.gf.shape[-1] - LANES) // 2
    return slice(ff, ff + LANES)


def feed(T, base, r):
    low = low_lanes(T)
    live_col, carry_col = carry_factor(T, base, r)
    r.acc1[...] = jnp.zeros_like(r.acc1)
    r.acc2[...] = jnp.zeros_like(r.acc2)
    u, d = feed_columns(r)
    o = out_columns(r)

    def part(p):
        up, down = panel(r.gf, p, u), panel(r.gf, p, d)
        r.h1[...] = nn(r.two[...], up)
        r.h2[...] = nn(r.cot[...], down)

        def body(rows, at, n):
            value, slope = gelu_parts(r.h1[rows, :])
            r.act[p, rows, :] = value.astype(BF)
            r.gh[p, rows, :] = (r.h2[rows, :] * slope).astype(BF)

        rows_loop(T, 64, body)
        r.acc1[...] += nt(r.act[p], down)
        r.acc2[...] += nt(r.gh[p], up)

    pair_loop(part)
    r.sums[...] = jnp.zeros_like(r.sums)

    def finish(rows, at, n):
        r.result[rows, :] = (r.mid[rows, :] + r.acc1[rows, :]).astype(BF)
        xhat, gn = r.xhat[rows, :], r.acc2[rows, :]
        r.sums[0:8, :] += by_eight(gn * xhat)
        r.sums[8:16, :] += by_eight(gn)
        back = norm_back(gn, xhat, r.inv[rows, 0:1], r.vec[4:5, :])
        grad = r.cot[rows, :].astype(F32) + back
        r.gmid[rows, :] = grad
        r.gb[rows, :] = grad.astype(BF)

    rows_loop(T, 64, finish)
    r.fsum[0:1, :] = jnp.sum(r.sums[0:8, :], axis=0, keepdims=True)
    r.fsum[1:2, :] = jnp.sum(r.sums[8:16, :], axis=0, keepdims=True)
    ones1 = head_ones(2 * LANES, LANES, HEAD_DIM, HEAD_DIM)
    row_ones = jnp.ones((16, 2 * LANES), BF)
    first_half = iota((T, LANES), 1) % HEAD_DIM < HEAD_DIM // 2

    def back(p):
        g = nn(r.gb[...], panel(r.gf, p, o)).astype(BF).astype(F32) * live_col
        total = [r.joined[2 * p], r.joined[2 * p + 1]]
        num = jnp.where(low, total[0], total[1])
        z = pltpu.roll(jnp.where(low, total[1], total[0]), HEAD_DIM, 1) + r.zfix[p].astype(F32)
        rden = lax.rsqrt(z * z + FLOOR2)
        dn = (g * rden).astype(BF).astype(F32)
        dz = nn(halves(dn * num), ones1) * (z * rden * rden)
        dz = pltpu.roll(dz * (-2.0 / HEAD_DIM), HEAD_DIM, 1)
        rough = dz.astype(BF).astype(F32)
        dz = jnp.where(first_half, rough, dz - rough)
        factor = jnp.exp(r.rb[p]) * carry_col
        for a in range(2):
            h = 2 * p + a
            joint = (jnp.where(low, dn, dz) if a == 0 else jnp.where(low, dz, dn)).astype(BF)
            r.dn[h] = joint
            r.dr[pl.ds(h, 1), :] = nt(row_ones, halves(joint.astype(F32) * total[a]))[0:1]
            adj = tn(joint, (r.qf[h].astype(F32) * widen(factor, a)).astype(BF))
            at, half = (1 - a) * HEAD_DIM, HEAD_DIM // 2
            normal = 0.5 * (adj[at : at + 1] + adj[at + half : at + half + 1])
            put_state(r.adj, h, adj[a * HEAD_DIM : (a + 1) * HEAD_DIM], normal, r.total[pl.ds(h, 1), :])

    pair_loop(back)


def up_grads(T, base, r):
    up, _ = feed_columns(r)
    pair_loop(lambda p: put_panel(r.ggf, p, up, tn(r.two[...], r.gh[p])))


def down_grads(T, base, r):
    _, down = feed_columns(r)

    def part(p):
        put_panel(r.ggf, p, down, tn(r.cot[...], r.act[p]))
        put_panel(r.ggf, p, out_columns(r), tn(r.gb[...], r.att[p]))

    pair_loop(part)


def put_panel(ref, p, cols, x):
    shape = ref.shape[1:4] + (x.shape[1],)
    ref[p, :, :, :, cols] = x.astype(BF).reshape(shape)


def back(T, base, r, tokens_all, near_hook=None, between=lambda: None, far_hook=None):
    D = r.tok.shape[1]
    low = low_lanes(T)
    _, carry_col = carry_factor(T, base, r)
    end_live = end_factor(T, base, r)
    ones1 = head_ones(2 * LANES, LANES, HEAD_DIM, HEAD_DIM)
    row_ones = jnp.ones((16, 2 * LANES), BF)
    r.acc1[...] = jnp.zeros_like(r.acc1)

    def feature_back(p, u, da):
        ds = nt(da, r.tabn[p]) * TABLE_SCALE
        uf = u.astype(F32)
        inv = lax.rsqrt(nn(halves(uf * uf), ones1) + 1e-6)
        uh = uf * inv
        return (inv * (ds - uh * nn(halves(uh * ds), ones1))).astype(BF)

    def angles(rows, source, feat, h):
        x, f = source[rows, :], feat[h, rows, :].astype(F32)
        return x[:, :FEATS] * f[:, FEATS:] - x[:, FEATS:] * f[:, :FEATS]

    def near(p):
        v = r.v[p]
        factor = jnp.exp(r.rb[p]) * carry_col
        for a in range(2):
            h = 2 * p + a
            r.s[...] = nt(r.dn[h], head_values(v, a, low))
            run_row = r.run[pl.ds(h, 1), :]

            def body(rows, at, n):
                gap = jnp.minimum(widen(r.rb[p, rows, :], a) - run_row, r.mask[rows, :])
                r.ds[rows, :] = (r.s[rows, :] * jnp.exp(gap)).astype(BF)

            rows_loop(T, 64, body)
            before = halves(state_of(r.inn, p, a), 0)
            r.s1[...] = nn(r.ds[...], r.kf[h]) + widen(factor, a) * nn(twice(r.dn[h]), before)
            r.s2[...] = tn(r.ds[...], r.qf[h])
            r.ghv[h] = tn(r.w[h], r.dn[h])

            def turn(rows, at, n):
                r.da[p, rows, a * FEATS : (a + 1) * FEATS] = angles(rows, r.s1, r.qf, h).astype(BF)
                r.da[p, rows, (2 + a) * FEATS : (3 + a) * FEATS] = angles(rows, r.s2, r.kf, h).astype(BF)

            rows_loop(T, 64, turn)

    def far(p):
        v = r.v[p]
        decay_end = jnp.exp(r.rb[p, T - 1 : T, :] - r.rb[p]) * end_live
        grad_v = []
        for a in range(2):
            h = 2 * p + a
            end, hv = state_of(r.aend, p, a), head_values(v, a, low)
            late = widen(decay_end, a) * nt(twice(r.kf[h]), halves(end))
            r.s2[...] = widen(decay_end, a) * nn(twice(hv), halves(end, 0))
            grad_hv = r.ghv[h] + late
            grad_v.append(grad_hv)

            def turn(rows, at, n):
                lanes = slice((2 + a) * FEATS, (3 + a) * FEATS)
                r.da[p, rows, lanes] = (r.da[p, rows, lanes].astype(F32) + angles(rows, r.s2, r.kf, h)).astype(BF)

            rows_loop(T, 64, turn)
            hvf = hv.astype(F32)
            k_side = nt(row_ones, halves(hvf * grad_hv))
            r.drun[pl.ds(h, 1), :] = r.dr[pl.ds(h, 1), :] - k_side[0:1]
            owed = jnp.sum(end * state_of(r.inn, p, a), axis=0, keepdims=True)
            owed = r.total[pl.ds(h, 1), 0:1] * jnp.sum(owed, axis=1, keepdims=True)
            owed = owed + jnp.sum(jnp.sum(hvf * late, axis=0, keepdims=True), axis=1, keepdims=True)
            r.owed[pl.ds(h, 1), :] = jnp.broadcast_to(owed, (1, LANES))
        grads = jnp.concatenate(
            [
                feature_back(p, r.k[p], r.da[p, :, 2 * FEATS :]),
                jnp.where(low, grad_v[0], grad_v[1]).astype(BF),
                feature_back(p, r.q[p], r.da[p, :, : 2 * FEATS]),
            ],
            axis=1,
        )
        weights = jnp.concatenate([panel(r.ga, p, KV), panel(r.ga, p, QUERY)], axis=1)
        r.acc1[...] += nt(grads, weights)
        put_panel(r.gga, p, slice(0, 3 * LANES), tn(r.normed[...], grads))

    run_pairs(near, near_hook)
    between()
    run_pairs(far, far_hook)
    pos = base + iota((8, T), 1)
    _, reset_row, live_row, _, filled = marks(pos, base, r.lengths)
    lane = iota((8, T), 1)
    run = r.drun[...]
    shift = 1
    while shift < T:
        run = run + jnp.where(lane < T - shift, pltpu.roll(run, T - shift, 1), 0.0)
        shift *= 2
    grad_decay = run + r.owed[:, 0:1]
    logits = r.logits[...]
    e = jnp.exp(-jnp.abs(logits))
    small, large = e / (1.0 + e), 1.0 / (1.0 + e)
    gate = jnp.where(logits >= 0.0, large, small)
    rest = jnp.where(logits >= 0.0, small, large)
    penalty = GATE_PEN * tokens_all / HEADS / jnp.broadcast_to(filled, (8, T)).astype(F32)
    grad_logits = grad_decay * live_row * (1.0 - reset_row) * rest + penalty * live_row * gate * rest
    both = halves(grad_logits, 0)
    r.acc1[...] += tn(both, r.gate[...].astype(BF))
    gate_rows = nn(both, r.normed[...])
    gate_rows = gate_rows[0:8] + gate_rows[8:16]
    bias = jnp.broadcast_to(jnp.sum(grad_logits, axis=1, keepdims=True), (8, D))
    r.sums[...] = jnp.zeros_like(r.sums)

    def finish(rows, at, n):
        xhat, inv = norm_stats(r.tok[rows, :].astype(F32))
        gn = r.acc1[rows, :]
        r.sums[0:8, :] += by_eight(gn * xhat)
        r.sums[8:16, :] += by_eight(gn)
        r.gtok[rows, :] = r.gmid[rows, :] + norm_back(gn, xhat, inv, r.vec[2:3, :])

    rows_loop(T, 64, finish)
    norm_gain = jnp.sum(r.sums[0:8, :], axis=0, keepdims=True)
    norm_shift = jnp.sum(r.sums[8:16, :], axis=0, keepdims=True)
    lines = [norm_gain, norm_shift, r.fsum[0:2, :]]
    for p in range(PAIRS):
        rows = jnp.concatenate([gate_rows[2 * p : 2 * p + 2]] + lines + [bias[2 * p : 2 * p + 2]], axis=0)
        for g in range(D // LANES):
            r.lines[p, g] = rows[:, g * LANES : (g + 1) * LANES]


class Refs:
    def __init__(self, **refs):
        self.__dict__.update(refs)


def buffers(T, D, att, rest, ff, seq):
    z = (PAIRS, seq // 2, 2, D // seq)
    pair = (PAIRS, T, LANES)
    return {
        "ga": (z + (att,), BF), "gf": (z + (rest,), BF), "gga": (z + (att - LANES,), BF), "ggf": (z + (rest,), BF),
        "gate": ((16, D), F32), "bias": ((8, D), F32), "vec": ((8, D), F32), "normed": ((T, D), BF),
        "logits": ((8, T), F32), "run": ((8, T), F32), "total": ((8, LANES), F32), "mask": ((T, T), F32),
        "s1": ((T, 2 * FEATS), F32), "s2": ((T, 2 * FEATS), F32), "s": ((T, T), F32),
        "tab": ((PAIRS, 2 * LANES, 2 * FEATS), BF), "tabn": ((PAIRS, LANES, 2 * FEATS), BF),
        "q": (pair, BF), "k": (pair, BF), "v": (pair, BF), "rb": (pair, F32),
        "qf": ((HEADS, T, 2 * FEATS), BF), "kf": ((HEADS, T, 2 * FEATS), BF),
        "out": (STATES, F32), "inn": (STATES, F32), "adj": (STATES, F32), "aend": (STATES, F32),
        "w": ((HEADS, T, T), BF), "own": ((HEADS, T, LANES), F32), "joined": ((HEADS, T, LANES), F32),
        "att": (pair, BF), "zfix": (pair, BF), "mid": ((T, D), F32), "xhat": ((T, D), F32), "inv": ((T, LANES), F32), "two": ((T, D), BF),
        "acc1": ((T, D), F32), "acc2": ((T, D), F32), "h1": ((T, ff), F32), "h2": ((T, ff), F32),
        "act": ((PAIRS, T, ff), BF), "gh": ((PAIRS, T, ff), BF), "sums": ((16, D), F32), "fsum": ((8, D), F32),
        "result": ((T, D), BF), "gmid": ((T, D), F32), "gb": ((T, D), BF), "dr": ((8, T), F32),
        "dn": ((HEADS, T, LANES), BF), "ds": ((T, T), BF), "da": ((PAIRS, T, 4 * FEATS), BF), "ghv": ((HEADS, T, LANES), F32),
        "lines": ((PAIRS, D // LANES, 8, LANES), F32),
        "drun": ((8, T), F32), "owed": ((8, LANES), F32), "gtok": ((T, D), F32),
    }


FRONT = (
    ("ga",),
    ("gate", "vec", "normed", "logits", "run", "total", "mask", "tabn", "q", "k", "v", "rb", "qf", "kf", "out", "w", "own", "zfix"),
    ("bias", "s1", "s2", "s", "tab"),
)
MIDDLE = (
    ("gf", "vec", "rb", "qf", "own", "zfix", "inn", "total"),
    ("ggf", "result", "gmid", "fsum", "dr", "dn", "adj"),
    ("joined", "att", "mid", "xhat", "inv", "two", "acc1", "acc2", "h1", "h2", "act", "gh", "sums", "gb"),
)
BACK = (
    ("ga", "gate", "vec", "normed", "logits", "run", "total", "mask", "tabn", "q", "k", "v", "rb", "qf", "kf",
     "w", "inn", "aend", "gmid", "fsum", "dr", "dn"),
    ("gga", "gtok", "lines"),
    ("s", "s1", "s2", "ds", "da", "ghv", "drun", "owed", "acc1", "sums"),
)
SHARED = {"joined": "own", "h1": "s", "gmid": "mid", "ds": "gb", "adj": "out", "da": "act", "ghv": "own"}


def front(T, base, r):
    tables(T, base, r)
    first_norm(T, base, r)
    keys(T, base, r)
    queries(T, base, r)


def middle(T, base, r):
    attend(T, base, r)
    feed(T, base, r)
    up_grads(T, base, r)
    down_grads(T, base, r)


def here(T):
    return (lax.axis_index("seq") * lax.axis_size("head") + lax.axis_index("head")) * T


def stage(which, names, specs, outer, args, state):
    reads, writes, scratch = names
    shape = lambda n: jax.ShapeDtypeStruct(*specs[n])
    vmem, smem = pl.BlockSpec(memory_space=pltpu.VMEM), pl.BlockSpec(memory_space=pltpu.SMEM)

    def kernel(*refs):
        base_ref, lengths, seed, tok, cot = refs[:5]
        rest = dict(zip(reads + writes + scratch, refs[5:]))
        which(base_ref[0], Refs(lengths=lengths, seed=seed, tok=tok, cot=cot, **rest))

    out = pl.pallas_call(
        kernel,
        out_shape=[shape(n) for n in writes],
        in_specs=[smem] * 3 + [vmem] * (2 + len(reads)),
        out_specs=[vmem] * len(writes),
        scratch_shapes=[pltpu.VMEM(*specs[n]) for n in scratch],
        compiler_params=pltpu.CompilerParams(vmem_limit_bytes=VMEM_BYTES),
        name=outer,
    )(*args, *[state[n] for n in reads])
    state.update(zip(writes, out))


def scan_states(out, reverse):
    seq, head = lax.axis_size("seq"), lax.axis_size("head")
    count = seq * head
    me = lax.axis_index("seq") * head + lax.axis_index("head")
    state = (out[:, DECAY : DECAY + 1, 0:1], out[:, :DECAY])
    step = 1
    order = lambda pairs: [(b, a) for a, b in pairs] if reverse else pairs
    axes = ("seq", "head")
    while step < count:
        moved = jax.tree.map(lambda x: lax.ppermute(x, axes, order([(i, i + step) for i in range(count - step)])), state)
        has = (me < count - step) if reverse else (me >= step)
        f, m = state
        state = (jnp.where(has, f * moved[0], f), m + jnp.where(has, f * moved[1], 0.0))
        step *= 2
    moved = lax.ppermute(state[1], axes, order([(i, i + 1) for i in range(count - 1)]))
    return jnp.concatenate([moved, jnp.zeros((HEADS, STATE_ROWS - DECAY, 2 * FEATS), F32)], axis=1)


def remote(src, dst, send, recv, to):
    return pltpu.make_async_remote_copy(
        src_ref=src, dst_ref=dst, send_sem=send, recv_sem=recv, device_id=to, device_id_type=MESH
    )


class Place:
    def __init__(self):
        self.seq, self.head = lax.axis_size("seq"), lax.axis_size("head")
        s, h = lax.axis_index("seq"), lax.axis_index("head")
        self.z, self.y, self.x, self.c = s // 2, s % 2, h // 2, h % 2
        self.depth = self.seq // 2
        self.count = self.seq * self.head
        self.me = s * self.head + h

    def device(self, z=None, y=None, x=None, c=None):
        pick = lambda given, own: own if given is None else given
        z, y, x, c = pick(z, self.z), pick(y, self.y), pick(x, self.x), pick(c, self.c)
        return (z * 2 + y, x * 2 + c)

    def number(self, i):
        return (i // self.head, i % self.head)

    def around(self, k):
        return (self.z + k) % self.depth

class Semaphores:
    def __init__(self, send, recv):
        self.send, self.recv, self.used = send, recv, 0

    def copy(self, src, dst, to):
        i = self.used
        self.used += 1
        return remote(src, dst, self.send.at[i], self.recv.at[i], to)


GATHER_COPIES = 2 * (3 + 1 + 2 + 2)
SCATTER_COPIES = 2 + 2 * (1 + 1 + 3)


def gather_stages(place, g, lanes, sems):
    half = g.shape[3] // 2
    z, y, x, c = place.z, place.y, place.x, place.c
    pair = x * 2 + c
    stages = [[], [], [], []]
    for part in range(2):
        rows = pl.ds(part * half, half)
        same = lambda ref, to: sems.copy(ref, ref, to)
        for k in range(1, place.depth):
            stages[0].append(same(g.at[pair, z, y, rows, lanes], place.device(z=place.around(k))))
        to_y, to_x = place.device(y=1 - y), place.device(x=1 - x)
        if part == 0:
            stages[1].append(same(g.at[pair, :, y, rows, lanes], to_y))
            stages[2].append(same(g.at[pair, :, :, rows, lanes], to_x))
        else:
            stages[1].append(same(g.at[pair, :, y, rows, lanes], to_x))
            for other in range(2):
                stages[2].append(same(g.at[other * 2 + c, :, y, rows, lanes], to_y))
        for other in range(2):
            stages[3].append(same(g.at[other * 2 + c, :, :, rows, lanes], place.device(c=1 - c)))
    return stages


def begin(stage):
    for copy in stage:
        copy.start()


def arrived(stage):
    for copy in stage:
        copy.wait_recv()


def sent(*stages):
    for stage in stages:
        for copy in stage:
            copy.wait_send()


class Gather:
    def __init__(self, place, ga, gf, sems):
        ff = (gf.shape[-1] - LANES) // 2
        lanes = lambda first, count: pl.ds(first, count)
        self.chunks = [
            gather_stages(place, ref, part, sems)
            for ref, part in (
                (ga, lanes(0, 3 * LANES)),
                (ga, lanes(3 * LANES, LANES)),
                (gf, lanes(0, LANES + ff)),
                (gf, lanes(LANES + ff, ff)),
            )
        ]

    def begin(self, chunk):
        begin(self.chunks[chunk][0])

    def step(self, chunk, stage):
        arrived(self.chunks[chunk][stage])
        if stage < 3:
            begin(self.chunks[chunk][stage + 1])

    def finish(self):
        for chunk in self.chunks:
            sent(*chunk)


def add_blocks(to, others, count, where):
    def one(i, carry):
        at = where(i)
        total = to[at].astype(F32)
        for ref, index in others:
            total = total + ref[index(i)].astype(F32)
        to[at] = total.astype(to.dtype)
        return carry

    lax.fori_loop(0, count, one, 0)


class Scatter:
    def __init__(self, place, gg, lanes, out, buf, sems):
        self.place, self.gg, self.lanes, self.out = place, gg, lanes, out
        self.r1, self.r2a, self.r2b, self.r3a, self.r3b, self.r4a, self.r4b = buf
        z, y, x, c, n = place.z, place.y, place.x, place.c, place.depth
        self.half = half = gg.shape[3] // 2
        first, last = pl.ds(0, half), pl.ds(half, half)
        other, to_y, to_x = place.device(c=1 - c), place.device(y=1 - y), place.device(x=1 - x)
        self.stages = [
            [sems.copy(gg.at[i * 2 + 1 - c, :, :, :, lanes], self.r1.at[i], other) for i in range(2)],
            [
                sems.copy(self.r1.at[1 - x, :, :, first], self.r2a, to_x),
                sems.copy(self.r1.at[:, :, 1 - y, last], self.r2b, to_y),
            ],
            [sems.copy(self.r2a.at[:, 1 - y], self.r3a, to_y), sems.copy(self.r2b.at[1 - x], self.r3b, to_x)],
            [
                sems.copy(ref.at[place.around(k)], slots.at[k - 1], place.device(z=place.around(k)))
                for ref, slots in ((self.r3a, self.r4a), (self.r3b, self.r4b))
                for k in range(1, n)
            ],
        ]

    def start(self):
        begin(self.stages[0])

    def step(self, i):
        place, n, half = self.place, self.place.depth, self.half
        y, x, c = place.y, place.x, place.c
        first, last = slice(0, half), slice(half, 2 * half)
        lanes = self.lanes
        arrived(self.stages[i])
        if i == 0:
            block = lambda j: (j // (2 * n), (j // 2) % n, j % 2)
            add_blocks(self.r1, [(self.gg, lambda j: ((j // (2 * n)) * 2 + c, (j // 2) % n, j % 2, slice(None), lanes))], 4 * n, block)
        elif i == 1:
            add_blocks(self.r2a, [(self.r1, lambda j: (x, j // 2, j % 2, first))], 2 * n, lambda j: (j // 2, j % 2))
            add_blocks(self.r2b, [(self.r1, lambda j: (j // n, j % n, y, last))], 2 * n, lambda j: (j // n, j % n))
        elif i == 2:
            add_blocks(self.r3a, [(self.r2a, lambda j: (j, y))], n, lambda j: (j,))
            add_blocks(self.r3b, [(self.r2b, lambda j: (x, j))], n, lambda j: (j,))
        else:
            for ref, slots, rows in ((self.r3a, self.r4a, first), (self.r3b, self.r4b, last)):
                total = ref[place.z].astype(F32)
                for k in range(n - 1):
                    total = total + slots[k].astype(F32)
                self.out[rows, lanes] = total
        if i < 3:
            begin(self.stages[i + 1])

    def finish(self):
        sent(*self.stages)


def scatter_buffers(seq, rows, cols):
    n, half = seq // 2, rows // 2
    return [
        pltpu.VMEM(shape + (cols,), BF)
        for shape in ((2, n, 2, rows), (n, 2, half), (2, n, half), (n, half), (n, half), (n - 1, half), (n - 1, half))
    ]


class Scan:
    def __init__(self, place, reverse, out, inn, box, planes, send, recv):
        self.place, self.reverse = place, reverse
        self.out, self.inn, self.planes = out, inn, planes
        self.pair, self.chip, self.box, self.back = box
        self.chips = HEADS // 2
        self.mine = place.y * 2 + place.x
        self.half, self.rest = place.c * self.chips, (1 - place.c) * self.chips
        self.sems = Semaphores(send, recv)
        other = place.device(c=1 - place.c)
        at = lambda ref, first: ref.at[pl.ds(first, self.chips)]
        near = [lax.rem(self.mine + k, self.chips) for k in range(1, self.chips)]
        chip = lambda m: place.device(y=m // 2, x=m % 2)
        total = planes.at[place.z]
        copy = self.sems.copy
        self.ways = [
            [copy(at(out, self.rest), self.pair, other)],
            [copy(self.chip.at[m], self.box.at[self.mine], chip(m)) for m in near],
            [copy(total, total, place.device(z=place.around(k))) for k in range(1, place.depth)],
            [copy(self.box.at[m], self.back.at[self.mine], chip(m)) for m in near],
            [copy(self.pair, at(inn, self.half), other)],
        ]

    def start(self):
        begin(self.ways[0])

    def chain(self, ref, count):
        kept = iota((STATE_ROWS, 2 * FEATS), 0) != DECAY
        state = jnp.where(kept, 0.0, 1.0)
        for i in range(count):
            d = count - 1 - i if self.reverse else i
            term = ref[d]
            ref[d] = state
            state = state * term[DECAY : DECAY + 1, :] + jnp.where(kept, term, 0.0)
        return state

    def earlier_is_mine(self):
        return (self.place.c == 0) != self.reverse

    def cores(self):
        arrived(self.ways[0])
        kept = iota((STATE_ROWS, 2 * FEATS), 0) != DECAY
        first = jnp.broadcast_to(self.earlier_is_mine(), kept.shape)
        for i in range(self.chips):
            mine, its = self.out[self.half + i], self.pair[i]
            early, late = jnp.where(first, mine, its), jnp.where(first, its, mine)
            self.chip[i] = early * late[DECAY : DECAY + 1, :] + jnp.where(kept, late, 0.0)
        begin(self.ways[1])
        self.box[self.mine] = self.chip[self.mine]

    def plane(self):
        arrived(self.ways[1])
        self.planes[self.place.z] = self.chain(self.box, self.chips)
        begin(self.ways[2])

    def line(self):
        arrived(self.ways[2])
        sent(self.ways[2])
        self.chain(self.planes, self.place.depth)
        before = self.planes[self.place.z]
        for m in range(self.chips):
            own = self.box[m]
            self.box[m] = own + own[DECAY : DECAY + 1, :] * before
        begin(self.ways[3])
        self.back[self.mine] = self.box[self.mine]

    def share(self):
        arrived(self.ways[3])
        sent(self.ways[0])
        first = jnp.broadcast_to(self.earlier_is_mine(), (STATE_ROWS, 2 * FEATS))
        for i in range(self.chips):
            mine, its, before = self.out[self.half + i], self.pair[i], self.back[i]
            early = jnp.where(first, mine, its)
            late = before * early[DECAY : DECAY + 1, :] + early
            self.inn[self.half + i] = jnp.where(first, before, late)
            self.pair[i] = jnp.where(first, late, before)
        begin(self.ways[4])

    def receive(self):
        arrived(self.ways[4])

    def finish(self):
        sent(self.ways[1], self.ways[3], self.ways[4])


class Lines:
    def __init__(self, place, lines, box, out, send, recv):
        self.place, self.lines, self.box, self.out, self.send, self.recv = place, lines, box, out, send, recv

    def tile(self, j):
        return self.lines.at[lax.rem(j, self.place.head), (j // self.place.head) * self.lines.shape[1] // self.place.seq]

    def start(self):
        me, count = self.place.me, self.place.count

        def one(k, carry):
            j = lax.rem(me + k, count)
            remote(self.tile(j), self.box.at[me], self.send, self.recv, self.place.number(j)).start()
            return carry

        lax.fori_loop(1, count, one, 0)
        self.box[me] = self.tile(me)[...]

    def finish(self):
        most = self.box.at[pl.ds(0, self.place.count - 1)]
        both = remote(most, most, self.send, self.recv, self.place.device(c=1 - self.place.c))
        both.wait_recv()

        def one(i, total):
            return total + self.box[i]

        self.out[...] = lax.fori_loop(0, self.place.count, one, jnp.zeros(self.out.shape, F32))
        both.wait_send()


def greet_all(place):
    barrier = pltpu.get_barrier_semaphore()

    def one(k, carry):
        to = place.number(lax.rem(place.me + k, place.count))
        pl.semaphore_signal(barrier, inc=1, device_id=to, device_id_type=MESH)
        return carry

    lax.fori_loop(1, place.count, one, 0)
    pl.semaphore_wait(barrier, place.count - 1)


def layer_kernel(names, specs, tokens_all, T, lengths, seed, tok, cot, att, rest, result, gtok, grad_a, grad_f, grad_lines, *scratch):
    place = Place()
    base = place.me * T
    arrays = dict(zip(names, scratch))
    arrays.update({name: arrays[other] for name, other in SHARED.items()})
    scratch = scratch[len(names) :]
    r = Refs(lengths=lengths, seed=seed, tok=tok, cot=cot, result=result, gtok=gtok, **arrays)
    widths = specs["scatter"]
    sums, scratch = [scratch[7 * i : 7 * i + 7] for i in range(3)], scratch[21:]
    boxes, planes, line_box, sems = (scratch[0:4], scratch[4:8]), scratch[8:10], scratch[10], scratch[11:]
    pair = place.x * 2 + place.c
    r.ga[pair, place.z, place.y] = att[...]
    r.gf[pair, place.z, place.y] = rest[...]
    gather = Gather(place, r.ga, r.gf, Semaphores(sems[0], sems[1]))
    forth = Scan(place, False, r.out, r.inn, boxes[0], planes[0], sems[2], sems[3])
    home = Scan(place, True, r.adj, r.aend, boxes[1], planes[1], sems[4], sems[5])
    later = Semaphores(sems[6], sems[7])
    up, down = feed_columns(r)
    sum_u = Scatter(place, r.ggf, up, grad_f, sums[0], later)
    sum_d = Scatter(place, r.ggf, slice(up.stop, down.stop), grad_f, sums[1], later)
    sum_a = Scatter(place, r.gga, slice(0, widths[2]), grad_a, sums[2], later)
    lines = Lines(place, r.lines, line_box, grad_lines, sems[8], sems[9])
    greet_all(place)

    g = gather.step
    gather.begin(0)
    gather.begin(1)
    tables(T, base, r)
    g(0, 0)
    gather.begin(2)
    g(0, 1)
    g(1, 0)
    g(0, 2)
    g(1, 1)
    g(2, 0)
    gather.begin(3)
    g(0, 3)
    first_norm(T, base, r)
    g(1, 2)
    g(2, 1)
    keys(T, base, r, {1: [(g, 3, 0)], 3: [(g, 2, 2), (g, 3, 1)]})
    forth.start()
    g(1, 3)
    queries(T, base, r, {0: [(forth.cores,)], 1: [(g, 3, 2), (forth.plane,)], 3: [(forth.line,)]})
    g(2, 3)
    forth.share()
    g(3, 3)
    forth.receive()
    forth.finish()
    attend(T, base, r)
    feed(T, base, r)
    home.start()
    up_grads(T, base, r)
    sum_u.start()
    home.cores()
    down_grads(T, base, r)
    sum_d.start()
    near = {0: [(home.plane,), (sum_u.step, 0)], 1: [(sum_d.step, 0)], 2: [(home.line,)], 3: [(sum_u.step, 1), (home.share,)]}
    far = {0: [(sum_d.step, 1)], 1: [(sum_u.step, 2)], 2: [(sum_d.step, 2)]}
    back(T, base, r, tokens_all, near, home.receive, far)
    sum_a.start()
    lines.start()
    sum_a.step(0)
    sum_u.step(3)
    sum_a.step(1)
    sum_d.step(3)
    sum_a.step(2)
    lines.finish()
    sum_a.step(3)
    gather.finish()
    home.finish()
    for each in (sum_u, sum_d, sum_a):
        each.finish()


def layer_near(lengths, seed, tokens, cotangent, att, rest, specs, seq, head):
    T, D = tokens.shape
    count = seq * head
    rows, ff = D // seq, specs["act"][0][2]
    held = [n for n in dict.fromkeys(sum((sum(names, ()) for names in (FRONT, MIDDLE, BACK)), ())) if n not in SHARED]
    held = [n for n in held if n not in ("result", "gtok")]
    dma = pltpu.SemaphoreType.DMA
    scratch = [pltpu.VMEM(*specs[n]) for n in held]
    panels = att.shape[1] - LANES
    widths = (ff, LANES + ff, panels)
    states = lambda count: pltpu.VMEM((count,) + STATES[1:], F32)
    for width in widths:
        scratch += scatter_buffers(seq, rows, width)
    scratch += [states(HEADS // 2)] * 8 + [states(seq // 2)] * 2 + [pltpu.VMEM((count, 8, LANES), F32)]
    scratch += [dma((4 * GATHER_COPIES,))] * 2 + [dma((16,))] * 4 + [dma((3 * SCATTER_COPIES,))] * 2 + [dma(())] * 2
    vmem, smem = pl.BlockSpec(memory_space=pltpu.VMEM), pl.BlockSpec(memory_space=pltpu.SMEM)
    shape = jax.ShapeDtypeStruct
    return pl.pallas_call(
        functools.partial(layer_kernel, held, {"scatter": widths}, T * count, T),
        out_shape=[shape((T, D), BF), shape((T, D), F32), shape((rows, panels), F32), shape((rows, rest.shape[1]), F32),
                   shape((8, LANES), F32)],
        in_specs=[smem] * 2 + [vmem] * 4,
        out_specs=[vmem] * 5,
        scratch_shapes=scratch,
        compiler_params=pltpu.CompilerParams(collective_id=0, has_side_effects=True, vmem_limit_bytes=LAYER_BYTES),
        name="layer",
    )(lengths, seed, tokens, cotangent, att, rest)


def bias_columns(gate_bias):
    hi = lax.reduce_precision(gate_bias, 8, 7)
    mid = lax.reduce_precision(gate_bias - hi, 8, 7)
    return jnp.stack([hi, mid, gate_bias - hi - mid], axis=1).astype(BF)


def gather_any(q, k, v, gate, vectors, bias, out, up, down, seq):
    D = q.shape[0] * seq

    def whole(w, rows, cols):
        w = lax.all_gather(w, rows, axis=0, tiled=True)
        return lax.all_gather(w, cols, axis=1, tiled=True)

    def panels(w):
        return w.reshape(D, PAIRS, w.shape[1] // PAIRS).transpose(1, 0, 2)

    q, k, v = (panels(whole(w, "seq", "head")) for w in (q, k, v))
    gates = panels(whole(gate, "seq", "head"))
    lines = [jnp.broadcast_to(lax.all_gather(w, "seq", tiled=True)[None, :, None], (PAIRS, D, 1)) for w in vectors]
    bias = bias_columns(lax.all_gather(bias, "head", tiled=True)).reshape(PAIRS, 1, 6)
    pad = jnp.zeros((PAIRS, D, LANES - 12), BF)
    ga = jnp.concatenate([k, v, gates] + lines + [jnp.broadcast_to(bias, (PAIRS, D, 6)), pad, q], axis=2)
    gf = [panels(whole(up, "seq", "head")), panels(whole(out, "head", "seq").T), panels(whole(down, "head", "seq").T)]
    gf = jnp.concatenate(gf, axis=2)
    shape = (PAIRS, seq // 2, 2, D // seq)
    return ga.reshape(shape + ga.shape[2:]), gf.reshape(shape + gf.shape[2:])


def unpack(grad_a, grad_f, lines, ff):
    rows = grad_a.shape[0]
    block = lambda i: grad_a[:, i * LANES : (i + 1) * LANES]
    place = lax.axis_index("seq") % (LANES // rows) * rows
    own = lax.dynamic_slice_in_dim(lines, place, rows, 1)
    return (
        own[2], own[3], block(2), block(0), block(1), own[0:2].T, lines[6:8, 0],
        grad_f[:, ff : ff + LANES].T, own[4], own[5], grad_f[:, :ff], grad_f[:, LANES + ff :].T,
    )


def scatter_any(gga, ggf, lines, ff):
    gga, ggf = (x.reshape(PAIRS, -1, x.shape[-1]).astype(F32) for x in (gga, ggf))

    def grid(x):
        x = x.transpose(1, 0, 2).reshape(x.shape[1], -1)
        x = lax.psum_scatter(x, "seq", scatter_dimension=0, tiled=True)
        return lax.psum_scatter(x, "head", scatter_dimension=1, tiled=True)

    block = lambda i: gga[:, :, i * LANES : (i + 1) * LANES]
    lines = lines.transpose(0, 2, 1, 3).reshape(PAIRS, 8, -1)
    gates = lines[:, 0:2].transpose(0, 2, 1)
    bias = lines[:, 6:8, 0].reshape(HEADS)
    bias = lax.psum_scatter(lax.psum(bias, "seq"), "head", scatter_dimension=0, tiled=True)
    lines = lax.psum_scatter(lax.psum(lines[0, 2:6].T, "head"), "seq", scatter_dimension=0, tiled=True)
    return (
        lines[:, 0], lines[:, 1], grid(block(2)), grid(block(0)), grid(block(1)), grid(gates), bias,
        grid(ggf[:, :, ff : ff + LANES]).T, lines[:, 2], lines[:, 3], grid(ggf[:, :, :ff]),
        grid(ggf[:, :, LANES + ff :]).T,
    )


def shards(
    tokens, lengths, feature_seed, norm_gain, norm_shift, query_weight, key_weight, value_weight, gate_weight, gate_bias,
    out_weight, ffn_gain, ffn_shift, up_weight, down_weight, cotangent,
):
    seq, head = lax.axis_size("seq"), lax.axis_size("head")
    T, D = tokens.shape
    rows = D // seq
    ff = up_weight.shape[1] * head // PAIRS
    vectors = (norm_gain, norm_shift, ffn_gain, ffn_shift)
    specs = buffers(T, D, ATT, LANES + 2 * ff, ff, seq)
    if (seq, head) == (HEADS, PAIRS):
        bias = jnp.broadcast_to(bias_columns(gate_bias).reshape(1, 6), (rows, 6))
        small = [gate_weight] + [w[:, None] for w in vectors] + [bias, jnp.zeros((rows, LANES - 12), BF)]
        att = jnp.concatenate([key_weight, value_weight] + small + [query_weight], axis=1)
        rest = jnp.concatenate([up_weight, out_weight.T, down_weight.T], axis=1)
        result, grad_tokens, grad_a, grad_f, lines = layer_near(
            lengths, feature_seed, tokens, cotangent, att, rest, specs, seq, head)
        return (result, grad_tokens) + unpack(grad_a, grad_f, lines, ff)
    ga, gf = gather_any(query_weight, key_weight, value_weight, gate_weight, vectors, gate_bias, out_weight, up_weight,
                        down_weight, seq)
    args = (here(T).astype(I32).reshape(1), lengths, feature_seed, tokens, cotangent)
    state = {"ga": ga, "gf": gf}
    stage(lambda base, r: front(T, base, r), FRONT, specs, "front", args, state)
    state["inn"] = scan_states(state["out"], False)
    stage(lambda base, r: middle(T, base, r), MIDDLE, specs, "middle", args, state)
    state["aend"] = scan_states(state["adj"], True)
    stage(lambda base, r: back(T, base, r, T * seq * head), BACK, specs, "back", args, state)
    return (state["result"], state["gtok"]) + scatter_any(state["gga"], state["ggf"], state["lines"], ff)


def solution(mesh):
    both, rows, grid = P(("seq", "head"), None), P("seq"), P("seq", "head")
    return jax.shard_map(
        shards,
        mesh=mesh,
        in_specs=(both, P(), P(), rows, rows, grid, grid, grid, grid, P("head"), P("head", "seq"), rows, rows, grid,
                  P("head", "seq"), both),
        out_specs=(both, both, rows, rows, grid, grid, grid, grid, P("head"), P("head", "seq"), rows, rows, grid,
                   P("head", "seq")),
        check_vma=False,
    )
```

```python
import functools
import math

import jax
import jax.numpy as jnp
from jax import lax
from jax.experimental import pallas as pl
from jax.experimental.pallas import tpu as pltpu
from jax.sharding import PartitionSpec as P

BF, F32, I32 = jnp.bfloat16, jnp.float32, jnp.int32
MESH = pl.DeviceIdType.MESH
HEADS, HEAD_DIM, FEATS = 8, 64, 128
PAIRS = HEADS // 2
LANES = 128
EPS, FLOOR2, GATE_PEN = 1e-5, 0.0625, 0.5
TABLE_SCALE = 1.0 / math.sqrt(21845.0)
FEAT_SCALE = 1.0 / math.sqrt(FEATS)
INV_TWO_PI, TWO_PI = 1.0 / (2.0 * math.pi), 2.0 * math.pi
SIN = (0.9999996027571254, -0.16666553170295112, 0.008332405799301931, -0.00019808693226998236,
       2.6997700314773084e-06, -2.036409109746239e-08)
COS = (0.9999992193982472, -0.4999942543676011, 0.04165980908449851, -0.0013858873219640337,
       2.420384320646774e-05, -2.1976364824224383e-07)
ERFC = (0.254829592, -0.284496736, 1.421413741, -1.453152027, 1.061405429)
ATT = 4 * LANES
KEY, SMALL, VALUE, QUERY = (slice(i * LANES, (i + 1) * LANES) for i in range(4))
NORMAL, DECAY, STATE_ROWS = HEAD_DIM, HEAD_DIM + 1, HEAD_DIM + 8
STATES = (HEADS, STATE_ROWS, 2 * FEATS)
VMEM_BYTES = 56 * 1024 * 1024
LAYER_BYTES = 63 * 1024 * 1024


def nn(a, b):
    return lax.dot_general(a, b, (((1,), (0,)), ((), ())), preferred_element_type=F32)


def nt(a, b):
    return lax.dot_general(a, b, (((1,), (1,)), ((), ())), preferred_element_type=F32)


def tn(a, b):
    return lax.dot_general(a, b, (((0,), (0,)), ((), ())), preferred_element_type=F32)


def halves(x, axis=1):
    hi = x.astype(BF)
    return jnp.concatenate([hi, (x - hi.astype(F32)).astype(BF)], axis=axis)


def iota(shape, dim):
    return lax.broadcasted_iota(I32, shape, dim)


def rows_loop(total, step, body):
    body(pl.ds(0, total), 0, total)


def pair_loop(body):
    def one(p, carry):
        body(p)
        return carry

    lax.fori_loop(0, PAIRS, one, 0)


def head_ones(rows, cols, row_span, col_span):
    same = (iota((rows, cols), 0) // row_span) % 2 == iota((rows, cols), 1) // col_span
    return jnp.where(same, 1.0, 0.0).astype(BF)


def marks(pos, base, lengths_ref):
    start = jnp.int32(0)
    segment = jnp.zeros(pos.shape, I32)
    reset = jnp.zeros(pos.shape, F32)
    carry = jnp.ones(pos.shape, F32)
    for d in range(lengths_ref.shape[0]):
        segment = segment + jnp.where(pos >= start, 1, 0)
        reset = jnp.where(pos == start, 1.0, reset)
        carry = jnp.where((pos >= start) & (pos - start <= pos - base), 0.0, carry)
        start = start + lengths_ref[d]
    live = jnp.where(pos < start, 1.0, 0.0)
    segment = segment + jnp.where(pos >= start, 1, 0)
    return segment, reset, live, carry, start


def horner(coefs, t):
    acc = jnp.full_like(t, coefs[-1])
    for c in coefs[-2::-1]:
        acc = acc * t + c
    return acc


def sincos(angle):
    r = angle - jnp.round(angle * INV_TWO_PI) * TWO_PI
    t = r * r
    return r * horner([c * FEAT_SCALE for c in SIN], t), horner([c * FEAT_SCALE for c in COS], t)


def gelu_parts(x):
    t = 1.0 / (1.0 + (0.3275911 / math.sqrt(2.0)) * jnp.abs(x))
    e = jnp.exp(-0.5 * x * x)
    q = 0.5 * t * horner(ERFC, t) * e
    cdf = jnp.where(x < 0.0, q, 1.0 - q)
    return x * cdf, cdf + x * e * (1.0 / math.sqrt(2.0 * math.pi))


def norm_stats(x):
    center = jnp.mean(x, axis=-1, keepdims=True)
    spread = jnp.mean(x * x, axis=-1, keepdims=True) - center * center
    inv = lax.rsqrt(spread + EPS)
    return (x - center) * inv, inv


def norm_back(grad, xhat, inv, gain):
    p = grad * gain
    return inv * (p - jnp.mean(p, axis=-1, keepdims=True) - xhat * jnp.mean(p * xhat, axis=-1, keepdims=True))


def by_eight(x):
    return jnp.sum(x.reshape(x.shape[0] // 8, 8, x.shape[1]), axis=0)


def panel(ref, p, cols):
    x = ref[p, :, :, :, cols]
    return x.reshape(x.shape[0] * x.shape[1] * x.shape[2], x.shape[3])


def low_lanes(rows):
    return iota((rows, LANES), 1) < HEAD_DIM


def widen(pair, a):
    return pair[:, a * HEAD_DIM : a * HEAD_DIM + 1]


def head_values(v, a, low):
    one = jnp.ones_like(v)
    return jnp.where(low, v, one) if a == 0 else jnp.where(low, one, v)


def state_of(states, p, a):
    own = states[2 * p + a, 0:HEAD_DIM, :]
    rest = jnp.broadcast_to(states[2 * p + a, NORMAL : NORMAL + 1, :], own.shape)
    return jnp.concatenate([own, rest] if a == 0 else [rest, own], axis=0)


def put_state(states, h, own, normal, decay):
    states[h, 0:HEAD_DIM, :] = own
    rest = jnp.zeros((STATE_ROWS - DECAY - 1, 2 * FEATS), F32)
    states[h, NORMAL:, :] = jnp.concatenate([normal, twice(decay), rest], axis=0)


def twice(x):
    return jnp.concatenate([x, x], axis=1)


def run_pairs(body, hook, order=None):
    def one(p):
        body(order(p) if order else p)
        for at, acts in (hook or {}).items():

            @pl.when(p == at)
            def _():
                for act, *given in acts:
                    act(*given)

    pair_loop(one)


def tables(T, base, r):
    pos = base + iota((8, T), 1)
    seg_row, _, live_row, _, _ = marks(pos, base, r.lengths)
    seg1, live1, pos1 = seg_row[0:1], live_row[0:1], pos[0:1]

    def mask_rows(rows, at, n):
        row_pos = base + at + iota((n, 1), 0)
        seg_col = marks(row_pos, base, r.lengths)[0]
        allowed = (seg_col == seg1) & (pos1 <= row_pos) & (live1 > 0.0)
        r.mask[rows, :] = jnp.where(allowed, 0.0, -1e30)

    rows_loop(T, 64, mask_rows)
    hash_seed = r.seed[0] * jnp.int32(-2048144789)

    def table(p):
        place = (p * LANES + iota((LANES, LANES), 0)) * FEATS + iota((LANES, LANES), 1)
        y = place * jnp.int32(-1640531535) + hash_seed
        y = y ^ lax.shift_right_logical(y, jnp.int32(15))
        y = y * jnp.int32(739982445)
        y = y ^ lax.shift_right_logical(y, jnp.int32(13))
        y = y * jnp.int32(695872825)
        y = y ^ lax.shift_right_logical(y, jnp.int32(16))
        s = jnp.full(y.shape, -510, I32)
        for k in range(4):
            s = s + (lax.shift_right_logical(y, jnp.int32(8 * k)) & jnp.int32(255))
        top = iota((LANES, LANES), 0) < HEAD_DIM
        odd = s & 1

        def diagonal(x):
            x = x.astype(F32)
            return jnp.concatenate([jnp.where(top, x, 0.0), jnp.where(top, 0.0, x)], axis=1).astype(BF)

        r.tab[p, 0:LANES, :] = diagonal(s - odd)
        r.tab[p, LANES:, :] = diagonal(odd)
        r.tabn[p] = diagonal(s)

    pair_loop(table)


def first_norm(T, base, r):
    pick = jnp.where(iota((16, LANES), 0) == iota((16, LANES), 1), 1.0, 0.0).astype(BF)
    for p in range(PAIRS):
        rows = nt(pick, panel(r.ga, p, SMALL))
        r.gate[2 * p : 2 * p + 2, :] = rows[0:2]
        r.gate[8 + 2 * p : 10 + 2 * p, :] = rows[0:2]
        r.bias[2 * p : 2 * p + 1, :] = rows[6:7] + rows[7:8] + rows[8:9]
        r.bias[2 * p + 1 : 2 * p + 2, :] = rows[9:10] + rows[10:11] + rows[11:12]
        if p == 0:
            r.vec[...] = rows[0:8]

    def norm_rows(rows, at, n):
        xhat, _ = norm_stats(r.tok[rows, :].astype(F32))
        r.normed[rows, :] = (xhat * r.vec[2:3, :] + r.vec[3:4, :]).astype(BF)

    rows_loop(T, 64, norm_rows)
    logits = nt(r.gate[...].astype(BF), r.normed[...])[0:8] + r.bias[:, 0:1]
    r.logits[...] = logits
    pos = base + iota((8, T), 1)
    _, reset_row, live_row, carry_row, _ = marks(pos, base, r.lengths)
    decay = -(jnp.log1p(jnp.exp(-jnp.abs(logits))) + jnp.maximum(-logits, 0.0)) * live_row * (1.0 - reset_row)
    run = decay
    lane = iota((8, T), 1)
    shift = 1
    while shift < T:
        run = run + jnp.where(lane >= shift, pltpu.roll(run, shift, 1), 0.0)
        shift *= 2
    r.run[...] = run
    r.total[...] = jnp.broadcast_to(jnp.exp(run[:, T - 1 : T]) * carry_row[:, T - 1 : T], (8, LANES))
    hi = run.astype(BF).astype(F32)
    mid = (run - hi).astype(BF).astype(F32)
    run3 = jnp.concatenate([hi, mid, run - hi - mid, jnp.zeros_like(hi)], axis=0).astype(BF)

    def spread(p):
        chosen = iota((32, LANES), 0) % 8 == 2 * p + iota((32, LANES), 1) // HEAD_DIM
        r.rb[p] = tn(run3, jnp.where(chosen, 1.0, 0.0).astype(BF))

    pair_loop(spread)


def features(T, r, p, u, out):
    ones2 = head_ones(2 * LANES, 2 * LANES, HEAD_DIM, LANES)
    r.s1[...] = nn(jnp.concatenate([u, u], axis=1), r.tab[p])
    uf = u.astype(F32)
    r.s2[...] = nn(halves(uf * uf), ones2)

    def body(rows, at, n):
        s, c = sincos(r.s1[rows, :] * (lax.rsqrt(r.s2[rows, :] + 1e-6) * TABLE_SCALE))
        for a in range(2):
            out[2 * p + a, rows, 0:FEATS] = s[:, a * FEATS : (a + 1) * FEATS].astype(BF)
            out[2 * p + a, rows, FEATS : 2 * FEATS] = c[:, a * FEATS : (a + 1) * FEATS].astype(BF)

    rows_loop(T, 64, body)


def end_factor(T, base, r):
    last_seg = marks(base + T - 1 + iota((8, LANES), 1) * 0, base, r.lengths)[0][0:1, 0:1]
    seg_col, _, live_col, _, _ = marks(base + iota((T, LANES), 0), base, r.lengths)
    return jnp.where(seg_col == last_seg, live_col, 0.0)


def keys(T, base, r, hook=None):
    def pair(p):
        r.k[p] = nn(r.normed[...], panel(r.ga, p, KEY)).astype(BF)
        features(T, r, p, r.k[p], r.kf)

    run_pairs(pair, hook)


def states(T, base, r):
    end_live = end_factor(T, base, r)

    def pair(p):
        r.v[p] = nn(r.normed[...], panel(r.ga, p, VALUE)).astype(BF)
        decay_end = jnp.exp(r.rb[p, T - 1 : T, :] - r.rb[p]) * end_live
        lane = iota((T, LANES), 1)
        factor = jnp.where(lane < 2, widen(decay_end, 0), widen(decay_end, 1))
        rough = factor.astype(BF).astype(F32)
        factor = jnp.where(lane % 2 == 0, rough, factor - rough)
        ends = tn(factor.astype(BF), jnp.concatenate([r.kf[2 * p], r.kf[2 * p + 1]], axis=1))
        for a in range(2):
            h = 2 * p + a
            scaled = (r.kf[h].astype(F32) * widen(decay_end, a)).astype(BF)
            state = tn(r.v[p], scaled)[a * HEAD_DIM : (a + 1) * HEAD_DIM]
            normal = ends[2 * a : 2 * a + 1, a * 2 * FEATS : (a + 1) * 2 * FEATS]
            normal = normal + ends[2 * a + 1 : 2 * a + 2, a * 2 * FEATS : (a + 1) * 2 * FEATS]
            put_state(r.out, h, state, normal, r.total[pl.ds(h, 1), :])

    pair_loop(pair)


def queries(T, base, r, hook=None):
    low = low_lanes(T)

    def pair(p):
        r.q[p] = nn(r.normed[...], panel(r.ga, p, QUERY)).astype(BF)
        features(T, r, p, r.q[p], r.qf)
        v = r.v[p]
        for a in range(2):
            h = 2 * p + a
            r.s[...] = nt(r.qf[h], r.kf[h])
            run_row = r.run[pl.ds(h, 1), :]

            def body(rows, at, n):
                gap = jnp.minimum(widen(r.rb[p, rows, :], a) - run_row, r.mask[rows, :])
                w = r.s[rows, :] * jnp.exp(gap)
                rounded = w.astype(BF)
                r.w[h, rows, :] = rounded
                rest = jnp.sum(w - rounded.astype(F32), axis=1, keepdims=True)
                r.zfix[p, rows, a * HEAD_DIM : (a + 1) * HEAD_DIM] = jnp.broadcast_to(rest, (n, HEAD_DIM)).astype(BF)

            rows_loop(T, 64, body)
            r.own[h] = nn(r.w[h], head_values(v, a, low))

    run_pairs(pair, hook)


def carry_factor(T, base, r):
    _, _, live_col, carry_col, _ = marks(base + iota((T, LANES), 0), base, r.lengths)
    return live_col, carry_col


def attend(T, base, r):
    low = low_lanes(T)
    live_col, carry_col = carry_factor(T, base, r)

    def join(p):
        factor = jnp.exp(r.rb[p]) * carry_col
        total = []
        for a in range(2):
            h = 2 * p + a
            carried = nt(twice(r.qf[h]), halves(state_of(r.inn, p, a)))
            joined = r.own[h] + widen(factor, a) * carried
            r.joined[h] = joined
            total.append(joined)
        num = jnp.where(low, total[0], total[1])
        z = pltpu.roll(jnp.where(low, total[1], total[0]), HEAD_DIM, 1) + r.zfix[p].astype(F32)
        r.att[p] = (live_col * num * lax.rsqrt(z * z + FLOOR2)).astype(BF)

    pair_loop(join)
    o = out_columns(r)
    branch = None
    for p in range(0, PAIRS, 2):
        part = nt(
            jnp.concatenate([r.att[p], r.att[p + 1]], axis=1),
            jnp.concatenate([panel(r.gf, p, o), panel(r.gf, p + 1, o)], axis=1),
        )
        branch = part if branch is None else branch + part
    r.mid[...] = branch

    def norm_rows(rows, at, n):
        mid = r.mid[rows, :] + r.tok[rows, :].astype(F32)
        r.mid[rows, :] = mid
        xhat, inv = norm_stats(mid)
        r.xhat[rows, :] = xhat
        r.inv[rows, :] = jnp.broadcast_to(inv, (n, LANES))
        r.two[rows, :] = (xhat * r.vec[4:5, :] + r.vec[5:6, :]).astype(BF)

    rows_loop(T, 64, norm_rows)


def feed_columns(r):
    ff = (r.gf.shape[-1] - LANES) // 2
    return slice(LANES + ff, LANES + 2 * ff), slice(LANES, LANES + ff)


def out_columns(r):
    return slice(0, LANES)


def cotangents(T, base, r):
    _, d = feed_columns(r)

    def part(p):
        r.h2[p] = nn(r.cot[...], panel(r.gf, p, d))

    pair_loop(part)


def feed(T, base, r):
    low = low_lanes(T)
    live_col, carry_col = carry_factor(T, base, r)
    r.acc1[...] = jnp.zeros_like(r.acc1)
    r.acc2[...] = jnp.zeros_like(r.acc2)
    u, d = feed_columns(r)
    o = out_columns(r)

    def part(p):
        up, down = panel(r.gf, p, u), panel(r.gf, p, d)
        r.h1[...] = nn(r.two[...], up)

        def body(rows, at, n):
            value, slope = gelu_parts(r.h1[rows, :])
            r.act[p, rows, :] = value.astype(BF)
            r.gh[p, rows, :] = (r.h2[p, rows, :] * slope).astype(BF)

        rows_loop(T, 64, body)
        r.acc1[...] += nt(r.act[p], down)
        r.acc2[...] += nt(r.gh[p], up)

    pair_loop(part)
    r.sums[...] = jnp.zeros_like(r.sums)

    def finish(rows, at, n):
        r.result[rows, :] = (r.mid[rows, :] + r.acc1[rows, :]).astype(BF)
        xhat, gn = r.xhat[rows, :], r.acc2[rows, :]
        r.sums[0:8, :] += by_eight(gn * xhat)
        r.sums[8:16, :] += by_eight(gn)
        back = norm_back(gn, xhat, r.inv[rows, 0:1], r.vec[4:5, :])
        grad = r.cot[rows, :].astype(F32) + back
        r.gmid[rows, :] = grad
        r.gb[rows, :] = grad.astype(BF)

    rows_loop(T, 64, finish)
    r.fsum[0:1, :] = jnp.sum(r.sums[0:8, :], axis=0, keepdims=True)
    r.fsum[1:2, :] = jnp.sum(r.sums[8:16, :], axis=0, keepdims=True)
    ones1 = head_ones(2 * LANES, LANES, HEAD_DIM, HEAD_DIM)
    row_ones = jnp.ones((16, 2 * LANES), BF)
    first_half = iota((T, LANES), 1) % HEAD_DIM < HEAD_DIM // 2

    def back(p):
        g = nn(r.gb[...], panel(r.gf, p, o)).astype(BF).astype(F32) * live_col
        total = [r.joined[2 * p], r.joined[2 * p + 1]]
        num = jnp.where(low, total[0], total[1])
        z = pltpu.roll(jnp.where(low, total[1], total[0]), HEAD_DIM, 1) + r.zfix[p].astype(F32)
        rden = lax.rsqrt(z * z + FLOOR2)
        dn = (g * rden).astype(BF).astype(F32)
        dz = nn(halves(dn * num), ones1) * (z * rden * rden)
        dz = pltpu.roll(dz * (-2.0 / HEAD_DIM), HEAD_DIM, 1)
        rough = dz.astype(BF).astype(F32)
        dz = jnp.where(first_half, rough, dz - rough)
        factor = jnp.exp(r.rb[p]) * carry_col
        for a in range(2):
            h = 2 * p + a
            joint = (jnp.where(low, dn, dz) if a == 0 else jnp.where(low, dz, dn)).astype(BF)
            r.dn[h] = joint
            r.dr[pl.ds(h, 1), :] = nt(row_ones, halves(joint.astype(F32) * total[a]))[0:1]
            adj = tn(joint, (r.qf[h].astype(F32) * widen(factor, a)).astype(BF))
            at, half = (1 - a) * HEAD_DIM, HEAD_DIM // 2
            normal = 0.5 * (adj[at : at + 1] + adj[at + half : at + half + 1])
            put_state(r.adj, h, adj[a * HEAD_DIM : (a + 1) * HEAD_DIM], normal, r.total[pl.ds(h, 1), :])

    pair_loop(back)


def up_grads(T, base, r):
    up, _ = feed_columns(r)
    pair_loop(lambda p: put_panel(r.ggf, p, up, tn(r.two[...], r.gh[p])))


def down_grads(T, base, r):
    _, down = feed_columns(r)

    def part(p):
        put_panel(r.ggf, p, down, tn(r.cot[...], r.act[p]))
        put_panel(r.ggf, p, out_columns(r), tn(r.gb[...], r.att[p]))

    pair_loop(part)


def put_panel(ref, p, cols, x):
    shape = ref.shape[1:4] + (x.shape[1],)
    ref[p, :, :, :, cols] = x.astype(BF).reshape(shape)


def back(T, base, r, tokens_all, near_hook=None, between=lambda: None, far_hook=None, order=None):
    D = r.tok.shape[1]
    low = low_lanes(T)
    _, carry_col = carry_factor(T, base, r)
    end_live = end_factor(T, base, r)
    ones1 = head_ones(2 * LANES, LANES, HEAD_DIM, HEAD_DIM)
    row_ones = jnp.ones((16, 2 * LANES), BF)
    r.acc1[...] = jnp.zeros_like(r.acc1)

    def feature_back(p, u, da):
        ds = nt(da, r.tabn[p]) * TABLE_SCALE
        uf = u.astype(F32)
        inv = lax.rsqrt(nn(halves(uf * uf), ones1) + 1e-6)
        uh = uf * inv
        return (inv * (ds - uh * nn(halves(uh * ds), ones1))).astype(BF)

    def angles(rows, source, feat, h):
        x, f = source[rows, :], feat[h, rows, :].astype(F32)
        return x[:, :FEATS] * f[:, FEATS:] - x[:, FEATS:] * f[:, :FEATS]

    def near(p):
        v = r.v[p]
        factor = jnp.exp(r.rb[p]) * carry_col
        for a in range(2):
            h = 2 * p + a
            r.s[...] = nt(r.dn[h], head_values(v, a, low))
            run_row = r.run[pl.ds(h, 1), :]

            def body(rows, at, n):
                gap = jnp.minimum(widen(r.rb[p, rows, :], a) - run_row, r.mask[rows, :])
                r.ds[rows, :] = (r.s[rows, :] * jnp.exp(gap)).astype(BF)

            rows_loop(T, 64, body)
            before = halves(state_of(r.inn, p, a), 0)
            r.s1[...] = nn(r.ds[...], r.kf[h]) + widen(factor, a) * nn(twice(r.dn[h]), before)
            r.s2[...] = tn(r.ds[...], r.qf[h])
            r.ghv[h] = tn(r.w[h], r.dn[h])

            def turn(rows, at, n):
                r.da[p, rows, a * FEATS : (a + 1) * FEATS] = angles(rows, r.s1, r.qf, h).astype(BF)
                r.da[p, rows, (2 + a) * FEATS : (3 + a) * FEATS] = angles(rows, r.s2, r.kf, h).astype(BF)

            rows_loop(T, 64, turn)
        grad = feature_back(p, r.q[p], r.da[p, :, : 2 * FEATS])
        r.acc1[...] += nt(grad, panel(r.ga, p, QUERY))
        put_panel(r.gga, p, slice(2 * LANES, 3 * LANES), tn(r.normed[...], grad))

    def far(p):
        v = r.v[p]
        decay_end = jnp.exp(r.rb[p, T - 1 : T, :] - r.rb[p]) * end_live
        grad_v = []
        for a in range(2):
            h = 2 * p + a
            end, hv = state_of(r.aend, p, a), head_values(v, a, low)
            late = widen(decay_end, a) * nt(twice(r.kf[h]), halves(end))
            r.s2[...] = widen(decay_end, a) * nn(twice(hv), halves(end, 0))
            grad_hv = r.ghv[h] + late
            grad_v.append(grad_hv)

            def turn(rows, at, n):
                lanes = slice((2 + a) * FEATS, (3 + a) * FEATS)
                r.da[p, rows, lanes] = (r.da[p, rows, lanes].astype(F32) + angles(rows, r.s2, r.kf, h)).astype(BF)

            rows_loop(T, 64, turn)
            hvf = hv.astype(F32)
            k_side = nt(row_ones, halves(hvf * grad_hv))
            r.drun[pl.ds(h, 1), :] = r.dr[pl.ds(h, 1), :] - k_side[0:1]
            owed = jnp.sum(end * state_of(r.inn, p, a), axis=0, keepdims=True)
            owed = r.total[pl.ds(h, 1), 0:1] * jnp.sum(owed, axis=1, keepdims=True)
            owed = owed + jnp.sum(jnp.sum(hvf * late, axis=0, keepdims=True), axis=1, keepdims=True)
            r.owed[pl.ds(h, 1), :] = jnp.broadcast_to(owed, (1, LANES))
        grad_v = jnp.where(low, grad_v[0], grad_v[1]).astype(BF)
        grads = jnp.concatenate([feature_back(p, r.k[p], r.da[p, :, 2 * FEATS :]), grad_v], axis=1)
        weights = jnp.concatenate([panel(r.ga, p, KEY), panel(r.ga, p, VALUE)], axis=1)
        r.acc1[...] += nt(grads, weights)
        put_panel(r.gga, p, slice(0, 2 * LANES), tn(r.normed[...], grads))

    run_pairs(near, near_hook, order)
    between()
    run_pairs(far, far_hook, order)
    pos = base + iota((8, T), 1)
    _, reset_row, live_row, _, filled = marks(pos, base, r.lengths)
    lane = iota((8, T), 1)
    run = r.drun[...]
    shift = 1
    while shift < T:
        run = run + jnp.where(lane < T - shift, pltpu.roll(run, T - shift, 1), 0.0)
        shift *= 2
    grad_decay = run + r.owed[:, 0:1]
    logits = r.logits[...]
    e = jnp.exp(-jnp.abs(logits))
    small, large = e / (1.0 + e), 1.0 / (1.0 + e)
    gate = jnp.where(logits >= 0.0, large, small)
    rest = jnp.where(logits >= 0.0, small, large)
    penalty = GATE_PEN * tokens_all / HEADS / jnp.broadcast_to(filled, (8, T)).astype(F32)
    grad_logits = grad_decay * live_row * (1.0 - reset_row) * rest + penalty * live_row * gate * rest
    both = halves(grad_logits, 0)
    r.acc1[...] += tn(both, r.gate[...].astype(BF))
    gate_rows = nn(both, r.normed[...])
    gate_rows = gate_rows[0:8] + gate_rows[8:16]
    bias = jnp.broadcast_to(jnp.sum(grad_logits, axis=1, keepdims=True), (8, D))
    r.sums[...] = jnp.zeros_like(r.sums)

    def finish(rows, at, n):
        xhat, inv = norm_stats(r.tok[rows, :].astype(F32))
        gn = r.acc1[rows, :]
        r.sums[0:8, :] += by_eight(gn * xhat)
        r.sums[8:16, :] += by_eight(gn)
        r.gtok[rows, :] = r.gmid[rows, :] + norm_back(gn, xhat, inv, r.vec[2:3, :])

    rows_loop(T, 64, finish)
    norm_gain = jnp.sum(r.sums[0:8, :], axis=0, keepdims=True)
    norm_shift = jnp.sum(r.sums[8:16, :], axis=0, keepdims=True)
    lines = [norm_gain, norm_shift, r.fsum[0:2, :]]
    for p in range(PAIRS):
        rows = jnp.concatenate([gate_rows[2 * p : 2 * p + 2]] + lines + [bias[2 * p : 2 * p + 2]], axis=0)
        for g in range(D // LANES):
            r.lines[p, g] = rows[:, g * LANES : (g + 1) * LANES]


class Refs:
    def __init__(self, **refs):
        self.__dict__.update(refs)


def buffers(T, D, att, rest, ff, seq):
    z = (PAIRS, seq // 2, 2, D // seq)
    pair = (PAIRS, T, LANES)
    return {
        "ga": (z + (att,), BF), "gf": (z + (rest,), BF), "gga": (z + (att - LANES,), BF), "ggf": (z + (rest,), BF),
        "gate": ((16, D), F32), "bias": ((8, D), F32), "vec": ((8, D), F32), "normed": ((T, D), BF),
        "logits": ((8, T), F32), "run": ((8, T), F32), "total": ((8, LANES), F32), "mask": ((T, T), F32),
        "s1": ((T, 2 * FEATS), F32), "s2": ((T, 2 * FEATS), F32), "s": ((T, T), F32),
        "tab": ((PAIRS, 2 * LANES, 2 * FEATS), BF), "tabn": ((PAIRS, LANES, 2 * FEATS), BF),
        "q": (pair, BF), "k": (pair, BF), "v": (pair, BF), "rb": (pair, F32),
        "qf": ((HEADS, T, 2 * FEATS), BF), "kf": ((HEADS, T, 2 * FEATS), BF),
        "out": (STATES, F32), "inn": (STATES, F32), "adj": (STATES, F32), "aend": (STATES, F32),
        "w": ((HEADS, T, T), BF), "own": ((HEADS, T, LANES), F32), "joined": ((HEADS, T, LANES), F32),
        "att": (pair, BF), "zfix": (pair, BF), "mid": ((T, D), F32), "xhat": ((T, D), F32), "inv": ((T, LANES), F32), "two": ((T, D), BF),
        "acc1": ((T, D), F32), "acc2": ((T, D), F32), "h1": ((T, ff), F32), "h2": ((PAIRS, T, ff), F32),
        "act": ((PAIRS, T, ff), BF), "gh": ((PAIRS, T, ff), BF), "sums": ((16, D), F32), "fsum": ((8, D), F32),
        "result": ((T, D), BF), "gmid": ((T, D), F32), "gb": ((T, D), BF), "dr": ((8, T), F32),
        "dn": ((HEADS, T, LANES), BF), "ds": ((T, T), BF), "da": ((PAIRS, T, 4 * FEATS), BF), "ghv": ((HEADS, T, LANES), F32),
        "lines": ((PAIRS, D // LANES, 8, LANES), F32),
        "drun": ((8, T), F32), "owed": ((8, LANES), F32), "gtok": ((T, D), F32),
    }


FRONT = (
    ("ga",),
    ("gate", "vec", "normed", "logits", "run", "total", "mask", "tabn", "q", "k", "v", "rb", "qf", "kf", "out", "w", "own", "zfix"),
    ("bias", "s1", "s2", "s", "tab"),
)
MIDDLE = (
    ("gf", "vec", "rb", "qf", "own", "zfix", "inn", "total"),
    ("ggf", "result", "gmid", "fsum", "dr", "dn", "adj"),
    ("joined", "att", "mid", "xhat", "inv", "two", "acc1", "acc2", "h1", "h2", "act", "gh", "sums", "gb"),
)
BACK = (
    ("ga", "gate", "vec", "normed", "logits", "run", "total", "mask", "tabn", "q", "k", "v", "rb", "qf", "kf",
     "w", "inn", "aend", "gmid", "fsum", "dr", "dn"),
    ("gga", "gtok", "lines"),
    ("s", "s1", "s2", "ds", "da", "ghv", "drun", "owed", "acc1", "sums"),
)
SHARED = {"joined": "own", "h1": "s", "gmid": "mid", "ds": "gb", "adj": "out", "da": "act", "ghv": "own"}


def front(T, base, r):
    tables(T, base, r)
    first_norm(T, base, r)
    keys(T, base, r)
    states(T, base, r)
    queries(T, base, r)


def middle(T, base, r):
    cotangents(T, base, r)
    attend(T, base, r)
    feed(T, base, r)
    up_grads(T, base, r)
    down_grads(T, base, r)


def here(T):
    return (lax.axis_index("seq") * lax.axis_size("head") + lax.axis_index("head")) * T


def stage(which, names, specs, outer, args, state):
    reads, writes, scratch = names
    shape = lambda n: jax.ShapeDtypeStruct(*specs[n])
    vmem, smem = pl.BlockSpec(memory_space=pltpu.VMEM), pl.BlockSpec(memory_space=pltpu.SMEM)

    def kernel(*refs):
        base_ref, lengths, seed, tok, cot = refs[:5]
        rest = dict(zip(reads + writes + scratch, refs[5:]))
        which(base_ref[0], Refs(lengths=lengths, seed=seed, tok=tok, cot=cot, **rest))

    out = pl.pallas_call(
        kernel,
        out_shape=[shape(n) for n in writes],
        in_specs=[smem] * 3 + [vmem] * (2 + len(reads)),
        out_specs=[vmem] * len(writes),
        scratch_shapes=[pltpu.VMEM(*specs[n]) for n in scratch],
        compiler_params=pltpu.CompilerParams(vmem_limit_bytes=VMEM_BYTES),
        name=outer,
    )(*args, *[state[n] for n in reads])
    state.update(zip(writes, out))


def scan_states(out, reverse):
    seq, head = lax.axis_size("seq"), lax.axis_size("head")
    count = seq * head
    me = lax.axis_index("seq") * head + lax.axis_index("head")
    state = (out[:, DECAY : DECAY + 1, 0:1], out[:, :DECAY])
    step = 1
    order = lambda pairs: [(b, a) for a, b in pairs] if reverse else pairs
    axes = ("seq", "head")
    while step < count:
        moved = jax.tree.map(lambda x: lax.ppermute(x, axes, order([(i, i + step) for i in range(count - step)])), state)
        has = (me < count - step) if reverse else (me >= step)
        f, m = state
        state = (jnp.where(has, f * moved[0], f), m + jnp.where(has, f * moved[1], 0.0))
        step *= 2
    moved = lax.ppermute(state[1], axes, order([(i, i + 1) for i in range(count - 1)]))
    return jnp.concatenate([moved, jnp.zeros((HEADS, STATE_ROWS - DECAY, 2 * FEATS), F32)], axis=1)


def remote(src, dst, send, recv, to):
    return pltpu.make_async_remote_copy(
        src_ref=src, dst_ref=dst, send_sem=send, recv_sem=recv, device_id=to, device_id_type=MESH
    )


class Place:
    def __init__(self):
        self.seq, self.head = lax.axis_size("seq"), lax.axis_size("head")
        s, h = lax.axis_index("seq"), lax.axis_index("head")
        self.z, self.y, self.x, self.c = s // 2, s % 2, h // 2, h % 2
        self.depth = self.seq // 2
        self.count = self.seq * self.head
        self.me = s * self.head + h

    def device(self, z=None, y=None, x=None, c=None):
        pick = lambda given, own: own if given is None else given
        z, y, x, c = pick(z, self.z), pick(y, self.y), pick(x, self.x), pick(c, self.c)
        return (z * 2 + y, x * 2 + c)

    def number(self, i):
        return (i // self.head, i % self.head)

    def around(self, k):
        return (self.z + k) % self.depth

class Semaphores:
    def __init__(self, send, recv):
        self.send, self.recv, self.used = send, recv, 0

    def copy(self, src, dst, to):
        i = self.used
        self.used += 1
        return remote(src, dst, self.send.at[i], self.recv.at[i], to)


GATHER_COPIES = 2 * (3 + 1 + 2 + 2)
SCATTER_COPIES = 2 + 2 * (1 + 1 + 3)


def gather_stages(place, g, lanes, sems):
    half = g.shape[3] // 2
    z, y, x, c = place.z, place.y, place.x, place.c
    pair = x * 2 + c
    stages = [[], [], [], []]
    for part in range(2):
        rows = pl.ds(part * half, half)
        same = lambda ref, to: sems.copy(ref, ref, to)
        for k in range(1, place.depth):
            stages[0].append(same(g.at[pair, z, y, rows, lanes], place.device(z=place.around(k))))
        to_y, to_x = place.device(y=1 - y), place.device(x=1 - x)
        if part == 0:
            stages[1].append(same(g.at[pair, :, y, rows, lanes], to_y))
            stages[2].append(same(g.at[pair, :, :, rows, lanes], to_x))
        else:
            stages[1].append(same(g.at[pair, :, y, rows, lanes], to_x))
            for other in range(2):
                stages[2].append(same(g.at[other * 2 + c, :, y, rows, lanes], to_y))
        for other in range(2):
            stages[3].append(same(g.at[other * 2 + c, :, :, rows, lanes], place.device(c=1 - c)))
    return stages


def begin(stage):
    for copy in stage:
        copy.start()


def arrived(stage):
    for copy in stage:
        copy.wait_recv()


def sent(*stages):
    for stage in stages:
        for copy in stage:
            copy.wait_send()


class Gather:
    def __init__(self, place, ga, gf, sems):
        ff = (gf.shape[-1] - LANES) // 2
        lanes = lambda first, count: pl.ds(first, count)
        self.chunks = [
            gather_stages(place, ref, part, sems)
            for ref, part in (
                (ga, lanes(0, 2 * LANES)),
                (ga, lanes(2 * LANES, 2 * LANES)),
                (gf, lanes(0, LANES + ff)),
                (gf, lanes(LANES + ff, ff)),
            )
        ]

    def begin(self, chunk):
        begin(self.chunks[chunk][0])

    def step(self, chunk, stage):
        arrived(self.chunks[chunk][stage])
        if stage < 3:
            begin(self.chunks[chunk][stage + 1])

    def finish(self):
        for chunk in self.chunks:
            sent(*chunk)


def add_blocks(to, others, count, where):
    def one(i, carry):
        at = where(i)
        total = to[at].astype(F32)
        for ref, index in others:
            total = total + ref[index(i)].astype(F32)
        to[at] = total.astype(to.dtype)
        return carry

    lax.fori_loop(0, count, one, 0)


class Scatter:
    def __init__(self, place, gg, lanes, out, buf, sems):
        self.place, self.gg, self.lanes, self.out = place, gg, lanes, out
        self.r1, self.r2a, self.r2b, self.r3a, self.r3b, self.r4a, self.r4b = buf
        z, y, x, c, n = place.z, place.y, place.x, place.c, place.depth
        self.half = half = gg.shape[3] // 2
        first, last = pl.ds(0, half), pl.ds(half, half)
        other, to_y, to_x = place.device(c=1 - c), place.device(y=1 - y), place.device(x=1 - x)
        self.stages = [
            [sems.copy(gg.at[i * 2 + 1 - c, :, :, :, lanes], self.r1.at[i], other) for i in range(2)],
            [
                sems.copy(self.r1.at[1 - x, :, :, first], self.r2a, to_x),
                sems.copy(self.r1.at[:, :, 1 - y, last], self.r2b, to_y),
            ],
            [sems.copy(self.r2a.at[:, 1 - y], self.r3a, to_y), sems.copy(self.r2b.at[1 - x], self.r3b, to_x)],
            [
                sems.copy(ref.at[place.around(k)], slots.at[k - 1], place.device(z=place.around(k)))
                for ref, slots in ((self.r3a, self.r4a), (self.r3b, self.r4b))
                for k in range(1, n)
            ],
        ]

    def start(self):
        begin(self.stages[0])

    def step(self, i):
        place, n, half = self.place, self.place.depth, self.half
        y, x, c = place.y, place.x, place.c
        first, last = slice(0, half), slice(half, 2 * half)
        lanes = self.lanes
        arrived(self.stages[i])
        if i == 0:
            block = lambda j: (j // (2 * n), (j // 2) % n, j % 2)
            add_blocks(self.r1, [(self.gg, lambda j: ((j // (2 * n)) * 2 + c, (j // 2) % n, j % 2, slice(None), lanes))], 4 * n, block)
        elif i == 1:
            add_blocks(self.r2a, [(self.r1, lambda j: (x, j // 2, j % 2, first))], 2 * n, lambda j: (j // 2, j % 2))
            add_blocks(self.r2b, [(self.r1, lambda j: (j // n, j % n, y, last))], 2 * n, lambda j: (j // n, j % n))
        elif i == 2:
            add_blocks(self.r3a, [(self.r2a, lambda j: (j, y))], n, lambda j: (j,))
            add_blocks(self.r3b, [(self.r2b, lambda j: (x, j))], n, lambda j: (j,))
        else:
            for ref, slots, rows in ((self.r3a, self.r4a, first), (self.r3b, self.r4b, last)):
                total = ref[place.z].astype(F32)
                for k in range(n - 1):
                    total = total + slots[k].astype(F32)
                self.out[rows, lanes] = total
        if i < 3:
            begin(self.stages[i + 1])

    def finish(self):
        sent(*self.stages)


def scatter_buffers(seq, rows, cols):
    n, half = seq // 2, rows // 2
    return [
        pltpu.VMEM(shape + (cols,), BF)
        for shape in ((2, n, 2, rows), (n, 2, half), (2, n, half), (n, half), (n, half), (n - 1, half), (n - 1, half))
    ]


class Scan:
    def __init__(self, place, reverse, out, inn, box, planes, send, recv):
        self.place, self.reverse = place, reverse
        self.out, self.inn, self.planes = out, inn, planes
        self.pair, self.chip, self.box, self.back = box
        self.chips = HEADS // 2
        self.mine = place.y * 2 + place.x
        self.half, self.rest = place.c * self.chips, (1 - place.c) * self.chips
        self.sems = Semaphores(send, recv)
        other = place.device(c=1 - place.c)
        at = lambda ref, first: ref.at[pl.ds(first, self.chips)]
        near = [lax.rem(self.mine + k, self.chips) for k in range(1, self.chips)]
        chip = lambda m: place.device(y=m // 2, x=m % 2)
        total = planes.at[place.z]
        copy = self.sems.copy
        self.ways = [
            [copy(at(out, self.rest), self.pair, other)],
            [copy(self.chip.at[m], self.box.at[self.mine], chip(m)) for m in near],
            [copy(total, total, place.device(z=place.around(k))) for k in range(1, place.depth)],
            [copy(self.box.at[m], self.back.at[self.mine], chip(m)) for m in near],
            [copy(self.pair, at(inn, self.half), other)],
        ]

    def start(self):
        begin(self.ways[0])

    def chain(self, ref, count):
        kept = iota((STATE_ROWS, 2 * FEATS), 0) != DECAY
        state = jnp.where(kept, 0.0, 1.0)
        for i in range(count):
            d = count - 1 - i if self.reverse else i
            term = ref[d]
            ref[d] = state
            state = state * term[DECAY : DECAY + 1, :] + jnp.where(kept, term, 0.0)
        return state

    def earlier_is_mine(self):
        return (self.place.c == 0) != self.reverse

    def cores(self):
        arrived(self.ways[0])
        kept = iota((STATE_ROWS, 2 * FEATS), 0) != DECAY
        first = jnp.broadcast_to(self.earlier_is_mine(), kept.shape)
        for i in range(self.chips):
            mine, its = self.out[self.half + i], self.pair[i]
            early, late = jnp.where(first, mine, its), jnp.where(first, its, mine)
            self.chip[i] = early * late[DECAY : DECAY + 1, :] + jnp.where(kept, late, 0.0)
        begin(self.ways[1])
        self.box[self.mine] = self.chip[self.mine]

    def plane(self):
        arrived(self.ways[1])
        self.planes[self.place.z] = self.chain(self.box, self.chips)
        begin(self.ways[2])

    def line(self):
        arrived(self.ways[2])
        sent(self.ways[2])
        self.chain(self.planes, self.place.depth)
        before = self.planes[self.place.z]
        for m in range(self.chips):
            own = self.box[m]
            self.box[m] = own + own[DECAY : DECAY + 1, :] * before
        begin(self.ways[3])
        self.back[self.mine] = self.box[self.mine]

    def share(self):
        arrived(self.ways[3])
        sent(self.ways[0])
        first = jnp.broadcast_to(self.earlier_is_mine(), (STATE_ROWS, 2 * FEATS))
        for i in range(self.chips):
            mine, its, before = self.out[self.half + i], self.pair[i], self.back[i]
            early = jnp.where(first, mine, its)
            late = before * early[DECAY : DECAY + 1, :] + early
            self.inn[self.half + i] = jnp.where(first, before, late)
            self.pair[i] = jnp.where(first, late, before)
        begin(self.ways[4])

    def receive(self):
        arrived(self.ways[4])

    def finish(self):
        sent(self.ways[1], self.ways[3], self.ways[4])


class Lines:
    def __init__(self, place, lines, out, buf, sems):
        self.place, self.lines, self.out = place, lines, out
        self.l1, self.l2, self.l3, self.l4 = buf
        z, y, x, c, copy = place.z, place.y, place.x, place.c, sems.copy
        around = range(1, place.depth)
        self.stages = [
            [copy(lines.at[i * 2 + 1 - c], self.l1.at[i], place.device(c=1 - c)) for i in range(2)],
            [copy(self.l1.at[1 - x], self.l2, place.device(x=1 - x))],
            [copy(self.l2, self.l3, place.device(y=1 - y))],
            [copy(self.l3.at[place.around(k)], self.l4.at[k - 1], place.device(z=place.around(k))) for k in around],
        ]

    def start(self):
        begin(self.stages[0])

    def step(self, i):
        place = self.place
        arrived(self.stages[i])
        if i == 0:
            for j in range(2):
                self.l1[j] += self.lines[j * 2 + place.c]
        elif i == 1:
            self.l2[...] += self.l1[place.x]
        elif i == 2:
            self.l3[...] += self.l2[...]
        else:
            total = self.l3[place.z]
            for k in range(place.depth - 1):
                total = total + self.l4[k]
            self.out[...] = total
        if i < 3:
            begin(self.stages[i + 1])

    def finish(self):
        sent(*self.stages)


LINES_COPIES = 2 + 1 + 1 + 3


def greet(place):
    x, y = 1 - place.x, 1 - place.y
    near = [place.device(c=1 - place.c), place.device(x=x), place.device(y=y), place.device(x=x, y=y)]
    near += [place.device(z=place.around(k)) for k in range(1, place.depth)]
    barrier = pltpu.get_barrier_semaphore()
    for device in near:
        pl.semaphore_signal(barrier, inc=1, device_id=device, device_id_type=MESH)
    return lambda: pl.semaphore_wait(barrier, len(near))


def pack(place, r, key, value, query, gate, vectors, bias, up, out, down):
    at = (place.x * 2 + place.c, place.z, place.y)
    rows, ff = key.shape[0], up.shape[1]
    r.gf[at + (slice(None), slice(LANES + ff, None))] = up[...]
    r.gf[at + (slice(None), slice(0, LANES))] = out[...]
    r.gf[at + (slice(None), slice(LANES, LANES + ff))] = down[...]
    r.ga[at + (slice(None), KEY)] = key[...]
    r.ga[at + (slice(None), VALUE)] = value[...]
    r.ga[at + (slice(None), QUERY)] = query[...]
    lines = [gate[...].astype(F32)] + [v[...].astype(F32) for v in vectors]
    lines = jnp.concatenate(lines + [jnp.zeros((10, rows), F32)], axis=0).astype(BF)
    spread = jnp.where(iota((16, LANES), 0) == iota((16, LANES), 1), 1.0, 0.0).astype(BF)
    small = tn(lines, spread)
    lane = iota((rows, LANES), 1)
    for j in range(2):
        left = jnp.full((rows, LANES), bias[j], F32)
        for k in range(3):
            piece = left.astype(BF).astype(F32)
            small = jnp.where(lane == 6 + 3 * j + k, piece, small)
            left = left - piece
    r.ga[at + (slice(None), SMALL)] = small.astype(BF)


def unpack_kernel(half, grad_a, grad_f, lines, result, gtok, *outs):
    out = dict(zip(OUTPUTS, outs))
    rows = grad_a.shape[0]
    ff = (grad_f.shape[1] - LANES) // 2
    out["result"][...] = result[...]
    out["tokens"][...] = gtok[...]
    for i, name in enumerate(("key", "value", "query")):
        out[name][...] = grad_a[:, i * LANES : (i + 1) * LANES]
    out["up"][...] = grad_f[:, LANES + ff :]
    out["out"][...] = grad_f[:, :LANES]
    out["down"][...] = grad_f[:, LANES : LANES + ff]
    own = jnp.where(half == 0, lines[:, :rows], lines[:, rows : 2 * rows])
    for i, name in enumerate(("norm_gain", "norm_shift", "ffn_gain", "ffn_shift")):
        out[name][...] = own[2 + i : 3 + i, :]
    out["gate"][...] = own[0:2, :]
    out["bias"][...] = lines[6:8, 0:1]


OUTPUTS = ("result", "tokens", "norm_gain", "norm_shift", "query", "key", "value", "gate", "bias", "out", "ffn_gain",
           "ffn_shift", "up", "down")


def layer_kernel(names, tokens_all, T, lengths, seed, bias, tok, cot, key, value, query, gate, *given):
    vectors, (up, out, down), given = given[0:4], given[4:7], given[7:]
    (result, gtok, grad_a, grad_f, grad_lines), scratch = given[:5], given[5:]
    place = Place()
    base = place.me * T
    arrays = dict(zip(names, scratch))
    arrays.update({name: arrays[other] for name, other in SHARED.items()})
    scratch = scratch[len(names) :]
    r = Refs(lengths=lengths, seed=seed, tok=tok, cot=cot, result=result, gtok=gtok, xhat=gtok, **arrays)
    sums, scratch = [scratch[7 * i : 7 * i + 7] for i in range(4)], scratch[28:]
    boxes, planes, line_box, sems = (scratch[0:4], scratch[4:8]), scratch[8:10], scratch[10:14], scratch[14:]
    meet = greet(place)
    pack(place, r, key, value, query, gate, vectors, bias, up, out, down)
    gather = Gather(place, r.ga, r.gf, Semaphores(sems[0], sems[1]))
    forth = Scan(place, False, r.out, r.inn, boxes[0], planes[0], sems[2], sems[3])
    home = Scan(place, True, r.adj, r.aend, boxes[1], planes[1], sems[4], sems[5])
    later = Semaphores(sems[6], sems[7])
    up, down = feed_columns(r)
    sum_u = Scatter(place, r.ggf, up, grad_f, sums[0], later)
    sum_d = Scatter(place, r.ggf, slice(0, down.stop), grad_f, sums[1], later)
    sum_q = Scatter(place, r.gga, slice(2 * LANES, 3 * LANES), grad_a, sums[2], later)
    sum_k = Scatter(place, r.gga, slice(0, 2 * LANES), grad_a, sums[3], later)
    lines = Lines(place, r.lines, grad_lines, line_box, later)
    meet()

    g = gather.step
    others_first = lambda i: (i % 2) * 2 + jnp.where(i < 2, 1 - place.c, place.c)
    gather.begin(0)
    tables(T, base, r)
    g(0, 0)
    gather.begin(1)
    g(0, 1)
    g(1, 0)
    gather.begin(2)
    g(0, 2)
    g(1, 1)
    g(0, 3)
    first_norm(T, base, r)
    g(2, 0)
    gather.begin(3)
    keys(T, base, r, {0: [(g, 1, 2)], 3: [(g, 2, 1), (g, 1, 3)]})
    states(T, base, r)
    forth.start()
    queries(T, base, r, {0: [(forth.cores,)], 1: [(g, 3, 0)], 2: [(forth.plane,)], 3: [(g, 2, 2), (g, 3, 1)]})
    g(2, 3)
    cotangents(T, base, r)
    forth.line()
    g(3, 2)
    forth.share()
    g(3, 3)
    forth.receive()
    forth.finish()
    attend(T, base, r)
    feed(T, base, r)
    home.start()
    up_grads(T, base, r)
    sum_u.start()
    home.cores()
    down_grads(T, base, r)
    sum_d.start()
    near = {0: [(home.plane,), (sum_u.step, 0)], 1: [(sum_d.step, 0)], 2: [(home.line,)],
            3: [(sum_q.start,), (sum_u.step, 1), (home.share,)]}
    far = {0: [(sum_q.step, 0), (sum_d.step, 1)], 1: [(sum_k.start,), (sum_u.step, 2)], 2: [(sum_q.step, 1)],
           3: [(sum_k.step, 0)]}
    back(T, base, r, tokens_all, near, home.receive, far, others_first)
    lines.start()
    sum_q.step(2)
    sum_d.step(2)
    sum_k.step(1)
    lines.step(0)
    sum_u.step(3)
    lines.step(1)
    sum_k.step(2)
    lines.step(2)
    sum_q.step(3)
    sum_d.step(3)
    sum_k.step(3)
    lines.step(3)
    gather.finish()
    home.finish()
    for each in (sum_u, sum_d, sum_q, sum_k, lines):
        each.finish()


def layer_near(lengths, seed, tokens, cotangent, weights, specs, seq, head):
    T, D = tokens.shape
    count = seq * head
    rows, ff = D // seq, specs["act"][0][2]
    held = [n for n in dict.fromkeys(sum((sum(names, ()) for names in (FRONT, MIDDLE, BACK)), ())) if n not in SHARED]
    held = [n for n in held if n not in ("result", "gtok", "xhat")]
    dma = pltpu.SemaphoreType.DMA
    scratch = [pltpu.VMEM(*specs[n]) for n in held]
    panels = 3 * LANES
    widths = (ff, LANES + ff, LANES, 2 * LANES)
    states = lambda count: pltpu.VMEM((count,) + STATES[1:], F32)
    for width in widths:
        scratch += scatter_buffers(seq, rows, width)
    scratch += [states(HEADS // 2)] * 8 + [states(seq // 2)] * 2
    tiles = lambda *lead: pltpu.VMEM(lead + (8, LANES), F32)
    scratch += [tiles(2, D // LANES), tiles(D // LANES), tiles(D // LANES), tiles(seq // 2 - 1)]
    scratch += [dma((4 * GATHER_COPIES,))] * 2 + [dma((16,))] * 4 + [dma((4 * SCATTER_COPIES + LINES_COPIES,))] * 2
    vmem, smem = pl.BlockSpec(memory_space=pltpu.VMEM), pl.BlockSpec(memory_space=pltpu.SMEM)
    shape = jax.ShapeDtypeStruct
    result, gtok, grad_a, grad_f, lines = pl.pallas_call(
        functools.partial(layer_kernel, held, T * count, T),
        out_shape=[shape((T, D), BF), shape((T, D), F32), shape((rows, panels), F32), shape((rows, 2 * ff + LANES), F32),
                   shape((8, LANES), F32)],
        in_specs=[smem] * 3 + [vmem] * 13,
        out_specs=[vmem] * 5,
        scratch_shapes=scratch,
        compiler_params=pltpu.CompilerParams(collective_id=0, has_side_effects=True, vmem_limit_bytes=LAYER_BYTES),
        name="layer",
    )(lengths, seed, weights[0], tokens, cotangent, *weights[1:])
    line, square = shape((1, rows), F32), shape((rows, LANES), F32)
    shapes = (shape((T, D), BF), shape((T, D), F32), line, line, square, square, square, shape((2, rows), F32),
              shape((2, 1), F32), square, line, line, shape((rows, ff), F32), shape((rows, ff), F32))

    def unpacked(*refs):
        unpack_kernel(lax.axis_index("seq") % 2, *refs)

    outs = pl.pallas_call(
        unpacked,
        out_shape=shapes,
        in_specs=[vmem] * 5,
        out_specs=[vmem] * len(shapes),
        compiler_params=pltpu.CompilerParams(vmem_limit_bytes=VMEM_BYTES),
        name="unpack",
    )(grad_a, grad_f, lines, result, gtok)
    flat = ("norm_gain", "norm_shift", "bias", "ffn_gain", "ffn_shift")
    turned = ("gate", "out", "down")
    return tuple(x.reshape(-1) if n in flat else x.T if n in turned else x for n, x in zip(OUTPUTS, outs))


def bias_columns(gate_bias):
    hi = lax.reduce_precision(gate_bias, 8, 7)
    mid = lax.reduce_precision(gate_bias - hi, 8, 7)
    return jnp.stack([hi, mid, gate_bias - hi - mid], axis=1).astype(BF)


def gather_any(q, k, v, gate, vectors, bias, out, up, down, seq):
    D = q.shape[0] * seq

    def whole(w, rows, cols):
        w = lax.all_gather(w, rows, axis=0, tiled=True)
        return lax.all_gather(w, cols, axis=1, tiled=True)

    def panels(w):
        return w.reshape(D, PAIRS, w.shape[1] // PAIRS).transpose(1, 0, 2)

    q, k, v = (panels(whole(w, "seq", "head")) for w in (q, k, v))
    gates = panels(whole(gate, "seq", "head"))
    lines = [jnp.broadcast_to(lax.all_gather(w, "seq", tiled=True)[None, :, None], (PAIRS, D, 1)) for w in vectors]
    bias = bias_columns(lax.all_gather(bias, "head", tiled=True)).reshape(PAIRS, 1, 6)
    pad = jnp.zeros((PAIRS, D, LANES - 12), BF)
    ga = jnp.concatenate([k, gates] + lines + [jnp.broadcast_to(bias, (PAIRS, D, 6)), pad, v, q], axis=2)
    gf = [panels(whole(out, "head", "seq").T), panels(whole(down, "head", "seq").T), panels(whole(up, "seq", "head"))]
    gf = jnp.concatenate(gf, axis=2)
    shape = (PAIRS, seq // 2, 2, D // seq)
    return ga.reshape(shape + ga.shape[2:]), gf.reshape(shape + gf.shape[2:])


def scatter_any(gga, ggf, lines, ff):
    gga, ggf = (x.reshape(PAIRS, -1, x.shape[-1]).astype(F32) for x in (gga, ggf))

    def grid(x):
        x = x.transpose(1, 0, 2).reshape(x.shape[1], -1)
        x = lax.psum_scatter(x, "seq", scatter_dimension=0, tiled=True)
        return lax.psum_scatter(x, "head", scatter_dimension=1, tiled=True)

    block = lambda i: gga[:, :, i * LANES : (i + 1) * LANES]
    lines = lines.transpose(0, 2, 1, 3).reshape(PAIRS, 8, -1)
    gates = lines[:, 0:2].transpose(0, 2, 1)
    bias = lines[:, 6:8, 0].reshape(HEADS)
    bias = lax.psum_scatter(lax.psum(bias, "seq"), "head", scatter_dimension=0, tiled=True)
    lines = lax.psum_scatter(lax.psum(lines[0, 2:6].T, "head"), "seq", scatter_dimension=0, tiled=True)
    return (
        lines[:, 0], lines[:, 1], grid(block(2)), grid(block(0)), grid(block(1)), grid(gates), bias,
        grid(ggf[:, :, :LANES]).T, lines[:, 2], lines[:, 3], grid(ggf[:, :, LANES + ff :]),
        grid(ggf[:, :, LANES : LANES + ff]).T,
    )


def shards(
    tokens, lengths, feature_seed, norm_gain, norm_shift, query_weight, key_weight, value_weight, gate_weight, gate_bias,
    out_weight, ffn_gain, ffn_shift, up_weight, down_weight, cotangent,
):
    seq, head = lax.axis_size("seq"), lax.axis_size("head")
    T, D = tokens.shape
    rows = D // seq
    ff = up_weight.shape[1] * head // PAIRS
    vectors = (norm_gain, norm_shift, ffn_gain, ffn_shift)
    specs = buffers(T, D, ATT, LANES + 2 * ff, ff, seq)
    if (seq, head) == (HEADS, PAIRS):
        weights = (gate_bias, key_weight, value_weight, query_weight, gate_weight.T)
        weights += tuple(w.reshape(1, rows) for w in vectors) + (up_weight, out_weight.T, down_weight.T)
        return layer_near(lengths, feature_seed, tokens, cotangent, weights, specs, seq, head)
    ga, gf = gather_any(query_weight, key_weight, value_weight, gate_weight, vectors, gate_bias, out_weight, up_weight,
                        down_weight, seq)
    args = (here(T).astype(I32).reshape(1), lengths, feature_seed, tokens, cotangent)
    state = {"ga": ga, "gf": gf}
    stage(lambda base, r: front(T, base, r), FRONT, specs, "front", args, state)
    state["inn"] = scan_states(state["out"], False)
    stage(lambda base, r: middle(T, base, r), MIDDLE, specs, "middle", args, state)
    state["aend"] = scan_states(state["adj"], True)
    stage(lambda base, r: back(T, base, r, T * seq * head), BACK, specs, "back", args, state)
    return (state["result"], state["gtok"]) + scatter_any(state["gga"], state["ggf"], state["lines"], ff)


def solution(mesh):
    both, rows, grid = P(("seq", "head"), None), P("seq"), P("seq", "head")
    return jax.shard_map(
        shards,
        mesh=mesh,
        in_specs=(both, P(), P(), rows, rows, grid, grid, grid, grid, P("head"), P("head", "seq"), rows, rows, grid,
                  P("head", "seq"), both),
        out_specs=(both, both, rows, rows, grid, grid, grid, grid, P("head"), P("head", "seq"), rows, rows, grid,
                   P("head", "seq")),
        check_vma=False,
    )
```

```python
import functools
import math

import jax
import jax.numpy as jnp
from jax import lax
from jax.experimental import pallas as pl
from jax.experimental.pallas import tpu as pltpu
from jax.sharding import PartitionSpec as P

BF, F32, I32 = jnp.bfloat16, jnp.float32, jnp.int32
MESH = pl.DeviceIdType.MESH
HEADS, HEAD_DIM, FEATS = 8, 64, 128
PAIRS = HEADS // 2
LANES = 128
EPS, FLOOR2, GATE_PEN = 1e-5, 0.0625, 0.5
TABLE_SCALE = 1.0 / math.sqrt(21845.0)
FEAT_SCALE = 1.0 / math.sqrt(FEATS)
INV_TWO_PI, TWO_PI = 1.0 / (2.0 * math.pi), 2.0 * math.pi
SIN = (0.9999996027571254, -0.16666553170295112, 0.008332405799301931, -0.00019808693226998236,
       2.6997700314773084e-06, -2.036409109746239e-08)
COS = (0.9999992193982472, -0.4999942543676011, 0.04165980908449851, -0.0013858873219640337,
       2.420384320646774e-05, -2.1976364824224383e-07)
ERFC = (0.254829592, -0.284496736, 1.421413741, -1.453152027, 1.061405429)
ATT = 3 * LANES
KEY, VALUE, QUERY = (slice(i * LANES, (i + 1) * LANES) for i in range(3))
NORMAL, DECAY, STATE_ROWS = HEAD_DIM, HEAD_DIM + 1, HEAD_DIM + 8
STATES = (HEADS, STATE_ROWS, 2 * FEATS)
VMEM_BYTES = 56 * 1024 * 1024
LAYER_BYTES = 63 * 1024 * 1024


def nn(a, b):
    return lax.dot_general(a, b, (((1,), (0,)), ((), ())), preferred_element_type=F32)


def nt(a, b):
    return lax.dot_general(a, b, (((1,), (1,)), ((), ())), preferred_element_type=F32)


def tn(a, b):
    return lax.dot_general(a, b, (((0,), (0,)), ((), ())), preferred_element_type=F32)


def halves(x, axis=1):
    hi = x.astype(BF)
    return jnp.concatenate([hi, (x - hi.astype(F32)).astype(BF)], axis=axis)


def iota(shape, dim):
    return lax.broadcasted_iota(I32, shape, dim)


def rows_loop(total, step, body):
    body(pl.ds(0, total), 0, total)


def pair_loop(body):
    def one(p, carry):
        body(p)
        return carry

    lax.fori_loop(0, PAIRS, one, 0)


def head_ones(rows, cols, row_span, col_span):
    same = (iota((rows, cols), 0) // row_span) % 2 == iota((rows, cols), 1) // col_span
    return jnp.where(same, 1.0, 0.0).astype(BF)


def marks(pos, base, lengths_ref):
    start = jnp.int32(0)
    segment = jnp.zeros(pos.shape, I32)
    reset = jnp.zeros(pos.shape, F32)
    carry = jnp.ones(pos.shape, F32)
    for d in range(lengths_ref.shape[0]):
        segment = segment + jnp.where(pos >= start, 1, 0)
        reset = jnp.where(pos == start, 1.0, reset)
        carry = jnp.where((pos >= start) & (pos - start <= pos - base), 0.0, carry)
        start = start + lengths_ref[d]
    live = jnp.where(pos < start, 1.0, 0.0)
    segment = segment + jnp.where(pos >= start, 1, 0)
    return segment, reset, live, carry, start


def horner(coefs, t):
    acc = jnp.full_like(t, coefs[-1])
    for c in coefs[-2::-1]:
        acc = acc * t + c
    return acc


def sincos(angle):
    r = angle - jnp.round(angle * INV_TWO_PI) * TWO_PI
    t = r * r
    return r * horner([c * FEAT_SCALE for c in SIN], t), horner([c * FEAT_SCALE for c in COS], t)


def gelu_parts(x):
    t = 1.0 / (1.0 + (0.3275911 / math.sqrt(2.0)) * jnp.abs(x))
    e = jnp.exp(-0.5 * x * x)
    q = 0.5 * t * horner(ERFC, t) * e
    cdf = jnp.where(x < 0.0, q, 1.0 - q)
    return x * cdf, cdf + x * e * (1.0 / math.sqrt(2.0 * math.pi))


def norm_stats(x):
    center = jnp.mean(x, axis=-1, keepdims=True)
    spread = jnp.mean(x * x, axis=-1, keepdims=True) - center * center
    inv = lax.rsqrt(spread + EPS)
    return (x - center) * inv, inv


def norm_back(grad, xhat, inv, gain):
    p = grad * gain
    return inv * (p - jnp.mean(p, axis=-1, keepdims=True) - xhat * jnp.mean(p * xhat, axis=-1, keepdims=True))


def by_eight(x):
    return jnp.sum(x.reshape(x.shape[0] // 8, 8, x.shape[1]), axis=0)


def panel(ref, p, cols):
    x = ref[p, :, :, :, cols]
    return x.reshape(x.shape[0] * x.shape[1] * x.shape[2], x.shape[3])


def low_lanes(rows):
    return iota((rows, LANES), 1) < HEAD_DIM


def widen(pair, a):
    return pair[:, a * HEAD_DIM : a * HEAD_DIM + 1]


def head_values(v, a, low):
    one = jnp.ones_like(v)
    return jnp.where(low, v, one) if a == 0 else jnp.where(low, one, v)


def state_of(states, p, a):
    own = states[2 * p + a, 0:HEAD_DIM, :]
    rest = jnp.broadcast_to(states[2 * p + a, NORMAL : NORMAL + 1, :], own.shape)
    return jnp.concatenate([own, rest] if a == 0 else [rest, own], axis=0)


def put_state(states, h, own, normal, decay):
    states[h, 0:HEAD_DIM, :] = own
    rest = jnp.zeros((STATE_ROWS - DECAY - 1, 2 * FEATS), F32)
    states[h, NORMAL:, :] = jnp.concatenate([normal, twice(decay), rest], axis=0)


def twice(x):
    return jnp.concatenate([x, x], axis=1)


def run_pairs(body, hook, order=None):
    def one(p):
        body(order(p) if order else p)
        for at, acts in (hook or {}).items():

            @pl.when(p == at)
            def _():
                for act, *given in acts:
                    act(*given)

    pair_loop(one)


def tables(T, base, r):
    pos = base + iota((8, T), 1)
    seg_row, _, live_row, _, _ = marks(pos, base, r.lengths)
    seg1, live1, pos1 = seg_row[0:1], live_row[0:1], pos[0:1]

    def mask_rows(rows, at, n):
        row_pos = base + at + iota((n, 1), 0)
        seg_col = marks(row_pos, base, r.lengths)[0]
        allowed = (seg_col == seg1) & (pos1 <= row_pos) & (live1 > 0.0)
        r.mask[rows, :] = jnp.where(allowed, 0.0, -1e30)

    rows_loop(T, 64, mask_rows)
    hash_seed = r.seed[0] * jnp.int32(-2048144789)

    def table(p):
        place = (p * LANES + iota((LANES, LANES), 0)) * FEATS + iota((LANES, LANES), 1)
        y = place * jnp.int32(-1640531535) + hash_seed
        y = y ^ lax.shift_right_logical(y, jnp.int32(15))
        y = y * jnp.int32(739982445)
        y = y ^ lax.shift_right_logical(y, jnp.int32(13))
        y = y * jnp.int32(695872825)
        y = y ^ lax.shift_right_logical(y, jnp.int32(16))
        s = jnp.full(y.shape, -510, I32)
        for k in range(4):
            s = s + (lax.shift_right_logical(y, jnp.int32(8 * k)) & jnp.int32(255))
        top = iota((LANES, LANES), 0) < HEAD_DIM
        odd = s & 1

        def diagonal(x):
            x = x.astype(F32)
            return jnp.concatenate([jnp.where(top, x, 0.0), jnp.where(top, 0.0, x)], axis=1).astype(BF)

        r.tab[p, 0:LANES, :] = diagonal(s - odd)
        r.tab[p, LANES:, :] = diagonal(odd)
        r.tabn[p] = diagonal(s)

    pair_loop(table)


def first_norm(T, base, r):
    for p in range(PAIRS):
        rows = r.small[p]
        r.gate[2 * p : 2 * p + 2, :] = rows[0:2]
        r.gate[8 + 2 * p : 10 + 2 * p, :] = rows[0:2]
        r.bias[2 * p : 2 * p + 1, :] = rows[6:7] + rows[7:8] + rows[8:9]
        r.bias[2 * p + 1 : 2 * p + 2, :] = rows[9:10] + rows[10:11] + rows[11:12]
        if p == 0:
            r.vec[...] = rows[0:8]

    def norm_rows(rows, at, n):
        xhat, _ = norm_stats(r.tok[rows, :].astype(F32))
        r.normed[rows, :] = (xhat * r.vec[2:3, :] + r.vec[3:4, :]).astype(BF)

    rows_loop(T, 64, norm_rows)
    logits = nt(r.gate[...].astype(BF), r.normed[...])[0:8] + r.bias[:, 0:1]
    r.logits[...] = logits
    pos = base + iota((8, T), 1)
    _, reset_row, live_row, carry_row, _ = marks(pos, base, r.lengths)
    decay = -(jnp.log1p(jnp.exp(-jnp.abs(logits))) + jnp.maximum(-logits, 0.0)) * live_row * (1.0 - reset_row)
    run = decay
    lane = iota((8, T), 1)
    shift = 1
    while shift < T:
        run = run + jnp.where(lane >= shift, pltpu.roll(run, shift, 1), 0.0)
        shift *= 2
    r.run[...] = run
    r.total[...] = jnp.broadcast_to(jnp.exp(run[:, T - 1 : T]) * carry_row[:, T - 1 : T], (8, LANES))
    hi = run.astype(BF).astype(F32)
    mid = (run - hi).astype(BF).astype(F32)
    run3 = jnp.concatenate([hi, mid, run - hi - mid, jnp.zeros_like(hi)], axis=0).astype(BF)

    def spread(p):
        chosen = iota((32, LANES), 0) % 8 == 2 * p + iota((32, LANES), 1) // HEAD_DIM
        r.rb[p] = tn(run3, jnp.where(chosen, 1.0, 0.0).astype(BF))

    pair_loop(spread)


def features(T, r, p, u, out):
    ones2 = head_ones(2 * LANES, 2 * LANES, HEAD_DIM, LANES)
    r.s1[...] = nn(jnp.concatenate([u, u], axis=1), r.tab[p])
    uf = u.astype(F32)
    r.s2[...] = nn(halves(uf * uf), ones2)

    def body(rows, at, n):
        s, c = sincos(r.s1[rows, :] * (lax.rsqrt(r.s2[rows, :] + 1e-6) * TABLE_SCALE))
        for a in range(2):
            out[2 * p + a, rows, 0:FEATS] = s[:, a * FEATS : (a + 1) * FEATS].astype(BF)
            out[2 * p + a, rows, FEATS : 2 * FEATS] = c[:, a * FEATS : (a + 1) * FEATS].astype(BF)

    rows_loop(T, 64, body)


def end_factor(T, base, r):
    last_seg = marks(base + T - 1 + iota((8, LANES), 1) * 0, base, r.lengths)[0][0:1, 0:1]
    seg_col, _, live_col, _, _ = marks(base + iota((T, LANES), 0), base, r.lengths)
    return jnp.where(seg_col == last_seg, live_col, 0.0)


def keys(T, base, r, hook=None):
    def pair(p):
        r.k[p] = nn(r.normed[...], panel(r.ga, p, KEY)).astype(BF)
        features(T, r, p, r.k[p], r.kf)

    run_pairs(pair, hook)


def states(T, base, r):
    end_live = end_factor(T, base, r)

    def pair(p):
        r.v[p] = nn(r.normed[...], panel(r.ga, p, VALUE)).astype(BF)
        decay_end = jnp.exp(r.rb[p, T - 1 : T, :] - r.rb[p]) * end_live
        lane = iota((T, LANES), 1)
        factor = jnp.where(lane < 2, widen(decay_end, 0), widen(decay_end, 1))
        rough = factor.astype(BF).astype(F32)
        factor = jnp.where(lane % 2 == 0, rough, factor - rough)
        ends = tn(factor.astype(BF), jnp.concatenate([r.kf[2 * p], r.kf[2 * p + 1]], axis=1))
        for a in range(2):
            h = 2 * p + a
            scaled = (r.kf[h].astype(F32) * widen(decay_end, a)).astype(BF)
            state = tn(r.v[p], scaled)[a * HEAD_DIM : (a + 1) * HEAD_DIM]
            normal = ends[2 * a : 2 * a + 1, a * 2 * FEATS : (a + 1) * 2 * FEATS]
            normal = normal + ends[2 * a + 1 : 2 * a + 2, a * 2 * FEATS : (a + 1) * 2 * FEATS]
            put_state(r.out, h, state, normal, r.total[pl.ds(h, 1), :])

    pair_loop(pair)


def queries(T, base, r, hook=None):
    low = low_lanes(T)

    def pair(p):
        r.q[p] = nn(r.normed[...], panel(r.ga, p, QUERY)).astype(BF)
        features(T, r, p, r.q[p], r.qf)
        v = r.v[p]
        for a in range(2):
            h = 2 * p + a
            r.s[...] = nt(r.qf[h], r.kf[h])
            run_row = r.run[pl.ds(h, 1), :]

            def body(rows, at, n):
                gap = jnp.minimum(widen(r.rb[p, rows, :], a) - run_row, r.mask[rows, :])
                w = r.s[rows, :] * jnp.exp(gap)
                rounded = w.astype(BF)
                r.w[h, rows, :] = rounded
                rest = jnp.sum(w - rounded.astype(F32), axis=1, keepdims=True)
                r.zfix[p, rows, a * HEAD_DIM : (a + 1) * HEAD_DIM] = jnp.broadcast_to(rest, (n, HEAD_DIM)).astype(BF)

            rows_loop(T, 64, body)
            r.own[h] = nn(r.w[h], head_values(v, a, low))

    run_pairs(pair, hook)


def carry_factor(T, base, r):
    _, _, live_col, carry_col, _ = marks(base + iota((T, LANES), 0), base, r.lengths)
    return live_col, carry_col


def attend(T, base, r):
    low = low_lanes(T)
    live_col, carry_col = carry_factor(T, base, r)

    def join(p):
        factor = jnp.exp(r.rb[p]) * carry_col
        total = []
        for a in range(2):
            h = 2 * p + a
            carried = nt(twice(r.qf[h]), halves(state_of(r.inn, p, a)))
            joined = r.own[h] + widen(factor, a) * carried
            r.joined[h] = joined
            total.append(joined)
        num = jnp.where(low, total[0], total[1])
        z = pltpu.roll(jnp.where(low, total[1], total[0]), HEAD_DIM, 1) + r.zfix[p].astype(F32)
        r.att[p] = (live_col * num * lax.rsqrt(z * z + FLOOR2)).astype(BF)

    pair_loop(join)
    o = out_columns(r)
    branch = None
    for p in range(0, PAIRS, 2):
        part = nt(
            jnp.concatenate([r.att[p], r.att[p + 1]], axis=1),
            jnp.concatenate([panel(r.gf, p, o), panel(r.gf, p + 1, o)], axis=1),
        )
        branch = part if branch is None else branch + part
    r.mid[...] = branch

    def norm_rows(rows, at, n):
        mid = r.mid[rows, :] + r.tok[rows, :].astype(F32)
        r.mid[rows, :] = mid
        xhat, inv = norm_stats(mid)
        r.xhat[rows, :] = xhat
        r.inv[rows, :] = jnp.broadcast_to(inv, (n, LANES))
        r.two[rows, :] = (xhat * r.vec[4:5, :] + r.vec[5:6, :]).astype(BF)

    rows_loop(T, 64, norm_rows)


def feed_columns(r):
    ff = (r.gf.shape[-1] - LANES) // 2
    return slice(LANES + ff, LANES + 2 * ff), slice(LANES, LANES + ff)


def out_columns(r):
    return slice(0, LANES)


def cotangents(T, base, r):
    _, d = feed_columns(r)

    def part(p):
        r.h2[p] = nn(r.cot[...], panel(r.gf, p, d))

    pair_loop(part)


def feed(T, base, r):
    low = low_lanes(T)
    live_col, carry_col = carry_factor(T, base, r)
    r.acc1[...] = jnp.zeros_like(r.acc1)
    r.acc2[...] = jnp.zeros_like(r.acc2)
    u, d = feed_columns(r)
    o = out_columns(r)

    def part(p):
        up, down = panel(r.gf, p, u), panel(r.gf, p, d)
        r.h1[...] = nn(r.two[...], up)

        def body(rows, at, n):
            value, slope = gelu_parts(r.h1[rows, :])
            r.act[p, rows, :] = value.astype(BF)
            r.gh[p, rows, :] = (r.h2[p, rows, :] * slope).astype(BF)

        rows_loop(T, 64, body)
        r.acc1[...] += nt(r.act[p], down)
        r.acc2[...] += nt(r.gh[p], up)

    pair_loop(part)
    r.sums[...] = jnp.zeros_like(r.sums)

    def finish(rows, at, n):
        r.result[rows, :] = (r.mid[rows, :] + r.acc1[rows, :]).astype(BF)
        xhat, gn = r.xhat[rows, :], r.acc2[rows, :]
        r.sums[0:8, :] += by_eight(gn * xhat)
        r.sums[8:16, :] += by_eight(gn)
        back = norm_back(gn, xhat, r.inv[rows, 0:1], r.vec[4:5, :])
        grad = r.cot[rows, :].astype(F32) + back
        r.gmid[rows, :] = grad
        r.gb[rows, :] = grad.astype(BF)

    rows_loop(T, 64, finish)
    r.fsum[0:1, :] = jnp.sum(r.sums[0:8, :], axis=0, keepdims=True)
    r.fsum[1:2, :] = jnp.sum(r.sums[8:16, :], axis=0, keepdims=True)
    ones1 = head_ones(2 * LANES, LANES, HEAD_DIM, HEAD_DIM)
    row_ones = jnp.ones((16, 2 * LANES), BF)
    first_half = iota((T, LANES), 1) % HEAD_DIM < HEAD_DIM // 2

    def back(p):
        g = nn(r.gb[...], panel(r.gf, p, o)).astype(BF).astype(F32) * live_col
        total = [r.joined[2 * p], r.joined[2 * p + 1]]
        num = jnp.where(low, total[0], total[1])
        z = pltpu.roll(jnp.where(low, total[1], total[0]), HEAD_DIM, 1) + r.zfix[p].astype(F32)
        rden = lax.rsqrt(z * z + FLOOR2)
        dn = (g * rden).astype(BF).astype(F32)
        dz = nn(halves(dn * num), ones1) * (z * rden * rden)
        dz = pltpu.roll(dz * (-2.0 / HEAD_DIM), HEAD_DIM, 1)
        rough = dz.astype(BF).astype(F32)
        dz = jnp.where(first_half, rough, dz - rough)
        factor = jnp.exp(r.rb[p]) * carry_col
        for a in range(2):
            h = 2 * p + a
            joint = (jnp.where(low, dn, dz) if a == 0 else jnp.where(low, dz, dn)).astype(BF)
            r.dn[h] = joint
            r.dr[pl.ds(h, 1), :] = nt(row_ones, halves(joint.astype(F32) * total[a]))[0:1]
            adj = tn(joint, (r.qf[h].astype(F32) * widen(factor, a)).astype(BF))
            at, half = (1 - a) * HEAD_DIM, HEAD_DIM // 2
            normal = 0.5 * (adj[at : at + 1] + adj[at + half : at + half + 1])
            put_state(r.adj, h, adj[a * HEAD_DIM : (a + 1) * HEAD_DIM], normal, r.total[pl.ds(h, 1), :])

    pair_loop(back)


def up_grads(T, base, r):
    up, _ = feed_columns(r)
    pair_loop(lambda p: put_panel(r.ggf, p, up, tn(r.two[...], r.gh[p])))


def down_grads(T, base, r):
    _, down = feed_columns(r)

    def part(p):
        put_panel(r.ggf, p, down, tn(r.cot[...], r.act[p]))
        put_panel(r.ggf, p, out_columns(r), tn(r.gb[...], r.att[p]))

    pair_loop(part)


def put_panel(ref, p, cols, x):
    shape = ref.shape[1:4] + (x.shape[1],)
    ref[p, :, :, :, cols] = x.astype(BF).reshape(shape)


def back(T, base, r, tokens_all, near_hook=None, between=lambda: None, far_hook=None, order=None):
    D = r.tok.shape[1]
    low = low_lanes(T)
    _, carry_col = carry_factor(T, base, r)
    end_live = end_factor(T, base, r)
    ones1 = head_ones(2 * LANES, LANES, HEAD_DIM, HEAD_DIM)
    row_ones = jnp.ones((16, 2 * LANES), BF)
    r.acc1[...] = jnp.zeros_like(r.acc1)

    def feature_back(p, u, da):
        ds = nt(da, r.tabn[p]) * TABLE_SCALE
        uf = u.astype(F32)
        inv = lax.rsqrt(nn(halves(uf * uf), ones1) + 1e-6)
        uh = uf * inv
        return (inv * (ds - uh * nn(halves(uh * ds), ones1))).astype(BF)

    def angles(rows, source, feat, h):
        x, f = source[rows, :], feat[h, rows, :].astype(F32)
        return x[:, :FEATS] * f[:, FEATS:] - x[:, FEATS:] * f[:, :FEATS]

    def near(p):
        v = r.v[p]
        factor = jnp.exp(r.rb[p]) * carry_col
        for a in range(2):
            h = 2 * p + a
            r.s[...] = nt(r.dn[h], head_values(v, a, low))
            run_row = r.run[pl.ds(h, 1), :]

            def body(rows, at, n):
                gap = jnp.minimum(widen(r.rb[p, rows, :], a) - run_row, r.mask[rows, :])
                r.ds[rows, :] = (r.s[rows, :] * jnp.exp(gap)).astype(BF)

            rows_loop(T, 64, body)
            before = halves(state_of(r.inn, p, a), 0)
            r.s1[...] = nn(r.ds[...], r.kf[h]) + widen(factor, a) * nn(twice(r.dn[h]), before)
            r.s2[...] = tn(r.ds[...], r.qf[h])
            r.ghv[h] = tn(r.w[h], r.dn[h])

            def turn(rows, at, n):
                r.da[p, rows, a * FEATS : (a + 1) * FEATS] = angles(rows, r.s1, r.qf, h).astype(BF)
                r.da[p, rows, (2 + a) * FEATS : (3 + a) * FEATS] = angles(rows, r.s2, r.kf, h).astype(BF)

            rows_loop(T, 64, turn)
        grad = feature_back(p, r.q[p], r.da[p, :, : 2 * FEATS])
        r.acc1[...] += nt(grad, panel(r.ga, p, QUERY))
        put_panel(r.gga, p, slice(2 * LANES, 3 * LANES), tn(r.normed[...], grad))

    def far(p):
        v = r.v[p]
        decay_end = jnp.exp(r.rb[p, T - 1 : T, :] - r.rb[p]) * end_live
        grad_v = []
        for a in range(2):
            h = 2 * p + a
            end, hv = state_of(r.aend, p, a), head_values(v, a, low)
            late = widen(decay_end, a) * nt(twice(r.kf[h]), halves(end))
            r.s2[...] = widen(decay_end, a) * nn(twice(hv), halves(end, 0))
            grad_hv = r.ghv[h] + late
            grad_v.append(grad_hv)

            def turn(rows, at, n):
                lanes = slice((2 + a) * FEATS, (3 + a) * FEATS)
                r.da[p, rows, lanes] = (r.da[p, rows, lanes].astype(F32) + angles(rows, r.s2, r.kf, h)).astype(BF)

            rows_loop(T, 64, turn)
            hvf = hv.astype(F32)
            k_side = nt(row_ones, halves(hvf * grad_hv))
            r.drun[pl.ds(h, 1), :] = r.dr[pl.ds(h, 1), :] - k_side[0:1]
            owed = jnp.sum(end * state_of(r.inn, p, a), axis=0, keepdims=True)
            owed = r.total[pl.ds(h, 1), 0:1] * jnp.sum(owed, axis=1, keepdims=True)
            owed = owed + jnp.sum(jnp.sum(hvf * late, axis=0, keepdims=True), axis=1, keepdims=True)
            r.owed[pl.ds(h, 1), :] = jnp.broadcast_to(owed, (1, LANES))
        grad_v = jnp.where(low, grad_v[0], grad_v[1]).astype(BF)
        grads = jnp.concatenate([feature_back(p, r.k[p], r.da[p, :, 2 * FEATS :]), grad_v], axis=1)
        r.acc1[...] += nt(grads, panel(r.ga, p, slice(0, 2 * LANES)))
        put_panel(r.gga, p, slice(0, 2 * LANES), tn(r.normed[...], grads))

    run_pairs(near, near_hook, order)
    between()
    run_pairs(far, far_hook, order)
    pos = base + iota((8, T), 1)
    _, reset_row, live_row, _, filled = marks(pos, base, r.lengths)
    lane = iota((8, T), 1)
    run = r.drun[...]
    shift = 1
    while shift < T:
        run = run + jnp.where(lane < T - shift, pltpu.roll(run, T - shift, 1), 0.0)
        shift *= 2
    grad_decay = run + r.owed[:, 0:1]
    logits = r.logits[...]
    e = jnp.exp(-jnp.abs(logits))
    small, large = e / (1.0 + e), 1.0 / (1.0 + e)
    gate = jnp.where(logits >= 0.0, large, small)
    rest = jnp.where(logits >= 0.0, small, large)
    penalty = GATE_PEN * tokens_all / HEADS / jnp.broadcast_to(filled, (8, T)).astype(F32)
    grad_logits = grad_decay * live_row * (1.0 - reset_row) * rest + penalty * live_row * gate * rest
    both = halves(grad_logits, 0)
    r.acc1[...] += tn(both, r.gate[...].astype(BF))
    gate_rows = nn(both, r.normed[...])
    gate_rows = gate_rows[0:8] + gate_rows[8:16]
    bias = jnp.broadcast_to(jnp.sum(grad_logits, axis=1, keepdims=True), (8, D))
    r.sums[...] = jnp.zeros_like(r.sums)

    def finish(rows, at, n):
        xhat, inv = norm_stats(r.tok[rows, :].astype(F32))
        gn = r.acc1[rows, :]
        r.sums[0:8, :] += by_eight(gn * xhat)
        r.sums[8:16, :] += by_eight(gn)
        r.gtok[rows, :] = r.gmid[rows, :] + norm_back(gn, xhat, inv, r.vec[2:3, :])

    rows_loop(T, 64, finish)
    norm_gain = jnp.sum(r.sums[0:8, :], axis=0, keepdims=True)
    norm_shift = jnp.sum(r.sums[8:16, :], axis=0, keepdims=True)
    lines = [norm_gain, norm_shift, r.fsum[0:2, :]]
    for p in range(PAIRS):
        rows = jnp.concatenate([gate_rows[2 * p : 2 * p + 2]] + lines + [bias[2 * p : 2 * p + 2]], axis=0)
        for g in range(D // LANES):
            r.lines[p, g] = rows[:, g * LANES : (g + 1) * LANES]


class Refs:
    def __init__(self, **refs):
        self.__dict__.update(refs)


def buffers(T, D, att, rest, ff, seq):
    z = (PAIRS, seq // 2, 2, D // seq)
    pair = (PAIRS, T, LANES)
    return {
        "ga": (z + (att,), BF), "gf": (z + (rest,), BF), "gga": (z + (att,), BF), "small": ((PAIRS, 16, D), F32), "ggf": (z + (rest,), BF),
        "gate": ((16, D), F32), "bias": ((8, D), F32), "vec": ((8, D), F32), "normed": ((T, D), BF),
        "logits": ((8, T), F32), "run": ((8, T), F32), "total": ((8, LANES), F32), "mask": ((T, T), F32),
        "s1": ((T, 2 * FEATS), F32), "s2": ((T, 2 * FEATS), F32), "s": ((T, T), F32),
        "tab": ((PAIRS, 2 * LANES, 2 * FEATS), BF), "tabn": ((PAIRS, LANES, 2 * FEATS), BF),
        "q": (pair, BF), "k": (pair, BF), "v": (pair, BF), "rb": (pair, F32),
        "qf": ((HEADS, T, 2 * FEATS), BF), "kf": ((HEADS, T, 2 * FEATS), BF),
        "out": (STATES, F32), "inn": (STATES, F32), "adj": (STATES, F32), "aend": (STATES, F32),
        "w": ((HEADS, T, T), BF), "own": ((HEADS, T, LANES), F32), "joined": ((HEADS, T, LANES), F32),
        "att": (pair, BF), "zfix": (pair, BF), "mid": ((T, D), F32), "xhat": ((T, D), F32), "inv": ((T, LANES), F32), "two": ((T, D), BF),
        "acc1": ((T, D), F32), "acc2": ((T, D), F32), "h1": ((T, ff), F32), "h2": ((PAIRS, T, ff), F32),
        "act": ((PAIRS, T, ff), BF), "gh": ((PAIRS, T, ff), BF), "sums": ((16, D), F32), "fsum": ((8, D), F32),
        "result": ((T, D), BF), "gmid": ((T, D), F32), "gb": ((T, D), BF), "dr": ((8, T), F32),
        "dn": ((HEADS, T, LANES), BF), "ds": ((T, T), BF), "da": ((PAIRS, T, 4 * FEATS), BF), "ghv": ((HEADS, T, LANES), F32),
        "lines": ((PAIRS, D // LANES, 8, LANES), F32),
        "drun": ((8, T), F32), "owed": ((8, LANES), F32), "gtok": ((T, D), F32),
    }


FRONT = (
    ("ga", "small"),
    ("gate", "vec", "normed", "logits", "run", "total", "mask", "tabn", "q", "k", "v", "rb", "qf", "kf", "out", "w", "own", "zfix"),
    ("bias", "s1", "s2", "s", "tab"),
)
MIDDLE = (
    ("gf", "vec", "rb", "qf", "own", "zfix", "inn", "total"),
    ("ggf", "result", "gmid", "fsum", "dr", "dn", "adj"),
    ("joined", "att", "mid", "xhat", "inv", "two", "acc1", "acc2", "h1", "h2", "act", "gh", "sums", "gb"),
)
BACK = (
    ("ga", "gate", "vec", "normed", "logits", "run", "total", "mask", "tabn", "q", "k", "v", "rb", "qf", "kf",
     "w", "inn", "aend", "gmid", "fsum", "dr", "dn"),
    ("gga", "gtok", "lines"),
    ("s", "s1", "s2", "ds", "da", "ghv", "drun", "owed", "acc1", "sums"),
)
SHARED = {"joined": "own", "h1": "s", "gmid": "mid", "ds": "gb", "adj": "out", "da": "act", "ghv": "own"}


def front(T, base, r):
    tables(T, base, r)
    first_norm(T, base, r)
    keys(T, base, r)
    states(T, base, r)
    queries(T, base, r)


def middle(T, base, r):
    cotangents(T, base, r)
    attend(T, base, r)
    feed(T, base, r)
    up_grads(T, base, r)
    down_grads(T, base, r)


def here(T):
    return (lax.axis_index("seq") * lax.axis_size("head") + lax.axis_index("head")) * T


def stage(which, names, specs, outer, args, state):
    reads, writes, scratch = names
    shape = lambda n: jax.ShapeDtypeStruct(*specs[n])
    vmem, smem = pl.BlockSpec(memory_space=pltpu.VMEM), pl.BlockSpec(memory_space=pltpu.SMEM)

    def kernel(*refs):
        base_ref, lengths, seed, tok, cot = refs[:5]
        rest = dict(zip(reads + writes + scratch, refs[5:]))
        which(base_ref[0], Refs(lengths=lengths, seed=seed, tok=tok, cot=cot, **rest))

    out = pl.pallas_call(
        kernel,
        out_shape=[shape(n) for n in writes],
        in_specs=[smem] * 3 + [vmem] * (2 + len(reads)),
        out_specs=[vmem] * len(writes),
        scratch_shapes=[pltpu.VMEM(*specs[n]) for n in scratch],
        compiler_params=pltpu.CompilerParams(vmem_limit_bytes=VMEM_BYTES),
        name=outer,
    )(*args, *[state[n] for n in reads])
    state.update(zip(writes, out))


def scan_states(out, reverse):
    seq, head = lax.axis_size("seq"), lax.axis_size("head")
    count = seq * head
    me = lax.axis_index("seq") * head + lax.axis_index("head")
    state = (out[:, DECAY : DECAY + 1, 0:1], out[:, :DECAY])
    step = 1
    order = lambda pairs: [(b, a) for a, b in pairs] if reverse else pairs
    axes = ("seq", "head")
    while step < count:
        moved = jax.tree.map(lambda x: lax.ppermute(x, axes, order([(i, i + step) for i in range(count - step)])), state)
        has = (me < count - step) if reverse else (me >= step)
        f, m = state
        state = (jnp.where(has, f * moved[0], f), m + jnp.where(has, f * moved[1], 0.0))
        step *= 2
    moved = lax.ppermute(state[1], axes, order([(i, i + 1) for i in range(count - 1)]))
    return jnp.concatenate([moved, jnp.zeros((HEADS, STATE_ROWS - DECAY, 2 * FEATS), F32)], axis=1)


def remote(src, dst, send, recv, to):
    return pltpu.make_async_remote_copy(
        src_ref=src, dst_ref=dst, send_sem=send, recv_sem=recv, device_id=to, device_id_type=MESH
    )


class Place:
    def __init__(self):
        self.seq, self.head = lax.axis_size("seq"), lax.axis_size("head")
        s, h = lax.axis_index("seq"), lax.axis_index("head")
        self.z, self.y, self.x, self.c = s // 2, s % 2, h // 2, h % 2
        self.depth = self.seq // 2
        self.count = self.seq * self.head
        self.me = s * self.head + h

    def device(self, z=None, y=None, x=None, c=None):
        pick = lambda given, own: own if given is None else given
        z, y, x, c = pick(z, self.z), pick(y, self.y), pick(x, self.x), pick(c, self.c)
        return (z * 2 + y, x * 2 + c)

    def number(self, i):
        return (i // self.head, i % self.head)

    def around(self, k):
        return (self.z + k) % self.depth

class Semaphores:
    def __init__(self, send, recv):
        self.send, self.recv, self.used = send, recv, 0

    def copy(self, src, dst, to):
        i = self.used
        self.used += 1
        return remote(src, dst, self.send.at[i], self.recv.at[i], to)


GATHER_COPIES = 2 * (3 + 1 + 2 + 2)
SCATTER_COPIES = 2 + 2 * (1 + 1 + 3)


def gather_stages(place, g, lanes, sems):
    half = g.shape[3] // 2
    z, y, x, c = place.z, place.y, place.x, place.c
    pair = x * 2 + c
    stages = [[], [], [], []]
    for part in range(2):
        rows = pl.ds(part * half, half)
        same = lambda ref, to: sems.copy(ref, ref, to)
        for k in range(1, place.depth):
            stages[0].append(same(g.at[pair, z, y, rows, lanes], place.device(z=place.around(k))))
        to_y, to_x = place.device(y=1 - y), place.device(x=1 - x)
        if part == 0:
            stages[1].append(same(g.at[pair, :, y, rows, lanes], to_y))
            stages[2].append(same(g.at[pair, :, :, rows, lanes], to_x))
        else:
            stages[1].append(same(g.at[pair, :, y, rows, lanes], to_x))
            for other in range(2):
                stages[2].append(same(g.at[other * 2 + c, :, y, rows, lanes], to_y))
        for other in range(2):
            stages[3].append(same(g.at[other * 2 + c, :, :, rows, lanes], place.device(c=1 - c)))
    return stages


def begin(stage):
    for copy in stage:
        copy.start()


def arrived(stage):
    for copy in stage:
        copy.wait_recv()


def sent(*stages):
    for stage in stages:
        for copy in stage:
            copy.wait_send()


class Gather:
    def __init__(self, place, ga, gf, gs, sems):
        ff = (gf.shape[-1] - LANES) // 2
        lanes = lambda first, count: pl.ds(first, count)
        self.chunks = [
            gather_stages(place, ref, part, sems)
            for ref, part in (
                (ga, lanes(0, LANES)),
                (ga, lanes(LANES, 2 * LANES)),
                (gf, lanes(0, LANES + ff)),
                (gf, lanes(LANES + ff, ff)),
            )
        ]

        z, y, x, c, pair = place.z, place.y, place.x, place.c, place.x * 2 + place.c
        first, same = self.chunks[0], lambda ref, **to: sems.copy(ref, ref, place.device(**to))
        first[0] += [same(gs.at[pair, z, y], z=place.around(k)) for k in range(1, place.depth)]
        first[1].append(same(gs.at[pair, :, y], y=1 - y))
        first[2].append(same(gs.at[pair], x=1 - x))
        first[3] += [same(gs.at[other * 2 + c], c=1 - c) for other in range(2)]

    def begin(self, chunk):
        begin(self.chunks[chunk][0])

    def step(self, chunk, stage):
        arrived(self.chunks[chunk][stage])
        if stage < 3:
            begin(self.chunks[chunk][stage + 1])

    def finish(self):
        for chunk in self.chunks:
            sent(*chunk)


def add_blocks(to, others, count, where):
    def one(i, carry):
        at = where(i)
        total = to[at].astype(F32)
        for ref, index in others:
            total = total + ref[index(i)].astype(F32)
        to[at] = total.astype(to.dtype)
        return carry

    lax.fori_loop(0, count, one, 0)


class Scatter:
    def __init__(self, place, gg, lanes, out, buf, sems):
        self.place, self.gg, self.lanes, self.out = place, gg, lanes, out
        self.r1, self.r2a, self.r2b, self.r3a, self.r3b, self.r4a, self.r4b = buf
        z, y, x, c, n = place.z, place.y, place.x, place.c, place.depth
        self.half = half = gg.shape[3] // 2
        first, last = pl.ds(0, half), pl.ds(half, half)
        other, to_y, to_x = place.device(c=1 - c), place.device(y=1 - y), place.device(x=1 - x)
        self.stages = [
            [sems.copy(gg.at[i * 2 + 1 - c, :, :, :, lanes], self.r1.at[i], other) for i in range(2)],
            [
                sems.copy(self.r1.at[1 - x, :, :, first], self.r2a, to_x),
                sems.copy(self.r1.at[:, :, 1 - y, last], self.r2b, to_y),
            ],
            [sems.copy(self.r2a.at[:, 1 - y], self.r3a, to_y), sems.copy(self.r2b.at[1 - x], self.r3b, to_x)],
            [
                sems.copy(ref.at[place.around(k)], slots.at[k - 1], place.device(z=place.around(k)))
                for ref, slots in ((self.r3a, self.r4a), (self.r3b, self.r4b))
                for k in range(1, n)
            ],
        ]

    def start(self):
        begin(self.stages[0])

    def step(self, i):
        place, n, half = self.place, self.place.depth, self.half
        y, x, c = place.y, place.x, place.c
        first, last = slice(0, half), slice(half, 2 * half)
        lanes = self.lanes
        arrived(self.stages[i])
        if i == 0:
            block = lambda j: (j // (2 * n), (j // 2) % n, j % 2)
            add_blocks(self.r1, [(self.gg, lambda j: ((j // (2 * n)) * 2 + c, (j // 2) % n, j % 2, slice(None), lanes))], 4 * n, block)
        elif i == 1:
            add_blocks(self.r2a, [(self.r1, lambda j: (x, j // 2, j % 2, first))], 2 * n, lambda j: (j // 2, j % 2))
            add_blocks(self.r2b, [(self.r1, lambda j: (j // n, j % n, y, last))], 2 * n, lambda j: (j // n, j % n))
        elif i == 2:
            add_blocks(self.r3a, [(self.r2a, lambda j: (j, y))], n, lambda j: (j,))
            add_blocks(self.r3b, [(self.r2b, lambda j: (x, j))], n, lambda j: (j,))
        else:
            for ref, slots, rows in ((self.r3a, self.r4a, first), (self.r3b, self.r4b, last)):
                total = ref[place.z].astype(F32)
                for k in range(n - 1):
                    total = total + slots[k].astype(F32)
                self.out[rows, lanes] = total
        if i < 3:
            begin(self.stages[i + 1])

    def finish(self):
        sent(*self.stages)


def scatter_buffers(seq, rows, cols):
    n, half = seq // 2, rows // 2
    return [
        pltpu.VMEM(shape + (cols,), BF)
        for shape in ((2, n, 2, rows), (n, 2, half), (2, n, half), (n, half), (n, half), (n - 1, half), (n - 1, half))
    ]


class Scan:
    def __init__(self, place, reverse, out, inn, box, planes, send, recv):
        self.place, self.reverse = place, reverse
        self.out, self.inn, self.planes = out, inn, planes
        self.pair, self.chip, self.box, self.back = box
        self.chips = HEADS // 2
        self.mine = place.y * 2 + place.x
        self.half, self.rest = place.c * self.chips, (1 - place.c) * self.chips
        self.sems = Semaphores(send, recv)
        other = place.device(c=1 - place.c)
        at = lambda ref, first: ref.at[pl.ds(first, self.chips)]
        near = [lax.rem(self.mine + k, self.chips) for k in range(1, self.chips)]
        chip = lambda m: place.device(y=m // 2, x=m % 2)
        total = planes.at[place.z]
        copy = self.sems.copy
        self.ways = [
            [copy(at(out, self.rest), self.pair, other)],
            [copy(self.chip.at[m], self.box.at[self.mine], chip(m)) for m in near],
            [copy(total, total, place.device(z=place.around(k))) for k in range(1, place.depth)],
            [copy(self.box.at[m], self.back.at[self.mine], chip(m)) for m in near],
            [copy(self.pair, at(inn, self.half), other)],
        ]

    def start(self):
        begin(self.ways[0])

    def chain(self, ref, count):
        kept = iota((STATE_ROWS, 2 * FEATS), 0) != DECAY
        state = jnp.where(kept, 0.0, 1.0)
        for i in range(count):
            d = count - 1 - i if self.reverse else i
            term = ref[d]
            ref[d] = state
            state = state * term[DECAY : DECAY + 1, :] + jnp.where(kept, term, 0.0)
        return state

    def earlier_is_mine(self):
        return (self.place.c == 0) != self.reverse

    def cores(self):
        arrived(self.ways[0])
        kept = iota((STATE_ROWS, 2 * FEATS), 0) != DECAY
        first = jnp.broadcast_to(self.earlier_is_mine(), kept.shape)
        for i in range(self.chips):
            mine, its = self.out[self.half + i], self.pair[i]
            early, late = jnp.where(first, mine, its), jnp.where(first, its, mine)
            self.chip[i] = early * late[DECAY : DECAY + 1, :] + jnp.where(kept, late, 0.0)
        begin(self.ways[1])
        self.box[self.mine] = self.chip[self.mine]

    def plane(self):
        arrived(self.ways[1])
        self.planes[self.place.z] = self.chain(self.box, self.chips)
        begin(self.ways[2])

    def line(self):
        arrived(self.ways[2])
        sent(self.ways[2])
        self.chain(self.planes, self.place.depth)
        before = self.planes[self.place.z]
        for m in range(self.chips):
            own = self.box[m]
            self.box[m] = own + own[DECAY : DECAY + 1, :] * before
        begin(self.ways[3])
        self.back[self.mine] = self.box[self.mine]

    def share(self):
        arrived(self.ways[3])
        sent(self.ways[0])
        first = jnp.broadcast_to(self.earlier_is_mine(), (STATE_ROWS, 2 * FEATS))
        for i in range(self.chips):
            mine, its, before = self.out[self.half + i], self.pair[i], self.back[i]
            early = jnp.where(first, mine, its)
            late = before * early[DECAY : DECAY + 1, :] + early
            self.inn[self.half + i] = jnp.where(first, before, late)
            self.pair[i] = jnp.where(first, late, before)
        begin(self.ways[4])

    def receive(self):
        arrived(self.ways[4])

    def finish(self):
        sent(self.ways[1], self.ways[3], self.ways[4])


class Lines:
    def __init__(self, place, lines, out, buf, sems):
        self.place, self.lines, self.out = place, lines, out
        self.l1, self.l2, self.l3, self.l4 = buf
        z, y, x, c, copy = place.z, place.y, place.x, place.c, sems.copy
        around = range(1, place.depth)
        self.stages = [
            [copy(lines.at[i * 2 + 1 - c], self.l1.at[i], place.device(c=1 - c)) for i in range(2)],
            [copy(self.l1.at[1 - x], self.l2, place.device(x=1 - x))],
            [copy(self.l2, self.l3, place.device(y=1 - y))],
            [copy(self.l3.at[place.around(k)], self.l4.at[k - 1], place.device(z=place.around(k))) for k in around],
        ]

    def start(self):
        begin(self.stages[0])

    def step(self, i):
        place = self.place
        arrived(self.stages[i])
        if i == 0:
            for j in range(2):
                self.l1[j] += self.lines[j * 2 + place.c]
        elif i == 1:
            self.l2[...] += self.l1[place.x]
        elif i == 2:
            self.l3[...] += self.l2[...]
        else:
            total = self.l3[place.z]
            for k in range(place.depth - 1):
                total = total + self.l4[k]
            self.out[...] = total
        if i < 3:
            begin(self.stages[i + 1])

    def finish(self):
        sent(*self.stages)


LINES_COPIES = 2 + 1 + 1 + 3


def greet(place):
    x, y = 1 - place.x, 1 - place.y
    near = [place.device(c=1 - place.c), place.device(x=x), place.device(y=y), place.device(x=x, y=y)]
    near += [place.device(z=place.around(k)) for k in range(1, place.depth)]
    barrier = pltpu.get_barrier_semaphore()
    for device in near:
        pl.semaphore_signal(barrier, inc=1, device_id=device, device_id_type=MESH)
    return lambda: pl.semaphore_wait(barrier, len(near))


def pack(place, r, key, value, query, gate, vectors, bias, up, out, down):
    at = (place.x * 2 + place.c, place.z, place.y)
    rows, ff = key.shape[0], up.shape[1]
    r.gf[at + (slice(None), slice(LANES + ff, None))] = up[...]
    r.gf[at + (slice(None), slice(0, LANES))] = out[...]
    r.gf[at + (slice(None), slice(LANES, LANES + ff))] = down[...]
    r.ga[at + (slice(None), KEY)] = key[...]
    r.ga[at + (slice(None), VALUE)] = value[...]
    r.ga[at + (slice(None), QUERY)] = query[...]
    lines = [gate[...].astype(F32)] + [v[...].astype(F32) for v in vectors]
    for j in range(2):
        left = jnp.full((1, rows), bias[j], F32)
        for _ in range(3):
            piece = left.astype(BF).astype(F32)
            lines.append(piece)
            left = left - piece
    lines = jnp.concatenate(lines + [jnp.zeros((4, rows), F32)], axis=0).astype(BF)
    wide = jnp.where(iota((rows, LANES), 0) == iota((rows, LANES), 1), 1.0, 0.0).astype(BF)
    r.gs[at] = nn(lines, wide).astype(BF)


def spread_small(r):
    for p in range(PAIRS):
        for z in range(r.gs.shape[1]):
            even, odd = r.gs[p, z, 0].astype(F32), r.gs[p, z, 1].astype(F32)
            tile = jnp.where(low_lanes(16), even, pltpu.roll(odd, HEAD_DIM, 1))
            r.small[p, :, z * LANES : (z + 1) * LANES] = tile


def unpack_kernel(half, grad_a, grad_f, lines, result, gtok, *outs):
    out = dict(zip(OUTPUTS, outs))
    rows = grad_a.shape[0]
    ff = (grad_f.shape[1] - LANES) // 2
    out["result"][...] = result[...]
    out["tokens"][...] = gtok[...]
    for i, name in enumerate(("key", "value", "query")):
        out[name][...] = grad_a[:, i * LANES : (i + 1) * LANES]
    out["up"][...] = grad_f[:, LANES + ff :]
    out["out"][...] = grad_f[:, :LANES]
    out["down"][...] = grad_f[:, LANES : LANES + ff]
    own = jnp.where(half == 0, lines[:, :rows], lines[:, rows : 2 * rows])
    for i, name in enumerate(("norm_gain", "norm_shift", "ffn_gain", "ffn_shift")):
        out[name][...] = own[2 + i : 3 + i, :]
    out["gate"][...] = own[0:2, :]
    out["bias"][...] = jnp.where(iota((1, LANES), 1) == 0, lines[6:7, :], lines[7:8, :])[:, 0:2]


OUTPUTS = ("result", "tokens", "norm_gain", "norm_shift", "query", "key", "value", "gate", "bias", "out", "ffn_gain",
           "ffn_shift", "up", "down")


def layer_kernel(names, tokens_all, T, lengths, seed, bias, tok_in, cot_in, key, value, query, gate, *given):
    vectors, (up, out, down), given = given[0:4], given[4:7], given[7:]
    (result_out, gtok_out, grad_a, grad_f, grad_lines), scratch = given[:5], given[5:]
    (tok, cot, result, gtok, moves), scratch = scratch[:5], scratch[5:]
    moves = [pltpu.make_async_copy(src, dst, moves.at[i]) for i, (src, dst) in enumerate(
        ((tok_in, tok), (cot_in, cot), (result, result_out), (gtok, gtok_out)))]
    moves[0].start()
    moves[1].start()
    place = Place()
    base = place.me * T
    arrays = dict(zip(names, scratch))
    arrays.update({name: arrays[other] for name, other in SHARED.items()})
    scratch = scratch[len(names) :]
    r = Refs(lengths=lengths, seed=seed, tok=tok, cot=cot, result=result, gtok=gtok, xhat=gtok, **arrays)
    sums, scratch = [scratch[7 * i : 7 * i + 7] for i in range(4)], scratch[28:]
    boxes, planes, line_box, sems = (scratch[0:4], scratch[4:8]), scratch[8:10], scratch[10:14], scratch[14:]
    meet = greet(place)
    pack(place, r, key, value, query, gate, vectors, bias, up, out, down)
    gather = Gather(place, r.ga, r.gf, r.gs, Semaphores(sems[0], sems[1]))
    forth = Scan(place, False, r.out, r.inn, boxes[0], planes[0], sems[2], sems[3])
    home = Scan(place, True, r.adj, r.aend, boxes[1], planes[1], sems[4], sems[5])
    later = Semaphores(sems[6], sems[7])
    up, down = feed_columns(r)
    sum_u = Scatter(place, r.ggf, up, grad_f, sums[0], later)
    sum_d = Scatter(place, r.ggf, slice(0, down.stop), grad_f, sums[1], later)
    sum_q = Scatter(place, r.gga, slice(2 * LANES, 3 * LANES), grad_a, sums[2], later)
    sum_k = Scatter(place, r.gga, slice(0, 2 * LANES), grad_a, sums[3], later)
    lines = Lines(place, r.lines, grad_lines, line_box, later)
    meet()

    g = gather.step
    others_first = lambda i: (i % 2) * 2 + jnp.where(i < 2, 1 - place.c, place.c)
    gather.begin(0)
    tables(T, base, r)
    g(0, 0)
    gather.begin(1)
    g(0, 1)
    g(1, 0)
    gather.begin(2)
    g(0, 2)
    g(1, 1)
    g(0, 3)
    spread_small(r)
    moves[0].wait()
    first_norm(T, base, r)
    g(2, 0)
    gather.begin(3)
    keys(T, base, r, {0: [(g, 1, 2)], 3: [(g, 2, 1), (g, 1, 3)]})
    states(T, base, r)
    forth.start()
    queries(T, base, r, {0: [(forth.cores,)], 1: [(g, 3, 0)], 2: [(forth.plane,)], 3: [(g, 2, 2), (g, 3, 1)]})
    g(2, 3)
    moves[1].wait()
    cotangents(T, base, r)
    forth.line()
    g(3, 2)
    forth.share()
    g(3, 3)
    forth.receive()
    forth.finish()
    attend(T, base, r)
    feed(T, base, r)
    home.start()
    moves[2].start()
    up_grads(T, base, r)
    sum_u.start()
    home.cores()
    down_grads(T, base, r)
    sum_d.start()
    near = {0: [(home.plane,), (sum_u.step, 0)], 2: [(home.line,)],
            3: [(sum_u.step, 1), (sum_q.start,), (home.share,), (sum_d.step, 0)]}
    far = {0: [(sum_q.step, 0)], 1: [(sum_k.start,), (sum_u.step, 2)], 2: [(sum_d.step, 1), (sum_q.step, 1)],
           3: [(sum_k.step, 0)]}
    back(T, base, r, tokens_all, near, home.receive, far, others_first)
    moves[3].start()
    lines.start()
    sum_q.step(2)
    sum_d.step(2)
    sum_k.step(1)
    lines.step(0)
    sum_u.step(3)
    lines.step(1)
    sum_k.step(2)
    lines.step(2)
    sum_q.step(3)
    sum_d.step(3)
    sum_k.step(3)
    lines.step(3)
    gather.finish()
    home.finish()
    moves[2].wait()
    moves[3].wait()
    for each in (sum_u, sum_d, sum_q, sum_k, lines):
        each.finish()


def layer_near(lengths, seed, tokens, cotangent, weights, specs, seq, head):
    T, D = tokens.shape
    count = seq * head
    rows, ff = D // seq, specs["act"][0][2]
    held = [n for n in dict.fromkeys(sum((sum(names, ()) for names in (FRONT, MIDDLE, BACK)), ())) if n not in SHARED]
    held = [n for n in held if n not in ("result", "gtok", "xhat")]
    dma = pltpu.SemaphoreType.DMA
    specs = dict(specs, gs=((PAIRS, seq // 2, 2, 16, LANES), BF))
    held.append("gs")
    wide = lambda kind: pltpu.VMEM((T, D), kind)
    scratch = [wide(BF), wide(BF), wide(BF), wide(F32), dma((4,))]
    scratch += [pltpu.VMEM(*specs[n]) for n in held]
    panels = 3 * LANES
    widths = (ff, LANES + ff, LANES, 2 * LANES)
    states = lambda count: pltpu.VMEM((count,) + STATES[1:], F32)
    for width in widths:
        scratch += scatter_buffers(seq, rows, width)
    scratch += [states(HEADS // 2)] * 8 + [states(seq // 2)] * 2
    tiles = lambda *lead: pltpu.VMEM(lead + (8, LANES), F32)
    scratch += [tiles(2, D // LANES), tiles(D // LANES), tiles(D // LANES), tiles(seq // 2 - 1)]
    scratch += [dma((5 * GATHER_COPIES,))] * 2 + [dma((16,))] * 4 + [dma((4 * SCATTER_COPIES + LINES_COPIES,))] * 2
    vmem, smem = pl.BlockSpec(memory_space=pltpu.VMEM), pl.BlockSpec(memory_space=pltpu.SMEM)
    shape, far = jax.ShapeDtypeStruct, pl.BlockSpec(memory_space=pl.ANY)
    result, gtok, grad_a, grad_f, lines = pl.pallas_call(
        functools.partial(layer_kernel, held, T * count, T),
        out_shape=[shape((T, D), BF), shape((T, D), F32), shape((rows, panels), F32), shape((rows, 2 * ff + LANES), F32),
                   shape((8, LANES), F32)],
        in_specs=[smem] * 3 + [far] * 2 + [vmem] * 11,
        out_specs=[far] * 2 + [vmem] * 3,
        scratch_shapes=scratch,
        compiler_params=pltpu.CompilerParams(collective_id=0, has_side_effects=True, vmem_limit_bytes=LAYER_BYTES),
        name="layer",
    )(lengths, seed, weights[0], tokens, cotangent, *weights[1:])
    line, square = shape((1, rows), F32), shape((rows, LANES), F32)
    shapes = (shape((T, D), BF), shape((T, D), F32), line, line, square, square, square, shape((2, rows), F32),
              shape((1, 2), F32), square, line, line, shape((rows, ff), F32), shape((rows, ff), F32))

    def unpacked(*refs):
        unpack_kernel(lax.axis_index("seq") % 2, *refs)

    outs = pl.pallas_call(
        unpacked,
        out_shape=shapes,
        in_specs=[vmem] * 5,
        out_specs=[vmem] * len(shapes),
        compiler_params=pltpu.CompilerParams(vmem_limit_bytes=VMEM_BYTES),
        name="unpack",
    )(grad_a, grad_f, lines, result, gtok)
    flat = ("norm_gain", "norm_shift", "bias", "ffn_gain", "ffn_shift")
    turned = ("gate", "out", "down")
    return tuple(x.reshape(-1) if n in flat else x.T if n in turned else x for n, x in zip(OUTPUTS, outs))


def bias_columns(gate_bias):
    hi = lax.reduce_precision(gate_bias, 8, 7)
    mid = lax.reduce_precision(gate_bias - hi, 8, 7)
    return jnp.stack([hi, mid, gate_bias - hi - mid], axis=1).astype(BF)


def gather_any(q, k, v, gate, vectors, bias, out, up, down, seq):
    D = q.shape[0] * seq

    def whole(w, rows, cols):
        w = lax.all_gather(w, rows, axis=0, tiled=True)
        return lax.all_gather(w, cols, axis=1, tiled=True)

    def panels(w):
        return w.reshape(D, PAIRS, w.shape[1] // PAIRS).transpose(1, 0, 2)

    q, k, v = (panels(whole(w, "seq", "head")) for w in (q, k, v))
    gates = panels(whole(gate, "seq", "head"))
    lines = [jnp.broadcast_to(lax.all_gather(w, "seq", tiled=True)[None, :, None], (PAIRS, D, 1)) for w in vectors]
    bias = bias_columns(lax.all_gather(bias, "head", tiled=True)).reshape(PAIRS, 1, 6)
    ga = jnp.concatenate([k, v, q], axis=2)
    rows = [gates.transpose(0, 2, 1)] + [w.transpose(0, 2, 1) for w in lines]
    rows += [jnp.broadcast_to(bias.transpose(0, 2, 1), (PAIRS, 6, D)), jnp.zeros((PAIRS, 4, D), BF)]
    small = jnp.concatenate(rows, axis=1).astype(F32)
    gf = [panels(whole(out, "head", "seq").T), panels(whole(down, "head", "seq").T), panels(whole(up, "seq", "head"))]
    gf = jnp.concatenate(gf, axis=2)
    shape = (PAIRS, seq // 2, 2, D // seq)
    return ga.reshape(shape + ga.shape[2:]), gf.reshape(shape + gf.shape[2:]), small


def scatter_any(gga, ggf, lines, ff):
    gga, ggf = (x.reshape(PAIRS, -1, x.shape[-1]).astype(F32) for x in (gga, ggf))

    def grid(x):
        x = x.transpose(1, 0, 2).reshape(x.shape[1], -1)
        x = lax.psum_scatter(x, "seq", scatter_dimension=0, tiled=True)
        return lax.psum_scatter(x, "head", scatter_dimension=1, tiled=True)

    block = lambda i: gga[:, :, i * LANES : (i + 1) * LANES]
    lines = lines.transpose(0, 2, 1, 3).reshape(PAIRS, 8, -1)
    gates = lines[:, 0:2].transpose(0, 2, 1)
    bias = lines[:, 6:8, 0].reshape(HEADS)
    bias = lax.psum_scatter(lax.psum(bias, "seq"), "head", scatter_dimension=0, tiled=True)
    lines = lax.psum_scatter(lax.psum(lines[0, 2:6].T, "head"), "seq", scatter_dimension=0, tiled=True)
    return (
        lines[:, 0], lines[:, 1], grid(block(2)), grid(block(0)), grid(block(1)), grid(gates), bias,
        grid(ggf[:, :, :LANES]).T, lines[:, 2], lines[:, 3], grid(ggf[:, :, LANES + ff :]),
        grid(ggf[:, :, LANES : LANES + ff]).T,
    )


def shards(
    tokens, lengths, feature_seed, norm_gain, norm_shift, query_weight, key_weight, value_weight, gate_weight, gate_bias,
    out_weight, ffn_gain, ffn_shift, up_weight, down_weight, cotangent,
):
    seq, head = lax.axis_size("seq"), lax.axis_size("head")
    T, D = tokens.shape
    rows = D // seq
    ff = up_weight.shape[1] * head // PAIRS
    vectors = (norm_gain, norm_shift, ffn_gain, ffn_shift)
    specs = buffers(T, D, ATT, LANES + 2 * ff, ff, seq)
    if (seq, head) == (HEADS, PAIRS):
        weights = (gate_bias, key_weight, value_weight, query_weight, gate_weight.T)
        weights += tuple(w.reshape(1, rows) for w in vectors) + (up_weight, out_weight.T, down_weight.T)
        return layer_near(lengths, feature_seed, tokens, cotangent, weights, specs, seq, head)
    ga, gf, small = gather_any(query_weight, key_weight, value_weight, gate_weight, vectors, gate_bias, out_weight, up_weight,
                        down_weight, seq)
    args = (here(T).astype(I32).reshape(1), lengths, feature_seed, tokens, cotangent)
    state = {"ga": ga, "gf": gf, "small": small}
    stage(lambda base, r: front(T, base, r), FRONT, specs, "front", args, state)
    state["inn"] = scan_states(state["out"], False)
    stage(lambda base, r: middle(T, base, r), MIDDLE, specs, "middle", args, state)
    state["aend"] = scan_states(state["adj"], True)
    stage(lambda base, r: back(T, base, r, T * seq * head), BACK, specs, "back", args, state)
    return (state["result"], state["gtok"]) + scatter_any(state["gga"], state["ggf"], state["lines"], ff)


def solution(mesh):
    both, rows, grid = P(("seq", "head"), None), P("seq"), P("seq", "head")
    return jax.shard_map(
        shards,
        mesh=mesh,
        in_specs=(both, P(), P(), rows, rows, grid, grid, grid, grid, P("head"), P("head", "seq"), rows, rows, grid,
                  P("head", "seq"), both),
        out_specs=(both, both, rows, rows, grid, grid, grid, grid, P("head"), P("head", "seq"), rows, rows, grid,
                   P("head", "seq")),
        check_vma=False,
    )
```

```python
import functools
import math

import jax
import jax.numpy as jnp
from jax import lax
from jax.experimental import pallas as pl
from jax.experimental.pallas import tpu as pltpu
from jax.sharding import PartitionSpec as P

BF, F32, I32 = jnp.bfloat16, jnp.float32, jnp.int32
MESH = pl.DeviceIdType.MESH
HEADS, HEAD_DIM, FEATS = 8, 64, 128
PAIRS = HEADS // 2
LANES = 128
EPS, FLOOR2, GATE_PEN = 1e-5, 0.0625, 0.5
TABLE_SCALE = 1.0 / math.sqrt(21845.0)
FEAT_SCALE = 1.0 / math.sqrt(FEATS)
INV_TWO_PI, TWO_PI = 1.0 / (2.0 * math.pi), 2.0 * math.pi
SIN = (0.9999996027571254, -0.16666553170295112, 0.008332405799301931, -0.00019808693226998236,
       2.6997700314773084e-06, -2.036409109746239e-08)
COS = (0.9999992193982472, -0.4999942543676011, 0.04165980908449851, -0.0013858873219640337,
       2.420384320646774e-05, -2.1976364824224383e-07)
ERFC = (0.254829592, -0.284496736, 1.421413741, -1.453152027, 1.061405429)
ATT = 3 * LANES
KEY, VALUE, QUERY = (slice(i * LANES, (i + 1) * LANES) for i in range(3))
NORMAL, DECAY, STATE_ROWS = HEAD_DIM, HEAD_DIM + 1, HEAD_DIM + 8
STATES = (HEADS, STATE_ROWS, 2 * FEATS)
VMEM_BYTES = 56 * 1024 * 1024
LAYER_BYTES = 63 * 1024 * 1024


def nn(a, b):
    return lax.dot_general(a, b, (((1,), (0,)), ((), ())), preferred_element_type=F32)


def nt(a, b):
    return lax.dot_general(a, b, (((1,), (1,)), ((), ())), preferred_element_type=F32)


def tn(a, b):
    return lax.dot_general(a, b, (((0,), (0,)), ((), ())), preferred_element_type=F32)


def halves(x, axis=1):
    hi = x.astype(BF)
    return jnp.concatenate([hi, (x - hi.astype(F32)).astype(BF)], axis=axis)


def iota(shape, dim):
    return lax.broadcasted_iota(I32, shape, dim)


def rows_loop(total, step, body):
    body(pl.ds(0, total), 0, total)


def pair_loop(body, straight=1):
    def one(i, carry):
        for k in range(straight):
            body(i * straight + k)
        return carry

    lax.fori_loop(0, PAIRS // straight, one, 0)


def head_ones(rows, cols, row_span, col_span):
    same = (iota((rows, cols), 0) // row_span) % 2 == iota((rows, cols), 1) // col_span
    return jnp.where(same, 1.0, 0.0).astype(BF)


def marks(pos, base, lengths_ref):
    start = jnp.int32(0)
    segment = jnp.zeros(pos.shape, I32)
    reset = jnp.zeros(pos.shape, F32)
    carry = jnp.ones(pos.shape, F32)
    for d in range(lengths_ref.shape[0]):
        segment = segment + jnp.where(pos >= start, 1, 0)
        reset = jnp.where(pos == start, 1.0, reset)
        carry = jnp.where((pos >= start) & (pos - start <= pos - base), 0.0, carry)
        start = start + lengths_ref[d]
    live = jnp.where(pos < start, 1.0, 0.0)
    segment = segment + jnp.where(pos >= start, 1, 0)
    return segment, reset, live, carry, start


def horner(coefs, t):
    acc = jnp.full_like(t, coefs[-1])
    for c in coefs[-2::-1]:
        acc = acc * t + c
    return acc


def sincos(angle):
    r = angle - jnp.round(angle * INV_TWO_PI) * TWO_PI
    t = r * r
    return r * horner([c * FEAT_SCALE for c in SIN], t), horner([c * FEAT_SCALE for c in COS], t)


def gelu_parts(x):
    t = 1.0 / (1.0 + (0.3275911 / math.sqrt(2.0)) * jnp.abs(x))
    e = jnp.exp(-0.5 * x * x)
    q = 0.5 * t * horner(ERFC, t) * e
    cdf = jnp.where(x < 0.0, q, 1.0 - q)
    return x * cdf, cdf + x * e * (1.0 / math.sqrt(2.0 * math.pi))


def norm_stats(x):
    center = jnp.mean(x, axis=-1, keepdims=True)
    spread = jnp.mean(x * x, axis=-1, keepdims=True) - center * center
    inv = lax.rsqrt(spread + EPS)
    return (x - center) * inv, inv


def norm_back(grad, xhat, inv, gain):
    p = grad * gain
    return inv * (p - jnp.mean(p, axis=-1, keepdims=True) - xhat * jnp.mean(p * xhat, axis=-1, keepdims=True))


def by_eight(x):
    return jnp.sum(x.reshape(x.shape[0] // 8, 8, x.shape[1]), axis=0)


def panel(ref, p, cols):
    x = ref[p, :, :, :, cols]
    return x.reshape(x.shape[0] * x.shape[1] * x.shape[2], x.shape[3])


def low_lanes(rows):
    return iota((rows, LANES), 1) < HEAD_DIM


def widen(pair, a):
    return pair[:, a * HEAD_DIM : a * HEAD_DIM + 1]


def head_values(v, a, low):
    one = jnp.ones_like(v)
    return jnp.where(low, v, one) if a == 0 else jnp.where(low, one, v)


def state_of(states, p, a):
    own = states[2 * p + a, 0:HEAD_DIM, :]
    rest = jnp.broadcast_to(states[2 * p + a, NORMAL : NORMAL + 1, :], own.shape)
    return jnp.concatenate([own, rest] if a == 0 else [rest, own], axis=0)


def put_state(states, h, own, normal, decay):
    states[h, 0:HEAD_DIM, :] = own
    rest = jnp.zeros((STATE_ROWS - DECAY - 1, 2 * FEATS), F32)
    states[h, NORMAL:, :] = jnp.concatenate([normal, twice(decay), rest], axis=0)


def twice(x):
    return jnp.concatenate([x, x], axis=1)


def run_pairs(body, hook, order=None, straight=1):
    def one(p):
        body(order(p) if order else p)
        for at, acts in (hook or {}).items():

            @pl.when(p == at)
            def _():
                for act, *given in acts:
                    act(*given)

    pair_loop(one, straight)


def tables(T, base, r):
    pos = base + iota((8, T), 1)
    seg_row, _, live_row, _, _ = marks(pos, base, r.lengths)
    seg1, live1, pos1 = seg_row[0:1], live_row[0:1], pos[0:1]

    def mask_rows(rows, at, n):
        row_pos = base + at + iota((n, 1), 0)
        seg_col = marks(row_pos, base, r.lengths)[0]
        allowed = (seg_col == seg1) & (pos1 <= row_pos) & (live1 > 0.0)
        r.mask[rows, :] = jnp.where(allowed, 0.0, -1e30)

    rows_loop(T, 64, mask_rows)
    hash_seed = r.seed[0] * jnp.int32(-2048144789)

    def table(p):
        place = (p * LANES + iota((LANES, LANES), 0)) * FEATS + iota((LANES, LANES), 1)
        y = place * jnp.int32(-1640531535) + hash_seed
        y = y ^ lax.shift_right_logical(y, jnp.int32(15))
        y = y * jnp.int32(739982445)
        y = y ^ lax.shift_right_logical(y, jnp.int32(13))
        y = y * jnp.int32(695872825)
        y = y ^ lax.shift_right_logical(y, jnp.int32(16))
        s = jnp.full(y.shape, -510, I32)
        for k in range(4):
            s = s + (lax.shift_right_logical(y, jnp.int32(8 * k)) & jnp.int32(255))
        top = iota((LANES, LANES), 0) < HEAD_DIM
        odd = s & 1

        def diagonal(x):
            x = x.astype(F32)
            return jnp.concatenate([jnp.where(top, x, 0.0), jnp.where(top, 0.0, x)], axis=1).astype(BF)

        r.tab[p, 0:LANES, :] = diagonal(s - odd)
        r.tab[p, LANES:, :] = diagonal(odd)
        r.tabn[p] = diagonal(s)

    pair_loop(table)


def standardise(T, base, r):
    r.xhat[...] = norm_stats(r.tok[...].astype(F32))[0]


def first_norm(T, base, r):
    for p in range(PAIRS):
        rows = r.small[p]
        r.gate[2 * p : 2 * p + 2, :] = rows[0:2]
        r.gate[8 + 2 * p : 10 + 2 * p, :] = rows[0:2]
        r.bias[2 * p : 2 * p + 1, :] = rows[6:7] + rows[7:8] + rows[8:9]
        r.bias[2 * p + 1 : 2 * p + 2, :] = rows[9:10] + rows[10:11] + rows[11:12]
        if p == 0:
            r.vec[...] = rows[0:8]

    r.normed[...] = (r.xhat[...] * r.vec[2:3, :] + r.vec[3:4, :]).astype(BF)
    logits = nt(r.gate[...].astype(BF), r.normed[...])[0:8] + r.bias[:, 0:1]
    r.logits[...] = logits
    pos = base + iota((8, T), 1)
    _, reset_row, live_row, carry_row, _ = marks(pos, base, r.lengths)
    decay = -(jnp.log1p(jnp.exp(-jnp.abs(logits))) + jnp.maximum(-logits, 0.0)) * live_row * (1.0 - reset_row)
    run = decay
    lane = iota((8, T), 1)
    shift = 1
    while shift < T:
        run = run + jnp.where(lane >= shift, pltpu.roll(run, shift, 1), 0.0)
        shift *= 2
    r.run[...] = run
    r.total[...] = jnp.broadcast_to(jnp.exp(run[:, T - 1 : T]) * carry_row[:, T - 1 : T], (8, LANES))
    hi = run.astype(BF).astype(F32)
    mid = (run - hi).astype(BF).astype(F32)
    run3 = jnp.concatenate([hi, mid, run - hi - mid, jnp.zeros_like(hi)], axis=0).astype(BF)

    def spread(p):
        chosen = iota((32, LANES), 0) % 8 == 2 * p + iota((32, LANES), 1) // HEAD_DIM
        r.rb[p] = tn(run3, jnp.where(chosen, 1.0, 0.0).astype(BF))

    pair_loop(spread)


def features(T, r, p, u, out):
    ones2 = head_ones(2 * LANES, 2 * LANES, HEAD_DIM, LANES)
    r.s1[...] = nn(jnp.concatenate([u, u], axis=1), r.tab[p])
    uf = u.astype(F32)
    r.s2[...] = nn(halves(uf * uf), ones2)

    def body(rows, at, n):
        s, c = sincos(r.s1[rows, :] * (lax.rsqrt(r.s2[rows, :] + 1e-6) * TABLE_SCALE))
        for a in range(2):
            out[2 * p + a, rows, 0:FEATS] = s[:, a * FEATS : (a + 1) * FEATS].astype(BF)
            out[2 * p + a, rows, FEATS : 2 * FEATS] = c[:, a * FEATS : (a + 1) * FEATS].astype(BF)

    rows_loop(T, 64, body)


def end_factor(T, base, r):
    last_seg = marks(base + T - 1 + iota((8, LANES), 1) * 0, base, r.lengths)[0][0:1, 0:1]
    seg_col, _, live_col, _, _ = marks(base + iota((T, LANES), 0), base, r.lengths)
    return jnp.where(seg_col == last_seg, live_col, 0.0)


def keys(T, base, r, hook=None):
    def pair(p):
        r.k[p] = nn(r.normed[...], panel(r.ga, p, KEY)).astype(BF)
        features(T, r, p, r.k[p], r.kf)

    run_pairs(pair, hook)


def states(T, base, r):
    end_live = end_factor(T, base, r)

    def pair(p):
        r.v[p] = nn(r.normed[...], panel(r.ga, p, VALUE)).astype(BF)
        decay_end = jnp.exp(r.rb[p, T - 1 : T, :] - r.rb[p]) * end_live
        lane = iota((T, LANES), 1)
        factor = jnp.where(lane < 2, widen(decay_end, 0), widen(decay_end, 1))
        rough = factor.astype(BF).astype(F32)
        factor = jnp.where(lane % 2 == 0, rough, factor - rough)
        ends = tn(factor.astype(BF), jnp.concatenate([r.kf[2 * p], r.kf[2 * p + 1]], axis=1))
        for a in range(2):
            h = 2 * p + a
            scaled = (r.kf[h].astype(F32) * widen(decay_end, a)).astype(BF)
            state = tn(r.v[p], scaled)[a * HEAD_DIM : (a + 1) * HEAD_DIM]
            normal = ends[2 * a : 2 * a + 1, a * 2 * FEATS : (a + 1) * 2 * FEATS]
            normal = normal + ends[2 * a + 1 : 2 * a + 2, a * 2 * FEATS : (a + 1) * 2 * FEATS]
            put_state(r.out, h, state, normal, r.total[pl.ds(h, 1), :])

    pair_loop(pair)


def queries(T, base, r, hook=None):
    low = low_lanes(T)

    def pair(p):
        r.q[p] = nn(r.normed[...], panel(r.ga, p, QUERY)).astype(BF)
        features(T, r, p, r.q[p], r.qf)
        v = r.v[p]
        for a in range(2):
            h = 2 * p + a
            r.s[...] = nt(r.qf[h], r.kf[h])
            run_row = r.run[pl.ds(h, 1), :]

            def body(rows, at, n):
                gap = jnp.minimum(widen(r.rb[p, rows, :], a) - run_row, r.mask[rows, :])
                w = r.s[rows, :] * jnp.exp(gap)
                rounded = w.astype(BF)
                r.w[h, rows, :] = rounded
                rest = jnp.sum(w - rounded.astype(F32), axis=1, keepdims=True)
                r.zfix[p, rows, a * HEAD_DIM : (a + 1) * HEAD_DIM] = jnp.broadcast_to(rest, (n, HEAD_DIM)).astype(BF)

            rows_loop(T, 64, body)
            r.own[h] = nn(r.w[h], head_values(v, a, low))

    run_pairs(pair, hook)


def carry_factor(T, base, r):
    _, _, live_col, carry_col, _ = marks(base + iota((T, LANES), 0), base, r.lengths)
    return live_col, carry_col


def attend(T, base, r):
    low = low_lanes(T)
    live_col, carry_col = carry_factor(T, base, r)

    def join(p):
        factor = jnp.exp(r.rb[p]) * carry_col
        total = []
        for a in range(2):
            h = 2 * p + a
            carried = nt(twice(r.qf[h]), halves(state_of(r.inn, p, a)))
            joined = r.own[h] + widen(factor, a) * carried
            r.joined[h] = joined
            total.append(joined)
        num = jnp.where(low, total[0], total[1])
        z = pltpu.roll(jnp.where(low, total[1], total[0]), HEAD_DIM, 1) + r.zfix[p].astype(F32)
        r.att[p] = (live_col * num * lax.rsqrt(z * z + FLOOR2)).astype(BF)

    pair_loop(join, 4)
    o = out_columns(r)
    branch = None
    for p in range(0, PAIRS, 2):
        part = nt(
            jnp.concatenate([r.att[p], r.att[p + 1]], axis=1),
            jnp.concatenate([panel(r.gf, p, o), panel(r.gf, p + 1, o)], axis=1),
        )
        branch = part if branch is None else branch + part
    r.mid[...] = branch

    def norm_rows(rows, at, n):
        mid = r.mid[rows, :] + r.tok[rows, :].astype(F32)
        r.mid[rows, :] = mid
        xhat, inv = norm_stats(mid)
        r.xhat[rows, :] = xhat
        r.inv[rows, :] = jnp.broadcast_to(inv, (n, LANES))
        r.two[rows, :] = (xhat * r.vec[4:5, :] + r.vec[5:6, :]).astype(BF)

    rows_loop(T, 64, norm_rows)


def feed_columns(r):
    ff = (r.gf.shape[-1] - LANES) // 2
    return slice(LANES + ff, LANES + 2 * ff), slice(LANES, LANES + ff)


def out_columns(r):
    return slice(0, LANES)


def cotangents(T, base, r):
    _, d = feed_columns(r)

    def part(p):
        r.h2[p] = nn(r.cot[...], panel(r.gf, p, d))

    pair_loop(part)


def feed(T, base, r):
    low = low_lanes(T)
    live_col, carry_col = carry_factor(T, base, r)
    r.acc1[...] = jnp.zeros_like(r.acc1)
    r.acc2[...] = jnp.zeros_like(r.acc2)
    u, d = feed_columns(r)
    o = out_columns(r)

    def part(p):
        up, down = panel(r.gf, p, u), panel(r.gf, p, d)
        r.h1[...] = nn(r.two[...], up)

        def body(rows, at, n):
            value, slope = gelu_parts(r.h1[rows, :])
            r.act[p, rows, :] = value.astype(BF)
            r.gh[p, rows, :] = (r.h2[p, rows, :] * slope).astype(BF)

        rows_loop(T, 64, body)
        r.acc1[...] += nt(r.act[p], down)
        r.acc2[...] += nt(r.gh[p], up)

    pair_loop(part)
    r.sums[...] = jnp.zeros_like(r.sums)

    def finish(rows, at, n):
        r.result[rows, :] = (r.mid[rows, :] + r.acc1[rows, :]).astype(BF)
        xhat, gn = r.xhat[rows, :], r.acc2[rows, :]
        r.sums[0:8, :] += by_eight(gn * xhat)
        r.sums[8:16, :] += by_eight(gn)
        back = norm_back(gn, xhat, r.inv[rows, 0:1], r.vec[4:5, :])
        grad = r.cot[rows, :].astype(F32) + back
        r.gmid[rows, :] = grad
        r.gb[rows, :] = grad.astype(BF)

    rows_loop(T, 64, finish)
    r.fsum[0:1, :] = jnp.sum(r.sums[0:8, :], axis=0, keepdims=True)
    r.fsum[1:2, :] = jnp.sum(r.sums[8:16, :], axis=0, keepdims=True)
    ones1 = head_ones(2 * LANES, LANES, HEAD_DIM, HEAD_DIM)
    row_ones = jnp.ones((16, 2 * LANES), BF)
    first_half = iota((T, LANES), 1) % HEAD_DIM < HEAD_DIM // 2

    def back(p):
        g = nn(r.gb[...], panel(r.gf, p, o)).astype(BF).astype(F32) * live_col
        total = [r.joined[2 * p], r.joined[2 * p + 1]]
        num = jnp.where(low, total[0], total[1])
        z = pltpu.roll(jnp.where(low, total[1], total[0]), HEAD_DIM, 1) + r.zfix[p].astype(F32)
        rden = lax.rsqrt(z * z + FLOOR2)
        dn = (g * rden).astype(BF).astype(F32)
        dz = nn(halves(dn * num), ones1) * (z * rden * rden)
        dz = pltpu.roll(dz * (-2.0 / HEAD_DIM), HEAD_DIM, 1)
        rough = dz.astype(BF).astype(F32)
        dz = jnp.where(first_half, rough, dz - rough)
        factor = jnp.exp(r.rb[p]) * carry_col
        for a in range(2):
            h = 2 * p + a
            joint = (jnp.where(low, dn, dz) if a == 0 else jnp.where(low, dz, dn)).astype(BF)
            r.dn[h] = joint
            r.dr[pl.ds(h, 1), :] = nt(row_ones, halves(joint.astype(F32) * total[a]))[0:1]
            adj = tn(joint, (r.qf[h].astype(F32) * widen(factor, a)).astype(BF))
            at, half = (1 - a) * HEAD_DIM, HEAD_DIM // 2
            normal = 0.5 * (adj[at : at + 1] + adj[at + half : at + half + 1])
            put_state(r.adj, h, adj[a * HEAD_DIM : (a + 1) * HEAD_DIM], normal, r.total[pl.ds(h, 1), :])

    pair_loop(back, 4)


def up_grads(T, base, r):
    up, _ = feed_columns(r)
    pair_loop(lambda p: put_panel(r.ggf, p, up, tn(r.two[...], r.gh[p])))


def down_grads(T, base, r):
    _, down = feed_columns(r)

    def part(p):
        put_panel(r.ggf, p, down, tn(r.cot[...], r.act[p]))
        put_panel(r.ggf, p, out_columns(r), tn(r.gb[...], r.att[p]))

    pair_loop(part)


def put_panel(ref, p, cols, x):
    shape = ref.shape[1:4] + (x.shape[1],)
    ref[p, :, :, :, cols] = x.astype(BF).reshape(shape)


def back(T, base, r, tokens_all, near_hook=None, between=lambda: None, far_hook=None, order=None):
    D = r.tok.shape[1]
    low = low_lanes(T)
    _, carry_col = carry_factor(T, base, r)
    end_live = end_factor(T, base, r)
    ones1 = head_ones(2 * LANES, LANES, HEAD_DIM, HEAD_DIM)
    row_ones = jnp.ones((16, 2 * LANES), BF)
    r.acc1[...] = jnp.zeros_like(r.acc1)

    def feature_back(p, u, da):
        ds = nt(da, r.tabn[p]) * TABLE_SCALE
        uf = u.astype(F32)
        inv = lax.rsqrt(nn(halves(uf * uf), ones1) + 1e-6)
        uh = uf * inv
        return (inv * (ds - uh * nn(halves(uh * ds), ones1))).astype(BF)

    def angles(rows, source, feat, h):
        x, f = source[rows, :], feat[h, rows, :].astype(F32)
        return x[:, :FEATS] * f[:, FEATS:] - x[:, FEATS:] * f[:, :FEATS]

    def near(p):
        v = r.v[p]
        factor = jnp.exp(r.rb[p]) * carry_col
        for a in range(2):
            h = 2 * p + a
            r.s[...] = nt(r.dn[h], head_values(v, a, low))
            run_row = r.run[pl.ds(h, 1), :]

            def body(rows, at, n):
                gap = jnp.minimum(widen(r.rb[p, rows, :], a) - run_row, r.mask[rows, :])
                r.ds[rows, :] = (r.s[rows, :] * jnp.exp(gap)).astype(BF)

            rows_loop(T, 64, body)
            before = halves(state_of(r.inn, p, a), 0)
            r.s1[...] = nn(r.ds[...], r.kf[h]) + widen(factor, a) * nn(twice(r.dn[h]), before)
            r.s2[...] = tn(r.ds[...], r.qf[h])
            r.ghv[h] = tn(r.w[h], r.dn[h])

            def turn(rows, at, n):
                r.da[p, rows, a * FEATS : (a + 1) * FEATS] = angles(rows, r.s1, r.qf, h).astype(BF)
                r.da[p, rows, (2 + a) * FEATS : (3 + a) * FEATS] = angles(rows, r.s2, r.kf, h).astype(BF)

            rows_loop(T, 64, turn)
        grad = feature_back(p, r.q[p], r.da[p, :, : 2 * FEATS])
        r.acc1[...] += nt(grad, panel(r.ga, p, QUERY))
        put_panel(r.gga, p, slice(2 * LANES, 3 * LANES), tn(r.normed[...], grad))

    def far(p):
        v = r.v[p]
        decay_end = jnp.exp(r.rb[p, T - 1 : T, :] - r.rb[p]) * end_live
        grad_v = []
        for a in range(2):
            h = 2 * p + a
            end, hv = state_of(r.aend, p, a), head_values(v, a, low)
            late = widen(decay_end, a) * nt(twice(r.kf[h]), halves(end))
            r.s2[...] = widen(decay_end, a) * nn(twice(hv), halves(end, 0))
            grad_hv = r.ghv[h] + late
            grad_v.append(grad_hv)

            def turn(rows, at, n):
                lanes = slice((2 + a) * FEATS, (3 + a) * FEATS)
                r.da[p, rows, lanes] = (r.da[p, rows, lanes].astype(F32) + angles(rows, r.s2, r.kf, h)).astype(BF)

            rows_loop(T, 64, turn)
            hvf = hv.astype(F32)
            k_side = nt(row_ones, halves(hvf * grad_hv))
            r.drun[pl.ds(h, 1), :] = r.dr[pl.ds(h, 1), :] - k_side[0:1]
            owed = jnp.sum(end * state_of(r.inn, p, a), axis=0, keepdims=True)
            owed = r.total[pl.ds(h, 1), 0:1] * jnp.sum(owed, axis=1, keepdims=True)
            owed = owed + jnp.sum(jnp.sum(hvf * late, axis=0, keepdims=True), axis=1, keepdims=True)
            r.owed[pl.ds(h, 1), :] = jnp.broadcast_to(owed, (1, LANES))
        grad_v = jnp.where(low, grad_v[0], grad_v[1]).astype(BF)
        grads = jnp.concatenate([feature_back(p, r.k[p], r.da[p, :, 2 * FEATS :]), grad_v], axis=1)
        r.acc1[...] += nt(grads, panel(r.ga, p, slice(0, 2 * LANES)))
        put_panel(r.gga, p, slice(0, 2 * LANES), tn(r.normed[...], grads))

    run_pairs(near, near_hook, order)
    between()
    run_pairs(far, far_hook, order)
    pos = base + iota((8, T), 1)
    _, reset_row, live_row, _, filled = marks(pos, base, r.lengths)
    lane = iota((8, T), 1)
    run = r.drun[...]
    shift = 1
    while shift < T:
        run = run + jnp.where(lane < T - shift, pltpu.roll(run, T - shift, 1), 0.0)
        shift *= 2
    grad_decay = run + r.owed[:, 0:1]
    logits = r.logits[...]
    e = jnp.exp(-jnp.abs(logits))
    small, large = e / (1.0 + e), 1.0 / (1.0 + e)
    gate = jnp.where(logits >= 0.0, large, small)
    rest = jnp.where(logits >= 0.0, small, large)
    penalty = GATE_PEN * tokens_all / HEADS / jnp.broadcast_to(filled, (8, T)).astype(F32)
    grad_logits = grad_decay * live_row * (1.0 - reset_row) * rest + penalty * live_row * gate * rest
    both = halves(grad_logits, 0)
    r.acc1[...] += tn(both, r.gate[...].astype(BF))
    gate_rows = nn(both, r.normed[...])
    gate_rows = gate_rows[0:8] + gate_rows[8:16]
    bias = jnp.broadcast_to(jnp.sum(grad_logits, axis=1, keepdims=True), (8, D))
    r.sums[...] = jnp.zeros_like(r.sums)

    def finish(rows, at, n):
        xhat, inv = norm_stats(r.tok[rows, :].astype(F32))
        gn = r.acc1[rows, :]
        r.sums[0:8, :] += by_eight(gn * xhat)
        r.sums[8:16, :] += by_eight(gn)
        r.gtok[rows, :] = r.gmid[rows, :] + norm_back(gn, xhat, inv, r.vec[2:3, :])

    rows_loop(T, 64, finish)
    norm_gain = jnp.sum(r.sums[0:8, :], axis=0, keepdims=True)
    norm_shift = jnp.sum(r.sums[8:16, :], axis=0, keepdims=True)
    lines = [norm_gain, norm_shift, r.fsum[0:2, :]]
    for p in range(PAIRS):
        rows = jnp.concatenate([gate_rows[2 * p : 2 * p + 2]] + lines + [bias[2 * p : 2 * p + 2]], axis=0)
        for g in range(D // LANES):
            r.lines[p, g] = rows[:, g * LANES : (g + 1) * LANES]


class Refs:
    def __init__(self, **refs):
        self.__dict__.update(refs)


def buffers(T, D, att, rest, ff, seq):
    z = (PAIRS, seq // 2, 2, D // seq)
    pair = (PAIRS, T, LANES)
    return {
        "ga": (z + (att,), BF), "gf": (z + (rest,), BF), "gga": (z + (att,), BF), "small": ((PAIRS, 16, D), F32), "ggf": (z + (rest,), BF),
        "gate": ((16, D), F32), "bias": ((8, D), F32), "vec": ((8, D), F32), "normed": ((T, D), BF),
        "logits": ((8, T), F32), "run": ((8, T), F32), "total": ((8, LANES), F32), "mask": ((T, T), F32),
        "s1": ((T, 2 * FEATS), F32), "s2": ((T, 2 * FEATS), F32), "s": ((T, T), F32),
        "tab": ((PAIRS, 2 * LANES, 2 * FEATS), BF), "tabn": ((PAIRS, LANES, 2 * FEATS), BF),
        "q": (pair, BF), "k": (pair, BF), "v": (pair, BF), "rb": (pair, F32),
        "qf": ((HEADS, T, 2 * FEATS), BF), "kf": ((HEADS, T, 2 * FEATS), BF),
        "out": (STATES, F32), "inn": (STATES, F32), "adj": (STATES, F32), "aend": (STATES, F32),
        "w": ((HEADS, T, T), BF), "own": ((HEADS, T, LANES), F32), "joined": ((HEADS, T, LANES), F32),
        "att": (pair, BF), "zfix": (pair, BF), "mid": ((T, D), F32), "xhat": ((T, D), F32), "inv": ((T, LANES), F32), "two": ((T, D), BF),
        "acc1": ((T, D), F32), "acc2": ((T, D), F32), "h1": ((T, ff), F32), "h2": ((PAIRS, T, ff), F32),
        "act": ((PAIRS, T, ff), BF), "gh": ((PAIRS, T, ff), BF), "sums": ((16, D), F32), "fsum": ((8, D), F32),
        "result": ((T, D), BF), "gmid": ((T, D), F32), "gb": ((T, D), BF), "dr": ((8, T), F32),
        "dn": ((HEADS, T, LANES), BF), "ds": ((T, T), BF), "da": ((PAIRS, T, 4 * FEATS), BF), "ghv": ((HEADS, T, LANES), F32),
        "lines": ((PAIRS, D // LANES, 8, LANES), F32),
        "drun": ((8, T), F32), "owed": ((8, LANES), F32), "gtok": ((T, D), F32),
    }


FRONT = (
    ("ga", "small"),
    ("gate", "vec", "normed", "logits", "run", "total", "mask", "tabn", "q", "k", "v", "rb", "qf", "kf", "out", "w", "own", "zfix"),
    ("bias", "s1", "s2", "s", "tab", "xhat"),
)
MIDDLE = (
    ("gf", "vec", "rb", "qf", "own", "zfix", "inn", "total"),
    ("ggf", "result", "gmid", "fsum", "dr", "dn", "adj"),
    ("joined", "att", "mid", "xhat", "inv", "two", "acc1", "acc2", "h1", "h2", "act", "gh", "sums", "gb"),
)
BACK = (
    ("ga", "gate", "vec", "normed", "logits", "run", "total", "mask", "tabn", "q", "k", "v", "rb", "qf", "kf",
     "w", "inn", "aend", "gmid", "fsum", "dr", "dn"),
    ("gga", "gtok", "lines"),
    ("s", "s1", "s2", "ds", "da", "ghv", "drun", "owed", "acc1", "sums"),
)
SHARED = {"joined": "own", "h1": "s", "gmid": "mid", "ds": "gb", "adj": "out", "da": "act", "ghv": "own"}


def front(T, base, r):
    tables(T, base, r)
    standardise(T, base, r)
    first_norm(T, base, r)
    keys(T, base, r)
    states(T, base, r)
    queries(T, base, r)


def middle(T, base, r):
    cotangents(T, base, r)
    attend(T, base, r)
    feed(T, base, r)
    up_grads(T, base, r)
    down_grads(T, base, r)


def here(T):
    return (lax.axis_index("seq") * lax.axis_size("head") + lax.axis_index("head")) * T


def stage(which, names, specs, outer, args, state):
    reads, writes, scratch = names
    shape = lambda n: jax.ShapeDtypeStruct(*specs[n])
    vmem, smem = pl.BlockSpec(memory_space=pltpu.VMEM), pl.BlockSpec(memory_space=pltpu.SMEM)

    def kernel(*refs):
        base_ref, lengths, seed, tok, cot = refs[:5]
        rest = dict(zip(reads + writes + scratch, refs[5:]))
        which(base_ref[0], Refs(lengths=lengths, seed=seed, tok=tok, cot=cot, **rest))

    out = pl.pallas_call(
        kernel,
        out_shape=[shape(n) for n in writes],
        in_specs=[smem] * 3 + [vmem] * (2 + len(reads)),
        out_specs=[vmem] * len(writes),
        scratch_shapes=[pltpu.VMEM(*specs[n]) for n in scratch],
        compiler_params=pltpu.CompilerParams(vmem_limit_bytes=VMEM_BYTES),
        name=outer,
    )(*args, *[state[n] for n in reads])
    state.update(zip(writes, out))


def scan_states(out, reverse):
    seq, head = lax.axis_size("seq"), lax.axis_size("head")
    count = seq * head
    me = lax.axis_index("seq") * head + lax.axis_index("head")
    state = (out[:, DECAY : DECAY + 1, 0:1], out[:, :DECAY])
    step = 1
    order = lambda pairs: [(b, a) for a, b in pairs] if reverse else pairs
    axes = ("seq", "head")
    while step < count:
        moved = jax.tree.map(lambda x: lax.ppermute(x, axes, order([(i, i + step) for i in range(count - step)])), state)
        has = (me < count - step) if reverse else (me >= step)
        f, m = state
        state = (jnp.where(has, f * moved[0], f), m + jnp.where(has, f * moved[1], 0.0))
        step *= 2
    moved = lax.ppermute(state[1], axes, order([(i, i + 1) for i in range(count - 1)]))
    return jnp.concatenate([moved, jnp.zeros((HEADS, STATE_ROWS - DECAY, 2 * FEATS), F32)], axis=1)


def remote(src, dst, send, recv, to):
    return pltpu.make_async_remote_copy(
        src_ref=src, dst_ref=dst, send_sem=send, recv_sem=recv, device_id=to, device_id_type=MESH
    )


class Place:
    def __init__(self):
        self.seq, self.head = lax.axis_size("seq"), lax.axis_size("head")
        s, h = lax.axis_index("seq"), lax.axis_index("head")
        self.z, self.y, self.x, self.c = s // 2, s % 2, h // 2, h % 2
        self.depth = self.seq // 2
        self.count = self.seq * self.head
        self.me = s * self.head + h

    def device(self, z=None, y=None, x=None, c=None):
        pick = lambda given, own: own if given is None else given
        z, y, x, c = pick(z, self.z), pick(y, self.y), pick(x, self.x), pick(c, self.c)
        return (z * 2 + y, x * 2 + c)

    def number(self, i):
        return (i // self.head, i % self.head)

    def around(self, k):
        return (self.z + k) % self.depth

class Semaphores:
    def __init__(self, send, recv):
        self.send, self.recv, self.used = send, recv, 0

    def copy(self, src, dst, to):
        i = self.used
        self.used += 1
        return remote(src, dst, self.send.at[i], self.recv.at[i], to)


GATHER_COPIES = 2 * (3 + 1 + 2 + 2)
SCATTER_COPIES = 2 + 2 * (1 + 1 + 3)


def gather_stages(place, g, lanes, sems):
    half = g.shape[3] // 2
    z, y, x, c = place.z, place.y, place.x, place.c
    pair = x * 2 + c
    stages = [[], [], [], []]
    for part in range(2):
        rows = pl.ds(part * half, half)
        same = lambda ref, to: sems.copy(ref, ref, to)
        for k in range(1, place.depth):
            stages[0].append(same(g.at[pair, z, y, rows, lanes], place.device(z=place.around(k))))
        to_y, to_x = place.device(y=1 - y), place.device(x=1 - x)
        if part == 0:
            stages[1].append(same(g.at[pair, :, y, rows, lanes], to_y))
            stages[2].append(same(g.at[pair, :, :, rows, lanes], to_x))
        else:
            stages[1].append(same(g.at[pair, :, y, rows, lanes], to_x))
            for other in range(2):
                stages[2].append(same(g.at[other * 2 + c, :, y, rows, lanes], to_y))
        for other in range(2):
            stages[3].append(same(g.at[other * 2 + c, :, :, rows, lanes], place.device(c=1 - c)))
    return stages


def begin(stage):
    for copy in stage:
        copy.start()


def arrived(stage):
    for copy in stage:
        copy.wait_recv()


def sent(*stages):
    for stage in stages:
        for copy in stage:
            copy.wait_send()


class Gather:
    def __init__(self, place, ga, gf, gs, sems):
        ff = (gf.shape[-1] - LANES) // 2
        lanes = lambda first, count: pl.ds(first, count)
        self.chunks = [
            gather_stages(place, ref, part, sems)
            for ref, part in (
                (ga, lanes(0, LANES)),
                (ga, lanes(LANES, 2 * LANES)),
                (gf, lanes(0, LANES + ff)),
                (gf, lanes(LANES + ff, ff)),
            )
        ]

        z, y, x, c, pair = place.z, place.y, place.x, place.c, place.x * 2 + place.c
        first, same = self.chunks[0], lambda ref, **to: sems.copy(ref, ref, place.device(**to))
        first[0] += [same(gs.at[pair, z, y], z=place.around(k)) for k in range(1, place.depth)]
        first[1].append(same(gs.at[pair, :, y], y=1 - y))
        first[2].append(same(gs.at[pair], x=1 - x))
        first[3] += [same(gs.at[other * 2 + c], c=1 - c) for other in range(2)]

    def begin(self, chunk):
        begin(self.chunks[chunk][0])

    def step(self, chunk, stage):
        arrived(self.chunks[chunk][stage])
        if stage < 3:
            begin(self.chunks[chunk][stage + 1])

    def finish(self):
        for chunk in self.chunks:
            sent(*chunk)


def add_blocks(to, others, count, where):
    def one(i, carry):
        at = where(i)
        total = to[at].astype(F32)
        for ref, index in others:
            total = total + ref[index(i)].astype(F32)
        to[at] = total.astype(to.dtype)
        return carry

    lax.fori_loop(0, count, one, 0)


class Scatter:
    def __init__(self, place, gg, lanes, out, buf, sems):
        self.place, self.gg, self.lanes, self.out = place, gg, lanes, out
        self.r1, self.r2a, self.r2b, self.r3a, self.r3b, self.r4a, self.r4b = buf
        z, y, x, c, n = place.z, place.y, place.x, place.c, place.depth
        self.half = half = gg.shape[3] // 2
        first, last = pl.ds(0, half), pl.ds(half, half)
        other, to_y, to_x = place.device(c=1 - c), place.device(y=1 - y), place.device(x=1 - x)
        self.stages = [
            [sems.copy(gg.at[i * 2 + 1 - c, :, :, :, lanes], self.r1.at[i], other) for i in range(2)],
            [
                sems.copy(self.r1.at[1 - x, :, :, first], self.r2a, to_x),
                sems.copy(self.r1.at[:, :, 1 - y, last], self.r2b, to_y),
            ],
            [sems.copy(self.r2a.at[:, 1 - y], self.r3a, to_y), sems.copy(self.r2b.at[1 - x], self.r3b, to_x)],
            [
                sems.copy(ref.at[place.around(k)], slots.at[k - 1], place.device(z=place.around(k)))
                for ref, slots in ((self.r3a, self.r4a), (self.r3b, self.r4b))
                for k in range(1, n)
            ],
        ]

    def start(self):
        begin(self.stages[0])

    def step(self, i):
        place, n, half = self.place, self.place.depth, self.half
        y, x, c = place.y, place.x, place.c
        first, last = slice(0, half), slice(half, 2 * half)
        lanes = self.lanes
        arrived(self.stages[i])
        if i == 0:
            block = lambda j: (j // (2 * n), (j // 2) % n, j % 2)
            add_blocks(self.r1, [(self.gg, lambda j: ((j // (2 * n)) * 2 + c, (j // 2) % n, j % 2, slice(None), lanes))], 4 * n, block)
        elif i == 1:
            add_blocks(self.r2a, [(self.r1, lambda j: (x, j // 2, j % 2, first))], 2 * n, lambda j: (j // 2, j % 2))
            add_blocks(self.r2b, [(self.r1, lambda j: (j // n, j % n, y, last))], 2 * n, lambda j: (j // n, j % n))
        elif i == 2:
            add_blocks(self.r3a, [(self.r2a, lambda j: (j, y))], n, lambda j: (j,))
            add_blocks(self.r3b, [(self.r2b, lambda j: (x, j))], n, lambda j: (j,))
        else:
            for ref, slots, rows in ((self.r3a, self.r4a, first), (self.r3b, self.r4b, last)):
                total = ref[place.z].astype(F32)
                for k in range(n - 1):
                    total = total + slots[k].astype(F32)
                self.out[rows, lanes] = total
        if i < 3:
            begin(self.stages[i + 1])

    def finish(self):
        sent(*self.stages)


def scatter_buffers(seq, rows, cols):
    n, half = seq // 2, rows // 2
    return [
        pltpu.VMEM(shape + (cols,), BF)
        for shape in ((2, n, 2, rows), (n, 2, half), (2, n, half), (n, half), (n, half), (n - 1, half), (n - 1, half))
    ]


class Scan:
    def __init__(self, place, reverse, out, inn, box, planes, send, recv):
        self.place, self.reverse = place, reverse
        self.out, self.inn, self.planes = out, inn, planes
        self.pair, self.chip, self.box, self.back = box
        self.chips = HEADS // 2
        self.mine = place.y * 2 + place.x
        self.half, self.rest = place.c * self.chips, (1 - place.c) * self.chips
        self.sems = Semaphores(send, recv)
        other = place.device(c=1 - place.c)
        at = lambda ref, first: ref.at[pl.ds(first, self.chips)]
        near = [lax.rem(self.mine + k, self.chips) for k in range(1, self.chips)]
        chip = lambda m: place.device(y=m // 2, x=m % 2)
        total = planes.at[place.z]
        copy = self.sems.copy
        self.ways = [
            [copy(at(out, self.rest), self.pair, other)],
            [copy(self.chip.at[m], self.box.at[self.mine], chip(m)) for m in near],
            [copy(total, total, place.device(z=place.around(k))) for k in range(1, place.depth)],
            [copy(self.box.at[m], self.back.at[self.mine], chip(m)) for m in near],
            [copy(self.pair, at(inn, self.half), other)],
        ]

    def start(self):
        begin(self.ways[0])

    def chain(self, ref, count):
        kept = iota((STATE_ROWS, 2 * FEATS), 0) != DECAY
        state = jnp.where(kept, 0.0, 1.0)
        for i in range(count):
            d = count - 1 - i if self.reverse else i
            term = ref[d]
            ref[d] = state
            state = state * term[DECAY : DECAY + 1, :] + jnp.where(kept, term, 0.0)
        return state

    def earlier_is_mine(self):
        return (self.place.c == 0) != self.reverse

    def cores(self):
        arrived(self.ways[0])
        kept = iota((STATE_ROWS, 2 * FEATS), 0) != DECAY
        first = jnp.broadcast_to(self.earlier_is_mine(), kept.shape)
        for i in range(self.chips):
            mine, its = self.out[self.half + i], self.pair[i]
            early, late = jnp.where(first, mine, its), jnp.where(first, its, mine)
            self.chip[i] = early * late[DECAY : DECAY + 1, :] + jnp.where(kept, late, 0.0)
        begin(self.ways[1])
        self.box[self.mine] = self.chip[self.mine]

    def plane(self):
        arrived(self.ways[1])
        self.planes[self.place.z] = self.chain(self.box, self.chips)
        begin(self.ways[2])

    def line(self):
        arrived(self.ways[2])
        sent(self.ways[2])
        self.chain(self.planes, self.place.depth)
        before = self.planes[self.place.z]
        for m in range(self.chips):
            own = self.box[m]
            self.box[m] = own + own[DECAY : DECAY + 1, :] * before
        begin(self.ways[3])
        self.back[self.mine] = self.box[self.mine]

    def share(self):
        arrived(self.ways[3])
        sent(self.ways[0])
        first = jnp.broadcast_to(self.earlier_is_mine(), (STATE_ROWS, 2 * FEATS))
        for i in range(self.chips):
            mine, its, before = self.out[self.half + i], self.pair[i], self.back[i]
            early = jnp.where(first, mine, its)
            late = before * early[DECAY : DECAY + 1, :] + early
            self.inn[self.half + i] = jnp.where(first, before, late)
            self.pair[i] = jnp.where(first, late, before)
        begin(self.ways[4])

    def receive(self):
        arrived(self.ways[4])

    def finish(self):
        sent(self.ways[1], self.ways[3], self.ways[4])


class Lines:
    def __init__(self, place, lines, out, buf, sems):
        self.place, self.lines, self.out = place, lines, out
        self.l1, self.l2, self.l3, self.l4 = buf
        z, y, x, c, copy = place.z, place.y, place.x, place.c, sems.copy
        around = range(1, place.depth)
        self.stages = [
            [copy(lines.at[i * 2 + 1 - c], self.l1.at[i], place.device(c=1 - c)) for i in range(2)],
            [copy(self.l1.at[1 - x], self.l2, place.device(x=1 - x))],
            [copy(self.l2, self.l3, place.device(y=1 - y))],
            [copy(self.l3.at[place.around(k)], self.l4.at[k - 1], place.device(z=place.around(k))) for k in around],
        ]

    def start(self):
        begin(self.stages[0])

    def step(self, i):
        place = self.place
        arrived(self.stages[i])
        if i == 0:
            for j in range(2):
                self.l1[j] += self.lines[j * 2 + place.c]
        elif i == 1:
            self.l2[...] += self.l1[place.x]
        elif i == 2:
            self.l3[...] += self.l2[...]
        else:
            total = self.l3[place.z]
            for k in range(place.depth - 1):
                total = total + self.l4[k]
            self.out[...] = total
        if i < 3:
            begin(self.stages[i + 1])

    def finish(self):
        sent(*self.stages)


LINES_COPIES = 2 + 1 + 1 + 3


def greet(place):
    x, y = 1 - place.x, 1 - place.y
    near = [place.device(c=1 - place.c), place.device(x=x), place.device(y=y), place.device(x=x, y=y)]
    near += [place.device(z=place.around(k)) for k in range(1, place.depth)]
    barrier = pltpu.get_barrier_semaphore()
    for device in near:
        pl.semaphore_signal(barrier, inc=1, device_id=device, device_id_type=MESH)
    return lambda: pl.semaphore_wait(barrier, len(near))


def pack(place, r, key, value, query, gate, vectors, bias, up, out, down):
    at = (place.x * 2 + place.c, place.z, place.y)
    rows, ff = key.shape[0], up.shape[1]
    r.gf[at + (slice(None), slice(LANES + ff, None))] = up[...]
    r.gf[at + (slice(None), slice(0, LANES))] = out[...]
    r.gf[at + (slice(None), slice(LANES, LANES + ff))] = down[...]
    r.ga[at + (slice(None), KEY)] = key[...]
    r.ga[at + (slice(None), VALUE)] = value[...]
    r.ga[at + (slice(None), QUERY)] = query[...]
    lines = [gate[...].astype(F32)] + [v[...].astype(F32) for v in vectors]
    for j in range(2):
        left = jnp.full((1, rows), bias[j], F32)
        for _ in range(3):
            piece = left.astype(BF).astype(F32)
            lines.append(piece)
            left = left - piece
    lines = jnp.concatenate(lines + [jnp.zeros((4, rows), F32)], axis=0).astype(BF)
    wide = jnp.where(iota((rows, LANES), 0) == iota((rows, LANES), 1), 1.0, 0.0).astype(BF)
    r.gs[at] = nn(lines, wide).astype(BF)


def spread_small(r):
    for p in range(PAIRS):
        for z in range(r.gs.shape[1]):
            even, odd = r.gs[p, z, 0].astype(F32), r.gs[p, z, 1].astype(F32)
            tile = jnp.where(low_lanes(16), even, pltpu.roll(odd, HEAD_DIM, 1))
            r.small[p, :, z * LANES : (z + 1) * LANES] = tile


def unpack_kernel(half, grad_a, grad_f, lines, result, gtok, *outs):
    out = dict(zip(OUTPUTS, outs))
    rows = grad_a.shape[0]
    ff = (grad_f.shape[1] - LANES) // 2
    out["result"][...] = result[...]
    out["tokens"][...] = gtok[...]
    for i, name in enumerate(("key", "value", "query")):
        out[name][...] = grad_a[:, i * LANES : (i + 1) * LANES]
    out["up"][...] = grad_f[:, LANES + ff :]
    out["out"][...] = grad_f[:, :LANES]
    out["down"][...] = grad_f[:, LANES : LANES + ff]
    own = jnp.where(half == 0, lines[:, :rows], lines[:, rows : 2 * rows])
    for i, name in enumerate(("norm_gain", "norm_shift", "ffn_gain", "ffn_shift")):
        out[name][...] = own[2 + i : 3 + i, :]
    out["gate"][...] = own[0:2, :]
    out["bias"][...] = jnp.where(iota((1, LANES), 1) == 0, lines[6:7, :], lines[7:8, :])[:, 0:2]


OUTPUTS = ("result", "tokens", "norm_gain", "norm_shift", "query", "key", "value", "gate", "bias", "out", "ffn_gain",
           "ffn_shift", "up", "down")


def layer_kernel(names, tokens_all, T, lengths, seed, bias, tok_in, cot_in, key, value, query, gate, *given):
    vectors, (up, out, down), given = given[0:4], given[4:7], given[7:]
    (result_out, gtok_out, grad_a, grad_f, grad_lines), scratch = given[:5], given[5:]
    (tok, cot, result, gtok, moves), scratch = scratch[:5], scratch[5:]
    moves = [pltpu.make_async_copy(src, dst, moves.at[i]) for i, (src, dst) in enumerate(
        ((tok_in, tok), (cot_in, cot), (result, result_out), (gtok, gtok_out)))]
    moves[0].start()
    moves[1].start()
    place = Place()
    base = place.me * T
    arrays = dict(zip(names, scratch))
    arrays.update({name: arrays[other] for name, other in SHARED.items()})
    scratch = scratch[len(names) :]
    r = Refs(lengths=lengths, seed=seed, tok=tok, cot=cot, result=result, gtok=gtok, xhat=gtok, **arrays)
    sums, scratch = [scratch[7 * i : 7 * i + 7] for i in range(4)], scratch[28:]
    boxes, planes, line_box, sems = (scratch[0:4], scratch[4:8]), scratch[8:10], scratch[10:14], scratch[14:]
    meet = greet(place)
    pack(place, r, key, value, query, gate, vectors, bias, up, out, down)
    gather = Gather(place, r.ga, r.gf, r.gs, Semaphores(sems[0], sems[1]))
    forth = Scan(place, False, r.out, r.inn, boxes[0], planes[0], sems[2], sems[3])
    home = Scan(place, True, r.adj, r.aend, boxes[1], planes[1], sems[4], sems[5])
    later = Semaphores(sems[6], sems[7])
    up, down = feed_columns(r)
    sum_u = Scatter(place, r.ggf, up, grad_f, sums[0], later)
    sum_d = Scatter(place, r.ggf, slice(0, down.stop), grad_f, sums[1], later)
    sum_q = Scatter(place, r.gga, slice(2 * LANES, 3 * LANES), grad_a, sums[2], later)
    sum_k = Scatter(place, r.gga, slice(0, 2 * LANES), grad_a, sums[3], later)
    lines = Lines(place, r.lines, grad_lines, line_box, later)
    meet()

    g = gather.step
    others_first = lambda i: (i % 2) * 2 + jnp.where(i < 2, 1 - place.c, place.c)
    gather.begin(0)
    tables(T, base, r)
    g(0, 0)
    gather.begin(1)
    g(0, 1)
    g(1, 0)
    gather.begin(2)
    g(0, 2)
    g(1, 1)
    moves[0].wait()
    standardise(T, base, r)
    g(0, 3)
    spread_small(r)
    first_norm(T, base, r)
    g(2, 0)
    gather.begin(3)
    keys(T, base, r, {0: [(g, 1, 2)], 3: [(g, 2, 1), (g, 1, 3)]})
    states(T, base, r)
    forth.start()
    queries(T, base, r, {0: [(forth.cores,)], 1: [(g, 3, 0)], 2: [(forth.plane,)], 3: [(g, 2, 2), (g, 3, 1)]})
    g(2, 3)
    moves[1].wait()
    cotangents(T, base, r)
    forth.line()
    g(3, 2)
    forth.share()
    g(3, 3)
    forth.receive()
    forth.finish()
    attend(T, base, r)
    feed(T, base, r)
    home.start()
    moves[2].start()
    up_grads(T, base, r)
    sum_u.start()
    home.cores()
    down_grads(T, base, r)
    sum_d.start()
    near = {0: [(home.plane,), (sum_u.step, 0)], 2: [(home.line,)],
            3: [(sum_u.step, 1), (sum_q.start,), (home.share,), (sum_d.step, 0)]}
    far = {0: [(sum_q.step, 0)], 1: [(sum_k.start,), (sum_u.step, 2)], 2: [(sum_d.step, 1), (sum_q.step, 1)],
           3: [(sum_k.step, 0)]}
    back(T, base, r, tokens_all, near, home.receive, far, others_first)
    moves[3].start()
    lines.start()
    sum_q.step(2)
    sum_d.step(2)
    sum_k.step(1)
    lines.step(0)
    sum_u.step(3)
    lines.step(1)
    sum_k.step(2)
    lines.step(2)
    sum_q.step(3)
    sum_d.step(3)
    sum_k.step(3)
    lines.step(3)
    gather.finish()
    home.finish()
    moves[2].wait()
    moves[3].wait()
    for each in (sum_u, sum_d, sum_q, sum_k, lines):
        each.finish()


def layer_near(lengths, seed, tokens, cotangent, weights, specs, seq, head):
    T, D = tokens.shape
    count = seq * head
    rows, ff = D // seq, specs["act"][0][2]
    held = [n for n in dict.fromkeys(sum((sum(names, ()) for names in (FRONT, MIDDLE, BACK)), ())) if n not in SHARED]
    held = [n for n in held if n not in ("result", "gtok", "xhat")]
    dma = pltpu.SemaphoreType.DMA
    specs = dict(specs, gs=((PAIRS, seq // 2, 2, 16, LANES), BF))
    held.append("gs")
    wide = lambda kind: pltpu.VMEM((T, D), kind)
    scratch = [wide(BF), wide(BF), wide(BF), wide(F32), dma((4,))]
    scratch += [pltpu.VMEM(*specs[n]) for n in held]
    panels = 3 * LANES
    widths = (ff, LANES + ff, LANES, 2 * LANES)
    states = lambda count: pltpu.VMEM((count,) + STATES[1:], F32)
    for width in widths:
        scratch += scatter_buffers(seq, rows, width)
    scratch += [states(HEADS // 2)] * 8 + [states(seq // 2)] * 2
    tiles = lambda *lead: pltpu.VMEM(lead + (8, LANES), F32)
    scratch += [tiles(2, D // LANES), tiles(D // LANES), tiles(D // LANES), tiles(seq // 2 - 1)]
    scratch += [dma((5 * GATHER_COPIES,))] * 2 + [dma((16,))] * 4 + [dma((4 * SCATTER_COPIES + LINES_COPIES,))] * 2
    vmem, smem = pl.BlockSpec(memory_space=pltpu.VMEM), pl.BlockSpec(memory_space=pltpu.SMEM)
    shape, far = jax.ShapeDtypeStruct, pl.BlockSpec(memory_space=pl.ANY)
    result, gtok, grad_a, grad_f, lines = pl.pallas_call(
        functools.partial(layer_kernel, held, T * count, T),
        out_shape=[shape((T, D), BF), shape((T, D), F32), shape((rows, panels), F32), shape((rows, 2 * ff + LANES), F32),
                   shape((8, LANES), F32)],
        in_specs=[smem] * 3 + [far] * 2 + [vmem] * 11,
        out_specs=[far] * 2 + [vmem] * 3,
        scratch_shapes=scratch,
        compiler_params=pltpu.CompilerParams(collective_id=0, has_side_effects=True, vmem_limit_bytes=LAYER_BYTES),
        name="layer",
    )(lengths, seed, weights[0], tokens, cotangent, *weights[1:])
    line, square = shape((1, rows), F32), shape((rows, LANES), F32)
    shapes = (shape((T, D), BF), shape((T, D), F32), line, line, square, square, square, shape((2, rows), F32),
              shape((1, 2), F32), square, line, line, shape((rows, ff), F32), shape((rows, ff), F32))

    def unpacked(*refs):
        unpack_kernel(lax.axis_index("seq") % 2, *refs)

    outs = pl.pallas_call(
        unpacked,
        out_shape=shapes,
        in_specs=[vmem] * 5,
        out_specs=[vmem] * len(shapes),
        compiler_params=pltpu.CompilerParams(vmem_limit_bytes=VMEM_BYTES),
        name="unpack",
    )(grad_a, grad_f, lines, result, gtok)
    flat = ("norm_gain", "norm_shift", "bias", "ffn_gain", "ffn_shift")
    turned = ("gate", "out", "down")
    return tuple(x.reshape(-1) if n in flat else x.T if n in turned else x for n, x in zip(OUTPUTS, outs))


def bias_columns(gate_bias):
    hi = lax.reduce_precision(gate_bias, 8, 7)
    mid = lax.reduce_precision(gate_bias - hi, 8, 7)
    return jnp.stack([hi, mid, gate_bias - hi - mid], axis=1).astype(BF)


def gather_any(q, k, v, gate, vectors, bias, out, up, down, seq):
    D = q.shape[0] * seq

    def whole(w, rows, cols):
        w = lax.all_gather(w, rows, axis=0, tiled=True)
        return lax.all_gather(w, cols, axis=1, tiled=True)

    def panels(w):
        return w.reshape(D, PAIRS, w.shape[1] // PAIRS).transpose(1, 0, 2)

    q, k, v = (panels(whole(w, "seq", "head")) for w in (q, k, v))
    gates = panels(whole(gate, "seq", "head"))
    lines = [jnp.broadcast_to(lax.all_gather(w, "seq", tiled=True)[None, :, None], (PAIRS, D, 1)) for w in vectors]
    bias = bias_columns(lax.all_gather(bias, "head", tiled=True)).reshape(PAIRS, 1, 6)
    ga = jnp.concatenate([k, v, q], axis=2)
    rows = [gates.transpose(0, 2, 1)] + [w.transpose(0, 2, 1) for w in lines]
    rows += [jnp.broadcast_to(bias.transpose(0, 2, 1), (PAIRS, 6, D)), jnp.zeros((PAIRS, 4, D), BF)]
    small = jnp.concatenate(rows, axis=1).astype(F32)
    gf = [panels(whole(out, "head", "seq").T), panels(whole(down, "head", "seq").T), panels(whole(up, "seq", "head"))]
    gf = jnp.concatenate(gf, axis=2)
    shape = (PAIRS, seq // 2, 2, D // seq)
    return ga.reshape(shape + ga.shape[2:]), gf.reshape(shape + gf.shape[2:]), small


def scatter_any(gga, ggf, lines, ff):
    gga, ggf = (x.reshape(PAIRS, -1, x.shape[-1]).astype(F32) for x in (gga, ggf))

    def grid(x):
        x = x.transpose(1, 0, 2).reshape(x.shape[1], -1)
        x = lax.psum_scatter(x, "seq", scatter_dimension=0, tiled=True)
        return lax.psum_scatter(x, "head", scatter_dimension=1, tiled=True)

    block = lambda i: gga[:, :, i * LANES : (i + 1) * LANES]
    lines = lines.transpose(0, 2, 1, 3).reshape(PAIRS, 8, -1)
    gates = lines[:, 0:2].transpose(0, 2, 1)
    bias = lines[:, 6:8, 0].reshape(HEADS)
    bias = lax.psum_scatter(lax.psum(bias, "seq"), "head", scatter_dimension=0, tiled=True)
    lines = lax.psum_scatter(lax.psum(lines[0, 2:6].T, "head"), "seq", scatter_dimension=0, tiled=True)
    return (
        lines[:, 0], lines[:, 1], grid(block(2)), grid(block(0)), grid(block(1)), grid(gates), bias,
        grid(ggf[:, :, :LANES]).T, lines[:, 2], lines[:, 3], grid(ggf[:, :, LANES + ff :]),
        grid(ggf[:, :, LANES : LANES + ff]).T,
    )


def shards(
    tokens, lengths, feature_seed, norm_gain, norm_shift, query_weight, key_weight, value_weight, gate_weight, gate_bias,
    out_weight, ffn_gain, ffn_shift, up_weight, down_weight, cotangent,
):
    seq, head = lax.axis_size("seq"), lax.axis_size("head")
    T, D = tokens.shape
    rows = D // seq
    ff = up_weight.shape[1] * head // PAIRS
    vectors = (norm_gain, norm_shift, ffn_gain, ffn_shift)
    specs = buffers(T, D, ATT, LANES + 2 * ff, ff, seq)
    if (seq, head) == (HEADS, PAIRS):
        weights = (gate_bias, key_weight, value_weight, query_weight, gate_weight.T)
        weights += tuple(w.reshape(1, rows) for w in vectors) + (up_weight, out_weight.T, down_weight.T)
        return layer_near(lengths, feature_seed, tokens, cotangent, weights, specs, seq, head)
    ga, gf, small = gather_any(query_weight, key_weight, value_weight, gate_weight, vectors, gate_bias, out_weight, up_weight,
                        down_weight, seq)
    args = (here(T).astype(I32).reshape(1), lengths, feature_seed, tokens, cotangent)
    state = {"ga": ga, "gf": gf, "small": small}
    stage(lambda base, r: front(T, base, r), FRONT, specs, "front", args, state)
    state["inn"] = scan_states(state["out"], False)
    stage(lambda base, r: middle(T, base, r), MIDDLE, specs, "middle", args, state)
    state["aend"] = scan_states(state["adj"], True)
    stage(lambda base, r: back(T, base, r, T * seq * head), BACK, specs, "back", args, state)
    return (state["result"], state["gtok"]) + scatter_any(state["gga"], state["ggf"], state["lines"], ff)


def solution(mesh):
    both, rows, grid = P(("seq", "head"), None), P("seq"), P("seq", "head")
    return jax.shard_map(
        shards,
        mesh=mesh,
        in_specs=(both, P(), P(), rows, rows, grid, grid, grid, grid, P("head"), P("head", "seq"), rows, rows, grid,
                  P("head", "seq"), both),
        out_specs=(both, both, rows, rows, grid, grid, grid, grid, P("head"), P("head", "seq"), rows, rows, grid,
                   P("head", "seq")),
        check_vma=False,
    )
```

```python
import functools
import math

import jax
import jax.numpy as jnp
from jax import lax
from jax.experimental import pallas as pl
from jax.experimental.pallas import tpu as pltpu
from jax.sharding import PartitionSpec as P

BF, F32, I32 = jnp.bfloat16, jnp.float32, jnp.int32
MESH = pl.DeviceIdType.MESH
HEADS, HEAD_DIM, FEATS = 8, 64, 128
PAIRS = HEADS // 2
LANES = 128
EPS, FLOOR2, GATE_PEN = 1e-5, 0.0625, 0.5
TABLE_SCALE = 1.0 / math.sqrt(21845.0)
FEAT_SCALE = 1.0 / math.sqrt(FEATS)
INV_TWO_PI, TWO_PI = 1.0 / (2.0 * math.pi), 2.0 * math.pi
SIN = (0.9999996027571254, -0.16666553170295112, 0.008332405799301931, -0.00019808693226998236,
       2.6997700314773084e-06, -2.036409109746239e-08)
COS = (0.9999992193982472, -0.4999942543676011, 0.04165980908449851, -0.0013858873219640337,
       2.420384320646774e-05, -2.1976364824224383e-07)
ERFC = (0.254829592, -0.284496736, 1.421413741, -1.453152027, 1.061405429)
ATT = 3 * LANES
KEY, VALUE, QUERY = (slice(i * LANES, (i + 1) * LANES) for i in range(3))
NORMAL, DECAY, STATE_ROWS = HEAD_DIM, HEAD_DIM + 1, HEAD_DIM + 8
STATES = (HEADS, STATE_ROWS, 2 * FEATS)
VMEM_BYTES = 56 * 1024 * 1024
LAYER_BYTES = 63 * 1024 * 1024


def nn(a, b):
    return lax.dot_general(a, b, (((1,), (0,)), ((), ())), preferred_element_type=F32)


def nt(a, b):
    return lax.dot_general(a, b, (((1,), (1,)), ((), ())), preferred_element_type=F32)


def tn(a, b):
    return lax.dot_general(a, b, (((0,), (0,)), ((), ())), preferred_element_type=F32)


def halves(x, axis=1):
    hi = x.astype(BF)
    return jnp.concatenate([hi, (x - hi.astype(F32)).astype(BF)], axis=axis)


def iota(shape, dim):
    return lax.broadcasted_iota(I32, shape, dim)


def rows_loop(total, step, body):
    body(pl.ds(0, total), 0, total)


def pair_loop(body, straight=1):
    def one(i, carry):
        for k in range(straight):
            body(i * straight + k)
        return carry

    lax.fori_loop(0, PAIRS // straight, one, 0)


def head_ones(rows, cols, row_span, col_span):
    same = (iota((rows, cols), 0) // row_span) % 2 == iota((rows, cols), 1) // col_span
    return jnp.where(same, 1.0, 0.0).astype(BF)


def marks(pos, base, lengths_ref):
    start = jnp.int32(0)
    segment = jnp.zeros(pos.shape, I32)
    reset = jnp.zeros(pos.shape, F32)
    carry = jnp.ones(pos.shape, F32)
    for d in range(lengths_ref.shape[0]):
        segment = segment + jnp.where(pos >= start, 1, 0)
        reset = jnp.where(pos == start, 1.0, reset)
        carry = jnp.where((pos >= start) & (pos - start <= pos - base), 0.0, carry)
        start = start + lengths_ref[d]
    live = jnp.where(pos < start, 1.0, 0.0)
    segment = segment + jnp.where(pos >= start, 1, 0)
    return segment, reset, live, carry, start


def horner(coefs, t):
    acc = jnp.full_like(t, coefs[-1])
    for c in coefs[-2::-1]:
        acc = acc * t + c
    return acc


def sincos(angle):
    r = angle - jnp.round(angle * INV_TWO_PI) * TWO_PI
    t = r * r
    return r * horner([c * FEAT_SCALE for c in SIN], t), horner([c * FEAT_SCALE for c in COS], t)


def gelu_parts(x):
    t = 1.0 / (1.0 + (0.3275911 / math.sqrt(2.0)) * jnp.abs(x))
    e = jnp.exp(-0.5 * x * x)
    q = 0.5 * t * horner(ERFC, t) * e
    cdf = jnp.where(x < 0.0, q, 1.0 - q)
    return x * cdf, cdf + x * e * (1.0 / math.sqrt(2.0 * math.pi))


def norm_stats(x):
    center = jnp.mean(x, axis=-1, keepdims=True)
    spread = jnp.mean(x * x, axis=-1, keepdims=True) - center * center
    inv = lax.rsqrt(spread + EPS)
    return (x - center) * inv, inv


def norm_back(grad, xhat, inv, gain):
    p = grad * gain
    return inv * (p - jnp.mean(p, axis=-1, keepdims=True) - xhat * jnp.mean(p * xhat, axis=-1, keepdims=True))


def by_eight(x):
    return jnp.sum(x.reshape(x.shape[0] // 8, 8, x.shape[1]), axis=0)


def panel(ref, p, cols):
    x = ref[p, :, :, :, cols]
    return x.reshape(x.shape[0] * x.shape[1] * x.shape[2], x.shape[3])


def low_lanes(rows):
    return iota((rows, LANES), 1) < HEAD_DIM


def widen(pair, a):
    return pair[:, a * HEAD_DIM : a * HEAD_DIM + 1]


def head_values(v, a, low):
    one = jnp.ones_like(v)
    return jnp.where(low, v, one) if a == 0 else jnp.where(low, one, v)


def state_of(states, p, a):
    own = states[2 * p + a, 0:HEAD_DIM, :]
    rest = jnp.broadcast_to(states[2 * p + a, NORMAL : NORMAL + 1, :], own.shape)
    return jnp.concatenate([own, rest] if a == 0 else [rest, own], axis=0)


def put_state(states, h, own, normal, decay):
    states[h, 0:HEAD_DIM, :] = own
    rest = jnp.zeros((STATE_ROWS - DECAY - 1, 2 * FEATS), F32)
    states[h, NORMAL:, :] = jnp.concatenate([normal, twice(decay), rest], axis=0)


def twice(x):
    return jnp.concatenate([x, x], axis=1)


def run_pairs(body, hook, order=None, straight=1):
    def one(p):
        body(order(p) if order else p)
        for at, acts in (hook or {}).items():

            @pl.when(p == at)
            def _():
                for act, *given in acts:
                    act(*given)

    pair_loop(one, straight)


def tables(T, base, r):
    pos = base + iota((8, T), 1)
    seg_row, _, live_row, _, _ = marks(pos, base, r.lengths)
    seg1, live1, pos1 = seg_row[0:1], live_row[0:1], pos[0:1]

    def mask_rows(rows, at, n):
        row_pos = base + at + iota((n, 1), 0)
        seg_col = marks(row_pos, base, r.lengths)[0]
        allowed = (seg_col == seg1) & (pos1 <= row_pos) & (live1 > 0.0)
        r.mask[rows, :] = jnp.where(allowed, 0.0, -1e30)

    rows_loop(T, 64, mask_rows)
    hash_seed = r.seed[0] * jnp.int32(-2048144789)

    def table(p):
        place = (p * LANES + iota((LANES, LANES), 0)) * FEATS + iota((LANES, LANES), 1)
        y = place * jnp.int32(-1640531535) + hash_seed
        y = y ^ lax.shift_right_logical(y, jnp.int32(15))
        y = y * jnp.int32(739982445)
        y = y ^ lax.shift_right_logical(y, jnp.int32(13))
        y = y * jnp.int32(695872825)
        y = y ^ lax.shift_right_logical(y, jnp.int32(16))
        s = jnp.full(y.shape, -510, I32)
        for k in range(4):
            s = s + (lax.shift_right_logical(y, jnp.int32(8 * k)) & jnp.int32(255))
        top = iota((LANES, LANES), 0) < HEAD_DIM
        odd = s & 1

        def diagonal(x):
            x = x.astype(F32)
            return jnp.concatenate([jnp.where(top, x, 0.0), jnp.where(top, 0.0, x)], axis=1).astype(BF)

        r.tab[p, 0:LANES, :] = diagonal(s - odd)
        r.tab[p, LANES:, :] = diagonal(odd)
        r.tabn[p] = diagonal(s)

    pair_loop(table)


def standardise(T, base, r):
    r.xhat[...] = norm_stats(r.tok[...].astype(F32))[0]


def first_norm(T, base, r):
    for p in range(PAIRS):
        rows = r.small[p]
        r.gate[2 * p : 2 * p + 2, :] = rows[0:2]
        r.gate[8 + 2 * p : 10 + 2 * p, :] = rows[0:2]
        r.bias[2 * p : 2 * p + 1, :] = rows[6:7] + rows[7:8] + rows[8:9]
        r.bias[2 * p + 1 : 2 * p + 2, :] = rows[9:10] + rows[10:11] + rows[11:12]
        if p == 0:
            r.vec[...] = rows[0:8]

    r.normed[...] = (r.xhat[...] * r.vec[2:3, :] + r.vec[3:4, :]).astype(BF)
    logits = nt(r.gate[...].astype(BF), r.normed[...])[0:8] + r.bias[:, 0:1]
    r.logits[...] = logits
    pos = base + iota((8, T), 1)
    _, reset_row, live_row, carry_row, _ = marks(pos, base, r.lengths)
    decay = -(jnp.log1p(jnp.exp(-jnp.abs(logits))) + jnp.maximum(-logits, 0.0)) * live_row * (1.0 - reset_row)
    run = decay
    lane = iota((8, T), 1)
    shift = 1
    while shift < T:
        run = run + jnp.where(lane >= shift, pltpu.roll(run, shift, 1), 0.0)
        shift *= 2
    r.run[...] = run
    r.total[...] = jnp.broadcast_to(jnp.exp(run[:, T - 1 : T]) * carry_row[:, T - 1 : T], (8, LANES))
    hi = run.astype(BF).astype(F32)
    mid = (run - hi).astype(BF).astype(F32)
    run3 = jnp.concatenate([hi, mid, run - hi - mid, jnp.zeros_like(hi)], axis=0).astype(BF)

    def spread(p):
        chosen = iota((32, LANES), 0) % 8 == 2 * p + iota((32, LANES), 1) // HEAD_DIM
        r.rb[p] = tn(run3, jnp.where(chosen, 1.0, 0.0).astype(BF))

    pair_loop(spread, PAIRS)


def features(T, r, p, u, out):
    ones2 = head_ones(2 * LANES, 2 * LANES, HEAD_DIM, LANES)
    r.s1[...] = nn(jnp.concatenate([u, u], axis=1), r.tab[p])
    uf = u.astype(F32)
    r.s2[...] = nn(halves(uf * uf), ones2)

    def body(rows, at, n):
        s, c = sincos(r.s1[rows, :] * (lax.rsqrt(r.s2[rows, :] + 1e-6) * TABLE_SCALE))
        for a in range(2):
            out[2 * p + a, rows, 0:FEATS] = s[:, a * FEATS : (a + 1) * FEATS].astype(BF)
            out[2 * p + a, rows, FEATS : 2 * FEATS] = c[:, a * FEATS : (a + 1) * FEATS].astype(BF)

    rows_loop(T, 64, body)


def end_factor(T, base, r):
    last_seg = marks(base + T - 1 + iota((8, LANES), 1) * 0, base, r.lengths)[0][0:1, 0:1]
    seg_col, _, live_col, _, _ = marks(base + iota((T, LANES), 0), base, r.lengths)
    return jnp.where(seg_col == last_seg, live_col, 0.0)


def keys(T, base, r, hook=None):
    def pair(p):
        r.k[p] = nn(r.normed[...], panel(r.ga, p, KEY)).astype(BF)
        features(T, r, p, r.k[p], r.kf)

    run_pairs(pair, hook)


def states(T, base, r):
    end_live = end_factor(T, base, r)

    def pair(p):
        r.v[p] = nn(r.normed[...], panel(r.ga, p, VALUE)).astype(BF)
        decay_end = jnp.exp(r.rb[p, T - 1 : T, :] - r.rb[p]) * end_live
        lane = iota((T, LANES), 1)
        factor = jnp.where(lane < 2, widen(decay_end, 0), widen(decay_end, 1))
        rough = factor.astype(BF).astype(F32)
        factor = jnp.where(lane % 2 == 0, rough, factor - rough)
        ends = tn(factor.astype(BF), jnp.concatenate([r.kf[2 * p], r.kf[2 * p + 1]], axis=1))
        for a in range(2):
            h = 2 * p + a
            scaled = (r.kf[h].astype(F32) * widen(decay_end, a)).astype(BF)
            state = tn(r.v[p], scaled)[a * HEAD_DIM : (a + 1) * HEAD_DIM]
            normal = ends[2 * a : 2 * a + 1, a * 2 * FEATS : (a + 1) * 2 * FEATS]
            normal = normal + ends[2 * a + 1 : 2 * a + 2, a * 2 * FEATS : (a + 1) * 2 * FEATS]
            put_state(r.out, h, state, normal, r.total[pl.ds(h, 1), :])

    pair_loop(pair)


def queries(T, base, r, hook=None):
    low = low_lanes(T)

    def pair(p):
        r.q[p] = nn(r.normed[...], panel(r.ga, p, QUERY)).astype(BF)
        features(T, r, p, r.q[p], r.qf)
        v = r.v[p]
        for a in range(2):
            h = 2 * p + a
            r.s[...] = nt(r.qf[h], r.kf[h])
            run_row = r.run[pl.ds(h, 1), :]

            def body(rows, at, n):
                gap = jnp.minimum(widen(r.rb[p, rows, :], a) - run_row, r.mask[rows, :])
                w = r.s[rows, :] * jnp.exp(gap)
                rounded = w.astype(BF)
                r.w[h, rows, :] = rounded
                rest = jnp.sum(w - rounded.astype(F32), axis=1, keepdims=True)
                r.zfix[p, rows, a * HEAD_DIM : (a + 1) * HEAD_DIM] = jnp.broadcast_to(rest, (n, HEAD_DIM)).astype(BF)

            rows_loop(T, 64, body)
            r.own[h] = nn(r.w[h], head_values(v, a, low))

    run_pairs(pair, hook)


def carry_factor(T, base, r):
    _, _, live_col, carry_col, _ = marks(base + iota((T, LANES), 0), base, r.lengths)
    return live_col, carry_col


def attend(T, base, r):
    low = low_lanes(T)
    live_col, carry_col = carry_factor(T, base, r)

    def join(p):
        factor = jnp.exp(r.rb[p]) * carry_col
        total = []
        for a in range(2):
            h = 2 * p + a
            carried = nt(twice(r.qf[h]), halves(state_of(r.inn, p, a)))
            joined = r.own[h] + widen(factor, a) * carried
            r.joined[h] = joined
            total.append(joined)
        num = jnp.where(low, total[0], total[1])
        z = pltpu.roll(jnp.where(low, total[1], total[0]), HEAD_DIM, 1) + r.zfix[p].astype(F32)
        r.att[p] = (live_col * num * lax.rsqrt(z * z + FLOOR2)).astype(BF)

    pair_loop(join, 4)
    o = out_columns(r)
    branch = None
    for p in range(0, PAIRS, 2):
        part = nt(
            jnp.concatenate([r.att[p], r.att[p + 1]], axis=1),
            jnp.concatenate([panel(r.gf, p, o), panel(r.gf, p + 1, o)], axis=1),
        )
        branch = part if branch is None else branch + part
    r.mid[...] = branch

    def norm_rows(rows, at, n):
        mid = r.mid[rows, :] + r.tok[rows, :].astype(F32)
        r.mid[rows, :] = mid
        xhat, inv = norm_stats(mid)
        r.xhat[rows, :] = xhat
        r.inv[rows, :] = jnp.broadcast_to(inv, (n, LANES))
        r.two[rows, :] = (xhat * r.vec[4:5, :] + r.vec[5:6, :]).astype(BF)

    rows_loop(T, 64, norm_rows)


def feed_columns(r):
    ff = (r.gf.shape[-1] - LANES) // 2
    return slice(LANES + ff, LANES + 2 * ff), slice(LANES, LANES + ff)


def out_columns(r):
    return slice(0, LANES)


def cotangents(T, base, r):
    _, d = feed_columns(r)

    def part(p):
        r.h2[p] = nn(r.cot[...], panel(r.gf, p, d))

    pair_loop(part)


def feed(T, base, r):
    low = low_lanes(T)
    live_col, carry_col = carry_factor(T, base, r)
    r.acc1[...] = jnp.zeros_like(r.acc1)
    r.acc2[...] = jnp.zeros_like(r.acc2)
    u, d = feed_columns(r)
    o = out_columns(r)

    def part(p):
        up, down = panel(r.gf, p, u), panel(r.gf, p, d)
        r.h1[...] = nn(r.two[...], up)

        def body(rows, at, n):
            value, slope = gelu_parts(r.h1[rows, :])
            r.act[p, rows, :] = value.astype(BF)
            r.gh[p, rows, :] = (r.h2[p, rows, :] * slope).astype(BF)

        rows_loop(T, 64, body)
        r.acc1[...] += nt(r.act[p], down)
        r.acc2[...] += nt(r.gh[p], up)

    pair_loop(part)
    r.sums[...] = jnp.zeros_like(r.sums)

    def finish(rows, at, n):
        r.result[rows, :] = (r.mid[rows, :] + r.acc1[rows, :]).astype(BF)
        xhat, gn = r.xhat[rows, :], r.acc2[rows, :]
        r.sums[0:8, :] += by_eight(gn * xhat)
        r.sums[8:16, :] += by_eight(gn)
        back = norm_back(gn, xhat, r.inv[rows, 0:1], r.vec[4:5, :])
        grad = r.cot[rows, :].astype(F32) + back
        r.gmid[rows, :] = grad
        r.gb[rows, :] = grad.astype(BF)

    rows_loop(T, 64, finish)
    r.fsum[0:1, :] = jnp.sum(r.sums[0:8, :], axis=0, keepdims=True)
    r.fsum[1:2, :] = jnp.sum(r.sums[8:16, :], axis=0, keepdims=True)
    ones1 = head_ones(2 * LANES, LANES, HEAD_DIM, HEAD_DIM)
    row_ones = jnp.ones((16, 2 * LANES), BF)
    first_half = iota((T, LANES), 1) % HEAD_DIM < HEAD_DIM // 2

    def back(p):
        g = nn(r.gb[...], panel(r.gf, p, o)).astype(BF).astype(F32) * live_col
        total = [r.joined[2 * p], r.joined[2 * p + 1]]
        num = jnp.where(low, total[0], total[1])
        z = pltpu.roll(jnp.where(low, total[1], total[0]), HEAD_DIM, 1) + r.zfix[p].astype(F32)
        rden = lax.rsqrt(z * z + FLOOR2)
        dn = (g * rden).astype(BF).astype(F32)
        dz = nn(halves(dn * num), ones1) * (z * rden * rden)
        dz = pltpu.roll(dz * (-2.0 / HEAD_DIM), HEAD_DIM, 1)
        rough = dz.astype(BF).astype(F32)
        dz = jnp.where(first_half, rough, dz - rough)
        factor = jnp.exp(r.rb[p]) * carry_col
        for a in range(2):
            h = 2 * p + a
            joint = (jnp.where(low, dn, dz) if a == 0 else jnp.where(low, dz, dn)).astype(BF)
            r.dn[h] = joint
            r.dr[pl.ds(h, 1), :] = nt(row_ones, halves(joint.astype(F32) * total[a]))[0:1]
            adj = tn(joint, (r.qf[h].astype(F32) * widen(factor, a)).astype(BF))
            at, half = (1 - a) * HEAD_DIM, HEAD_DIM // 2
            normal = 0.5 * (adj[at : at + 1] + adj[at + half : at + half + 1])
            put_state(r.adj, h, adj[a * HEAD_DIM : (a + 1) * HEAD_DIM], normal, r.total[pl.ds(h, 1), :])

    pair_loop(back, 4)


def up_grads(T, base, r):
    up, _ = feed_columns(r)
    pair_loop(lambda p: put_panel(r.ggf, p, up, tn(r.two[...], r.gh[p])), PAIRS)


def down_grads(T, base, r):
    _, down = feed_columns(r)

    def part(p):
        put_panel(r.ggf, p, down, tn(r.cot[...], r.act[p]))
        put_panel(r.ggf, p, out_columns(r), tn(r.gb[...], r.att[p]))

    pair_loop(part, PAIRS)


def put_panel(ref, p, cols, x):
    shape = ref.shape[1:4] + (x.shape[1],)
    ref[p, :, :, :, cols] = x.astype(BF).reshape(shape)


def back(T, base, r, tokens_all, near_hook=None, between=lambda: None, far_hook=None, order=None):
    D = r.tok.shape[1]
    low = low_lanes(T)
    _, carry_col = carry_factor(T, base, r)
    end_live = end_factor(T, base, r)
    ones1 = head_ones(2 * LANES, LANES, HEAD_DIM, HEAD_DIM)
    row_ones = jnp.ones((16, 2 * LANES), BF)
    r.acc1[...] = jnp.zeros_like(r.acc1)

    def feature_back(p, u, da):
        ds = nt(da, r.tabn[p]) * TABLE_SCALE
        uf = u.astype(F32)
        inv = lax.rsqrt(nn(halves(uf * uf), ones1) + 1e-6)
        uh = uf * inv
        return (inv * (ds - uh * nn(halves(uh * ds), ones1))).astype(BF)

    def angles(rows, source, feat, h):
        x, f = source[rows, :], feat[h, rows, :].astype(F32)
        return x[:, :FEATS] * f[:, FEATS:] - x[:, FEATS:] * f[:, :FEATS]

    def near(p):
        v = r.v[p]
        factor = jnp.exp(r.rb[p]) * carry_col
        for a in range(2):
            h = 2 * p + a
            r.s[...] = nt(r.dn[h], head_values(v, a, low))
            run_row = r.run[pl.ds(h, 1), :]

            def body(rows, at, n):
                gap = jnp.minimum(widen(r.rb[p, rows, :], a) - run_row, r.mask[rows, :])
                r.ds[rows, :] = (r.s[rows, :] * jnp.exp(gap)).astype(BF)

            rows_loop(T, 64, body)
            before = halves(state_of(r.inn, p, a), 0)
            r.s1[...] = nn(r.ds[...], r.kf[h]) + widen(factor, a) * nn(twice(r.dn[h]), before)
            r.s2[...] = tn(r.ds[...], r.qf[h])
            r.ghv[h] = tn(r.w[h], r.dn[h])

            def turn(rows, at, n):
                r.da[p, rows, a * FEATS : (a + 1) * FEATS] = angles(rows, r.s1, r.qf, h).astype(BF)
                r.da[p, rows, (2 + a) * FEATS : (3 + a) * FEATS] = angles(rows, r.s2, r.kf, h).astype(BF)

            rows_loop(T, 64, turn)
        grad = feature_back(p, r.q[p], r.da[p, :, : 2 * FEATS])
        r.acc1[...] += nt(grad, panel(r.ga, p, QUERY))
        put_panel(r.gga, p, slice(2 * LANES, 3 * LANES), tn(r.normed[...], grad))

    def far(p):
        v = r.v[p]
        decay_end = jnp.exp(r.rb[p, T - 1 : T, :] - r.rb[p]) * end_live
        grad_v = []
        for a in range(2):
            h = 2 * p + a
            end, hv = state_of(r.aend, p, a), head_values(v, a, low)
            late = widen(decay_end, a) * nt(twice(r.kf[h]), halves(end))
            r.s2[...] = widen(decay_end, a) * nn(twice(hv), halves(end, 0))
            grad_hv = r.ghv[h] + late
            grad_v.append(grad_hv)

            def turn(rows, at, n):
                lanes = slice((2 + a) * FEATS, (3 + a) * FEATS)
                r.da[p, rows, lanes] = (r.da[p, rows, lanes].astype(F32) + angles(rows, r.s2, r.kf, h)).astype(BF)

            rows_loop(T, 64, turn)
            hvf = hv.astype(F32)
            k_side = nt(row_ones, halves(hvf * grad_hv))
            r.drun[pl.ds(h, 1), :] = r.dr[pl.ds(h, 1), :] - k_side[0:1]
            owed = jnp.sum(end * state_of(r.inn, p, a), axis=0, keepdims=True)
            owed = r.total[pl.ds(h, 1), 0:1] * jnp.sum(owed, axis=1, keepdims=True)
            owed = owed + jnp.sum(jnp.sum(hvf * late, axis=0, keepdims=True), axis=1, keepdims=True)
            r.owed[pl.ds(h, 1), :] = jnp.broadcast_to(owed, (1, LANES))
        grad_v = jnp.where(low, grad_v[0], grad_v[1]).astype(BF)
        grads = jnp.concatenate([feature_back(p, r.k[p], r.da[p, :, 2 * FEATS :]), grad_v], axis=1)
        r.acc1[...] += nt(grads, panel(r.ga, p, slice(0, 2 * LANES)))
        put_panel(r.gga, p, slice(0, 2 * LANES), tn(r.normed[...], grads))

    run_pairs(near, near_hook, order)
    between()
    run_pairs(far, far_hook, order)
    pos = base + iota((8, T), 1)
    _, reset_row, live_row, _, filled = marks(pos, base, r.lengths)
    lane = iota((8, T), 1)
    run = r.drun[...]
    shift = 1
    while shift < T:
        run = run + jnp.where(lane < T - shift, pltpu.roll(run, T - shift, 1), 0.0)
        shift *= 2
    grad_decay = run + r.owed[:, 0:1]
    logits = r.logits[...]
    e = jnp.exp(-jnp.abs(logits))
    small, large = e / (1.0 + e), 1.0 / (1.0 + e)
    gate = jnp.where(logits >= 0.0, large, small)
    rest = jnp.where(logits >= 0.0, small, large)
    penalty = GATE_PEN * tokens_all / HEADS / jnp.broadcast_to(filled, (8, T)).astype(F32)
    grad_logits = grad_decay * live_row * (1.0 - reset_row) * rest + penalty * live_row * gate * rest
    both = halves(grad_logits, 0)
    r.acc1[...] += tn(both, r.gate[...].astype(BF))
    gate_rows = nn(both, r.normed[...])
    gate_rows = gate_rows[0:8] + gate_rows[8:16]
    bias = jnp.broadcast_to(jnp.sum(grad_logits, axis=1, keepdims=True), (8, D))
    r.sums[...] = jnp.zeros_like(r.sums)

    def finish(rows, at, n):
        xhat, inv = norm_stats(r.tok[rows, :].astype(F32))
        gn = r.acc1[rows, :]
        r.sums[0:8, :] += by_eight(gn * xhat)
        r.sums[8:16, :] += by_eight(gn)
        r.gtok[rows, :] = r.gmid[rows, :] + norm_back(gn, xhat, inv, r.vec[2:3, :])

    rows_loop(T, 64, finish)
    norm_gain = jnp.sum(r.sums[0:8, :], axis=0, keepdims=True)
    norm_shift = jnp.sum(r.sums[8:16, :], axis=0, keepdims=True)
    lines = [norm_gain, norm_shift, r.fsum[0:2, :]]
    for p in range(PAIRS):
        rows = jnp.concatenate([gate_rows[2 * p : 2 * p + 2]] + lines + [bias[2 * p : 2 * p + 2]], axis=0)
        for g in range(D // LANES):
            r.lines[p, g] = rows[:, g * LANES : (g + 1) * LANES]


class Refs:
    def __init__(self, **refs):
        self.__dict__.update(refs)


def buffers(T, D, att, rest, ff, seq):
    z = (PAIRS, seq // 2, 2, D // seq)
    pair = (PAIRS, T, LANES)
    return {
        "ga": (z + (att,), BF), "gf": (z + (rest,), BF), "gga": (z + (att,), BF), "small": ((PAIRS, 16, D), F32), "ggf": (z + (rest,), BF),
        "gate": ((16, D), F32), "bias": ((8, D), F32), "vec": ((8, D), F32), "normed": ((T, D), BF),
        "logits": ((8, T), F32), "run": ((8, T), F32), "total": ((8, LANES), F32), "mask": ((T, T), F32),
        "s1": ((T, 2 * FEATS), F32), "s2": ((T, 2 * FEATS), F32), "s": ((T, T), F32),
        "tab": ((PAIRS, 2 * LANES, 2 * FEATS), BF), "tabn": ((PAIRS, LANES, 2 * FEATS), BF),
        "q": (pair, BF), "k": (pair, BF), "v": (pair, BF), "rb": (pair, F32),
        "qf": ((HEADS, T, 2 * FEATS), BF), "kf": ((HEADS, T, 2 * FEATS), BF),
        "out": (STATES, F32), "inn": (STATES, F32), "adj": (STATES, F32), "aend": (STATES, F32),
        "w": ((HEADS, T, T), BF), "own": ((HEADS, T, LANES), F32), "joined": ((HEADS, T, LANES), F32),
        "att": (pair, BF), "zfix": (pair, BF), "mid": ((T, D), F32), "xhat": ((T, D), F32), "inv": ((T, LANES), F32), "two": ((T, D), BF),
        "acc1": ((T, D), F32), "acc2": ((T, D), F32), "h1": ((T, ff), F32), "h2": ((PAIRS, T, ff), F32),
        "act": ((PAIRS, T, ff), BF), "gh": ((PAIRS, T, ff), BF), "sums": ((16, D), F32), "fsum": ((8, D), F32),
        "result": ((T, D), BF), "gmid": ((T, D), F32), "gb": ((T, D), BF), "dr": ((8, T), F32),
        "dn": ((HEADS, T, LANES), BF), "ds": ((T, T), BF), "da": ((PAIRS, T, 4 * FEATS), BF), "ghv": ((HEADS, T, LANES), F32),
        "lines": ((PAIRS, D // LANES, 8, LANES), F32),
        "drun": ((8, T), F32), "owed": ((8, LANES), F32), "gtok": ((T, D), F32),
    }


FRONT = (
    ("ga", "small"),
    ("gate", "vec", "normed", "logits", "run", "total", "mask", "tabn", "q", "k", "v", "rb", "qf", "kf", "out", "w", "own", "zfix"),
    ("bias", "s1", "s2", "s", "tab", "xhat"),
)
MIDDLE = (
    ("gf", "vec", "rb", "qf", "own", "zfix", "inn", "total"),
    ("ggf", "result", "gmid", "fsum", "dr", "dn", "adj"),
    ("joined", "att", "mid", "xhat", "inv", "two", "acc1", "acc2", "h1", "h2", "act", "gh", "sums", "gb"),
)
BACK = (
    ("ga", "gate", "vec", "normed", "logits", "run", "total", "mask", "tabn", "q", "k", "v", "rb", "qf", "kf",
     "w", "inn", "aend", "gmid", "fsum", "dr", "dn"),
    ("gga", "gtok", "lines"),
    ("s", "s1", "s2", "ds", "da", "ghv", "drun", "owed", "acc1", "sums"),
)
SHARED = {"joined": "own", "h1": "s", "gmid": "mid", "ds": "gb", "adj": "out", "da": "act", "ghv": "own"}


def front(T, base, r):
    tables(T, base, r)
    standardise(T, base, r)
    first_norm(T, base, r)
    keys(T, base, r)
    states(T, base, r)
    queries(T, base, r)


def middle(T, base, r):
    cotangents(T, base, r)
    attend(T, base, r)
    feed(T, base, r)
    up_grads(T, base, r)
    down_grads(T, base, r)


def here(T):
    return (lax.axis_index("seq") * lax.axis_size("head") + lax.axis_index("head")) * T


def stage(which, names, specs, outer, args, state):
    reads, writes, scratch = names
    shape = lambda n: jax.ShapeDtypeStruct(*specs[n])
    vmem, smem = pl.BlockSpec(memory_space=pltpu.VMEM), pl.BlockSpec(memory_space=pltpu.SMEM)

    def kernel(*refs):
        base_ref, lengths, seed, tok, cot = refs[:5]
        rest = dict(zip(reads + writes + scratch, refs[5:]))
        which(base_ref[0], Refs(lengths=lengths, seed=seed, tok=tok, cot=cot, **rest))

    out = pl.pallas_call(
        kernel,
        out_shape=[shape(n) for n in writes],
        in_specs=[smem] * 3 + [vmem] * (2 + len(reads)),
        out_specs=[vmem] * len(writes),
        scratch_shapes=[pltpu.VMEM(*specs[n]) for n in scratch],
        compiler_params=pltpu.CompilerParams(vmem_limit_bytes=VMEM_BYTES),
        name=outer,
    )(*args, *[state[n] for n in reads])
    state.update(zip(writes, out))


def scan_states(out, reverse):
    seq, head = lax.axis_size("seq"), lax.axis_size("head")
    count = seq * head
    me = lax.axis_index("seq") * head + lax.axis_index("head")
    state = (out[:, DECAY : DECAY + 1, 0:1], out[:, :DECAY])
    step = 1
    order = lambda pairs: [(b, a) for a, b in pairs] if reverse else pairs
    axes = ("seq", "head")
    while step < count:
        moved = jax.tree.map(lambda x: lax.ppermute(x, axes, order([(i, i + step) for i in range(count - step)])), state)
        has = (me < count - step) if reverse else (me >= step)
        f, m = state
        state = (jnp.where(has, f * moved[0], f), m + jnp.where(has, f * moved[1], 0.0))
        step *= 2
    moved = lax.ppermute(state[1], axes, order([(i, i + 1) for i in range(count - 1)]))
    return jnp.concatenate([moved, jnp.zeros((HEADS, STATE_ROWS - DECAY, 2 * FEATS), F32)], axis=1)


def remote(src, dst, send, recv, to):
    return pltpu.make_async_remote_copy(
        src_ref=src, dst_ref=dst, send_sem=send, recv_sem=recv, device_id=to, device_id_type=MESH
    )


class Place:
    def __init__(self):
        self.seq, self.head = lax.axis_size("seq"), lax.axis_size("head")
        s, h = lax.axis_index("seq"), lax.axis_index("head")
        self.z, self.y, self.x, self.c = s // 2, s % 2, h // 2, h % 2
        self.depth = self.seq // 2
        self.count = self.seq * self.head
        self.me = s * self.head + h

    def device(self, z=None, y=None, x=None, c=None):
        pick = lambda given, own: own if given is None else given
        z, y, x, c = pick(z, self.z), pick(y, self.y), pick(x, self.x), pick(c, self.c)
        return (z * 2 + y, x * 2 + c)

    def number(self, i):
        return (i // self.head, i % self.head)

    def around(self, k):
        return (self.z + k) % self.depth

class Semaphores:
    def __init__(self, send, recv):
        self.send, self.recv, self.used = send, recv, 0

    def copy(self, src, dst, to):
        i = self.used
        self.used += 1
        return remote(src, dst, self.send.at[i], self.recv.at[i], to)


GATHER_COPIES = 2 * (3 + 1 + 2 + 2)
SCATTER_COPIES = 2 + 2 * (1 + 1 + 3)


def gather_stages(place, g, lanes, sems):
    half = g.shape[3] // 2
    z, y, x, c = place.z, place.y, place.x, place.c
    pair = x * 2 + c
    stages = [[], [], [], []]
    for part in range(2):
        rows = pl.ds(part * half, half)
        same = lambda ref, to: sems.copy(ref, ref, to)
        for k in range(1, place.depth):
            stages[0].append(same(g.at[pair, z, y, rows, lanes], place.device(z=place.around(k))))
        to_y, to_x = place.device(y=1 - y), place.device(x=1 - x)
        if part == 0:
            stages[1].append(same(g.at[pair, :, y, rows, lanes], to_y))
            stages[2].append(same(g.at[pair, :, :, rows, lanes], to_x))
        else:
            stages[1].append(same(g.at[pair, :, y, rows, lanes], to_x))
            for other in range(2):
                stages[2].append(same(g.at[other * 2 + c, :, y, rows, lanes], to_y))
        for other in range(2):
            stages[3].append(same(g.at[other * 2 + c, :, :, rows, lanes], place.device(c=1 - c)))
    return stages


def begin(stage):
    for copy in stage:
        copy.start()


def arrived(stage):
    for copy in stage:
        copy.wait_recv()


def sent(*stages):
    for stage in stages:
        for copy in stage:
            copy.wait_send()


class Gather:
    def __init__(self, place, ga, gf, gs, sems):
        ff = (gf.shape[-1] - LANES) // 2
        lanes = lambda first, count: pl.ds(first, count)
        self.chunks = [
            gather_stages(place, ref, part, sems)
            for ref, part in (
                (ga, lanes(0, LANES)),
                (ga, lanes(LANES, 2 * LANES)),
                (gf, lanes(0, LANES + ff)),
                (gf, lanes(LANES + ff, ff)),
            )
        ]

        z, y, x, c, pair = place.z, place.y, place.x, place.c, place.x * 2 + place.c
        first, same = self.chunks[0], lambda ref, **to: sems.copy(ref, ref, place.device(**to))
        first[0] += [same(gs.at[pair, z, y], z=place.around(k)) for k in range(1, place.depth)]
        first[1].append(same(gs.at[pair, :, y], y=1 - y))
        first[2].append(same(gs.at[pair], x=1 - x))
        first[3] += [same(gs.at[other * 2 + c], c=1 - c) for other in range(2)]

    def begin(self, chunk):
        begin(self.chunks[chunk][0])

    def step(self, chunk, stage):
        arrived(self.chunks[chunk][stage])
        if stage < 3:
            begin(self.chunks[chunk][stage + 1])

    def finish(self):
        for chunk in self.chunks:
            sent(*chunk)


def add_blocks(to, others, count, where):
    def one(i, carry):
        at = where(i)
        total = to[at].astype(F32)
        for ref, index in others:
            total = total + ref[index(i)].astype(F32)
        to[at] = total.astype(to.dtype)
        return carry

    lax.fori_loop(0, count, one, 0)


class Scatter:
    def __init__(self, place, gg, lanes, out, buf, sems):
        self.place, self.gg, self.lanes, self.out = place, gg, lanes, out
        self.r1, self.r2a, self.r2b, self.r3a, self.r3b, self.r4a, self.r4b = buf
        z, y, x, c, n = place.z, place.y, place.x, place.c, place.depth
        self.half = half = gg.shape[3] // 2
        first, last = pl.ds(0, half), pl.ds(half, half)
        other, to_y, to_x = place.device(c=1 - c), place.device(y=1 - y), place.device(x=1 - x)
        self.stages = [
            [sems.copy(gg.at[i * 2 + 1 - c, :, :, :, lanes], self.r1.at[i], other) for i in range(2)],
            [
                sems.copy(self.r1.at[1 - x, :, :, first], self.r2a, to_x),
                sems.copy(self.r1.at[:, :, 1 - y, last], self.r2b, to_y),
            ],
            [sems.copy(self.r2a.at[:, 1 - y], self.r3a, to_y), sems.copy(self.r2b.at[1 - x], self.r3b, to_x)],
            [
                sems.copy(ref.at[place.around(k)], slots.at[k - 1], place.device(z=place.around(k)))
                for ref, slots in ((self.r3a, self.r4a), (self.r3b, self.r4b))
                for k in range(1, n)
            ],
        ]

    def start(self):
        begin(self.stages[0])

    def step(self, i):
        place, n, half = self.place, self.place.depth, self.half
        y, x, c = place.y, place.x, place.c
        first, last = slice(0, half), slice(half, 2 * half)
        lanes = self.lanes
        arrived(self.stages[i])
        if i == 0:
            block = lambda j: (j // (2 * n), (j // 2) % n, j % 2)
            add_blocks(self.r1, [(self.gg, lambda j: ((j // (2 * n)) * 2 + c, (j // 2) % n, j % 2, slice(None), lanes))], 4 * n, block)
        elif i == 1:
            add_blocks(self.r2a, [(self.r1, lambda j: (x, j // 2, j % 2, first))], 2 * n, lambda j: (j // 2, j % 2))
            add_blocks(self.r2b, [(self.r1, lambda j: (j // n, j % n, y, last))], 2 * n, lambda j: (j // n, j % n))
        elif i == 2:
            add_blocks(self.r3a, [(self.r2a, lambda j: (j, y))], n, lambda j: (j,))
            add_blocks(self.r3b, [(self.r2b, lambda j: (x, j))], n, lambda j: (j,))
        else:
            for ref, slots, rows in ((self.r3a, self.r4a, first), (self.r3b, self.r4b, last)):
                total = ref[place.z].astype(F32)
                for k in range(n - 1):
                    total = total + slots[k].astype(F32)
                self.out[rows, lanes] = total
        if i < 3:
            begin(self.stages[i + 1])

    def finish(self):
        sent(*self.stages)


def scatter_buffers(seq, rows, cols):
    n, half = seq // 2, rows // 2
    return [
        pltpu.VMEM(shape + (cols,), BF)
        for shape in ((2, n, 2, rows), (n, 2, half), (2, n, half), (n, half), (n, half), (n - 1, half), (n - 1, half))
    ]


class Scan:
    def __init__(self, place, reverse, out, inn, box, planes, send, recv):
        self.place, self.reverse = place, reverse
        self.out, self.inn, self.planes = out, inn, planes
        self.pair, self.chip, self.box, self.back = box
        self.chips = HEADS // 2
        self.mine = place.y * 2 + place.x
        self.half, self.rest = place.c * self.chips, (1 - place.c) * self.chips
        self.sems = Semaphores(send, recv)
        other = place.device(c=1 - place.c)
        at = lambda ref, first: ref.at[pl.ds(first, self.chips)]
        near = [lax.rem(self.mine + k, self.chips) for k in range(1, self.chips)]
        chip = lambda m: place.device(y=m // 2, x=m % 2)
        total = planes.at[place.z]
        copy = self.sems.copy
        self.ways = [
            [copy(at(out, self.rest), self.pair, other)],
            [copy(self.chip.at[m], self.box.at[self.mine], chip(m)) for m in near],
            [copy(total, total, place.device(z=place.around(k))) for k in range(1, place.depth)],
            [copy(self.box.at[m], self.back.at[self.mine], chip(m)) for m in near],
            [copy(self.pair, at(inn, self.half), other)],
        ]

    def start(self):
        begin(self.ways[0])

    def chain(self, ref, count):
        kept = iota((STATE_ROWS, 2 * FEATS), 0) != DECAY
        state = jnp.where(kept, 0.0, 1.0)
        for i in range(count):
            d = count - 1 - i if self.reverse else i
            term = ref[d]
            ref[d] = state
            state = state * term[DECAY : DECAY + 1, :] + jnp.where(kept, term, 0.0)
        return state

    def earlier_is_mine(self):
        return (self.place.c == 0) != self.reverse

    def cores(self):
        arrived(self.ways[0])
        kept = iota((STATE_ROWS, 2 * FEATS), 0) != DECAY
        first = jnp.broadcast_to(self.earlier_is_mine(), kept.shape)
        for i in range(self.chips):
            mine, its = self.out[self.half + i], self.pair[i]
            early, late = jnp.where(first, mine, its), jnp.where(first, its, mine)
            self.chip[i] = early * late[DECAY : DECAY + 1, :] + jnp.where(kept, late, 0.0)
        begin(self.ways[1])
        self.box[self.mine] = self.chip[self.mine]

    def plane(self):
        arrived(self.ways[1])
        self.planes[self.place.z] = self.chain(self.box, self.chips)
        begin(self.ways[2])

    def line(self):
        arrived(self.ways[2])
        sent(self.ways[2])
        self.chain(self.planes, self.place.depth)
        before = self.planes[self.place.z]
        for m in range(self.chips):
            own = self.box[m]
            self.box[m] = own + own[DECAY : DECAY + 1, :] * before
        begin(self.ways[3])
        self.back[self.mine] = self.box[self.mine]

    def share(self):
        arrived(self.ways[3])
        sent(self.ways[0])
        first = jnp.broadcast_to(self.earlier_is_mine(), (STATE_ROWS, 2 * FEATS))
        for i in range(self.chips):
            mine, its, before = self.out[self.half + i], self.pair[i], self.back[i]
            early = jnp.where(first, mine, its)
            late = before * early[DECAY : DECAY + 1, :] + early
            self.inn[self.half + i] = jnp.where(first, before, late)
            self.pair[i] = jnp.where(first, late, before)
        begin(self.ways[4])

    def receive(self):
        arrived(self.ways[4])

    def finish(self):
        sent(self.ways[1], self.ways[3], self.ways[4])


class Lines:
    def __init__(self, place, lines, out, buf, sems):
        self.place, self.lines, self.out = place, lines, out
        self.l1, self.l2, self.l3, self.l4 = buf
        z, y, x, c, copy = place.z, place.y, place.x, place.c, sems.copy
        around = range(1, place.depth)
        self.stages = [
            [copy(lines.at[i * 2 + 1 - c], self.l1.at[i], place.device(c=1 - c)) for i in range(2)],
            [copy(self.l1.at[1 - x], self.l2, place.device(x=1 - x))],
            [copy(self.l2, self.l3, place.device(y=1 - y))],
            [copy(self.l3.at[place.around(k)], self.l4.at[k - 1], place.device(z=place.around(k))) for k in around],
        ]

    def start(self):
        begin(self.stages[0])

    def step(self, i):
        place = self.place
        arrived(self.stages[i])
        if i == 0:
            for j in range(2):
                self.l1[j] += self.lines[j * 2 + place.c]
        elif i == 1:
            self.l2[...] += self.l1[place.x]
        elif i == 2:
            self.l3[...] += self.l2[...]
        else:
            total = self.l3[place.z]
            for k in range(place.depth - 1):
                total = total + self.l4[k]
            self.out[...] = total
        if i < 3:
            begin(self.stages[i + 1])

    def finish(self):
        sent(*self.stages)


LINES_COPIES = 2 + 1 + 1 + 3


def greet(place):
    x, y = 1 - place.x, 1 - place.y
    near = [place.device(c=1 - place.c), place.device(x=x), place.device(y=y), place.device(x=x, y=y)]
    near += [place.device(z=place.around(k)) for k in range(1, place.depth)]
    barrier = pltpu.get_barrier_semaphore()
    for device in near:
        pl.semaphore_signal(barrier, inc=1, device_id=device, device_id_type=MESH)
    return lambda: pl.semaphore_wait(barrier, len(near))


def pack(place, r, key, value, query, gate, vectors, bias, up, out, down):
    at = (place.x * 2 + place.c, place.z, place.y)
    rows, ff = key.shape[0], up.shape[1]
    r.gf[at + (slice(None), slice(LANES + ff, None))] = up[...]
    r.gf[at + (slice(None), slice(0, LANES))] = out[...]
    r.gf[at + (slice(None), slice(LANES, LANES + ff))] = down[...]
    r.ga[at + (slice(None), KEY)] = key[...]
    r.ga[at + (slice(None), VALUE)] = value[...]
    r.ga[at + (slice(None), QUERY)] = query[...]
    lines = [gate[...].astype(F32)] + [v[...].astype(F32) for v in vectors]
    for j in range(2):
        left = jnp.full((1, rows), bias[j], F32)
        for _ in range(3):
            piece = left.astype(BF).astype(F32)
            lines.append(piece)
            left = left - piece
    lines = jnp.concatenate(lines + [jnp.zeros((4, rows), F32)], axis=0).astype(BF)
    wide = jnp.where(iota((rows, LANES), 0) == iota((rows, LANES), 1), 1.0, 0.0).astype(BF)
    r.gs[at] = nn(lines, wide).astype(BF)


def spread_small(r):
    for p in range(PAIRS):
        for z in range(r.gs.shape[1]):
            even, odd = r.gs[p, z, 0].astype(F32), r.gs[p, z, 1].astype(F32)
            tile = jnp.where(low_lanes(16), even, pltpu.roll(odd, HEAD_DIM, 1))
            r.small[p, :, z * LANES : (z + 1) * LANES] = tile


def unpack_kernel(half, grad_a, grad_f, lines, result, gtok, *outs):
    out = dict(zip(OUTPUTS, outs))
    rows = grad_a.shape[0]
    ff = (grad_f.shape[1] - LANES) // 2
    out["result"][...] = result[...]
    out["tokens"][...] = gtok[...]
    for i, name in enumerate(("key", "value", "query")):
        out[name][...] = grad_a[:, i * LANES : (i + 1) * LANES]
    out["up"][...] = grad_f[:, LANES + ff :]
    out["out"][...] = grad_f[:, :LANES]
    out["down"][...] = grad_f[:, LANES : LANES + ff]
    own = jnp.where(half == 0, lines[:, :rows], lines[:, rows : 2 * rows])
    for i, name in enumerate(("norm_gain", "norm_shift", "ffn_gain", "ffn_shift")):
        out[name][...] = own[2 + i : 3 + i, :]
    out["gate"][...] = own[0:2, :]
    out["bias"][...] = jnp.where(iota((1, LANES), 1) == 0, lines[6:7, :], lines[7:8, :])[:, 0:2]


OUTPUTS = ("result", "tokens", "norm_gain", "norm_shift", "query", "key", "value", "gate", "bias", "out", "ffn_gain",
           "ffn_shift", "up", "down")


def layer_kernel(names, tokens_all, T, lengths, seed, bias, tok_in, cot_in, key, value, query, gate, *given):
    vectors, (up, out, down), given = given[0:4], given[4:7], given[7:]
    (result_out, gtok_out, grad_a, grad_f, grad_lines), scratch = given[:5], given[5:]
    (tok, cot, result, gtok, moves), scratch = scratch[:5], scratch[5:]
    moves = [pltpu.make_async_copy(src, dst, moves.at[i]) for i, (src, dst) in enumerate(
        ((tok_in, tok), (cot_in, cot), (result, result_out), (gtok, gtok_out)))]
    moves[0].start()
    moves[1].start()
    place = Place()
    base = place.me * T
    arrays = dict(zip(names, scratch))
    arrays.update({name: arrays[other] for name, other in SHARED.items()})
    scratch = scratch[len(names) :]
    r = Refs(lengths=lengths, seed=seed, tok=tok, cot=cot, result=result, gtok=gtok, xhat=gtok, **arrays)
    sums, scratch = [scratch[7 * i : 7 * i + 7] for i in range(4)], scratch[28:]
    boxes, planes, line_box, sems = (scratch[0:4], scratch[4:8]), scratch[8:10], scratch[10:14], scratch[14:]
    meet = greet(place)
    pack(place, r, key, value, query, gate, vectors, bias, up, out, down)
    gather = Gather(place, r.ga, r.gf, r.gs, Semaphores(sems[0], sems[1]))
    forth = Scan(place, False, r.out, r.inn, boxes[0], planes[0], sems[2], sems[3])
    home = Scan(place, True, r.adj, r.aend, boxes[1], planes[1], sems[4], sems[5])
    later = Semaphores(sems[6], sems[7])
    up, down = feed_columns(r)
    sum_u = Scatter(place, r.ggf, up, grad_f, sums[0], later)
    sum_d = Scatter(place, r.ggf, slice(0, down.stop), grad_f, sums[1], later)
    sum_q = Scatter(place, r.gga, slice(2 * LANES, 3 * LANES), grad_a, sums[2], later)
    sum_k = Scatter(place, r.gga, slice(0, 2 * LANES), grad_a, sums[3], later)
    lines = Lines(place, r.lines, grad_lines, line_box, later)
    meet()

    g = gather.step
    others_first = lambda i: (i % 2) * 2 + jnp.where(i < 2, 1 - place.c, place.c)
    gather.begin(0)
    tables(T, base, r)
    g(0, 0)
    gather.begin(1)
    g(0, 1)
    g(1, 0)
    gather.begin(2)
    g(0, 2)
    g(1, 1)
    moves[0].wait()
    standardise(T, base, r)
    g(0, 3)
    spread_small(r)
    first_norm(T, base, r)
    g(2, 0)
    gather.begin(3)
    keys(T, base, r, {0: [(g, 1, 2)], 3: [(g, 2, 1), (g, 1, 3)]})
    states(T, base, r)
    forth.start()
    queries(T, base, r, {0: [(forth.cores,)], 1: [(g, 3, 0)], 2: [(forth.plane,)], 3: [(g, 2, 2), (g, 3, 1)]})
    g(2, 3)
    moves[1].wait()
    cotangents(T, base, r)
    forth.line()
    g(3, 2)
    forth.share()
    g(3, 3)
    forth.receive()
    forth.finish()
    attend(T, base, r)
    feed(T, base, r)
    home.start()
    moves[2].start()
    up_grads(T, base, r)
    sum_u.start()
    home.cores()
    down_grads(T, base, r)
    sum_d.start()
    near = {0: [(home.plane,), (sum_u.step, 0)], 2: [(home.line,)],
            3: [(sum_u.step, 1), (sum_q.start,), (home.share,), (sum_d.step, 0)]}
    far = {0: [(sum_q.step, 0)], 1: [(sum_k.start,), (sum_u.step, 2)], 2: [(sum_d.step, 1), (sum_q.step, 1)],
           3: [(sum_k.step, 0)]}
    back(T, base, r, tokens_all, near, home.receive, far, others_first)
    moves[3].start()
    lines.start()
    sum_q.step(2)
    sum_d.step(2)
    sum_k.step(1)
    lines.step(0)
    sum_u.step(3)
    lines.step(1)
    sum_k.step(2)
    lines.step(2)
    sum_q.step(3)
    sum_d.step(3)
    sum_k.step(3)
    lines.step(3)
    gather.finish()
    home.finish()
    moves[2].wait()
    moves[3].wait()
    for each in (sum_u, sum_d, sum_q, sum_k, lines):
        each.finish()


def layer_near(lengths, seed, tokens, cotangent, weights, specs, seq, head):
    T, D = tokens.shape
    count = seq * head
    rows, ff = D // seq, specs["act"][0][2]
    held = [n for n in dict.fromkeys(sum((sum(names, ()) for names in (FRONT, MIDDLE, BACK)), ())) if n not in SHARED]
    held = [n for n in held if n not in ("result", "gtok", "xhat")]
    dma = pltpu.SemaphoreType.DMA
    specs = dict(specs, gs=((PAIRS, seq // 2, 2, 16, LANES), BF))
    held.append("gs")
    wide = lambda kind: pltpu.VMEM((T, D), kind)
    scratch = [wide(BF), wide(BF), wide(BF), wide(F32), dma((4,))]
    scratch += [pltpu.VMEM(*specs[n]) for n in held]
    panels = 3 * LANES
    widths = (ff, LANES + ff, LANES, 2 * LANES)
    states = lambda count: pltpu.VMEM((count,) + STATES[1:], F32)
    for width in widths:
        scratch += scatter_buffers(seq, rows, width)
    scratch += [states(HEADS // 2)] * 8 + [states(seq // 2)] * 2
    tiles = lambda *lead: pltpu.VMEM(lead + (8, LANES), F32)
    scratch += [tiles(2, D // LANES), tiles(D // LANES), tiles(D // LANES), tiles(seq // 2 - 1)]
    scratch += [dma((5 * GATHER_COPIES,))] * 2 + [dma((16,))] * 4 + [dma((4 * SCATTER_COPIES + LINES_COPIES,))] * 2
    vmem, smem = pl.BlockSpec(memory_space=pltpu.VMEM), pl.BlockSpec(memory_space=pltpu.SMEM)
    shape, far = jax.ShapeDtypeStruct, pl.BlockSpec(memory_space=pl.ANY)
    result, gtok, grad_a, grad_f, lines = pl.pallas_call(
        functools.partial(layer_kernel, held, T * count, T),
        out_shape=[shape((T, D), BF), shape((T, D), F32), shape((rows, panels), F32), shape((rows, 2 * ff + LANES), F32),
                   shape((8, LANES), F32)],
        in_specs=[smem] * 3 + [far] * 2 + [vmem] * 11,
        out_specs=[far] * 2 + [vmem] * 3,
        scratch_shapes=scratch,
        compiler_params=pltpu.CompilerParams(collective_id=0, has_side_effects=True, vmem_limit_bytes=LAYER_BYTES),
        name="layer",
    )(lengths, seed, weights[0], tokens, cotangent, *weights[1:])
    line, square = shape((1, rows), F32), shape((rows, LANES), F32)
    shapes = (shape((T, D), BF), shape((T, D), F32), line, line, square, square, square, shape((2, rows), F32),
              shape((1, 2), F32), square, line, line, shape((rows, ff), F32), shape((rows, ff), F32))

    def unpacked(*refs):
        unpack_kernel(lax.axis_index("seq") % 2, *refs)

    outs = pl.pallas_call(
        unpacked,
        out_shape=shapes,
        in_specs=[vmem] * 5,
        out_specs=[vmem] * len(shapes),
        compiler_params=pltpu.CompilerParams(vmem_limit_bytes=VMEM_BYTES),
        name="unpack",
    )(grad_a, grad_f, lines, result, gtok)
    flat = ("norm_gain", "norm_shift", "bias", "ffn_gain", "ffn_shift")
    turned = ("gate", "out", "down")
    return tuple(x.reshape(-1) if n in flat else x.T if n in turned else x for n, x in zip(OUTPUTS, outs))


def bias_columns(gate_bias):
    hi = lax.reduce_precision(gate_bias, 8, 7)
    mid = lax.reduce_precision(gate_bias - hi, 8, 7)
    return jnp.stack([hi, mid, gate_bias - hi - mid], axis=1).astype(BF)


def gather_any(q, k, v, gate, vectors, bias, out, up, down, seq):
    D = q.shape[0] * seq

    def whole(w, rows, cols):
        w = lax.all_gather(w, rows, axis=0, tiled=True)
        return lax.all_gather(w, cols, axis=1, tiled=True)

    def panels(w):
        return w.reshape(D, PAIRS, w.shape[1] // PAIRS).transpose(1, 0, 2)

    q, k, v = (panels(whole(w, "seq", "head")) for w in (q, k, v))
    gates = panels(whole(gate, "seq", "head"))
    lines = [jnp.broadcast_to(lax.all_gather(w, "seq", tiled=True)[None, :, None], (PAIRS, D, 1)) for w in vectors]
    bias = bias_columns(lax.all_gather(bias, "head", tiled=True)).reshape(PAIRS, 1, 6)
    ga = jnp.concatenate([k, v, q], axis=2)
    rows = [gates.transpose(0, 2, 1)] + [w.transpose(0, 2, 1) for w in lines]
    rows += [jnp.broadcast_to(bias.transpose(0, 2, 1), (PAIRS, 6, D)), jnp.zeros((PAIRS, 4, D), BF)]
    small = jnp.concatenate(rows, axis=1).astype(F32)
    gf = [panels(whole(out, "head", "seq").T), panels(whole(down, "head", "seq").T), panels(whole(up, "seq", "head"))]
    gf = jnp.concatenate(gf, axis=2)
    shape = (PAIRS, seq // 2, 2, D // seq)
    return ga.reshape(shape + ga.shape[2:]), gf.reshape(shape + gf.shape[2:]), small


def scatter_any(gga, ggf, lines, ff):
    gga, ggf = (x.reshape(PAIRS, -1, x.shape[-1]).astype(F32) for x in (gga, ggf))

    def grid(x):
        x = x.transpose(1, 0, 2).reshape(x.shape[1], -1)
        x = lax.psum_scatter(x, "seq", scatter_dimension=0, tiled=True)
        return lax.psum_scatter(x, "head", scatter_dimension=1, tiled=True)

    block = lambda i: gga[:, :, i * LANES : (i + 1) * LANES]
    lines = lines.transpose(0, 2, 1, 3).reshape(PAIRS, 8, -1)
    gates = lines[:, 0:2].transpose(0, 2, 1)
    bias = lines[:, 6:8, 0].reshape(HEADS)
    bias = lax.psum_scatter(lax.psum(bias, "seq"), "head", scatter_dimension=0, tiled=True)
    lines = lax.psum_scatter(lax.psum(lines[0, 2:6].T, "head"), "seq", scatter_dimension=0, tiled=True)
    return (
        lines[:, 0], lines[:, 1], grid(block(2)), grid(block(0)), grid(block(1)), grid(gates), bias,
        grid(ggf[:, :, :LANES]).T, lines[:, 2], lines[:, 3], grid(ggf[:, :, LANES + ff :]),
        grid(ggf[:, :, LANES : LANES + ff]).T,
    )


def shards(
    tokens, lengths, feature_seed, norm_gain, norm_shift, query_weight, key_weight, value_weight, gate_weight, gate_bias,
    out_weight, ffn_gain, ffn_shift, up_weight, down_weight, cotangent,
):
    seq, head = lax.axis_size("seq"), lax.axis_size("head")
    T, D = tokens.shape
    rows = D // seq
    ff = up_weight.shape[1] * head // PAIRS
    vectors = (norm_gain, norm_shift, ffn_gain, ffn_shift)
    specs = buffers(T, D, ATT, LANES + 2 * ff, ff, seq)
    if (seq, head) == (HEADS, PAIRS):
        weights = (gate_bias, key_weight, value_weight, query_weight, gate_weight.T)
        weights += tuple(w.reshape(1, rows) for w in vectors) + (up_weight, out_weight.T, down_weight.T)
        return layer_near(lengths, feature_seed, tokens, cotangent, weights, specs, seq, head)
    ga, gf, small = gather_any(query_weight, key_weight, value_weight, gate_weight, vectors, gate_bias, out_weight, up_weight,
                        down_weight, seq)
    args = (here(T).astype(I32).reshape(1), lengths, feature_seed, tokens, cotangent)
    state = {"ga": ga, "gf": gf, "small": small}
    stage(lambda base, r: front(T, base, r), FRONT, specs, "front", args, state)
    state["inn"] = scan_states(state["out"], False)
    stage(lambda base, r: middle(T, base, r), MIDDLE, specs, "middle", args, state)
    state["aend"] = scan_states(state["adj"], True)
    stage(lambda base, r: back(T, base, r, T * seq * head), BACK, specs, "back", args, state)
    return (state["result"], state["gtok"]) + scatter_any(state["gga"], state["ggf"], state["lines"], ff)


def solution(mesh):
    both, rows, grid = P(("seq", "head"), None), P("seq"), P("seq", "head")
    return jax.shard_map(
        shards,
        mesh=mesh,
        in_specs=(both, P(), P(), rows, rows, grid, grid, grid, grid, P("head"), P("head", "seq"), rows, rows, grid,
                  P("head", "seq"), both),
        out_specs=(both, both, rows, rows, grid, grid, grid, grid, P("head"), P("head", "seq"), rows, rows, grid,
                   P("head", "seq")),
        check_vma=False,
    )
```
